32 devices in a mesh: dp: 8 (over z, x), blk: 4 (over y, core).
Axes of the slice: x: 2, y: 2, z: 4, core: 2. Of those that a mesh axis runs over, the one named last changes fastest.
Arguments:
- inputs: bfloat16 [8, 512, 768], P('dp', 'blk'), may hold values from -6 to 6
- doc_lengths: int32 [8, 8], P('dp'), may hold values from 1 to 505, as said below
- project_in: bfloat16 [768, 2304], P(('dp', 'blk')), may hold values from -0.3125 to 0.3125
- project_out: bfloat16 [768, 768], P(('dp', 'blk')), may hold values from -0.875 to 0.875
- gate_weight: bfloat16 [768, 3072], P(('dp', 'blk')), may hold values from -0.21875 to 0.21875
- up_weight: bfloat16 [768, 3072], P(('dp', 'blk')), may hold values from -0.21875 to 0.21875
- down_weight: bfloat16 [3072, 768], P(('dp', 'blk')), may hold values from -0.15625 to 0.15625
- first_gain: bfloat16 [768], P(('dp', 'blk')), may hold values from 0.099609375 to 1.8984375
- first_bias: bfloat16 [768], P(('dp', 'blk')), may hold values from -1.5 to 1.5
- second_gain: bfloat16 [768], P(('dp', 'blk')), may hold values from 0.099609375 to 1.8984375
- second_bias: bfloat16 [768], P(('dp', 'blk')), may hold values from -1.5 to 1.5
- cotangent: bfloat16 [8, 512, 768], P('dp', 'blk'), may hold values from -6 to 6
Outputs:
- outputs: bfloat16 [8, 512, 768], P('dp', 'blk')
- input_grad: bfloat16 [8, 512, 768], P('dp', 'blk')
- project_in_grad: float32 [768, 2304], P(('dp', 'blk'))
- project_out_grad: float32 [768, 768], P(('dp', 'blk'))
- gate_grad: float32 [768, 3072], P(('dp', 'blk'))
- up_grad: float32 [768, 3072], P(('dp', 'blk'))
- down_grad: float32 [3072, 768], P(('dp', 'blk'))
- first_gain_grad: float32 [768], P(('dp', 'blk'))
- first_bias_grad: float32 [768], P(('dp', 'blk'))
- second_gain_grad: float32 [768], P(('dp', 'blk'))
- second_bias_grad: float32 [768], P(('dp', 'blk'))
The draws below stay inside these ranges and needn't reach their ends.
Inputs may be any that keep to these rules, and one draw needn't show every extreme that they name: `doc_lengths`: each row's entries sum to 512; entries 0 to 6 are document lengths in order and entry 7 counts padding at the row's end, 1 or more; document 1 starts within the row's first 128 positions and ends within its last 128; in some row every entry but document 1 is 1.
All inputs are finite; a program needn't handle non-finite values.
Results may differ from the reference program's by a relative error of at most 0.024.
Values may be sent and summed in bfloat16 or wider, within the bound.
A program may use at most 128 MiB of HBM per device.

```python
import jax
import jax.numpy as jnp
from jax import lax

D = 768
HEADS = 12
FF = 3072
TOK_DEV = 128
DOCS = 8
ROWS = 8
ROW_LEN = 512


def draw_doc_lengths(key, part):
    key = jax.random.fold_in(key, 7)
    key_first, key_padding, key_tail, key_cuts, key_pick = jax.random.split(key, 5)
    tail_docs = DOCS - 3
    chosen = jax.random.randint(key_pick, (), 0, ROWS)
    forced = (jnp.arange(ROWS, dtype=jnp.int32) == chosen)[:, None]
    first_doc = jax.random.randint(key_first, (ROWS, 1), 1, TOK_DEV // 2 + 1)
    first_doc = jnp.where(forced, 1, first_doc)
    padding = jax.random.randint(key_padding, (ROWS, 1), 1, TOK_DEV // 4 + 1)
    padding = jnp.where(forced, 1, padding)
    tail_total = jax.random.randint(key_tail, (ROWS, 1), tail_docs, TOK_DEV // 2 + 1)
    tail_total = jnp.where(forced, tail_docs, tail_total)
    cut_points = jnp.sort(jax.random.randint(key_cuts, (ROWS, tail_docs - 1), 0, tail_total - tail_docs + 1), axis=1)
    boundaries = jnp.concatenate([jnp.zeros((ROWS, 1), jnp.int32), cut_points, tail_total - tail_docs], axis=1)
    tail_lengths = boundaries[:, 1:] - boundaries[:, :-1] + 1
    middle = ROW_LEN - first_doc - padding - tail_total
    return jnp.concatenate([first_doc, middle, tail_lengths, padding], axis=1).astype(jnp.int32)


def spiked(drawn, own_key, source, target, shards_of, factor):
    def block_of(dim):
        return (jnp.arange(drawn.shape[dim]) // (drawn.shape[dim] // shards_of)).reshape((-1,) + (1,) * (drawn.ndim - 1 - dim))

    near = jax.random.permutation(own_key, shards_of)[block_of(target)]
    other_side = (block_of(target) + shards_of // 2) % shards_of
    return jnp.where((block_of(source) == near) | (block_of(source) == other_side), factor * drawn, drawn)


def levels(own_key, dims, pieces, low, top_value):
    def one(dim, shards_of):
        draws = jax.random.uniform(jax.random.fold_in(jax.random.fold_in(own_key, 6), dim), (shards_of,), jnp.float32, low / len(pieces), top_value / len(pieces))
        return jnp.repeat(jnp.exp(draws), dims[dim] // shards_of).reshape((-1,) + (1,) * (len(dims) - dim - 1))

    level = one(*pieces[0])
    for cut in pieces[1:]:
        level = level * one(*cut)
    return level


def centred(stream_key, shape, scale, bound, cuts=(), kind=jnp.bfloat16):
    loudness = levels(stream_key, shape, cuts, -0.22, 0.18) if cuts else 1.0
    array = jax.random.normal(stream_key, shape, jnp.float32) * scale * loudness
    return jnp.minimum(jnp.maximum(array, -bound), bound).astype(kind)


def gaussian_with(rng, dims, scale, reach, shards, heavy, kind=jnp.bfloat16):
    entries = scale * jax.random.normal(rng, dims, jnp.float32)
    if shards:
        entries = entries * levels(rng, dims, shards, -0.22, 0.18)
    return jnp.clip(spiked(entries, jax.random.fold_in(rng, 3), *heavy), -reach, reach).astype(kind)


def setup_inputs(seed: int = 0) -> dict:
    streams_of = jax.random.split(jax.random.key(seed), 13)
    return {
        "inputs": centred(streams_of[0], (ROWS, ROW_LEN, D), 1.0, 6.0, ((0, 8), (1, 4))),
        "doc_lengths": draw_doc_lengths(jax.random.fold_in(streams_of[12], 71), 0),
        "project_in": centred(streams_of[2], (D, 3 * D), (D // 2) ** -0.5, 0.3125, ((0, 32),)),
        "project_out": centred(streams_of[3], (D, D), (D // 16) ** -0.5, 0.875, ((0, 32),)),
        "gate_weight": centred(streams_of[4], (D, FF), D ** -0.5, 0.21875, ((0, 32),)),
        "up_weight": centred(streams_of[5], (D, FF), D ** -0.5, 0.21875, ((0, 32),)),
        "down_weight": centred(streams_of[6], (FF, D), (FF // 2) ** -0.5, 0.15625, ((0, 32),)),
        "first_gain": jnp.clip(1.0 + 0.18 * jax.random.normal(streams_of[7], (D,), jnp.float32), 0.099609375, 1.8984375).astype(jnp.bfloat16),
        "first_bias": centred(streams_of[8], (D,), 0.3, 1.5, ((0, 32),)),
        "second_gain": jnp.clip(1.0 + 0.18 * jax.random.normal(streams_of[9], (D,), jnp.float32), 0.099609375, 1.8984375).astype(jnp.bfloat16),
        "second_bias": centred(streams_of[10], (D,), 0.3, 1.5, ((0, 32),)),
        "cotangent": gaussian_with(streams_of[11], (ROWS, ROW_LEN, D), 1.0, 6.0, ((0, 8), (1, 4)), (1, 2, 4, 2.0)),
    }


NEG = -1e+30
EPS = 1e-05
BASE = 1000.0
HIGH = lax.Precision.HIGHEST

@jax.custom_vjp
def low(v):
    return lax.optimization_barrier(v.astype(jnp.bfloat16)).astype(jnp.float32)

@jax.custom_vjp
def low_back(v):
    return v

def low_keep(v):
    return (low(v), None)

def low_pass(kept, grad):
    return (grad,)

def back_keep(v):
    return (v, None)

def back_low(kept, grad):
    return (low(grad),)
low.defvjp(low_keep, low_pass)
low_back.defvjp(back_keep, back_low)

def doc_layout(lengths_row, positions):
    bounds = jnp.cumsum(lengths_row).astype(jnp.int32)
    passed = positions[:, None] >= bounds[None, :]
    segment = lax.optimization_barrier(jnp.sum(passed.astype(jnp.int32), axis=1)).astype(jnp.int32)
    begins = lax.optimization_barrier(jnp.sum(jnp.where(passed, lengths_row[None, :], 0), axis=1)).astype(jnp.int32)
    return (segment, (positions - begins).astype(jnp.int32))

def rotary(vectors, offsets):
    half_size = vectors.shape[-1] // 2
    frequency = BASE ** (-2.0 * jnp.arange(half_size, dtype=jnp.float32) / vectors.shape[-1])
    angles = offsets.astype(jnp.float32)[:, None] * frequency[None, :]
    cosine = jnp.concatenate([jnp.cos(angles), jnp.cos(angles)], axis=1)[:, None, :]
    sine_rows = jnp.concatenate([jnp.sin(angles), jnp.sin(angles)], axis=1)[:, None, :]
    first_half = vectors[..., :half_size]
    second_half = vectors[..., half_size:]
    turned = jnp.concatenate([-second_half, first_half], axis=-1)
    return vectors * cosine + turned * sine_rows

def layer_norm(residual, gain_row, bias_row):
    row_mean = lax.optimization_barrier(jnp.mean(residual, axis=-1, keepdims=True))
    centered = residual - row_mean
    variance = lax.optimization_barrier(jnp.mean(centered * centered, axis=-1, keepdims=True))
    return centered * lax.rsqrt(variance + EPS) * gain_row + bias_row

def attend_block(query_tile, key_row, value_row, seg_query, seg_key):
    score_scale = query_tile.shape[-1] ** (-0.5)
    scores = low_back(jnp.einsum('qhd,khd->hqk', query_tile, key_row, precision=HIGH) * score_scale)
    allowed = (seg_query[:, None] == seg_key[None, :])[None, :, :]
    masked = jnp.where(allowed, scores, NEG)
    row_top = lax.optimization_barrier(jnp.max(masked, axis=2, keepdims=True))
    row_total = lax.optimization_barrier(jnp.sum(jnp.where(allowed, jnp.exp(masked - row_top), 0.0), axis=2, keepdims=True))
    prob_rows = low(jnp.where(allowed, jnp.exp(masked - (row_top + jnp.log(row_total))), 0.0))
    return jnp.einsum('hqk,khd->qhd', prob_rows, value_row, precision=HIGH)

def forward(inputs, project_in, project_out, gate_weight, up_weight, down_weight, first_gain, first_bias, second_gain, second_bias, segment, offsets, keep_mask):
    row_count, row_len, width = inputs.shape
    head_size = width // HEADS
    flat_in = inputs.reshape(row_count * row_len, width)
    joined = low_back(jnp.dot(flat_in, project_in, precision=HIGH))
    shaped = joined.reshape(row_count, row_len, 3, HEADS, head_size)
    queries = low_back(low(jax.vmap(rotary)(shaped[:, :, 0], offsets)))
    key_rows = low_back(low(jax.vmap(rotary)(shaped[:, :, 1], offsets)))
    value_rows = low_back(low(shaped[:, :, 2]))

    def row_attention(packed):
        query_row, key_row, value_row, seg_row = packed
        blocks = query_row.reshape(row_len // TOK_DEV, TOK_DEV, HEADS, head_size)
        seg_blocks = seg_row.reshape(row_len // TOK_DEV, TOK_DEV)
        block_step = jax.checkpoint(lambda pair: attend_block(pair[0], key_row, value_row, pair[1], seg_row))
        return lax.map(block_step, (blocks, seg_blocks)).reshape(row_len, width)
    mixed = lax.map(row_attention, (queries, key_rows, value_rows, segment))
    attended = low_back(low(mixed * keep_mask[:, :, None]))
    branch = low_back(jnp.dot(attended.reshape(-1, width), project_out, precision=HIGH))
    hidden = layer_norm(flat_in + branch, first_gain, first_bias)
    hidden_low = low(hidden)
    gate_pre = low_back(jnp.dot(hidden_low, gate_weight, precision=HIGH))
    up_pre = low_back(jnp.dot(hidden_low, up_weight, precision=HIGH))
    activated = low(jax.nn.silu(gate_pre) * up_pre)
    mlp_out = low_back(jnp.dot(activated, down_weight, precision=HIGH))
    return layer_norm(hidden + mlp_out, second_gain, second_bias).reshape(row_count, row_len, width)

def reference(inputs, doc_lengths, project_in, project_out, gate_weight, up_weight, down_weight, first_gain, first_bias, second_gain, second_bias, cotangent):
    row_len = inputs.shape[1]
    positions = jnp.arange(row_len, dtype=jnp.int32)
    segment, offsets = jax.vmap(lambda lengths_row: doc_layout(lengths_row, positions))(doc_lengths)
    keep_mask = (segment < doc_lengths.shape[1] - 1).astype(jnp.float32)

    def wrapped(inputs_f, in_f, out_f, gate_f, up_f, down_f, gain_one, bias_one, gain_two, bias_two):
        return forward(inputs_f, in_f, out_f, gate_f, up_f, down_f, gain_one, bias_one, gain_two, bias_two, segment, offsets, keep_mask)
    outputs, pull_back = jax.vjp(wrapped, inputs.astype(jnp.float32), project_in.astype(jnp.float32), project_out.astype(jnp.float32), gate_weight.astype(jnp.float32), up_weight.astype(jnp.float32), down_weight.astype(jnp.float32), first_gain.astype(jnp.float32), first_bias.astype(jnp.float32), second_gain.astype(jnp.float32), second_bias.astype(jnp.float32))
    gradients = pull_back(cotangent.astype(jnp.float32))
    return (outputs.astype(jnp.bfloat16), gradients[0].astype(jnp.bfloat16), gradients[1], gradients[2], gradients[3], gradients[4], gradients[5], gradients[6], gradients[7], gradients[8], gradients[9])
```

```python
import functools

import jax
import jax.numpy as jnp
import numpy as np
from jax import lax
from jax.experimental import pallas as pl
from jax.experimental.pallas import tpu as pltpu
from jax.sharding import PartitionSpec as P

HEADS = 12


NEG = -1e30
EPS = 1e-05
BASE = 1000.0


def doc_layout(lengths_row, positions):
    bounds = jnp.cumsum(lengths_row)
    passed = positions[:, None] >= bounds[None, :]
    segment = jnp.sum(passed.astype(jnp.int32), axis=1)
    begins = jnp.sum(jnp.where(passed, lengths_row[None, :], 0), axis=1)
    return (segment, positions - begins)


def rotary(vectors, offsets):
    half_size = vectors.shape[-1] // 2
    frequency = BASE ** (-2.0 * jnp.arange(half_size, dtype=jnp.float32) / vectors.shape[-1])
    angles = offsets.astype(jnp.float32)[:, None] * frequency[None, :]
    cosine = jnp.concatenate([jnp.cos(angles), jnp.cos(angles)], axis=1)[:, None, :]
    sine_rows = jnp.concatenate([jnp.sin(angles), jnp.sin(angles)], axis=1)[:, None, :]
    first_half = vectors[..., :half_size]
    second_half = vectors[..., half_size:]
    turned = jnp.concatenate([-second_half, first_half], axis=-1)
    return vectors * cosine + turned * sine_rows


def layer_norm(residual, gain_row, bias_row):
    row_mean = jnp.mean(residual, axis=-1, keepdims=True)
    centered = residual - row_mean
    variance = jnp.mean(centered * centered, axis=-1, keepdims=True)
    return centered * lax.rsqrt(variance + EPS) * gain_row + bias_row


def contract_rows(left, right):
    return lax.dot_general(
        left, right, (((0,), (0,)), ((), ())), preferred_element_type=jnp.float32
    )


def contract_cols(left, right):
    return lax.dot_general(
        left, right, (((1,), (1,)), ((), ())), preferred_element_type=jnp.float32
    )


def tile_scores(query_tile, key_tile, seg_query, seg_key, score_scale):
    scores = (
        jnp.einsum("qhd,khd->hqk", query_tile, key_tile, preferred_element_type=jnp.float32)
        * score_scale
    )
    allowed = (seg_query[:, None] == seg_key[None, :])[None, :, :]
    return (jnp.where(allowed, scores, NEG), allowed)


def run_groups(pieces, group, lengths_row, seg_query, carried, tile_fn, extra_shape):
    group_count = pieces[0].shape[0] // group

    def group_step(carried_in, number):
        offset = number * group
        tile_set = tuple(
            (lax.dynamic_slice_in_dim(piece_rows, offset, group, 0) for piece_rows in pieces)
        )
        positions = offset + jnp.arange(group, dtype=jnp.int32)
        seg_key, unused_offsets = doc_layout(lengths_row, positions)
        touches = (seg_key[0] <= seg_query[-1]) & (seg_query[0] <= seg_key[-1])

        def active(state_in):
            return tile_fn(state_in, tile_set, seg_key)

        def skipped(state_in):
            return (state_in, jnp.zeros(extra_shape, jnp.float32))

        return lax.cond(touches, active, skipped, carried_in)

    return lax.scan(group_step, carried, jnp.arange(group_count, dtype=jnp.int32))


def shards(
    inputs,
    doc_lengths,
    project_in,
    project_out,
    gate_weight,
    up_weight,
    down_weight,
    first_gain,
    first_bias,
    second_gain,
    second_bias,
    cotangent,
):
    group = inputs.shape[1]
    width = inputs.shape[2]
    head_count = HEADS
    head_size = width // head_count
    score_scale = head_size ** (-0.5)
    cycle_rank = lax.axis_index("blk")
    positions = cycle_rank * group + jnp.arange(group, dtype=jnp.int32)
    lengths_row = doc_lengths[0]
    seg_query, offsets = doc_layout(lengths_row, positions)
    keep_mask = seg_query < lengths_row.shape[0] - 1
    keep_float = keep_mask.astype(jnp.float32)
    fetched = (
        lax.all_gather(project_in, ("dp", "blk"), axis=0, tiled=True),
        lax.all_gather(project_out, ("dp", "blk"), axis=0, tiled=True),
        lax.all_gather(gate_weight, ("dp", "blk"), axis=0, tiled=True),
        lax.all_gather(up_weight, ("dp", "blk"), axis=0, tiled=True),
        lax.all_gather(down_weight, ("dp", "blk"), axis=0, tiled=True),
        lax.all_gather(first_gain, ("dp", "blk"), axis=0, tiled=True),
        lax.all_gather(first_bias, ("dp", "blk"), axis=0, tiled=True),
        lax.all_gather(second_gain, ("dp", "blk"), axis=0, tiled=True),
        lax.all_gather(second_bias, ("dp", "blk"), axis=0, tiled=True),
    )
    full_in, full_out, full_gate, full_up, full_down = (
        fetched[0],
        fetched[1],
        fetched[2],
        fetched[3],
        fetched[4],
    )
    gain_one = fetched[5].astype(jnp.float32)
    bias_one = fetched[6].astype(jnp.float32)
    gain_two = fetched[7].astype(jnp.float32)
    bias_two = fetched[8].astype(jnp.float32)
    tokens_low = inputs[0]
    tokens_f = tokens_low.astype(jnp.float32)
    joined = jnp.dot(tokens_low, full_in, preferred_element_type=jnp.float32)
    query_raw = joined[:, :width].reshape(group, head_count, head_size)
    key_raw = joined[:, width : 2 * width].reshape(group, head_count, head_size)
    value_low = joined[:, 2 * width :].astype(jnp.bfloat16)
    query_rot, query_pull = jax.vjp(lambda vectors: rotary(vectors, offsets), query_raw)
    key_rot, key_pull = jax.vjp(lambda vectors: rotary(vectors, offsets), key_raw)
    query_low = query_rot.astype(jnp.bfloat16)
    key_low = key_rot.reshape(group, width).astype(jnp.bfloat16)

    def stats_tile(carried, tile_set, seg_key):
        row_top, row_total = carried
        key_tile = tile_set[0].reshape(group, head_count, head_size)
        scores, allowed = tile_scores(query_low, key_tile, seg_query, seg_key, score_scale)
        new_top = jnp.maximum(row_top, jnp.max(scores, axis=2))
        shrink = jnp.exp(row_top - new_top)
        added = jnp.sum(jnp.where(allowed, jnp.exp(scores - new_top[:, :, None]), 0.0), axis=2)
        return ((new_top, row_total * shrink + added), jnp.zeros((1,), jnp.float32))

    init_stats = (
        jnp.full((head_count, group), NEG, jnp.float32),
        jnp.zeros((head_count, group), jnp.float32),
    )
    carried = init_stats
    carried, unused = run_groups(
        (lax.all_gather(key_low, "blk", axis=0, tiled=True),),
        group,
        lengths_row,
        seg_query,
        carried,
        stats_tile,
        (1,),
    )
    row_top, row_total = carried
    log_total = row_top + jnp.log(row_total)

    def output_tile(accum, tile_set, seg_key):
        key_tile = tile_set[0].reshape(group, head_count, head_size)
        value_tile = tile_set[1].reshape(group, head_count, head_size)
        scores, allowed = tile_scores(query_low, key_tile, seg_query, seg_key, score_scale)
        prob_low = jnp.where(allowed, jnp.exp(scores - log_total[:, :, None]), 0.0).astype(
            jnp.bfloat16
        )
        accum = accum + jnp.einsum(
            "hqk,khd->qhd", prob_low, value_tile, preferred_element_type=jnp.float32
        )
        return (accum, jnp.zeros((1,), jnp.float32))

    zero_accum = jnp.zeros((group, head_count, head_size), jnp.float32)
    accum = zero_accum
    accum, unused = run_groups(
        (
            lax.all_gather(key_low, "blk", axis=0, tiled=True),
            lax.all_gather(value_low, "blk", axis=0, tiled=True),
        ),
        group,
        lengths_row,
        seg_query,
        accum,
        output_tile,
        (1,),
    )
    attend_low = (accum * keep_float[:, None, None]).reshape(group, width).astype(jnp.bfloat16)
    branch = jnp.dot(attend_low, full_out, preferred_element_type=jnp.float32)
    residual_one = tokens_f + branch
    hidden, norm_one_pull = jax.vjp(layer_norm, residual_one, gain_one, bias_one)
    hidden_low = hidden.astype(jnp.bfloat16)
    gate_pre = jnp.dot(hidden_low, full_gate, preferred_element_type=jnp.float32)
    up_pre = jnp.dot(hidden_low, full_up, preferred_element_type=jnp.float32)
    activated, swiglu_pull = jax.vjp(
        lambda gate_in, up_in: jax.nn.silu(gate_in) * up_in, gate_pre, up_pre
    )
    active_low = activated.astype(jnp.bfloat16)
    mlp_out = jnp.dot(active_low, full_down, preferred_element_type=jnp.float32)
    outputs_f, norm_two_pull = jax.vjp(layer_norm, hidden + mlp_out, gain_two, bias_two)
    refetched = (
        lax.all_gather(project_in, ("dp", "blk"), axis=0, tiled=True),
        lax.all_gather(project_out, ("dp", "blk"), axis=0, tiled=True),
        lax.all_gather(gate_weight, ("dp", "blk"), axis=0, tiled=True),
        lax.all_gather(up_weight, ("dp", "blk"), axis=0, tiled=True),
        lax.all_gather(down_weight, ("dp", "blk"), axis=0, tiled=True),
    )
    full_in, full_out, full_gate, full_up, full_down = (
        refetched[0],
        refetched[1],
        refetched[2],
        refetched[3],
        refetched[4],
    )
    d_res_two, second_gain_part, second_bias_part = norm_two_pull(cotangent[0].astype(jnp.float32))
    d_mlp_low = d_res_two.astype(jnp.bfloat16)
    down_part = contract_rows(active_low, d_mlp_low)
    d_active = contract_cols(d_mlp_low, full_down)
    d_gate, d_up = swiglu_pull(d_active)
    d_gate_low = d_gate.astype(jnp.bfloat16)
    d_up_low = d_up.astype(jnp.bfloat16)
    gate_part = contract_rows(hidden_low, d_gate_low)
    up_part = contract_rows(hidden_low, d_up_low)
    d_hidden = d_res_two + contract_cols(d_gate_low, full_gate) + contract_cols(d_up_low, full_up)
    d_res_one, first_gain_part, first_bias_part = norm_one_pull(d_hidden)
    d_branch_low = d_res_one.astype(jnp.bfloat16)
    out_part = contract_rows(attend_low, d_branch_low)
    d_attend = contract_cols(d_branch_low, full_out).astype(jnp.bfloat16)
    d_attend_low = (d_attend * keep_mask[:, None].astype(jnp.bfloat16)).reshape(
        group, head_count, head_size
    )
    delta = jnp.einsum("qhd,qhd->hq", d_attend_low.astype(jnp.float32), accum)

    def back_tile(grad_query, tile_set, seg_key):
        key_tile = tile_set[0].reshape(group, head_count, head_size)
        value_tile = tile_set[1].reshape(group, head_count, head_size)
        scores, allowed = tile_scores(query_low, key_tile, seg_query, seg_key, score_scale)
        prob_rows = jnp.where(allowed, jnp.exp(scores - log_total[:, :, None]), 0.0)
        d_probs = jnp.einsum(
            "qhd,khd->hqk", d_attend_low, value_tile, preferred_element_type=jnp.float32
        )
        d_score_low = (prob_rows * (d_probs - delta[:, :, None])).astype(jnp.bfloat16)
        grad_query = (
            grad_query
            + jnp.einsum("hqk,khd->qhd", d_score_low, key_tile, preferred_element_type=jnp.float32)
            * score_scale
        )
        grad_key = (
            jnp.einsum("hqk,qhd->khd", d_score_low, query_low, preferred_element_type=jnp.float32)
            * score_scale
        )
        grad_value = jnp.einsum(
            "hqk,qhd->khd",
            prob_rows.astype(jnp.bfloat16),
            d_attend_low,
            preferred_element_type=jnp.float32,
        )
        return (
            grad_query,
            jnp.concatenate(
                [grad_key.reshape(group, width), grad_value.reshape(group, width)], axis=1
            ),
        )

    grad_query = zero_accum
    grad_query, blocks = run_groups(
        (
            lax.all_gather(key_low, "blk", axis=0, tiled=True),
            lax.all_gather(value_low, "blk", axis=0, tiled=True),
        ),
        group,
        lengths_row,
        seg_query,
        grad_query,
        back_tile,
        (group, 2 * width),
    )
    blocks = blocks.reshape(-1, 2 * width)
    back_result = (grad_query, blocks)
    grad_query = back_result[0]
    owned_pairs = lax.psum_scatter(
        back_result[1].astype(jnp.bfloat16), "blk", scatter_dimension=0, tiled=True
    ).astype(jnp.float32)
    key_sum = owned_pairs[:, :width]
    value_sum = owned_pairs[:, width:]
    d_query_pre = query_pull(grad_query.astype(jnp.bfloat16).astype(jnp.float32))[0]
    d_key_low = key_sum.astype(jnp.bfloat16).astype(jnp.float32)
    d_key_pre = key_pull(d_key_low.reshape(group, head_count, head_size))[0]
    d_value_low = value_sum.astype(jnp.bfloat16).astype(jnp.float32)
    d_joined_low = jnp.concatenate(
        [d_query_pre.reshape(group, width), d_key_pre.reshape(group, width), d_value_low], axis=1
    ).astype(jnp.bfloat16)
    in_part = contract_rows(tokens_low, d_joined_low)
    input_grad = (d_res_one + contract_cols(d_joined_low, full_in)).astype(jnp.bfloat16)
    by_rows = (
        lax.psum_scatter(
            in_part.astype(jnp.bfloat16), "dp", scatter_dimension=0, tiled=True
        ).astype(jnp.float32),
        lax.psum_scatter(
            out_part.astype(jnp.bfloat16), "dp", scatter_dimension=0, tiled=True
        ).astype(jnp.float32),
        lax.psum_scatter(
            gate_part.astype(jnp.bfloat16), "dp", scatter_dimension=0, tiled=True
        ).astype(jnp.float32),
        lax.psum_scatter(
            up_part.astype(jnp.bfloat16), "dp", scatter_dimension=0, tiled=True
        ).astype(jnp.float32),
        lax.psum_scatter(
            down_part.astype(jnp.bfloat16), "dp", scatter_dimension=0, tiled=True
        ).astype(jnp.float32),
        lax.psum_scatter(
            first_gain_part.astype(jnp.bfloat16), "dp", scatter_dimension=0, tiled=True
        ).astype(jnp.float32),
        lax.psum_scatter(
            first_bias_part.astype(jnp.bfloat16), "dp", scatter_dimension=0, tiled=True
        ).astype(jnp.float32),
        lax.psum_scatter(
            second_gain_part.astype(jnp.bfloat16), "dp", scatter_dimension=0, tiled=True
        ).astype(jnp.float32),
        lax.psum_scatter(
            second_bias_part.astype(jnp.bfloat16), "dp", scatter_dimension=0, tiled=True
        ).astype(jnp.float32),
    )
    summed = (
        lax.psum_scatter(
            by_rows[0].astype(jnp.bfloat16), "blk", scatter_dimension=0, tiled=True
        ).astype(jnp.float32),
        lax.psum_scatter(
            by_rows[1].astype(jnp.bfloat16), "blk", scatter_dimension=0, tiled=True
        ).astype(jnp.float32),
        lax.psum_scatter(
            by_rows[2].astype(jnp.bfloat16), "blk", scatter_dimension=0, tiled=True
        ).astype(jnp.float32),
        lax.psum_scatter(
            by_rows[3].astype(jnp.bfloat16), "blk", scatter_dimension=0, tiled=True
        ).astype(jnp.float32),
        lax.psum_scatter(
            by_rows[4].astype(jnp.bfloat16), "blk", scatter_dimension=0, tiled=True
        ).astype(jnp.float32),
        lax.psum_scatter(
            by_rows[5].astype(jnp.bfloat16), "blk", scatter_dimension=0, tiled=True
        ).astype(jnp.float32),
        lax.psum_scatter(
            by_rows[6].astype(jnp.bfloat16), "blk", scatter_dimension=0, tiled=True
        ).astype(jnp.float32),
        lax.psum_scatter(
            by_rows[7].astype(jnp.bfloat16), "blk", scatter_dimension=0, tiled=True
        ).astype(jnp.float32),
        lax.psum_scatter(
            by_rows[8].astype(jnp.bfloat16), "blk", scatter_dimension=0, tiled=True
        ).astype(jnp.float32),
    )
    return (
        outputs_f.astype(jnp.bfloat16)[None],
        input_grad[None],
        summed[0],
        summed[1],
        summed[2],
        summed[3],
        summed[4],
        summed[5],
        summed[6],
        summed[7],
        summed[8],
    )


MESH_IDS = pl.DeviceIdType.MESH
LANES = 128
HALF = 64
QUART = 32


def mm(left, right):
    return lax.dot_general(
        left, right, (((1,), (0,)), ((), ())), preferred_element_type=jnp.float32
    )


def mt(left, right):
    return lax.dot_general(
        left, right, (((1,), (1,)), ((), ())), preferred_element_type=jnp.float32
    )


def tm(left, right):
    return lax.dot_general(
        left, right, (((0,), (0,)), ((), ())), preferred_element_type=jnp.float32
    )


class Wire:
    def __init__(self, send_sem, recv_sem):
        self.send_sem, self.recv_sem = send_sem, recv_sem
        self.count, self.sent = 0, []

    def push(self, src, dst, peer):
        slot = self.count
        self.count += 1
        copy = pltpu.make_async_remote_copy(
            src_ref=src,
            dst_ref=dst,
            send_sem=self.send_sem.at[slot],
            recv_sem=self.recv_sem.at[slot],
            device_id=peer,
            device_id_type=MESH_IDS,
        )
        copy.start()
        self.sent.append(copy)
        return slot

    def arrive(self, slot, dst, peer):
        pltpu.make_async_remote_copy(
            src_ref=dst,
            dst_ref=dst,
            send_sem=self.send_sem.at[slot],
            recv_sem=self.recv_sem.at[slot],
            device_id=peer,
            device_id_type=MESH_IDS,
        ).wait_recv()

    def finish(self):
        for copy in self.sent:
            copy.wait_send()


def fused(
    depth,
    lens,
    freq,
    xin,
    cot,
    p_in,
    p_mlp,
    p_out,
    p_down,
    outputs,
    input_grad,
    g_in,
    g_mlp,
    g_out,
    g_down,
    xs,
    r_in,
    r_mlp,
    s_out,
    w_in,
    w_gate,
    w_up,
    w_down,
    w_out,
    params,
    cos_tab,
    sin_tab,
    seg_tab,
    qm,
    kw,
    vw,
    prob,
    att,
    s_att,
    r_att,
    norm_one,
    hid,
    hs,
    gate_pre,
    up_pre,
    act,
    s_mix,
    r_mix,
    dres_two,
    dms,
    dgate,
    dup,
    s_dh,
    r_dh,
    dres_one,
    s_da,
    r_da,
    acc_q,
    acc_k,
    acc_v,
    dj,
    s_ig,
    r_ig,
    pr_in,
    rx_in,
    sz_in,
    rz_in,
    pr_gate,
    rx_gate,
    sz_gate,
    rz_gate,
    pr_up,
    rx_up,
    sz_up,
    rz_up,
    pr_down,
    rx_down,
    sz_down,
    rz_down,
    b_out,
    rb_out,
    pr_out,
    rx_out,
    sz_out,
    rz_out,
    f_gate,
    s_gmlp,
    r_gmlp,
    s_gin,
    r_gin,
    send_sem,
    recv_sem,
):
    planes, cols = depth, 4
    tok = xin.shape[0]
    row_len = tok * cols
    dp = lax.axis_index("dp")
    blk = lax.axis_index("blk")
    z, x = dp // 2, dp % 2
    bf16, f32 = jnp.bfloat16, jnp.float32

    def side():
        return (z * 2 + (1 - x), blk)

    def tier(k):
        return (((z + k) % planes) * 2 + x, blk)

    def tier_from(k):
        return (z + planes - k) % planes

    def lane(k):
        return (dp, (blk + k) % cols)

    def lane_from(k):
        return (blk + cols - k) % cols

    tiers, lanes = range(1, planes), range(1, cols)
    wire = Wire(send_sem, recv_sem)
    barrier = pltpu.get_barrier_semaphore()
    peers = [side()] + [tier(k) for k in tiers] + [lane(k) for k in lanes]
    for peer in peers:
        pl.semaphore_signal(barrier, inc=1, device_id=peer, device_id_type=MESH_IDS)
    pl.semaphore_wait(barrier, len(peers))

    def to_lanes(source_of, target):
        return [wire.push(source_of((blk + k) % cols), target.at[blk], lane(k)) for k in lanes]

    def from_lanes(slots, target):
        for k, slot in zip(lanes, slots):
            wire.arrive(slot, target.at[lane_from(k)], lane(k))

    def spread_tiers(source, target):
        return [wire.push(source, target.at[dp], tier(k)) for k in tiers]

    def from_tier(slots, target, k):
        wire.arrive(slots[k - 1], target.at[tier_from(k) * 2 + x], tier(k))

    def spread_side(source, target, plane):
        return wire.push(source, target.at[plane * 2 + x], side())

    def from_side(slot, target, plane):
        wire.arrive(slot, target.at[plane * 2 + (1 - x)], side())

    own_out = s_out.at[blk]
    in_slots = to_lanes(lambda to: p_in.at[to], r_in)
    out_tiers = spread_tiers(p_out, own_out)
    out_sides = [spread_side(p_out, own_out, z)]
    x_slots = to_lanes(lambda to: xin, xs)
    mlp_slots = to_lanes(lambda to: p_mlp.at[to], r_mlp)
    xs[blk] = xin[...]
    r_in[blk] = p_in[blk]
    r_mlp[blk] = p_mlp[blk]
    s_out[blk, dp] = p_out[...]
    w_down[dp] = p_down[...]

    lengths = [lens[0, j] for j in range(lens.shape[1])]

    def layout(positions):
        segment = jnp.zeros_like(positions)
        begins = jnp.zeros_like(positions)
        bound = jnp.int32(0)
        for length in lengths:
            bound = bound + length
            passed = positions >= bound
            segment = segment + jnp.where(passed, 1, 0)
            begins = begins + jnp.where(passed, length, 0)
        return segment, positions - begins

    seg_rows, offsets = layout(lax.broadcasted_iota(jnp.int32, (row_len, LANES), 0))
    seg_tab[...] = seg_rows
    seg_key = layout(lax.broadcasted_iota(jnp.int32, (8, row_len), 1))[0][0:1]
    lane_ids = lax.broadcasted_iota(jnp.int32, (1, LANES), 1)
    low_half = lane_ids < HALF
    front = lane_ids % HALF < QUART
    angles = offsets.astype(f32) * freq[0:1]
    cos_tab[...] = jnp.cos(angles)
    sin_tab[...] = jnp.where(front, -1.0, 1.0) * jnp.sin(angles)

    def turn(window):
        return jnp.where(
            front, pltpu.roll(window, LANES - QUART, 1), pltpu.roll(window, QUART, 1)
        )

    from_lanes(in_slots, r_in)
    rows = 24
    w_in[dp] = jnp.concatenate(
        [r_in[j, 0:rows, :].astype(f32) for j in range(cols)], axis=0
    ).astype(bf16)
    in_tiers = spread_tiers(w_in.at[dp], w_in)
    in_sides = [spread_side(w_in.at[dp], w_in, z)]
    from_lanes(mlp_slots, r_mlp)
    mlp_own = [r_mlp[j].astype(f32) for j in range(cols)]
    w_gate[dp] = jnp.concatenate([part[0:rows] for part in mlp_own], axis=0).astype(bf16)
    w_up[dp] = jnp.concatenate([part[rows:] for part in mlp_own], axis=0).astype(bf16)
    gate_tiers = spread_tiers(w_gate.at[dp], w_gate)
    up_tiers = spread_tiers(w_up.at[dp], w_up)
    down_tiers = spread_tiers(p_down, w_down)

    def relay(tier_slots, side_slots, target):
        for k in tiers:
            from_tier(tier_slots, target, k)
            plane = tier_from(k)
            side_slots.append(spread_side(target.at[plane * 2 + x], target, plane))

    def settle(side_slots, target):
        for k in range(planes):
            from_side(side_slots[k], target, tier_from(k))

    relay(out_tiers, out_sides, own_out)
    relay(in_tiers, in_sides, w_in)
    gate_sides = [spread_side(w_gate.at[dp], w_gate, z)]
    settle(out_sides, own_out)
    out_lanes = to_lanes(lambda to: own_out, s_out)
    from_lanes(x_slots, xs)
    settle(in_sides, w_in)

    width = xin.shape[1]
    group = 2
    chunk = group * tok

    def project(step, carry):
        start = pl.multiple_of(step * chunk, chunk)
        here = pl.ds(start, chunk)
        tokens = xs[pl.ds(step * group, group)].reshape(chunk, width)
        joined = mm(tokens, w_in[...].reshape(width, w_in.shape[2]))
        cosine, sine = cos_tab[here, :], sin_tab[here, :]

        def rotate(number):
            window = joined[:, number * LANES : (number + 1) * LANES]
            return window * cosine + turn(window) * sine

        scale = HALF ** -0.5
        queries = rotate(0).astype(bf16).astype(f32) * scale
        qm[0, here, :] = jnp.where(low_half, queries, 0.0).astype(bf16)
        qm[1, here, :] = jnp.where(low_half, 0.0, queries).astype(bf16)
        kw[0, here, :] = rotate(1).astype(bf16)
        vw[0, here, :] = joined[:, 2 * LANES : 3 * LANES].astype(bf16)
        both = rotate(3)
        qm[2, here, :] = jnp.where(low_half, both.astype(bf16).astype(f32) * scale, 0.0).astype(bf16)
        kw[1, here, :] = jnp.where(low_half, pltpu.roll(both, HALF, 1), 0.0).astype(bf16)
        vw[1, here, :] = joined[:, 4 * LANES : 5 * LANES].astype(bf16)
        return carry

    lax.fori_loop(0, cols // group, project, 0)

    def attend(head):
        window = head // 2

        def step_fn(step, carry):
            here = pl.ds(pl.multiple_of(step * chunk, chunk), chunk)
            scores = mt(qm[head, here, :], kw[window])
            allowed = seg_tab[here, :][:, 0:1] == seg_key
            scores = jnp.where(allowed, scores, NEG)
            top = jnp.max(scores, axis=1, keepdims=True)
            raised = jnp.exp(scores - top)
            total = jnp.sum(raised, axis=1, keepdims=True)
            prob_low = (raised * (1.0 / total)).astype(bf16)
            prob[head, here, :] = prob_low
            mixed = mm(prob_low, vw[window])
            if head == 1:
                mixed = jnp.where(low_half, att[0, here, :], mixed)
            att[window, here, :] = mixed
            return carry

        lax.fori_loop(0, row_len // chunk, step_fn, 0)

    attend(0)
    relay(gate_tiers, gate_sides, w_gate)
    up_sides = [spread_side(w_up.at[dp], w_up, z)]
    attend(1)
    relay(up_tiers, up_sides, w_up)
    down_sides = [spread_side(p_down, w_down, z)]
    attend(2)

    last_segment = lens.shape[1] - 1
    for j in range(cols):
        here = slice(j * tok, (j + 1) * tok)
        kept = seg_tab[here, :] < last_segment
        s_att[j, :, 0:LANES] = jnp.where(kept, att[0, here, :], 0.0).astype(bf16)
        s_att[j, :, LANES : 2 * LANES] = jnp.where(kept, att[1, here, :], 0.0).astype(bf16)
    att_slots = to_lanes(lambda to: s_att.at[to], r_att)
    r_att[blk] = s_att[blk]

    from_lanes(out_lanes, s_out)
    shards = planes * 2 * cols
    per_quarter = shards // cols
    head_rows = per_quarter * rows
    for quarter in range(cols):
        w_out[quarter, 0:head_rows, :] = jnp.concatenate(
            [
                s_out[s % cols, s // cols, 0:rows, :].astype(f32)
                for s in range(quarter * per_quarter, (quarter + 1) * per_quarter)
            ],
            axis=0,
        ).astype(bf16)
        w_out[quarter, head_rows:, :] = jnp.zeros(
            (w_out.shape[1] - head_rows, width), bf16
        )
    column = lax.broadcasted_iota(jnp.int32, (LANES, width), 1).astype(f32)
    owner = jnp.floor((column + 0.5) * (1.0 / rows))
    inside = column - owner * rows
    unit = (
        inside == lax.broadcasted_iota(jnp.int32, (LANES, width), 0).astype(f32)
    ).astype(bf16)
    tails = jnp.concatenate(
        [
            s_out[s % cols, s // cols, rows : rows + 8, 0:LANES].astype(f32)
            for s in range(shards)
        ],
        axis=0,
    ).astype(bf16)
    shard_ids = lax.broadcasted_iota(jnp.int32, (shards, 8, width), 0).astype(f32)
    shard_hit = (shard_ids == owner[0:1].reshape(1, 1, width)).astype(f32)
    params[...] = jnp.sum(mm(tails, unit).reshape(shards, 8, width) * shard_hit, axis=0)
    gain_one, bias_one = params[0:1, :], params[1:2, :]
    gain_two, bias_two = params[2:3, :], params[3:4, :]

    def normalize(residual):
        centered = residual - jnp.mean(residual, axis=1, keepdims=True)
        variance = jnp.mean(centered * centered, axis=1, keepdims=True)
        spread = lax.rsqrt(variance + EPS)
        return centered * spread, spread

    def normalize_back(grad, normal, spread, gain):
        inner = grad * gain
        mean_inner = jnp.mean(inner, axis=1, keepdims=True)
        mean_both = jnp.mean(inner * normal, axis=1, keepdims=True)
        return (inner - mean_inner - normal * mean_both) * spread

    def column_sum(value):
        return jnp.sum(value, axis=0, keepdims=True)

    from_lanes(att_slots, r_att)
    branch = mm(r_att[0], w_out[0])
    for quarter in range(1, cols):
        branch = branch + mm(r_att[quarter], w_out[quarter])
    normal, spread_one = normalize(xin[...].astype(f32) + branch)
    norm_one[...] = normal
    hidden = normal * gain_one + bias_one
    hid[...] = hidden
    hs[blk] = hidden.astype(bf16)
    hid_slots = to_lanes(lambda to: hs.at[blk], hs)
    relay(down_tiers, down_sides, w_down)
    settle(gate_sides, w_gate)
    settle(up_sides, w_up)
    from_lanes(hid_slots, hs)

    units = w_gate.shape[2]
    wide = 256
    strips = units // wide

    def expand(step, carry):
        here = pl.ds(pl.multiple_of(step * wide, wide), wide)
        tokens = hs[...].reshape(row_len, width)
        gate = mm(tokens, w_gate[:, :, here].reshape(width, wide))
        up = mm(tokens, w_up[:, :, here].reshape(width, wide))
        gate_pre[:, here] = gate
        up_pre[:, here] = up
        act[:, here] = (gate / (1.0 + jnp.exp(-gate)) * up).astype(bf16)
        return carry

    lax.fori_loop(0, strips, expand, 0)
    settle(down_sides, w_down)

    def contract(step, carry):
        here = pl.ds(pl.multiple_of(step * wide, wide), wide)
        mixed = mm(act[...], w_down[:, :, here].reshape(units, wide))
        s_mix[:, :, here] = mixed.reshape(cols, tok, wide).astype(bf16)
        return carry

    lax.fori_loop(0, width // wide, contract, 0)
    mix_slots = to_lanes(lambda to: s_mix.at[to], r_mix)
    r_mix[blk] = s_mix[blk]
    from_lanes(mix_slots, r_mix)
    mlp_out = r_mix[0].astype(f32)
    for j in range(1, cols):
        mlp_out = mlp_out + r_mix[j].astype(f32)
    normal, spread_two = normalize(hid[...] + mlp_out)
    outputs[...] = (normal * gain_two + bias_two).astype(bf16)
    grad = cot[...].astype(f32)
    second_gain = column_sum(grad * normal)
    second_bias = column_sum(grad)
    d_two = normalize_back(grad, normal, spread_two, gain_two)
    dres_two[...] = d_two
    dms[blk] = d_two.astype(bf16)
    dm_slots = to_lanes(lambda to: dms.at[blk], dms)
    from_lanes(dm_slots, dms)

    def send_side(part, inbox):
        order = [(z + k) % planes for k in list(tiers) + [0]]
        return [wire.push(part.at[1 - x, to], inbox.at[to], side()) for to in order]

    def pass_on(part, inbox, staged, landing, side_slots):
        tier_slots = []
        for k in tiers:
            to = (z + k) % planes
            wire.arrive(side_slots[k - 1], inbox.at[to], side())
            staged[to] = (part[x, to].astype(f32) + inbox[to].astype(f32)).astype(bf16)
            tier_slots.append(wire.push(staged.at[to], landing.at[k], tier(k)))
        wire.arrive(side_slots[planes - 1], inbox.at[z], side())
        return tier_slots

    def total_of(part, inbox, landing, tier_slots):
        total = part[x, z].astype(f32) + inbox[z].astype(f32)
        for k in tiers:
            wire.arrive(tier_slots[k - 1], landing.at[k], tier(k))
            total = total + landing[k].astype(f32)
        return total

    half = 4

    def fill_parts(part, left_of, right):
        height = part.shape[2]

        def step_fn(step, carry):
            here = pl.ds(pl.multiple_of(step * half * height, LANES), half * height)
            product = tm(left_of(here), right())
            for j in range(half):
                part[j % 2, step * (half // 2) + j // 2] = product[
                    j * height : (j + 1) * height
                ].astype(bf16)
            return carry

        lax.fori_loop(0, planes * 2 // half, step_fn, 0)

    fill_parts(pr_down, lambda here: act[:, here], lambda: dms[...].reshape(row_len, width))
    down_x = send_side(pr_down, rx_down)

    block = w_down.shape[1]

    def active_grads(step, carry):
        here = pl.ds(pl.multiple_of(step * half * block, LANES), half * block)
        d_active = mt(
            dms[...].reshape(row_len, width),
            w_down[pl.ds(step * half, half)].reshape(half * block, width),
        )
        gate, up = gate_pre[:, here], up_pre[:, here]
        sg = 1.0 / (1.0 + jnp.exp(-gate))
        dgate[:, here] = (d_active * up * sg * (1.0 + gate * (1.0 - sg))).astype(bf16)
        dup[:, here] = (d_active * gate * sg).astype(bf16)
        return carry

    lax.fori_loop(0, planes * 2 // half, active_grads, 0)
    block = w_gate.shape[1]

    def hidden_grads(step, carry):
        here = pl.ds(pl.multiple_of(step * half * block, LANES), half * block)
        those = pl.ds(step * half, half)
        mixed = mt(dgate[...], w_gate[those].reshape(half * block, units)) + mt(
            dup[...], w_up[those].reshape(half * block, units)
        )
        s_dh[:, :, here] = mixed.reshape(cols, tok, half * block).astype(bf16)
        return carry

    lax.fori_loop(0, planes * 2 // half, hidden_grads, 0)
    dh_slots = to_lanes(lambda to: s_dh.at[to], r_dh)
    r_dh[blk] = s_dh[blk]

    def hidden_rows(here):
        return hs[:, :, here].reshape(row_len, half * block)

    fill_parts(pr_gate, hidden_rows, lambda: dgate[...])
    gate_x = send_side(pr_gate, rx_gate)
    fill_parts(pr_up, hidden_rows, lambda: dup[...])
    up_x = send_side(pr_up, rx_up)

    from_lanes(dh_slots, r_dh)
    d_hidden = dres_two[...]
    for j in range(cols):
        d_hidden = d_hidden + r_dh[j].astype(f32)
    normal = norm_one[...]
    first_gain = column_sum(d_hidden * normal)
    first_bias = column_sum(d_hidden)
    d_one = normalize_back(d_hidden, normal, spread_one, gain_one)
    dres_one[...] = d_one
    d_branch = d_one.astype(bf16)
    mine = pl.ds(pl.multiple_of(blk * tok, tok), tok)
    kept = seg_tab[mine, :][:, 0:1] < last_segment
    for quarter in range(cols):
        pulled = mt(d_branch, w_out[quarter]).astype(bf16).astype(f32)
        s_da[quarter] = jnp.where(kept, pulled, 0.0).astype(bf16)
    da_slots = to_lanes(lambda to: s_da.at[to], r_da)
    r_da[blk] = s_da[blk]

    vectors = jnp.concatenate(
        [first_gain, first_bias, second_gain, second_bias, jnp.zeros((4, width), f32)], axis=0
    )
    tails = mt(
        (shard_hit * vectors.reshape(1, 8, width)).reshape(shards * 8, width).astype(bf16), unit
    )
    for quarter in range(cols):
        product = tm(r_att[quarter], d_branch)
        for t in range(per_quarter):
            s = quarter * per_quarter + t
            owner_dp = s // cols
            lower = jnp.concatenate(
                [tails[s * 8 : s * 8 + 8], jnp.zeros((8, width - LANES), f32)], axis=1
            )
            b_out[s % cols, owner_dp % 2, owner_dp // 2] = jnp.concatenate(
                [product[t * rows : (t + 1) * rows], lower], axis=0
            ).astype(bf16)
    out_blk = to_lanes(lambda to: b_out.at[to], rb_out)
    rb_out[blk] = b_out[blk]

    down_z = pass_on(pr_down, rx_down, sz_down, rz_down, down_x)
    from_lanes(da_slots, r_da)

    def attend_back(head):
        window = head // 2
        fresh = head != 1

        def step_fn(step, carry):
            here = pl.ds(pl.multiple_of(step * chunk, chunk), chunk)
            d_out = r_da[pl.ds(step * group, group), :, window * LANES : (window + 1) * LANES]
            d_out = d_out.reshape(chunk, LANES).astype(f32)
            if head == 0:
                d_out = jnp.where(low_half, d_out, 0.0)
            if head == 1:
                d_out = jnp.where(low_half, 0.0, d_out)
            d_low = d_out.astype(bf16)
            delta = jnp.sum(d_out * att[window, here, :], axis=1, keepdims=True)
            prob_low = prob[head, here, :]
            d_prob = mt(d_low, vw[window])
            d_score = (prob_low.astype(f32) * (d_prob - delta)).astype(bf16)
            d_query = mm(d_score, kw[window]) * (HALF ** -0.5)
            if head == 1:
                d_query = jnp.where(low_half, acc_q[0, here, :], d_query)
            acc_q[window, here, :] = d_query
            d_key = tm(d_score, qm[head, here, :])
            d_value = tm(prob_low, d_low)
            if fresh:

                @pl.when(step == 0)
                def _():
                    acc_k[window] = d_key
                    acc_v[window] = d_value

                @pl.when(step != 0)
                def _():
                    acc_k[window] = acc_k[window] + d_key
                    acc_v[window] = acc_v[window] + d_value
            else:
                acc_k[window] = acc_k[window] + d_key
                acc_v[window] = acc_v[window] + d_value
            return carry

        lax.fori_loop(0, row_len // chunk, step_fn, 0)

    attend_back(0)
    attend_back(1)
    attend_back(2)

    cosine, sine = cos_tab[...], sin_tab[...]

    def rotate_back(vector):
        vector = vector.astype(bf16).astype(f32)
        return (vector * cosine - turn(vector) * sine).astype(bf16)

    dj[:, 0:LANES] = rotate_back(acc_q[0])
    dj[:, LANES : 2 * LANES] = rotate_back(acc_k[0])
    dj[:, 2 * LANES : 3 * LANES] = acc_v[0].astype(bf16)
    dj[:, 3 * LANES : 4 * LANES] = rotate_back(acc_q[1] + pltpu.roll(acc_k[1], HALF, 1))
    dj[:, 4 * LANES : 5 * LANES] = acc_v[1].astype(bf16)

    from_lanes(out_blk, rb_out)
    for side_at in range(2):
        gathered = rb_out[0, side_at].astype(f32)
        for j in range(1, cols):
            gathered = gathered + rb_out[j, side_at].astype(f32)
        pr_out[side_at] = gathered.astype(bf16)
    out_x = send_side(pr_out, rx_out)

    fill_parts(pr_in, lambda here: xs[:, :, here].reshape(row_len, half * block), lambda: dj[...])
    in_x = send_side(pr_in, rx_in)

    def input_grads(step, carry):
        here = pl.ds(pl.multiple_of(step * half * block, LANES), half * block)
        mixed = mt(dj[...], w_in[pl.ds(step * half, half)].reshape(half * block, w_in.shape[2]))
        s_ig[:, :, here] = mixed.reshape(cols, tok, half * block).astype(bf16)
        return carry

    lax.fori_loop(0, planes * 2 // half, input_grads, 0)
    ig_slots = to_lanes(lambda to: s_ig.at[to], r_ig)
    r_ig[blk] = s_ig[blk]

    gate_z = pass_on(pr_gate, rx_gate, sz_gate, rz_gate, gate_x)
    g_down[...] = total_of(pr_down, rx_down, rz_down, down_z)
    up_z = pass_on(pr_up, rx_up, sz_up, rz_up, up_x)
    gate_total = total_of(pr_gate, rx_gate, rz_gate, gate_z)
    f_gate[...] = gate_total
    out_z = pass_on(pr_out, rx_out, sz_out, rz_out, out_x)
    from_lanes(ig_slots, r_ig)
    grad_in = dres_one[...]
    for j in range(cols):
        grad_in = grad_in + r_ig[j].astype(f32)
    input_grad[...] = grad_in.astype(bf16)
    up_total = total_of(pr_up, rx_up, rz_up, up_z)
    gate_total = f_gate[...]
    for j in range(cols):
        here = slice(j * rows, (j + 1) * rows)
        s_gmlp[j] = jnp.concatenate([gate_total[here], up_total[here]], axis=0).astype(bf16)
    gmlp_slots = to_lanes(lambda to: s_gmlp.at[to], r_gmlp)
    r_gmlp[blk] = s_gmlp[blk]
    in_z = pass_on(pr_in, rx_in, sz_in, rz_in, in_x)
    g_out[...] = total_of(pr_out, rx_out, rz_out, out_z)
    from_lanes(gmlp_slots, r_gmlp)
    g_mlp[...] = r_gmlp[...]
    in_total = total_of(pr_in, rx_in, rz_in, in_z)
    for j in range(cols):
        s_gin[j] = jnp.concatenate(
            [in_total[j * rows : (j + 1) * rows], jnp.zeros((8, in_total.shape[1]), f32)], axis=0
        ).astype(bf16)
    gin_slots = to_lanes(lambda to: s_gin.at[to], r_gin)
    r_gin[blk] = s_gin[blk]
    from_lanes(gin_slots, r_gin)
    g_in[...] = r_gin[...]
    wire.finish()


def fast_shards(
    depth,
    inputs,
    doc_lengths,
    project_in,
    project_out,
    gate_weight,
    up_weight,
    down_weight,
    first_gain,
    first_bias,
    second_gain,
    second_bias,
    cotangent,
):
    cols = 4
    tok, width = inputs.shape[1:]
    rows = project_in.shape[0]
    ff = gate_weight.shape[1]
    ring = depth * 2
    row_len = tok * cols
    units = ff // cols
    block = units // ring
    head_width = width // cols
    in_width = 5 * LANES
    bf16, f32 = jnp.bfloat16, jnp.float32

    kinds = project_in.reshape(rows, 3, cols, head_width)
    pairs, singles = kinds[..., :LANES], kinds[..., LANES:]
    p_in = jnp.concatenate(
        [pairs[:, 0], pairs[:, 1], pairs[:, 2], singles[:, 0], singles[:, 1], singles[:, 2]],
        axis=-1,
    ).transpose(1, 0, 2)
    p_in = jnp.pad(p_in, ((0, 0), (0, 32 - rows), (0, in_width - p_in.shape[2])))

    def by_owner(weight):
        return weight.reshape(rows, ring, cols, block).transpose(2, 0, 1, 3).reshape(cols, rows, units)

    p_mlp = jnp.concatenate([by_owner(gate_weight), by_owner(up_weight)], axis=1)
    vectors = jnp.stack([first_gain, first_bias, second_gain, second_bias])
    p_out = jnp.concatenate(
        [project_out, jnp.pad(vectors, ((0, 4), (0, width - rows)))], axis=0
    )
    lane_ids = np.arange(LANES) % QUART
    freq = jnp.asarray(
        np.broadcast_to(BASE ** (-2.0 * lane_ids / HALF), (8, LANES)).astype(np.float32)
    )

    def scratch(*shape, kind=bf16):
        return pltpu.VMEM(shape, kind)

    def sums(height, across):
        return [
            scratch(2, depth, height, across),
            scratch(depth, height, across),
            scratch(depth, height, across),
            scratch(depth, height, across),
        ]

    stacked = scratch(cols, tok, width)
    heads = 3
    buffers = [
        stacked,
        scratch(cols, 32, in_width),
        scratch(cols, 2 * rows, units),
        scratch(cols, ring, 32, width),
        scratch(ring, cols * rows, in_width),
        scratch(ring, cols * rows, units),
        scratch(ring, cols * rows, units),
        scratch(ring, block, width),
        scratch(cols, 2 * LANES, width),
        scratch(8, width, kind=f32),
        scratch(row_len, LANES, kind=f32),
        scratch(row_len, LANES, kind=f32),
        scratch(row_len, LANES, kind=jnp.int32),
        scratch(heads, row_len, LANES),
        scratch(2, row_len, LANES),
        scratch(2, row_len, LANES),
        scratch(heads, row_len, row_len),
        scratch(2, row_len, LANES, kind=f32),
        scratch(cols, tok, 2 * LANES),
        scratch(cols, tok, 2 * LANES),
        scratch(tok, width, kind=f32),
        scratch(tok, width, kind=f32),
        stacked,
        scratch(row_len, units, kind=f32),
        scratch(row_len, units, kind=f32),
        scratch(row_len, units),
        stacked,
        stacked,
        scratch(tok, width, kind=f32),
        stacked,
        scratch(row_len, units),
        scratch(row_len, units),
        stacked,
        stacked,
        scratch(tok, width, kind=f32),
        scratch(cols, tok, 2 * LANES),
        scratch(cols, tok, 2 * LANES),
        scratch(2, row_len, LANES, kind=f32),
        scratch(2, row_len, LANES, kind=f32),
        scratch(2, row_len, LANES, kind=f32),
        scratch(row_len, in_width),
        stacked,
        stacked,
        *sums(cols * rows, in_width),
        *sums(cols * rows, units),
        *sums(cols * rows, units),
        *sums(block, width),
        scratch(cols, 2, depth, 32, width),
        scratch(cols, 2, depth, 32, width),
        *sums(32, width),
        scratch(cols * rows, units, kind=f32),
        scratch(cols, 2 * rows, units),
        scratch(cols, 2 * rows, units),
        scratch(cols, 32, in_width),
        scratch(cols, 32, in_width),
        pltpu.SemaphoreType.DMA((160,)),
        pltpu.SemaphoreType.DMA((160,)),
    ]
    vmem = pl.BlockSpec(memory_space=pltpu.VMEM)
    tokens = row_len * width
    outputs, input_grad, g_in, g_mlp, g_out, g_down = pl.pallas_call(
        functools.partial(fused, depth),
        out_shape=(
            jax.ShapeDtypeStruct((tok, width), bf16),
            jax.ShapeDtypeStruct((tok, width), bf16),
            jax.ShapeDtypeStruct((cols, 32, in_width), bf16),
            jax.ShapeDtypeStruct((cols, 2 * rows, units), bf16),
            jax.ShapeDtypeStruct((32, width), f32),
            jax.ShapeDtypeStruct((block, width), f32),
        ),
        in_specs=[pl.BlockSpec(memory_space=pltpu.SMEM)] + [vmem] * 7,
        out_specs=(vmem,) * 6,
        scratch_shapes=buffers,
        compiler_params=pltpu.CompilerParams(
            collective_id=0, has_side_effects=True, vmem_limit_bytes=60 * 2**20
        ),
        cost_estimate=pl.CostEstimate(
            flops=6 * tokens * (3 * units + 4 * head_width),
            bytes_accessed=8 * 2**20,
            transcendentals=3 * row_len * row_len,
        ),
        name="layer",
    )(doc_lengths, freq, inputs[0], cotangent[0], p_in, p_mlp, p_out, down_weight)

    wide_in = g_in[:, :rows].astype(f32).transpose(1, 0, 2)
    kind_pairs = wide_in[..., : 3 * LANES].reshape(rows, cols, 3, LANES)
    kind_singles = wide_in[..., 3 * LANES : 3 * LANES + 3 * HALF].reshape(rows, cols, 3, HALF)
    in_grad = jnp.concatenate([kind_pairs, kind_singles], axis=-1)
    in_grad = in_grad.transpose(0, 2, 1, 3).reshape(rows, 3 * width)

    def by_column(part):
        return (
            part.reshape(cols, rows, ring, block)
            .transpose(1, 2, 0, 3)
            .reshape(rows, ff)
            .astype(f32)
        )

    small = g_out[rows : rows + 4, :rows]
    return (
        outputs[None],
        input_grad[None],
        in_grad,
        g_out[:rows],
        by_column(g_mlp[:, :rows]),
        by_column(g_mlp[:, rows:]),
        g_down,
        small[0],
        small[1],
        small[2],
        small[3],
    )


def pick(sizes):
    def chosen(*args):
        tok, width = args[0].shape[1:]
        ring, cols = sizes["dp"], sizes["blk"]
        fits = (
            ring == 8
            and cols == 4
            and tok == LANES
            and HEADS == 3 * cols
            and width == HEADS * HALF
            and args[2].shape[0] == 24
            and args[4].shape[1] == 4 * width
        )
        if fits:
            return fast_shards(ring // 2, *args)
        return shards(*args)

    return chosen


def solution(mesh):
    placed = (
        P("dp", "blk", None),
        P("dp", None),
        P(("dp", "blk"), None),
        P(("dp", "blk"), None),
        P(("dp", "blk"), None),
        P(("dp", "blk"), None),
        P(("dp", "blk"), None),
        P(("dp", "blk")),
        P(("dp", "blk")),
        P(("dp", "blk")),
        P(("dp", "blk")),
        P("dp", "blk", None),
    )
    return jax.shard_map(
        pick(dict(mesh.shape)),
        mesh=mesh,
        in_specs=placed,
        out_specs=(
            P("dp", "blk", None),
            P("dp", "blk", None),
            P(("dp", "blk"), None),
            P(("dp", "blk"), None),
            P(("dp", "blk"), None),
            P(("dp", "blk"), None),
            P(("dp", "blk"), None),
            P(("dp", "blk")),
            P(("dp", "blk")),
            P(("dp", "blk")),
            P(("dp", "blk")),
        ),
        check_vma=False,
    )
```

```python
import functools

import jax
import jax.numpy as jnp
import numpy as np
from jax import lax
from jax.experimental import pallas as pl
from jax.experimental.pallas import tpu as pltpu
from jax.sharding import PartitionSpec as P

HEADS = 12


NEG = -1e30
EPS = 1e-05
BASE = 1000.0


def doc_layout(lengths_row, positions):
    bounds = jnp.cumsum(lengths_row)
    passed = positions[:, None] >= bounds[None, :]
    segment = jnp.sum(passed.astype(jnp.int32), axis=1)
    begins = jnp.sum(jnp.where(passed, lengths_row[None, :], 0), axis=1)
    return (segment, positions - begins)


def rotary(vectors, offsets):
    half_size = vectors.shape[-1] // 2
    frequency = BASE ** (-2.0 * jnp.arange(half_size, dtype=jnp.float32) / vectors.shape[-1])
    angles = offsets.astype(jnp.float32)[:, None] * frequency[None, :]
    cosine = jnp.concatenate([jnp.cos(angles), jnp.cos(angles)], axis=1)[:, None, :]
    sine_rows = jnp.concatenate([jnp.sin(angles), jnp.sin(angles)], axis=1)[:, None, :]
    first_half = vectors[..., :half_size]
    second_half = vectors[..., half_size:]
    turned = jnp.concatenate([-second_half, first_half], axis=-1)
    return vectors * cosine + turned * sine_rows


def layer_norm(residual, gain_row, bias_row):
    row_mean = jnp.mean(residual, axis=-1, keepdims=True)
    centered = residual - row_mean
    variance = jnp.mean(centered * centered, axis=-1, keepdims=True)
    return centered * lax.rsqrt(variance + EPS) * gain_row + bias_row


def contract_rows(left, right):
    return lax.dot_general(
        left, right, (((0,), (0,)), ((), ())), preferred_element_type=jnp.float32
    )


def contract_cols(left, right):
    return lax.dot_general(
        left, right, (((1,), (1,)), ((), ())), preferred_element_type=jnp.float32
    )


def tile_scores(query_tile, key_tile, seg_query, seg_key, score_scale):
    scores = (
        jnp.einsum("qhd,khd->hqk", query_tile, key_tile, preferred_element_type=jnp.float32)
        * score_scale
    )
    allowed = (seg_query[:, None] == seg_key[None, :])[None, :, :]
    return (jnp.where(allowed, scores, NEG), allowed)


def run_groups(pieces, group, lengths_row, seg_query, carried, tile_fn, extra_shape):
    group_count = pieces[0].shape[0] // group

    def group_step(carried_in, number):
        offset = number * group
        tile_set = tuple(
            (lax.dynamic_slice_in_dim(piece_rows, offset, group, 0) for piece_rows in pieces)
        )
        positions = offset + jnp.arange(group, dtype=jnp.int32)
        seg_key, unused_offsets = doc_layout(lengths_row, positions)
        touches = (seg_key[0] <= seg_query[-1]) & (seg_query[0] <= seg_key[-1])

        def active(state_in):
            return tile_fn(state_in, tile_set, seg_key)

        def skipped(state_in):
            return (state_in, jnp.zeros(extra_shape, jnp.float32))

        return lax.cond(touches, active, skipped, carried_in)

    return lax.scan(group_step, carried, jnp.arange(group_count, dtype=jnp.int32))


def shards(
    inputs,
    doc_lengths,
    project_in,
    project_out,
    gate_weight,
    up_weight,
    down_weight,
    first_gain,
    first_bias,
    second_gain,
    second_bias,
    cotangent,
):
    group = inputs.shape[1]
    width = inputs.shape[2]
    head_count = HEADS
    head_size = width // head_count
    score_scale = head_size ** (-0.5)
    cycle_rank = lax.axis_index("blk")
    positions = cycle_rank * group + jnp.arange(group, dtype=jnp.int32)
    lengths_row = doc_lengths[0]
    seg_query, offsets = doc_layout(lengths_row, positions)
    keep_mask = seg_query < lengths_row.shape[0] - 1
    keep_float = keep_mask.astype(jnp.float32)
    fetched = (
        lax.all_gather(project_in, ("dp", "blk"), axis=0, tiled=True),
        lax.all_gather(project_out, ("dp", "blk"), axis=0, tiled=True),
        lax.all_gather(gate_weight, ("dp", "blk"), axis=0, tiled=True),
        lax.all_gather(up_weight, ("dp", "blk"), axis=0, tiled=True),
        lax.all_gather(down_weight, ("dp", "blk"), axis=0, tiled=True),
        lax.all_gather(first_gain, ("dp", "blk"), axis=0, tiled=True),
        lax.all_gather(first_bias, ("dp", "blk"), axis=0, tiled=True),
        lax.all_gather(second_gain, ("dp", "blk"), axis=0, tiled=True),
        lax.all_gather(second_bias, ("dp", "blk"), axis=0, tiled=True),
    )
    full_in, full_out, full_gate, full_up, full_down = (
        fetched[0],
        fetched[1],
        fetched[2],
        fetched[3],
        fetched[4],
    )
    gain_one = fetched[5].astype(jnp.float32)
    bias_one = fetched[6].astype(jnp.float32)
    gain_two = fetched[7].astype(jnp.float32)
    bias_two = fetched[8].astype(jnp.float32)
    tokens_low = inputs[0]
    tokens_f = tokens_low.astype(jnp.float32)
    joined = jnp.dot(tokens_low, full_in, preferred_element_type=jnp.float32)
    query_raw = joined[:, :width].reshape(group, head_count, head_size)
    key_raw = joined[:, width : 2 * width].reshape(group, head_count, head_size)
    value_low = joined[:, 2 * width :].astype(jnp.bfloat16)
    query_rot, query_pull = jax.vjp(lambda vectors: rotary(vectors, offsets), query_raw)
    key_rot, key_pull = jax.vjp(lambda vectors: rotary(vectors, offsets), key_raw)
    query_low = query_rot.astype(jnp.bfloat16)
    key_low = key_rot.reshape(group, width).astype(jnp.bfloat16)

    def stats_tile(carried, tile_set, seg_key):
        row_top, row_total = carried
        key_tile = tile_set[0].reshape(group, head_count, head_size)
        scores, allowed = tile_scores(query_low, key_tile, seg_query, seg_key, score_scale)
        new_top = jnp.maximum(row_top, jnp.max(scores, axis=2))
        shrink = jnp.exp(row_top - new_top)
        added = jnp.sum(jnp.where(allowed, jnp.exp(scores - new_top[:, :, None]), 0.0), axis=2)
        return ((new_top, row_total * shrink + added), jnp.zeros((1,), jnp.float32))

    init_stats = (
        jnp.full((head_count, group), NEG, jnp.float32),
        jnp.zeros((head_count, group), jnp.float32),
    )
    carried = init_stats
    carried, unused = run_groups(
        (lax.all_gather(key_low, "blk", axis=0, tiled=True),),
        group,
        lengths_row,
        seg_query,
        carried,
        stats_tile,
        (1,),
    )
    row_top, row_total = carried
    log_total = row_top + jnp.log(row_total)

    def output_tile(accum, tile_set, seg_key):
        key_tile = tile_set[0].reshape(group, head_count, head_size)
        value_tile = tile_set[1].reshape(group, head_count, head_size)
        scores, allowed = tile_scores(query_low, key_tile, seg_query, seg_key, score_scale)
        prob_low = jnp.where(allowed, jnp.exp(scores - log_total[:, :, None]), 0.0).astype(
            jnp.bfloat16
        )
        accum = accum + jnp.einsum(
            "hqk,khd->qhd", prob_low, value_tile, preferred_element_type=jnp.float32
        )
        return (accum, jnp.zeros((1,), jnp.float32))

    zero_accum = jnp.zeros((group, head_count, head_size), jnp.float32)
    accum = zero_accum
    accum, unused = run_groups(
        (
            lax.all_gather(key_low, "blk", axis=0, tiled=True),
            lax.all_gather(value_low, "blk", axis=0, tiled=True),
        ),
        group,
        lengths_row,
        seg_query,
        accum,
        output_tile,
        (1,),
    )
    attend_low = (accum * keep_float[:, None, None]).reshape(group, width).astype(jnp.bfloat16)
    branch = jnp.dot(attend_low, full_out, preferred_element_type=jnp.float32)
    residual_one = tokens_f + branch
    hidden, norm_one_pull = jax.vjp(layer_norm, residual_one, gain_one, bias_one)
    hidden_low = hidden.astype(jnp.bfloat16)
    gate_pre = jnp.dot(hidden_low, full_gate, preferred_element_type=jnp.float32)
    up_pre = jnp.dot(hidden_low, full_up, preferred_element_type=jnp.float32)
    activated, swiglu_pull = jax.vjp(
        lambda gate_in, up_in: jax.nn.silu(gate_in) * up_in, gate_pre, up_pre
    )
    active_low = activated.astype(jnp.bfloat16)
    mlp_out = jnp.dot(active_low, full_down, preferred_element_type=jnp.float32)
    outputs_f, norm_two_pull = jax.vjp(layer_norm, hidden + mlp_out, gain_two, bias_two)
    refetched = (
        lax.all_gather(project_in, ("dp", "blk"), axis=0, tiled=True),
        lax.all_gather(project_out, ("dp", "blk"), axis=0, tiled=True),
        lax.all_gather(gate_weight, ("dp", "blk"), axis=0, tiled=True),
        lax.all_gather(up_weight, ("dp", "blk"), axis=0, tiled=True),
        lax.all_gather(down_weight, ("dp", "blk"), axis=0, tiled=True),
    )
    full_in, full_out, full_gate, full_up, full_down = (
        refetched[0],
        refetched[1],
        refetched[2],
        refetched[3],
        refetched[4],
    )
    d_res_two, second_gain_part, second_bias_part = norm_two_pull(cotangent[0].astype(jnp.float32))
    d_mlp_low = d_res_two.astype(jnp.bfloat16)
    down_part = contract_rows(active_low, d_mlp_low)
    d_active = contract_cols(d_mlp_low, full_down)
    d_gate, d_up = swiglu_pull(d_active)
    d_gate_low = d_gate.astype(jnp.bfloat16)
    d_up_low = d_up.astype(jnp.bfloat16)
    gate_part = contract_rows(hidden_low, d_gate_low)
    up_part = contract_rows(hidden_low, d_up_low)
    d_hidden = d_res_two + contract_cols(d_gate_low, full_gate) + contract_cols(d_up_low, full_up)
    d_res_one, first_gain_part, first_bias_part = norm_one_pull(d_hidden)
    d_branch_low = d_res_one.astype(jnp.bfloat16)
    out_part = contract_rows(attend_low, d_branch_low)
    d_attend = contract_cols(d_branch_low, full_out).astype(jnp.bfloat16)
    d_attend_low = (d_attend * keep_mask[:, None].astype(jnp.bfloat16)).reshape(
        group, head_count, head_size
    )
    delta = jnp.einsum("qhd,qhd->hq", d_attend_low.astype(jnp.float32), accum)

    def back_tile(grad_query, tile_set, seg_key):
        key_tile = tile_set[0].reshape(group, head_count, head_size)
        value_tile = tile_set[1].reshape(group, head_count, head_size)
        scores, allowed = tile_scores(query_low, key_tile, seg_query, seg_key, score_scale)
        prob_rows = jnp.where(allowed, jnp.exp(scores - log_total[:, :, None]), 0.0)
        d_probs = jnp.einsum(
            "qhd,khd->hqk", d_attend_low, value_tile, preferred_element_type=jnp.float32
        )
        d_score_low = (prob_rows * (d_probs - delta[:, :, None])).astype(jnp.bfloat16)
        grad_query = (
            grad_query
            + jnp.einsum("hqk,khd->qhd", d_score_low, key_tile, preferred_element_type=jnp.float32)
            * score_scale
        )
        grad_key = (
            jnp.einsum("hqk,qhd->khd", d_score_low, query_low, preferred_element_type=jnp.float32)
            * score_scale
        )
        grad_value = jnp.einsum(
            "hqk,qhd->khd",
            prob_rows.astype(jnp.bfloat16),
            d_attend_low,
            preferred_element_type=jnp.float32,
        )
        return (
            grad_query,
            jnp.concatenate(
                [grad_key.reshape(group, width), grad_value.reshape(group, width)], axis=1
            ),
        )

    grad_query = zero_accum
    grad_query, blocks = run_groups(
        (
            lax.all_gather(key_low, "blk", axis=0, tiled=True),
            lax.all_gather(value_low, "blk", axis=0, tiled=True),
        ),
        group,
        lengths_row,
        seg_query,
        grad_query,
        back_tile,
        (group, 2 * width),
    )
    blocks = blocks.reshape(-1, 2 * width)
    back_result = (grad_query, blocks)
    grad_query = back_result[0]
    owned_pairs = lax.psum_scatter(
        back_result[1].astype(jnp.bfloat16), "blk", scatter_dimension=0, tiled=True
    ).astype(jnp.float32)
    key_sum = owned_pairs[:, :width]
    value_sum = owned_pairs[:, width:]
    d_query_pre = query_pull(grad_query.astype(jnp.bfloat16).astype(jnp.float32))[0]
    d_key_low = key_sum.astype(jnp.bfloat16).astype(jnp.float32)
    d_key_pre = key_pull(d_key_low.reshape(group, head_count, head_size))[0]
    d_value_low = value_sum.astype(jnp.bfloat16).astype(jnp.float32)
    d_joined_low = jnp.concatenate(
        [d_query_pre.reshape(group, width), d_key_pre.reshape(group, width), d_value_low], axis=1
    ).astype(jnp.bfloat16)
    in_part = contract_rows(tokens_low, d_joined_low)
    input_grad = (d_res_one + contract_cols(d_joined_low, full_in)).astype(jnp.bfloat16)
    by_rows = (
        lax.psum_scatter(
            in_part.astype(jnp.bfloat16), "dp", scatter_dimension=0, tiled=True
        ).astype(jnp.float32),
        lax.psum_scatter(
            out_part.astype(jnp.bfloat16), "dp", scatter_dimension=0, tiled=True
        ).astype(jnp.float32),
        lax.psum_scatter(
            gate_part.astype(jnp.bfloat16), "dp", scatter_dimension=0, tiled=True
        ).astype(jnp.float32),
        lax.psum_scatter(
            up_part.astype(jnp.bfloat16), "dp", scatter_dimension=0, tiled=True
        ).astype(jnp.float32),
        lax.psum_scatter(
            down_part.astype(jnp.bfloat16), "dp", scatter_dimension=0, tiled=True
        ).astype(jnp.float32),
        lax.psum_scatter(
            first_gain_part.astype(jnp.bfloat16), "dp", scatter_dimension=0, tiled=True
        ).astype(jnp.float32),
        lax.psum_scatter(
            first_bias_part.astype(jnp.bfloat16), "dp", scatter_dimension=0, tiled=True
        ).astype(jnp.float32),
        lax.psum_scatter(
            second_gain_part.astype(jnp.bfloat16), "dp", scatter_dimension=0, tiled=True
        ).astype(jnp.float32),
        lax.psum_scatter(
            second_bias_part.astype(jnp.bfloat16), "dp", scatter_dimension=0, tiled=True
        ).astype(jnp.float32),
    )
    summed = (
        lax.psum_scatter(
            by_rows[0].astype(jnp.bfloat16), "blk", scatter_dimension=0, tiled=True
        ).astype(jnp.float32),
        lax.psum_scatter(
            by_rows[1].astype(jnp.bfloat16), "blk", scatter_dimension=0, tiled=True
        ).astype(jnp.float32),
        lax.psum_scatter(
            by_rows[2].astype(jnp.bfloat16), "blk", scatter_dimension=0, tiled=True
        ).astype(jnp.float32),
        lax.psum_scatter(
            by_rows[3].astype(jnp.bfloat16), "blk", scatter_dimension=0, tiled=True
        ).astype(jnp.float32),
        lax.psum_scatter(
            by_rows[4].astype(jnp.bfloat16), "blk", scatter_dimension=0, tiled=True
        ).astype(jnp.float32),
        lax.psum_scatter(
            by_rows[5].astype(jnp.bfloat16), "blk", scatter_dimension=0, tiled=True
        ).astype(jnp.float32),
        lax.psum_scatter(
            by_rows[6].astype(jnp.bfloat16), "blk", scatter_dimension=0, tiled=True
        ).astype(jnp.float32),
        lax.psum_scatter(
            by_rows[7].astype(jnp.bfloat16), "blk", scatter_dimension=0, tiled=True
        ).astype(jnp.float32),
        lax.psum_scatter(
            by_rows[8].astype(jnp.bfloat16), "blk", scatter_dimension=0, tiled=True
        ).astype(jnp.float32),
    )
    return (
        outputs_f.astype(jnp.bfloat16)[None],
        input_grad[None],
        summed[0],
        summed[1],
        summed[2],
        summed[3],
        summed[4],
        summed[5],
        summed[6],
        summed[7],
        summed[8],
    )


MESH_IDS = pl.DeviceIdType.MESH
LANES = 128
HALF = 64
QUART = 32


def mm(left, right):
    return lax.dot_general(
        left, right, (((1,), (0,)), ((), ())), preferred_element_type=jnp.float32
    )


def mt(left, right):
    return lax.dot_general(
        left, right, (((1,), (1,)), ((), ())), preferred_element_type=jnp.float32
    )


def tm(left, right):
    return lax.dot_general(
        left, right, (((0,), (0,)), ((), ())), preferred_element_type=jnp.float32
    )


class Wire:
    def __init__(self, send_sem, recv_sem, is_inner):
        self.send_sem, self.recv_sem, self.is_inner = send_sem, recv_sem, is_inner
        self.sends, self.slots = 0, 0
        self.sent = {None: [], True: [], False: []}

    def slot(self):
        self.slots += 1
        return self.slots - 1

    def copy(self, src, dst, peer, slot):
        self.sends += 1
        return pltpu.make_async_remote_copy(
            src_ref=src,
            dst_ref=dst,
            send_sem=self.send_sem.at[self.sends - 1],
            recv_sem=self.recv_sem.at[slot],
            device_id=peer,
            device_id_type=MESH_IDS,
        )

    def push(self, src, dst, peer, slot=None, inner=None):
        slot = self.slot() if slot is None else slot
        copy = self.copy(src, dst, peer, slot)
        self.sent[inner].append(copy)
        if inner is None:
            copy.start()
        else:
            pl.when(self.is_inner == inner)(copy.start)
        return slot

    def arrive(self, slot, dst, peer):
        pltpu.make_async_remote_copy(
            src_ref=dst,
            dst_ref=dst,
            send_sem=self.send_sem.at[0],
            recv_sem=self.recv_sem.at[slot],
            device_id=peer,
            device_id_type=MESH_IDS,
        ).wait_recv()

    def finish(self):
        for inner, copies in self.sent.items():

            def drain(copies=copies):
                for copy in copies:
                    copy.wait_send()

            if inner is None:
                drain()
            else:
                pl.when(self.is_inner == inner)(drain)


class Plane:
    def __init__(self, planes):
        dp, self.blk = lax.axis_index("dp"), lax.axis_index("blk")
        self.z, self.x = dp // 2, dp % 2
        self.dp = dp
        self.partner = self.z + 1 - 2 * (self.z % 2)
        self.other = planes // 2 - self.z // (planes // 2)
        self.outer = (planes - 1) * (self.other - 1)
        self.inner = ((self.z + 1) // 2) % 2
        self.order = (self.other, self.outer, self.partner, self.z)
        self.side = (self.z * 2 + (1 - self.x), self.blk)

    def at(self, plane):
        return (plane * 2 + self.x, self.blk)


class Spread:
    def __init__(self, wire, place, target, tail):
        self.wire, self.place, self.target = wire, place, target
        self.height, self.main = target.shape[1], target.shape[1] - tail

    def block(self, plane, column):
        return self.target.at[plane * 2 + column, 0 : self.main]

    def pair(self, plane):
        return self.target.at[pl.ds(plane * 2, 2), self.main : self.height]

    def along(self, source, own, slots):
        p = self.place
        self.wire.push(source, own, p.at(p.partner), slots[2])
        self.wire.push(source, own, p.at(p.other), slots[0] + (1 - p.inner))

    def start(self):
        p, wire = self.place, self.wire
        self.z_slots = [wire.slot() for _ in range(3)]
        own = self.block(p.z, p.x)
        self.along(own, own, self.z_slots)

    def start_side(self):
        p, wire = self.place, self.wire
        self.x_slots = [wire.slot() for _ in range(4)]
        own = self.block(p.z, p.x)
        wire.push(own, own, p.side, self.x_slots[3])
        if self.main < self.height:
            rest = self.target.at[p.dp, self.main : self.height]
            self.rest_slot = wire.push(rest, rest, p.side)

    def tail(self):
        p, wire = self.place, self.wire
        rest = self.target.at[p.z * 2 + (1 - p.x), self.main : self.height]
        wire.arrive(self.rest_slot, rest, p.side)
        self.t_slots = [wire.slot() for _ in range(3)]
        self.along(self.pair(p.z), self.pair(p.z), self.t_slots)

    def relay(self, j):
        p, wire = self.place, self.wire
        plane = p.order[j]
        block = self.block(plane, p.x)
        wire.arrive(self.z_slots[j], block, p.side)
        if j < 2:
            wire.push(block, block, p.at(p.partner), self.z_slots[j], inner=True)
        wire.push(block, block, p.side, self.x_slots[j])
        if self.main < self.height:
            pair = self.pair(plane)
            wire.arrive(self.t_slots[j], pair, p.side)
            if j < 2:
                wire.push(pair, pair, p.at(p.partner), self.t_slots[j], inner=True)

    def settle(self):
        p = self.place
        for j in range(4):
            self.wire.arrive(self.x_slots[j], self.block(p.order[j], 1 - p.x), p.side)


class Collect:
    def __init__(self, wire, place, buffers):
        self.wire, self.place = wire, place
        self.part, self.inbox, self.staged, self.landing = buffers[:4]
        self.height, self.main = self.part.shape[2], self.inbox.shape[1]
        self.split = self.main < self.height
        if self.split:
            self.t_landing, self.t_staged, self.t_cross, self.t_kept = buffers[4:]

    def pair(self, plane):
        return self.part.at[:, plane, self.main : self.height]

    def send(self):
        p, wire = self.place, self.wire
        self.x_slots = [wire.slot() for _ in range(4)]
        for j in (1, 0, 2, 3):
            plane = p.order[j]
            wire.push(
                self.part.at[1 - p.x, plane, 0 : self.main],
                self.inbox.at[plane],
                p.side,
                self.x_slots[j],
            )
        self.z_slots = [wire.slot() for _ in range(4)]
        if self.split:
            self.t_slots = [wire.slot() for _ in range(4)]
            for j in range(3):
                wire.push(
                    self.pair(p.order[j]),
                    self.t_landing.at[j],
                    p.at(p.partner),
                    self.t_slots[j],
                    inner=None if j == 2 else False,
                )

    def first(self, j):
        p, wire = self.place, self.wire
        plane = p.order[j]
        wire.arrive(self.x_slots[j], self.inbox.at[plane], p.side)
        both = self.part[p.x, plane, 0 : self.main].astype(jnp.float32)
        both = both + self.inbox[plane].astype(jnp.float32)
        self.staged[plane] = both.astype(jnp.bfloat16)
        wire.push(
            self.staged.at[plane],
            self.landing.at[j],
            p.at(p.partner),
            self.z_slots[j],
            inner=None if j == 2 else False,
        )

    def second(self, j):
        p, wire = self.place, self.wire
        plane = p.order[j]
        copy = wire.copy(self.staged.at[plane], self.landing.at[3], p.at(plane), self.z_slots[3])
        wire.sent[True].append(copy)
        if self.split:
            t_copy = wire.copy(
                self.t_staged.at[j], self.t_landing.at[3], p.at(plane), self.t_slots[3]
            )
            wire.sent[True].append(t_copy)

        @pl.when(wire.is_inner)
        def _():
            wire.arrive(self.z_slots[j], self.landing.at[j], p.side)
            both = self.staged[plane].astype(jnp.float32) + self.landing[j].astype(jnp.float32)
            self.staged[plane] = both.astype(jnp.bfloat16)
            copy.start()
            if self.split:
                wire.arrive(self.t_slots[j], self.t_landing.at[j], p.side)
                rest = self.part[:, plane, self.main : self.height].astype(jnp.float32)
                rest = rest + self.t_landing[j].astype(jnp.float32)
                self.t_staged[j] = rest.astype(jnp.bfloat16)
                t_copy.start()

    def tail(self):
        p, wire = self.place, self.wire
        for j in (2, 3):
            wire.arrive(self.t_slots[j], self.t_landing.at[j], p.side)

        def rest_of(column):
            rest = self.part[column, p.z, self.main : self.height].astype(jnp.float32)
            for j in (2, 3):
                rest = rest + self.t_landing[j, column].astype(jnp.float32)
            return rest

        self.t_kept[...] = rest_of(p.x)
        self.t_cross[0] = rest_of(1 - p.x).astype(jnp.bfloat16)
        self.cross_slot = wire.push(self.t_cross.at[0], self.t_cross.at[1], p.side)

    def total(self):
        p, wire = self.place, self.wire
        wire.arrive(self.x_slots[3], self.inbox.at[p.z], p.side)
        total = self.part[p.x, p.z, 0 : self.main].astype(jnp.float32)
        total = total + self.inbox[p.z].astype(jnp.float32)
        for j in (2, 3):
            wire.arrive(self.z_slots[j], self.landing.at[j], p.side)
            total = total + self.landing[j].astype(jnp.float32)
        if not self.split:
            return total
        wire.arrive(self.cross_slot, self.t_cross.at[1], p.side)
        rest = self.t_kept[...] + self.t_cross[1].astype(jnp.float32)
        return jnp.concatenate([total, rest], axis=0)


def fused(
    depth,
    lens,
    freq,
    xin,
    cot,
    p_in,
    p_mlp,
    p_out,
    p_down,
    outputs,
    input_grad,
    g_in,
    g_mlp,
    g_out,
    g_down,
    xs,
    r_in,
    r_mlp,
    s_out,
    w_in,
    w_gate,
    w_up,
    w_down,
    w_out,
    params,
    cos_tab,
    sin_tab,
    seg_tab,
    qm,
    kw,
    vw,
    prob,
    att,
    s_att,
    r_att,
    norm_one,
    hid,
    hs,
    gate_pre,
    up_pre,
    act,
    s_mix,
    r_mix,
    t_mix,
    dres_two,
    dms,
    dgate,
    dup,
    s_dh,
    r_dh,
    t_dh,
    dres_one,
    s_da,
    r_da,
    acc_q,
    acc_k,
    acc_v,
    dj,
    s_ig,
    r_ig,
    t_ig,
    sum_in,
    sum_gate,
    sum_up,
    sum_down,
    b_out,
    rb_out,
    sum_out,
    f_gate,
    s_gmlp,
    r_gmlp,
    s_gin,
    r_gin,
    send_sem,
    recv_sem,
):
    planes, cols = depth, 4
    tok = xin.shape[0]
    row_len = tok * cols
    place = Plane(planes)
    dp, blk = place.dp, place.blk
    bf16, f32 = jnp.bfloat16, jnp.float32

    row_of, core_of = blk // 2, blk % 2
    near_at = row_of * 2 + (1 - core_of)
    across_at = (1 - row_of) * 2 + core_of
    corner_at = (1 - row_of) * 2 + (1 - core_of)
    near, across = (dp, near_at), (dp, across_at)

    def lane(k):
        return (dp, (blk + k) % cols)

    def lane_from(k):
        return (blk + cols - k) % cols

    lanes = range(1, cols)
    wire = Wire(send_sem, recv_sem, place.inner == 1)
    barrier = pltpu.get_barrier_semaphore()
    peers = [place.side] + [place.at(plane) for plane in place.order[:3]]
    peers = peers + [lane(k) for k in lanes]
    for peer in peers:
        pl.semaphore_signal(barrier, inc=1, device_id=peer, device_id_type=MESH_IDS)
    pl.semaphore_wait(barrier, len(peers))

    def to_lanes(source_of, target):
        return [wire.push(source_of((blk + k) % cols), target.at[blk], lane(k)) for k in lanes]

    def from_lanes(slots, target):
        for k, slot in zip(lanes, slots):
            wire.arrive(slot, target.at[lane_from(k)], lane(k))

    def gather_start(source, target):
        return [
            wire.push(source, target.at[blk], across),
            wire.push(source, target.at[blk], near),
        ]

    def gather_relay(slots, target):
        wire.arrive(slots[0], target.at[across_at], across)
        slots.append(wire.push(target.at[across_at], target.at[across_at], near))

    def gather_done(slots, target):
        wire.arrive(slots[1], target.at[near_at], near)
        wire.arrive(slots[2], target.at[corner_at], near)

    def sum_start(part, inbox):
        return [
            wire.push(part.at[corner_at], inbox.at[0], near),
            wire.push(part.at[near_at], inbox.at[1], near),
        ]

    def sum_relay(slots, part, inbox, staged):
        wire.arrive(slots[0], inbox.at[0], near)
        staged[...] = (part[across_at].astype(f32) + inbox[0].astype(f32)).astype(bf16)
        slots.append(wire.push(staged, inbox.at[2], across))

    def sum_done(slots, part, inbox):
        wire.arrive(slots[1], inbox.at[1], near)
        total = part[blk].astype(f32) + inbox[1].astype(f32)
        wire.arrive(slots[2], inbox.at[2], across)
        return total + inbox[2].astype(f32)

    in_slots = to_lanes(lambda to: p_in.at[to], r_in)
    s_out[blk, dp] = p_out[...]
    w_down[dp] = p_down[...]
    tail = 0
    out_spread = Spread(wire, place, s_out.at[blk], 0)
    out_spread.start()
    out_spread.start_side()
    down_spread = Spread(wire, place, w_down, tail)
    down_spread.start()
    down_spread.start_side()
    mlp_slots = to_lanes(lambda to: p_mlp.at[to], r_mlp)
    xs[blk] = xin[...]
    x_slots = gather_start(xin, xs)
    r_in[blk] = p_in[blk]
    r_mlp[blk] = p_mlp[blk]

    lengths = [lens[0, j] for j in range(lens.shape[1])]

    def layout(positions):
        segment = jnp.zeros_like(positions)
        begins = jnp.zeros_like(positions)
        bound = jnp.int32(0)
        for length in lengths:
            bound = bound + length
            passed = positions >= bound
            segment = segment + jnp.where(passed, 1, 0)
            begins = begins + jnp.where(passed, length, 0)
        return segment, positions - begins

    seg_rows, offsets = layout(lax.broadcasted_iota(jnp.int32, (row_len, LANES), 0))
    seg_tab[...] = seg_rows
    seg_key = layout(lax.broadcasted_iota(jnp.int32, (8, row_len), 1))[0][0:1]
    lane_ids = lax.broadcasted_iota(jnp.int32, (1, LANES), 1)
    low_half = lane_ids < HALF
    front = lane_ids % HALF < QUART
    angles = offsets.astype(f32) * freq[0:1]
    cos_tab[...] = jnp.cos(angles)
    sin_tab[...] = jnp.where(front, -1.0, 1.0) * jnp.sin(angles)

    def turn(window):
        return jnp.where(
            front, pltpu.roll(window, LANES - QUART, 1), pltpu.roll(window, QUART, 1)
        )

    from_lanes(in_slots, r_in)
    rows = 24
    w_in[dp] = jnp.concatenate(
        [r_in[j, 0:rows, :].astype(f32) for j in range(cols)], axis=0
    ).astype(bf16)
    in_spread = Spread(wire, place, w_in, tail)
    in_spread.start()
    in_spread.start_side()
    for j in (2, 0, 1):
        out_spread.relay(j)
    from_lanes(mlp_slots, r_mlp)
    mlp_own = [r_mlp[j].astype(f32) for j in range(cols)]
    w_gate[dp] = jnp.concatenate([part[0:rows] for part in mlp_own], axis=0).astype(bf16)
    w_up[dp] = jnp.concatenate([part[rows:] for part in mlp_own], axis=0).astype(bf16)
    gate_spread = Spread(wire, place, w_gate, tail)
    up_spread = Spread(wire, place, w_up, tail)
    gate_spread.start()
    for j in (2, 0, 1):
        in_spread.relay(j)
    gate_spread.start_side()
    up_spread.start()
    up_spread.start_side()
    gather_relay(x_slots, xs)
    out_spread.settle()
    out_lanes = gather_start(s_out.at[blk], s_out)
    for j in (2, 0, 1):
        down_spread.relay(j)
    gather_done(x_slots, xs)
    in_spread.settle()

    width = xin.shape[1]
    group = 2
    chunk = group * tok

    def project(step, carry):
        start = pl.multiple_of(step * chunk, chunk)
        here = pl.ds(start, chunk)
        tokens = xs[pl.ds(step * group, group)].reshape(chunk, width)
        joined = mm(tokens, w_in[...].reshape(width, w_in.shape[2]))
        cosine, sine = cos_tab[here, :], sin_tab[here, :]

        def rotate(number):
            window = joined[:, number * LANES : (number + 1) * LANES]
            return window * cosine + turn(window) * sine

        scale = HALF ** -0.5
        queries = rotate(0).astype(bf16).astype(f32) * scale
        qm[0, here, :] = jnp.where(low_half, queries, 0.0).astype(bf16)
        qm[1, here, :] = jnp.where(low_half, 0.0, queries).astype(bf16)
        kw[0, here, :] = rotate(1).astype(bf16)
        vw[0, here, :] = joined[:, 2 * LANES : 3 * LANES].astype(bf16)
        both = rotate(3)
        qm[2, here, :] = jnp.where(low_half, both.astype(bf16).astype(f32) * scale, 0.0).astype(bf16)
        kw[1, here, :] = jnp.where(low_half, pltpu.roll(both, HALF, 1), 0.0).astype(bf16)
        vw[1, here, :] = joined[:, 4 * LANES : 5 * LANES].astype(bf16)
        return carry

    lax.fori_loop(0, cols // group, project, 0)

    def attend(head):
        window = head // 2

        def step_fn(step, carry):
            here = pl.ds(pl.multiple_of(step * chunk, chunk), chunk)
            scores = mt(qm[head, here, :], kw[window])
            allowed = seg_tab[here, :][:, 0:1] == seg_key
            scores = jnp.where(allowed, scores, NEG)
            top = jnp.max(scores, axis=1, keepdims=True)
            raised = jnp.exp(scores - top)
            total = jnp.sum(raised, axis=1, keepdims=True)
            prob_low = (raised * (1.0 / total)).astype(bf16)
            prob[head, here, :] = prob_low
            mixed = mm(prob_low, vw[window])
            if head == 1:
                mixed = jnp.where(low_half, att[0, here, :], mixed)
            att[window, here, :] = mixed
            return carry

        lax.fori_loop(0, row_len // chunk, step_fn, 0)

    attend(0)
    attend(1)
    attend(2)
    last_segment = lens.shape[1] - 1
    for j in range(cols):
        here = slice(j * tok, (j + 1) * tok)
        kept = seg_tab[here, :] < last_segment
        s_att[j, :, 0:LANES] = jnp.where(kept, att[0, here, :], 0.0).astype(bf16)
        s_att[j, :, LANES : 2 * LANES] = jnp.where(kept, att[1, here, :], 0.0).astype(bf16)
    att_slots = to_lanes(lambda to: s_att.at[to], r_att)
    r_att[blk] = s_att[blk]

    gather_relay(out_lanes, s_out)
    for j in (2, 0, 1):
        gate_spread.relay(j)
    gather_done(out_lanes, s_out)
    shards = planes * 2 * cols
    per_quarter = shards // cols
    head_rows = per_quarter * rows
    for quarter in range(cols):
        w_out[quarter, 0:head_rows, :] = jnp.concatenate(
            [
                s_out[s % cols, s // cols, 0:rows, :].astype(f32)
                for s in range(quarter * per_quarter, (quarter + 1) * per_quarter)
            ],
            axis=0,
        ).astype(bf16)
        w_out[quarter, head_rows:, :] = jnp.zeros(
            (w_out.shape[1] - head_rows, width), bf16
        )
    column = lax.broadcasted_iota(jnp.int32, (LANES, width), 1).astype(f32)
    owner = jnp.floor((column + 0.5) * (1.0 / rows))
    inside = column - owner * rows
    unit = (
        inside == lax.broadcasted_iota(jnp.int32, (LANES, width), 0).astype(f32)
    ).astype(bf16)
    tails = jnp.concatenate(
        [
            s_out[s % cols, s // cols, rows : rows + 8, 0:LANES].astype(f32)
            for s in range(shards)
        ],
        axis=0,
    ).astype(bf16)
    shard_ids = lax.broadcasted_iota(jnp.int32, (shards, 8, width), 0).astype(f32)
    shard_hit = (shard_ids == owner[0:1].reshape(1, 1, width)).astype(f32)
    params[...] = jnp.sum(mm(tails, unit).reshape(shards, 8, width) * shard_hit, axis=0)
    gain_one, bias_one = params[0:1, :], params[1:2, :]
    gain_two, bias_two = params[2:3, :], params[3:4, :]

    def normalize(residual):
        centered = residual - jnp.mean(residual, axis=1, keepdims=True)
        variance = jnp.mean(centered * centered, axis=1, keepdims=True)
        spread = lax.rsqrt(variance + EPS)
        return centered * spread, spread

    def normalize_back(grad, normal, spread, gain):
        inner = grad * gain
        mean_inner = jnp.mean(inner, axis=1, keepdims=True)
        mean_both = jnp.mean(inner * normal, axis=1, keepdims=True)
        return (inner - mean_inner - normal * mean_both) * spread

    def column_sum(value):
        return jnp.sum(value, axis=0, keepdims=True)

    from_lanes(att_slots, r_att)
    branch = mm(r_att[0], w_out[0])
    for quarter in range(1, cols):
        branch = branch + mm(r_att[quarter], w_out[quarter])
    normal, spread_one = normalize(xin[...].astype(f32) + branch)
    norm_one[...] = normal
    hidden = normal * gain_one + bias_one
    hid[...] = hidden
    hs[blk] = hidden.astype(bf16)
    hid_slots = gather_start(hs.at[blk], hs)
    gate_spread.settle()
    gather_relay(hid_slots, hs)
    for j in (2, 0, 1):
        up_spread.relay(j)
    gather_done(hid_slots, hs)
    up_spread.settle()

    units = w_gate.shape[2]
    wide = 256
    strips = units // wide

    def expand(step, carry):
        here = pl.ds(pl.multiple_of(step * wide, wide), wide)
        tokens = hs[...].reshape(row_len, width)
        gate = mm(tokens, w_gate[:, :, here].reshape(width, wide))
        up = mm(tokens, w_up[:, :, here].reshape(width, wide))
        gate_pre[:, here] = gate
        up_pre[:, here] = up
        act[:, here] = (gate / (1.0 + jnp.exp(-gate)) * up).astype(bf16)
        return carry

    lax.fori_loop(0, strips, expand, 0)
    down_spread.settle()

    def contract(step, carry):
        here = pl.ds(pl.multiple_of(step * wide, wide), wide)
        mixed = mm(act[...], w_down[:, :, here].reshape(units, wide))
        s_mix[:, :, here] = mixed.reshape(cols, tok, wide).astype(bf16)
        return carry

    lax.fori_loop(0, width // wide, contract, 0)
    mix_slots = sum_start(s_mix, r_mix)
    sum_relay(mix_slots, s_mix, r_mix, t_mix)
    mlp_out = sum_done(mix_slots, s_mix, r_mix)
    normal, spread_two = normalize(hid[...] + mlp_out)
    outputs[...] = (normal * gain_two + bias_two).astype(bf16)
    grad = cot[...].astype(f32)
    second_gain = column_sum(grad * normal)
    second_bias = column_sum(grad)
    d_two = normalize_back(grad, normal, spread_two, gain_two)
    dres_two[...] = d_two
    dms[blk] = d_two.astype(bf16)
    dm_slots = gather_start(dms.at[blk], dms)
    gather_relay(dm_slots, dms)
    gather_done(dm_slots, dms)

    down_sum = Collect(wire, place, sum_down)
    gate_sum = Collect(wire, place, sum_gate)
    up_sum = Collect(wire, place, sum_up)
    in_sum = Collect(wire, place, sum_in)
    out_sum = Collect(wire, place, sum_out)
    half = 4

    def fill_parts(part, left_of, right):
        height = part.shape[2]

        def step_fn(step, carry):
            here = pl.ds(pl.multiple_of(step * half * height, LANES), half * height)
            product = tm(left_of(here), right())
            for j in range(half):
                part[j % 2, step * (half // 2) + j // 2] = product[
                    j * height : (j + 1) * height
                ].astype(bf16)
            return carry

        lax.fori_loop(0, planes * 2 // half, step_fn, 0)

    fill_parts(down_sum.part, lambda here: act[:, here], lambda: dms[...].reshape(row_len, width))
    down_sum.send()

    block = w_down.shape[1]

    def active_grads(step, carry):
        here = pl.ds(pl.multiple_of(step * half * block, LANES), half * block)
        d_active = mt(
            dms[...].reshape(row_len, width),
            w_down[pl.ds(step * half, half)].reshape(half * block, width),
        )
        gate, up = gate_pre[:, here], up_pre[:, here]
        sg = 1.0 / (1.0 + jnp.exp(-gate))
        dgate[:, here] = (d_active * up * sg * (1.0 + gate * (1.0 - sg))).astype(bf16)
        dup[:, here] = (d_active * gate * sg).astype(bf16)
        return carry

    lax.fori_loop(0, planes * 2 // half, active_grads, 0)
    block = w_gate.shape[1]

    def hidden_grads(step, carry):
        here = pl.ds(pl.multiple_of(step * half * block, LANES), half * block)
        those = pl.ds(step * half, half)
        mixed = mt(dgate[...], w_gate[those].reshape(half * block, units)) + mt(
            dup[...], w_up[those].reshape(half * block, units)
        )
        s_dh[:, :, here] = mixed.reshape(cols, tok, half * block).astype(bf16)
        return carry

    lax.fori_loop(0, planes * 2 // half, hidden_grads, 0)
    dh_slots = sum_start(s_dh, r_dh)

    def hidden_rows(here):
        return hs[:, :, here].reshape(row_len, half * block)

    fill_parts(gate_sum.part, hidden_rows, lambda: dgate[...])
    gate_sum.send()
    sum_relay(dh_slots, s_dh, r_dh, t_dh)
    fill_parts(up_sum.part, hidden_rows, lambda: dup[...])
    up_sum.send()
    down_sum.first(1)
    down_sum.first(0)
    d_hidden = dres_two[...] + sum_done(dh_slots, s_dh, r_dh)
    down_sum.second(1)
    down_sum.first(2)
    normal = norm_one[...]
    first_gain = column_sum(d_hidden * normal)
    first_bias = column_sum(d_hidden)
    d_one = normalize_back(d_hidden, normal, spread_one, gain_one)
    dres_one[...] = d_one
    d_branch = d_one.astype(bf16)
    mine = pl.ds(pl.multiple_of(blk * tok, tok), tok)
    kept = seg_tab[mine, :][:, 0:1] < last_segment
    for quarter in range(cols):
        pulled = mt(d_branch, w_out[quarter]).astype(bf16).astype(f32)
        s_da[quarter] = jnp.where(kept, pulled, 0.0).astype(bf16)
    da_slots = to_lanes(lambda to: s_da.at[to], r_da)
    r_da[blk] = s_da[blk]

    vectors = jnp.concatenate(
        [first_gain, first_bias, second_gain, second_bias, jnp.zeros((4, width), f32)], axis=0
    )
    tails = mt(
        (shard_hit * vectors.reshape(1, 8, width)).reshape(shards * 8, width).astype(bf16), unit
    )
    for quarter in range(cols):
        product = tm(r_att[quarter], d_branch)
        for t in range(per_quarter):
            s = quarter * per_quarter + t
            owner_dp = s // cols
            lower = jnp.concatenate(
                [tails[s * 8 : s * 8 + 8], jnp.zeros((8, width - LANES), f32)], axis=1
            )
            b_out[s % cols, owner_dp % 2, owner_dp // 2] = jnp.concatenate(
                [product[t * rows : (t + 1) * rows], lower], axis=0
            ).astype(bf16)
    out_blk = to_lanes(lambda to: b_out.at[to], rb_out)
    rb_out[blk] = b_out[blk]

    down_sum.second(0)
    from_lanes(da_slots, r_da)
    def attend_back(head):
        window = head // 2
        fresh = head != 1

        def step_fn(step, carry):
            here = pl.ds(pl.multiple_of(step * chunk, chunk), chunk)
            d_out = r_da[pl.ds(step * group, group), :, window * LANES : (window + 1) * LANES]
            d_out = d_out.reshape(chunk, LANES).astype(f32)
            if head == 0:
                d_out = jnp.where(low_half, d_out, 0.0)
            if head == 1:
                d_out = jnp.where(low_half, 0.0, d_out)
            d_low = d_out.astype(bf16)
            delta = jnp.sum(d_out * att[window, here, :], axis=1, keepdims=True)
            prob_low = prob[head, here, :]
            d_prob = mt(d_low, vw[window])
            d_score = (prob_low.astype(f32) * (d_prob - delta)).astype(bf16)
            d_query = mm(d_score, kw[window]) * (HALF ** -0.5)
            if head == 1:
                d_query = jnp.where(low_half, acc_q[0, here, :], d_query)
            acc_q[window, here, :] = d_query
            d_key = tm(d_score, qm[head, here, :])
            d_value = tm(prob_low, d_low)
            if fresh:

                @pl.when(step == 0)
                def _():
                    acc_k[window] = d_key
                    acc_v[window] = d_value

                @pl.when(step != 0)
                def _():
                    acc_k[window] = acc_k[window] + d_key
                    acc_v[window] = acc_v[window] + d_value
            else:
                acc_k[window] = acc_k[window] + d_key
                acc_v[window] = acc_v[window] + d_value
            return carry

        lax.fori_loop(0, row_len // chunk, step_fn, 0)

    attend_back(0)
    gate_sum.first(1)
    attend_back(1)
    attend_back(2)

    cosine, sine = cos_tab[...], sin_tab[...]

    def rotate_back(vector):
        vector = vector.astype(bf16).astype(f32)
        return (vector * cosine - turn(vector) * sine).astype(bf16)

    dj[:, 0:LANES] = rotate_back(acc_q[0])
    dj[:, LANES : 2 * LANES] = rotate_back(acc_k[0])
    dj[:, 2 * LANES : 3 * LANES] = acc_v[0].astype(bf16)
    dj[:, 3 * LANES : 4 * LANES] = rotate_back(acc_q[1] + pltpu.roll(acc_k[1], HALF, 1))
    dj[:, 4 * LANES : 5 * LANES] = acc_v[1].astype(bf16)

    gate_sum.first(0)
    fill_parts(in_sum.part, lambda here: xs[:, :, here].reshape(row_len, half * block), lambda: dj[...])

    def input_grads(step, carry):
        here = pl.ds(pl.multiple_of(step * half * block, LANES), half * block)
        mixed = mt(dj[...], w_in[pl.ds(step * half, half)].reshape(half * block, w_in.shape[2]))
        s_ig[:, :, here] = mixed.reshape(cols, tok, half * block).astype(bf16)
        return carry

    lax.fori_loop(0, planes * 2 // half, input_grads, 0)
    ig_slots = sum_start(s_ig, r_ig)

    gate_sum.second(1)
    gate_sum.first(2)
    sum_relay(ig_slots, s_ig, r_ig, t_ig)
    g_down[...] = down_sum.total()
    gate_sum.second(0)
    up_sum.first(1)
    from_lanes(out_blk, rb_out)
    for side_at in range(2):
        gathered = rb_out[0, side_at].astype(f32)
        for j in range(1, cols):
            gathered = gathered + rb_out[j, side_at].astype(f32)
        out_sum.part[side_at] = gathered.astype(bf16)
    out_sum.send()
    in_sum.send()
    up_sum.first(0)
    up_sum.second(1)
    up_sum.first(2)
    f_gate[...] = gate_sum.total()
    up_sum.second(0)
    grad_in = dres_one[...] + sum_done(ig_slots, s_ig, r_ig)
    input_grad[...] = grad_in.astype(bf16)
    for j in (1, 0, 2):
        out_sum.first(j)
    in_sum.first(1)
    up_total = up_sum.total()
    gate_total = f_gate[...]
    for j in range(cols):
        here = slice(j * rows, (j + 1) * rows)
        s_gmlp[j] = jnp.concatenate([gate_total[here], up_total[here]], axis=0).astype(bf16)
    gmlp_slots = to_lanes(lambda to: s_gmlp.at[to], r_gmlp)
    r_gmlp[blk] = s_gmlp[blk]
    in_sum.first(0)
    out_sum.second(1)
    out_sum.second(0)
    in_sum.second(1)
    in_sum.first(2)
    in_sum.second(0)
    g_out[...] = out_sum.total()
    from_lanes(gmlp_slots, r_gmlp)
    g_mlp[...] = r_gmlp[...]
    in_total = in_sum.total()
    for j in range(cols):
        s_gin[j] = jnp.concatenate(
            [in_total[j * rows : (j + 1) * rows], jnp.zeros((8, in_total.shape[1]), f32)], axis=0
        ).astype(bf16)
    gin_slots = to_lanes(lambda to: s_gin.at[to], r_gin)
    r_gin[blk] = s_gin[blk]
    from_lanes(gin_slots, r_gin)
    g_in[...] = r_gin[...]
    wire.finish()


def fast_shards(
    depth,
    inputs,
    doc_lengths,
    project_in,
    project_out,
    gate_weight,
    up_weight,
    down_weight,
    first_gain,
    first_bias,
    second_gain,
    second_bias,
    cotangent,
):
    cols = 4
    tok, width = inputs.shape[1:]
    rows = project_in.shape[0]
    ff = gate_weight.shape[1]
    ring = depth * 2
    row_len = tok * cols
    units = ff // cols
    block = units // ring
    head_width = width // cols
    in_width = 5 * LANES
    bf16, f32 = jnp.bfloat16, jnp.float32

    kinds = project_in.reshape(rows, 3, cols, head_width)
    pairs, singles = kinds[..., :LANES], kinds[..., LANES:]
    p_in = jnp.concatenate(
        [pairs[:, 0], pairs[:, 1], pairs[:, 2], singles[:, 0], singles[:, 1], singles[:, 2]],
        axis=-1,
    ).transpose(1, 0, 2)
    p_in = jnp.pad(p_in, ((0, 0), (0, 32 - rows), (0, in_width - p_in.shape[2])))

    def by_owner(weight):
        return weight.reshape(rows, ring, cols, block).transpose(2, 0, 1, 3).reshape(cols, rows, units)

    p_mlp = jnp.concatenate([by_owner(gate_weight), by_owner(up_weight)], axis=1)
    vectors = jnp.stack([first_gain, first_bias, second_gain, second_bias])
    p_out = jnp.concatenate(
        [project_out, jnp.pad(vectors, ((0, 4), (0, width - rows)))], axis=0
    )
    lane_ids = np.arange(LANES) % QUART
    freq = jnp.asarray(
        np.broadcast_to(BASE ** (-2.0 * lane_ids / HALF), (8, LANES)).astype(np.float32)
    )

    def scratch(*shape, kind=bf16):
        return pltpu.VMEM(shape, kind)

    def sums(height, across, tail=0):
        main = height - tail
        buffers = [
            scratch(2, depth, height, across),
            scratch(depth, main, across),
            scratch(depth, main, across),
            scratch(4, main, across),
        ]
        if tail:
            buffers = buffers + [
                scratch(4, 2, tail, across),
                scratch(2, 2, tail, across),
                scratch(2, tail, across),
                scratch(tail, across, kind=f32),
            ]
        return tuple(buffers)

    stacked = scratch(cols, tok, width)
    heads = 3
    buffers = [
        stacked,
        scratch(cols, 32, in_width),
        scratch(cols, 2 * rows, units),
        scratch(cols, ring, 32, width),
        scratch(ring, cols * rows, in_width),
        scratch(ring, cols * rows, units),
        scratch(ring, cols * rows, units),
        scratch(ring, block, width),
        scratch(cols, 2 * LANES, width),
        scratch(8, width, kind=f32),
        scratch(row_len, LANES, kind=f32),
        scratch(row_len, LANES, kind=f32),
        scratch(row_len, LANES, kind=jnp.int32),
        scratch(heads, row_len, LANES),
        scratch(2, row_len, LANES),
        scratch(2, row_len, LANES),
        scratch(heads, row_len, row_len),
        scratch(2, row_len, LANES, kind=f32),
        scratch(cols, tok, 2 * LANES),
        scratch(cols, tok, 2 * LANES),
        scratch(tok, width, kind=f32),
        scratch(tok, width, kind=f32),
        stacked,
        scratch(row_len, units, kind=f32),
        scratch(row_len, units, kind=f32),
        scratch(row_len, units),
        stacked,
        scratch(3, tok, width),
        scratch(tok, width),
        scratch(tok, width, kind=f32),
        stacked,
        scratch(row_len, units),
        scratch(row_len, units),
        stacked,
        scratch(3, tok, width),
        scratch(tok, width),
        scratch(tok, width, kind=f32),
        scratch(cols, tok, 2 * LANES),
        scratch(cols, tok, 2 * LANES),
        scratch(2, row_len, LANES, kind=f32),
        scratch(2, row_len, LANES, kind=f32),
        scratch(2, row_len, LANES, kind=f32),
        scratch(row_len, in_width),
        stacked,
        scratch(3, tok, width),
        scratch(tok, width),
        sums(cols * rows, in_width),
        sums(cols * rows, units),
        sums(cols * rows, units),
        sums(block, width),
        scratch(cols, 2, depth, 32, width),
        scratch(cols, 2, depth, 32, width),
        sums(32, width, 0),
        scratch(cols * rows, units, kind=f32),
        scratch(cols, 2 * rows, units),
        scratch(cols, 2 * rows, units),
        scratch(cols, 32, in_width),
        scratch(cols, 32, in_width),
        pltpu.SemaphoreType.DMA((240,)),
        pltpu.SemaphoreType.DMA((240,)),
    ]
    vmem = pl.BlockSpec(memory_space=pltpu.VMEM)
    tokens = row_len * width
    outputs, input_grad, g_in, g_mlp, g_out, g_down = pl.pallas_call(
        functools.partial(fused, depth),
        out_shape=(
            jax.ShapeDtypeStruct((tok, width), bf16),
            jax.ShapeDtypeStruct((tok, width), bf16),
            jax.ShapeDtypeStruct((cols, 32, in_width), bf16),
            jax.ShapeDtypeStruct((cols, 2 * rows, units), bf16),
            jax.ShapeDtypeStruct((32, width), f32),
            jax.ShapeDtypeStruct((block, width), f32),
        ),
        in_specs=[pl.BlockSpec(memory_space=pltpu.SMEM)] + [vmem] * 7,
        out_specs=(vmem,) * 6,
        scratch_shapes=buffers,
        compiler_params=pltpu.CompilerParams(
            collective_id=0, has_side_effects=True, vmem_limit_bytes=60 * 2**20
        ),
        cost_estimate=pl.CostEstimate(
            flops=6 * tokens * (3 * units + 4 * head_width),
            bytes_accessed=8 * 2**20,
            transcendentals=3 * row_len * row_len,
        ),
        name="layer",
    )(doc_lengths, freq, inputs[0], cotangent[0], p_in, p_mlp, p_out, down_weight)

    wide_in = g_in[:, :rows].astype(f32).transpose(1, 0, 2)
    kind_pairs = wide_in[..., : 3 * LANES].reshape(rows, cols, 3, LANES)
    kind_singles = wide_in[..., 3 * LANES : 3 * LANES + 3 * HALF].reshape(rows, cols, 3, HALF)
    in_grad = jnp.concatenate([kind_pairs, kind_singles], axis=-1)
    in_grad = in_grad.transpose(0, 2, 1, 3).reshape(rows, 3 * width)

    def by_column(part):
        return (
            part.reshape(cols, rows, ring, block)
            .transpose(1, 2, 0, 3)
            .reshape(rows, ff)
            .astype(f32)
        )

    small = g_out[rows : rows + 4, :rows]
    return (
        outputs[None],
        input_grad[None],
        in_grad,
        g_out[:rows],
        by_column(g_mlp[:, :rows]),
        by_column(g_mlp[:, rows:]),
        g_down,
        small[0],
        small[1],
        small[2],
        small[3],
    )


def pick(sizes):
    def chosen(*args):
        tok, width = args[0].shape[1:]
        ring, cols = sizes["dp"], sizes["blk"]
        fits = (
            ring == 8
            and cols == 4
            and tok == LANES
            and HEADS == 3 * cols
            and width == HEADS * HALF
            and args[2].shape[0] == 24
            and args[4].shape[1] == 4 * width
        )
        if fits:
            return fast_shards(ring // 2, *args)
        return shards(*args)

    return chosen


def solution(mesh):
    placed = (
        P("dp", "blk", None),
        P("dp", None),
        P(("dp", "blk"), None),
        P(("dp", "blk"), None),
        P(("dp", "blk"), None),
        P(("dp", "blk"), None),
        P(("dp", "blk"), None),
        P(("dp", "blk")),
        P(("dp", "blk")),
        P(("dp", "blk")),
        P(("dp", "blk")),
        P("dp", "blk", None),
    )
    return jax.shard_map(
        pick(dict(mesh.shape)),
        mesh=mesh,
        in_specs=placed,
        out_specs=(
            P("dp", "blk", None),
            P("dp", "blk", None),
            P(("dp", "blk"), None),
            P(("dp", "blk"), None),
            P(("dp", "blk"), None),
            P(("dp", "blk"), None),
            P(("dp", "blk"), None),
            P(("dp", "blk")),
            P(("dp", "blk")),
            P(("dp", "blk")),
            P(("dp", "blk")),
        ),
        check_vma=False,
    )
```

```python
import functools

import jax
import jax.numpy as jnp
import numpy as np
from jax import lax
from jax.experimental import pallas as pl
from jax.experimental.pallas import tpu as pltpu
from jax.sharding import PartitionSpec as P

HEADS = 12


NEG = -1e30
EPS = 1e-05
BASE = 1000.0


def doc_layout(lengths_row, positions):
    bounds = jnp.cumsum(lengths_row)
    passed = positions[:, None] >= bounds[None, :]
    segment = jnp.sum(passed.astype(jnp.int32), axis=1)
    begins = jnp.sum(jnp.where(passed, lengths_row[None, :], 0), axis=1)
    return (segment, positions - begins)


def rotary(vectors, offsets):
    half_size = vectors.shape[-1] // 2
    frequency = BASE ** (-2.0 * jnp.arange(half_size, dtype=jnp.float32) / vectors.shape[-1])
    angles = offsets.astype(jnp.float32)[:, None] * frequency[None, :]
    cosine = jnp.concatenate([jnp.cos(angles), jnp.cos(angles)], axis=1)[:, None, :]
    sine_rows = jnp.concatenate([jnp.sin(angles), jnp.sin(angles)], axis=1)[:, None, :]
    first_half = vectors[..., :half_size]
    second_half = vectors[..., half_size:]
    turned = jnp.concatenate([-second_half, first_half], axis=-1)
    return vectors * cosine + turned * sine_rows


def layer_norm(residual, gain_row, bias_row):
    row_mean = jnp.mean(residual, axis=-1, keepdims=True)
    centered = residual - row_mean
    variance = jnp.mean(centered * centered, axis=-1, keepdims=True)
    return centered * lax.rsqrt(variance + EPS) * gain_row + bias_row


def contract_rows(left, right):
    return lax.dot_general(
        left, right, (((0,), (0,)), ((), ())), preferred_element_type=jnp.float32
    )


def contract_cols(left, right):
    return lax.dot_general(
        left, right, (((1,), (1,)), ((), ())), preferred_element_type=jnp.float32
    )


def tile_scores(query_tile, key_tile, seg_query, seg_key, score_scale):
    scores = (
        jnp.einsum("qhd,khd->hqk", query_tile, key_tile, preferred_element_type=jnp.float32)
        * score_scale
    )
    allowed = (seg_query[:, None] == seg_key[None, :])[None, :, :]
    return (jnp.where(allowed, scores, NEG), allowed)


def run_groups(pieces, group, lengths_row, seg_query, carried, tile_fn, extra_shape):
    group_count = pieces[0].shape[0] // group

    def group_step(carried_in, number):
        offset = number * group
        tile_set = tuple(
            (lax.dynamic_slice_in_dim(piece_rows, offset, group, 0) for piece_rows in pieces)
        )
        positions = offset + jnp.arange(group, dtype=jnp.int32)
        seg_key, unused_offsets = doc_layout(lengths_row, positions)
        touches = (seg_key[0] <= seg_query[-1]) & (seg_query[0] <= seg_key[-1])

        def active(state_in):
            return tile_fn(state_in, tile_set, seg_key)

        def skipped(state_in):
            return (state_in, jnp.zeros(extra_shape, jnp.float32))

        return lax.cond(touches, active, skipped, carried_in)

    return lax.scan(group_step, carried, jnp.arange(group_count, dtype=jnp.int32))


def shards(
    inputs,
    doc_lengths,
    project_in,
    project_out,
    gate_weight,
    up_weight,
    down_weight,
    first_gain,
    first_bias,
    second_gain,
    second_bias,
    cotangent,
):
    group = inputs.shape[1]
    width = inputs.shape[2]
    head_count = HEADS
    head_size = width // head_count
    score_scale = head_size ** (-0.5)
    cycle_rank = lax.axis_index("blk")
    positions = cycle_rank * group + jnp.arange(group, dtype=jnp.int32)
    lengths_row = doc_lengths[0]
    seg_query, offsets = doc_layout(lengths_row, positions)
    keep_mask = seg_query < lengths_row.shape[0] - 1
    keep_float = keep_mask.astype(jnp.float32)
    fetched = (
        lax.all_gather(project_in, ("dp", "blk"), axis=0, tiled=True),
        lax.all_gather(project_out, ("dp", "blk"), axis=0, tiled=True),
        lax.all_gather(gate_weight, ("dp", "blk"), axis=0, tiled=True),
        lax.all_gather(up_weight, ("dp", "blk"), axis=0, tiled=True),
        lax.all_gather(down_weight, ("dp", "blk"), axis=0, tiled=True),
        lax.all_gather(first_gain, ("dp", "blk"), axis=0, tiled=True),
        lax.all_gather(first_bias, ("dp", "blk"), axis=0, tiled=True),
        lax.all_gather(second_gain, ("dp", "blk"), axis=0, tiled=True),
        lax.all_gather(second_bias, ("dp", "blk"), axis=0, tiled=True),
    )
    full_in, full_out, full_gate, full_up, full_down = (
        fetched[0],
        fetched[1],
        fetched[2],
        fetched[3],
        fetched[4],
    )
    gain_one = fetched[5].astype(jnp.float32)
    bias_one = fetched[6].astype(jnp.float32)
    gain_two = fetched[7].astype(jnp.float32)
    bias_two = fetched[8].astype(jnp.float32)
    tokens_low = inputs[0]
    tokens_f = tokens_low.astype(jnp.float32)
    joined = jnp.dot(tokens_low, full_in, preferred_element_type=jnp.float32)
    query_raw = joined[:, :width].reshape(group, head_count, head_size)
    key_raw = joined[:, width : 2 * width].reshape(group, head_count, head_size)
    value_low = joined[:, 2 * width :].astype(jnp.bfloat16)
    query_rot, query_pull = jax.vjp(lambda vectors: rotary(vectors, offsets), query_raw)
    key_rot, key_pull = jax.vjp(lambda vectors: rotary(vectors, offsets), key_raw)
    query_low = query_rot.astype(jnp.bfloat16)
    key_low = key_rot.reshape(group, width).astype(jnp.bfloat16)

    def stats_tile(carried, tile_set, seg_key):
        row_top, row_total = carried
        key_tile = tile_set[0].reshape(group, head_count, head_size)
        scores, allowed = tile_scores(query_low, key_tile, seg_query, seg_key, score_scale)
        new_top = jnp.maximum(row_top, jnp.max(scores, axis=2))
        shrink = jnp.exp(row_top - new_top)
        added = jnp.sum(jnp.where(allowed, jnp.exp(scores - new_top[:, :, None]), 0.0), axis=2)
        return ((new_top, row_total * shrink + added), jnp.zeros((1,), jnp.float32))

    init_stats = (
        jnp.full((head_count, group), NEG, jnp.float32),
        jnp.zeros((head_count, group), jnp.float32),
    )
    carried = init_stats
    carried, unused = run_groups(
        (lax.all_gather(key_low, "blk", axis=0, tiled=True),),
        group,
        lengths_row,
        seg_query,
        carried,
        stats_tile,
        (1,),
    )
    row_top, row_total = carried
    log_total = row_top + jnp.log(row_total)

    def output_tile(accum, tile_set, seg_key):
        key_tile = tile_set[0].reshape(group, head_count, head_size)
        value_tile = tile_set[1].reshape(group, head_count, head_size)
        scores, allowed = tile_scores(query_low, key_tile, seg_query, seg_key, score_scale)
        prob_low = jnp.where(allowed, jnp.exp(scores - log_total[:, :, None]), 0.0).astype(
            jnp.bfloat16
        )
        accum = accum + jnp.einsum(
            "hqk,khd->qhd", prob_low, value_tile, preferred_element_type=jnp.float32
        )
        return (accum, jnp.zeros((1,), jnp.float32))

    zero_accum = jnp.zeros((group, head_count, head_size), jnp.float32)
    accum = zero_accum
    accum, unused = run_groups(
        (
            lax.all_gather(key_low, "blk", axis=0, tiled=True),
            lax.all_gather(value_low, "blk", axis=0, tiled=True),
        ),
        group,
        lengths_row,
        seg_query,
        accum,
        output_tile,
        (1,),
    )
    attend_low = (accum * keep_float[:, None, None]).reshape(group, width).astype(jnp.bfloat16)
    branch = jnp.dot(attend_low, full_out, preferred_element_type=jnp.float32)
    residual_one = tokens_f + branch
    hidden, norm_one_pull = jax.vjp(layer_norm, residual_one, gain_one, bias_one)
    hidden_low = hidden.astype(jnp.bfloat16)
    gate_pre = jnp.dot(hidden_low, full_gate, preferred_element_type=jnp.float32)
    up_pre = jnp.dot(hidden_low, full_up, preferred_element_type=jnp.float32)
    activated, swiglu_pull = jax.vjp(
        lambda gate_in, up_in: jax.nn.silu(gate_in) * up_in, gate_pre, up_pre
    )
    active_low = activated.astype(jnp.bfloat16)
    mlp_out = jnp.dot(active_low, full_down, preferred_element_type=jnp.float32)
    outputs_f, norm_two_pull = jax.vjp(layer_norm, hidden + mlp_out, gain_two, bias_two)
    refetched = (
        lax.all_gather(project_in, ("dp", "blk"), axis=0, tiled=True),
        lax.all_gather(project_out, ("dp", "blk"), axis=0, tiled=True),
        lax.all_gather(gate_weight, ("dp", "blk"), axis=0, tiled=True),
        lax.all_gather(up_weight, ("dp", "blk"), axis=0, tiled=True),
        lax.all_gather(down_weight, ("dp", "blk"), axis=0, tiled=True),
    )
    full_in, full_out, full_gate, full_up, full_down = (
        refetched[0],
        refetched[1],
        refetched[2],
        refetched[3],
        refetched[4],
    )
    d_res_two, second_gain_part, second_bias_part = norm_two_pull(cotangent[0].astype(jnp.float32))
    d_mlp_low = d_res_two.astype(jnp.bfloat16)
    down_part = contract_rows(active_low, d_mlp_low)
    d_active = contract_cols(d_mlp_low, full_down)
    d_gate, d_up = swiglu_pull(d_active)
    d_gate_low = d_gate.astype(jnp.bfloat16)
    d_up_low = d_up.astype(jnp.bfloat16)
    gate_part = contract_rows(hidden_low, d_gate_low)
    up_part = contract_rows(hidden_low, d_up_low)
    d_hidden = d_res_two + contract_cols(d_gate_low, full_gate) + contract_cols(d_up_low, full_up)
    d_res_one, first_gain_part, first_bias_part = norm_one_pull(d_hidden)
    d_branch_low = d_res_one.astype(jnp.bfloat16)
    out_part = contract_rows(attend_low, d_branch_low)
    d_attend = contract_cols(d_branch_low, full_out).astype(jnp.bfloat16)
    d_attend_low = (d_attend * keep_mask[:, None].astype(jnp.bfloat16)).reshape(
        group, head_count, head_size
    )
    delta = jnp.einsum("qhd,qhd->hq", d_attend_low.astype(jnp.float32), accum)

    def back_tile(grad_query, tile_set, seg_key):
        key_tile = tile_set[0].reshape(group, head_count, head_size)
        value_tile = tile_set[1].reshape(group, head_count, head_size)
        scores, allowed = tile_scores(query_low, key_tile, seg_query, seg_key, score_scale)
        prob_rows = jnp.where(allowed, jnp.exp(scores - log_total[:, :, None]), 0.0)
        d_probs = jnp.einsum(
            "qhd,khd->hqk", d_attend_low, value_tile, preferred_element_type=jnp.float32
        )
        d_score_low = (prob_rows * (d_probs - delta[:, :, None])).astype(jnp.bfloat16)
        grad_query = (
            grad_query
            + jnp.einsum("hqk,khd->qhd", d_score_low, key_tile, preferred_element_type=jnp.float32)
            * score_scale
        )
        grad_key = (
            jnp.einsum("hqk,qhd->khd", d_score_low, query_low, preferred_element_type=jnp.float32)
            * score_scale
        )
        grad_value = jnp.einsum(
            "hqk,qhd->khd",
            prob_rows.astype(jnp.bfloat16),
            d_attend_low,
            preferred_element_type=jnp.float32,
        )
        return (
            grad_query,
            jnp.concatenate(
                [grad_key.reshape(group, width), grad_value.reshape(group, width)], axis=1
            ),
        )

    grad_query = zero_accum
    grad_query, blocks = run_groups(
        (
            lax.all_gather(key_low, "blk", axis=0, tiled=True),
            lax.all_gather(value_low, "blk", axis=0, tiled=True),
        ),
        group,
        lengths_row,
        seg_query,
        grad_query,
        back_tile,
        (group, 2 * width),
    )
    blocks = blocks.reshape(-1, 2 * width)
    back_result = (grad_query, blocks)
    grad_query = back_result[0]
    owned_pairs = lax.psum_scatter(
        back_result[1].astype(jnp.bfloat16), "blk", scatter_dimension=0, tiled=True
    ).astype(jnp.float32)
    key_sum = owned_pairs[:, :width]
    value_sum = owned_pairs[:, width:]
    d_query_pre = query_pull(grad_query.astype(jnp.bfloat16).astype(jnp.float32))[0]
    d_key_low = key_sum.astype(jnp.bfloat16).astype(jnp.float32)
    d_key_pre = key_pull(d_key_low.reshape(group, head_count, head_size))[0]
    d_value_low = value_sum.astype(jnp.bfloat16).astype(jnp.float32)
    d_joined_low = jnp.concatenate(
        [d_query_pre.reshape(group, width), d_key_pre.reshape(group, width), d_value_low], axis=1
    ).astype(jnp.bfloat16)
    in_part = contract_rows(tokens_low, d_joined_low)
    input_grad = (d_res_one + contract_cols(d_joined_low, full_in)).astype(jnp.bfloat16)
    by_rows = (
        lax.psum_scatter(
            in_part.astype(jnp.bfloat16), "dp", scatter_dimension=0, tiled=True
        ).astype(jnp.float32),
        lax.psum_scatter(
            out_part.astype(jnp.bfloat16), "dp", scatter_dimension=0, tiled=True
        ).astype(jnp.float32),
        lax.psum_scatter(
            gate_part.astype(jnp.bfloat16), "dp", scatter_dimension=0, tiled=True
        ).astype(jnp.float32),
        lax.psum_scatter(
            up_part.astype(jnp.bfloat16), "dp", scatter_dimension=0, tiled=True
        ).astype(jnp.float32),
        lax.psum_scatter(
            down_part.astype(jnp.bfloat16), "dp", scatter_dimension=0, tiled=True
        ).astype(jnp.float32),
        lax.psum_scatter(
            first_gain_part.astype(jnp.bfloat16), "dp", scatter_dimension=0, tiled=True
        ).astype(jnp.float32),
        lax.psum_scatter(
            first_bias_part.astype(jnp.bfloat16), "dp", scatter_dimension=0, tiled=True
        ).astype(jnp.float32),
        lax.psum_scatter(
            second_gain_part.astype(jnp.bfloat16), "dp", scatter_dimension=0, tiled=True
        ).astype(jnp.float32),
        lax.psum_scatter(
            second_bias_part.astype(jnp.bfloat16), "dp", scatter_dimension=0, tiled=True
        ).astype(jnp.float32),
    )
    summed = (
        lax.psum_scatter(
            by_rows[0].astype(jnp.bfloat16), "blk", scatter_dimension=0, tiled=True
        ).astype(jnp.float32),
        lax.psum_scatter(
            by_rows[1].astype(jnp.bfloat16), "blk", scatter_dimension=0, tiled=True
        ).astype(jnp.float32),
        lax.psum_scatter(
            by_rows[2].astype(jnp.bfloat16), "blk", scatter_dimension=0, tiled=True
        ).astype(jnp.float32),
        lax.psum_scatter(
            by_rows[3].astype(jnp.bfloat16), "blk", scatter_dimension=0, tiled=True
        ).astype(jnp.float32),
        lax.psum_scatter(
            by_rows[4].astype(jnp.bfloat16), "blk", scatter_dimension=0, tiled=True
        ).astype(jnp.float32),
        lax.psum_scatter(
            by_rows[5].astype(jnp.bfloat16), "blk", scatter_dimension=0, tiled=True
        ).astype(jnp.float32),
        lax.psum_scatter(
            by_rows[6].astype(jnp.bfloat16), "blk", scatter_dimension=0, tiled=True
        ).astype(jnp.float32),
        lax.psum_scatter(
            by_rows[7].astype(jnp.bfloat16), "blk", scatter_dimension=0, tiled=True
        ).astype(jnp.float32),
        lax.psum_scatter(
            by_rows[8].astype(jnp.bfloat16), "blk", scatter_dimension=0, tiled=True
        ).astype(jnp.float32),
    )
    return (
        outputs_f.astype(jnp.bfloat16)[None],
        input_grad[None],
        summed[0],
        summed[1],
        summed[2],
        summed[3],
        summed[4],
        summed[5],
        summed[6],
        summed[7],
        summed[8],
    )


MESH_IDS = pl.DeviceIdType.MESH
LANES = 128
HALF = 64
QUART = 32
DT = 48


def mm(left, right):
    return lax.dot_general(
        left, right, (((1,), (0,)), ((), ())), preferred_element_type=jnp.float32
    )


def mt(left, right):
    return lax.dot_general(
        left, right, (((1,), (1,)), ((), ())), preferred_element_type=jnp.float32
    )


def tm(left, right):
    return lax.dot_general(
        left, right, (((0,), (0,)), ((), ())), preferred_element_type=jnp.float32
    )


def window_at(value, start):
    aligned = min(max(start // LANES * LANES, 0), value.shape[1] - LANES)
    if aligned == start:
        return value[:, aligned : aligned + LANES]
    aligned = min(aligned, value.shape[1] - 2 * LANES)
    two = value[:, aligned : aligned + 2 * LANES]
    return pltpu.roll(two, (aligned - start) % (2 * LANES), 1)[:, :LANES]


def gather_lanes(value, block, first, source):
    lanes = lax.broadcasted_iota(jnp.int32, (1, LANES), 1)
    result = None
    for number in range(first // block, (first + LANES - 1) // block + 1):
        piece = window_at(value, source(number, first))
        begin = number * block - first
        result = piece if result is None else jnp.where(lanes < begin, result, piece)
    return result


class Wire:
    def __init__(self, send_sem, recv_sem, is_inner):
        self.send_sem, self.recv_sem, self.is_inner = send_sem, recv_sem, is_inner
        self.sends, self.slots = 0, 0
        self.sent = {None: [], True: [], False: []}

    def slot(self):
        self.slots += 1
        return self.slots - 1

    def copy(self, src, dst, peer, slot):
        self.sends += 1
        return pltpu.make_async_remote_copy(
            src_ref=src,
            dst_ref=dst,
            send_sem=self.send_sem.at[self.sends - 1],
            recv_sem=self.recv_sem.at[slot],
            device_id=peer,
            device_id_type=MESH_IDS,
        )

    def push(self, src, dst, peer, slot=None, inner=None):
        slot = self.slot() if slot is None else slot
        copy = self.copy(src, dst, peer, slot)
        self.sent[inner].append(copy)
        if inner is None:
            copy.start()
        else:
            pl.when(self.is_inner == inner)(copy.start)
        return slot

    def arrive(self, slot, dst, peer):
        pltpu.make_async_remote_copy(
            src_ref=dst,
            dst_ref=dst,
            send_sem=self.send_sem.at[0],
            recv_sem=self.recv_sem.at[slot],
            device_id=peer,
            device_id_type=MESH_IDS,
        ).wait_recv()

    def finish(self):
        for inner, copies in self.sent.items():

            def drain(copies=copies):
                for copy in copies:
                    copy.wait_send()

            if inner is None:
                drain()
            else:
                pl.when(self.is_inner == inner)(drain)


class Plane:
    def __init__(self, planes):
        dp, self.blk = lax.axis_index("dp"), lax.axis_index("blk")
        self.z, self.x = dp // 2, dp % 2
        self.dp = dp
        self.partner = self.z + 1 - 2 * (self.z % 2)
        self.other = planes // 2 - self.z // (planes // 2)
        self.outer = (planes - 1) * (self.other - 1)
        self.inner = ((self.z + 1) // 2) % 2
        self.order = (self.other, self.outer, self.partner, self.z)
        self.side = (self.z * 2 + (1 - self.x), self.blk)

    def at(self, plane):
        return (plane * 2 + self.x, self.blk)


class Spread:
    def __init__(self, wire, place, target, tail):
        self.wire, self.place, self.target = wire, place, target
        self.height, self.main = target.shape[1], target.shape[1] - tail

    def block(self, plane, column):
        return self.target.at[plane * 2 + column, 0 : self.main]

    def pair(self, plane):
        return self.target.at[pl.ds(plane * 2, 2), self.main : self.height]

    def along(self, own, slots):
        p = self.place
        self.wire.push(own, own, p.at(p.partner), slots[2], inner=False)
        self.wire.push(own, own, p.at(p.other), slots[0] + (1 - p.inner))

    def outward(self, own, slots):
        p = self.place
        self.wire.push(own, own, p.at(p.partner), slots[2], inner=True)

    def start(self):
        p, wire = self.place, self.wire
        self.z_slots = [wire.slot() for _ in range(3)]
        self.along(self.block(p.z, p.x), self.z_slots)

    def start_out(self):
        p = self.place
        self.outward(self.block(p.z, p.x), self.z_slots)

    def start_side(self):
        p, wire = self.place, self.wire
        self.x_slots = [wire.slot() for _ in range(4)]
        own = self.block(p.z, p.x)
        wire.push(own, own, p.side, self.x_slots[3])
        if self.main < self.height:
            rest = self.target.at[p.dp, self.main : self.height]
            self.rest_slot = wire.push(rest, rest, p.side)

    def tail(self):
        p, wire = self.place, self.wire
        rest = self.target.at[p.z * 2 + (1 - p.x), self.main : self.height]
        wire.arrive(self.rest_slot, rest, p.side)
        self.t_slots = [wire.slot() for _ in range(3)]
        self.along(self.pair(p.z), self.t_slots)

    def tail_out(self):
        self.outward(self.pair(self.place.z), self.t_slots)

    def relay(self, j):
        p, wire = self.place, self.wire
        plane = p.order[j]
        block = self.block(plane, p.x)
        wire.arrive(self.z_slots[j], block, p.side)
        if j < 2:
            wire.push(block, block, p.at(p.partner), self.z_slots[j], inner=True)
        wire.push(block, block, p.side, self.x_slots[j])
    def pass_tail(self, j):
        p, wire = self.place, self.wire
        pair = self.pair(p.order[j])
        copy = wire.copy(pair, pair, p.at(p.partner), self.t_slots[j])
        wire.sent[True].append(copy)

        @pl.when(wire.is_inner)
        def _():
            wire.arrive(self.t_slots[j], pair, p.side)
            copy.start()

    def settle_tail(self):
        p, wire = self.place, self.wire
        wire.arrive(self.t_slots[2], self.pair(p.order[2]), p.side)

        @pl.when(jnp.logical_not(wire.is_inner))
        def _():
            for j in range(2):
                wire.arrive(self.t_slots[j], self.pair(p.order[j]), p.side)

    def settle(self):
        p = self.place
        for j in range(4):
            self.wire.arrive(self.x_slots[j], self.block(p.order[j], 1 - p.x), p.side)


class Collect:
    def __init__(self, wire, place, buffers):
        self.wire, self.place = wire, place
        self.part, self.inbox, self.staged, self.landing = buffers[:4]
        self.height, self.main = self.part.shape[2], self.inbox.shape[1]
        self.split = self.main < self.height
        if self.split:
            self.t_landing, self.t_staged, self.t_cross, self.t_kept = buffers[4:]

    def pair(self, plane):
        return self.part.at[:, plane, self.main : self.height]

    def send(self):
        p, wire = self.place, self.wire
        self.x_slots = [wire.slot() for _ in range(4)]
        for j in (1, 0, 2, 3):
            plane = p.order[j]
            wire.push(
                self.part.at[1 - p.x, plane, 0 : self.main],
                self.inbox.at[plane],
                p.side,
                self.x_slots[j],
            )
        self.z_slots = [wire.slot() for _ in range(4)]
        if self.split:
            self.t_slots = [wire.slot() for _ in range(4)]
            for j in (1, 0, 2):
                wire.push(
                    self.pair(p.order[j]),
                    self.t_landing.at[j],
                    p.at(p.partner),
                    self.t_slots[j],
                    inner=None if j == 2 else False,
                )

    def first(self, j):
        p, wire = self.place, self.wire
        plane = p.order[j]
        wire.arrive(self.x_slots[j], self.inbox.at[plane], p.side)
        both = self.part[p.x, plane, 0 : self.main].astype(jnp.float32)
        both = both + self.inbox[plane].astype(jnp.float32)
        self.staged[plane] = both.astype(jnp.bfloat16)
        wire.push(
            self.staged.at[plane],
            self.landing.at[j],
            p.at(p.partner),
            self.z_slots[j],
            inner=None if j == 2 else False,
        )

    def second(self, j):
        p, wire = self.place, self.wire
        plane = p.order[j]
        copy = wire.copy(self.staged.at[plane], self.landing.at[3], p.at(plane), self.z_slots[3])
        wire.sent[True].append(copy)

        @pl.when(wire.is_inner)
        def _():
            wire.arrive(self.z_slots[j], self.landing.at[j], p.side)
            both = self.staged[plane].astype(jnp.float32) + self.landing[j].astype(jnp.float32)
            self.staged[plane] = both.astype(jnp.bfloat16)
            copy.start()

    def second_tail(self, j):
        p, wire = self.place, self.wire
        plane = p.order[j]
        copy = wire.copy(self.t_staged.at[j], self.t_landing.at[3], p.at(plane), self.t_slots[3])
        wire.sent[True].append(copy)

        @pl.when(wire.is_inner)
        def _():
            wire.arrive(self.t_slots[j], self.t_landing.at[j], p.side)
            rest = self.part[:, plane, self.main : self.height].astype(jnp.float32)
            rest = rest + self.t_landing[j].astype(jnp.float32)
            self.t_staged[j] = rest.astype(jnp.bfloat16)
            copy.start()

    def tail(self):
        p, wire = self.place, self.wire
        for j in (2, 3):
            wire.arrive(self.t_slots[j], self.t_landing.at[j], p.side)

        def rest_of(column):
            rest = self.part[column, p.z, self.main : self.height].astype(jnp.float32)
            for j in (2, 3):
                rest = rest + self.t_landing[j, column].astype(jnp.float32)
            return rest

        self.t_kept[...] = rest_of(p.x)
        self.t_cross[0] = rest_of(1 - p.x).astype(jnp.bfloat16)
        self.cross_slot = wire.push(self.t_cross.at[0], self.t_cross.at[1], p.side)

    def total(self):
        p, wire = self.place, self.wire
        wire.arrive(self.x_slots[3], self.inbox.at[p.z], p.side)
        total = self.part[p.x, p.z, 0 : self.main].astype(jnp.float32)
        total = total + self.inbox[p.z].astype(jnp.float32)
        for j in (2, 3):
            wire.arrive(self.z_slots[j], self.landing.at[j], p.side)
            total = total + self.landing[j].astype(jnp.float32)
        if not self.split:
            return total
        wire.arrive(self.cross_slot, self.t_cross.at[1], p.side)
        rest = self.t_kept[...] + self.t_cross[1].astype(jnp.float32)
        return jnp.concatenate([total, rest], axis=0)


def fused(
    depth,
    lens,
    freq,
    xin,
    cot,
    in_rows,
    gate_rows,
    up_rows,
    out_rows,
    p_down,
    gain_a,
    bias_a,
    gain_b,
    bias_b,
    outputs,
    input_grad,
    g_in,
    g_mlp,
    g_out,
    g_down,
    xs,
    p_in,
    p_mlp,
    vectors_tab,
    r_in,
    r_mlp,
    s_out,
    w_in,
    w_gate,
    w_up,
    w_down,
    w_out,
    params,
    cos_tab,
    sin_tab,
    seg_tab,
    qm,
    kw,
    vw,
    prob,
    att,
    s_att,
    r_att,
    norm_one,
    hid,
    hs,
    gate_pre,
    up_pre,
    act,
    s_mix,
    r_mix,
    t_mix,
    dres_two,
    dms,
    dgate,
    dup,
    s_dh,
    r_dh,
    t_dh,
    dres_one,
    s_da,
    r_da,
    acc_q,
    acc_k,
    acc_v,
    dj,
    s_ig,
    r_ig,
    t_ig,
    sum_in,
    sum_gate,
    sum_up,
    sum_down,
    b_out,
    rb_out,
    tb_out,
    sum_out,
    f_gate,
    s_gmlp,
    r_gmlp,
    s_gin,
    r_gin,
    send_sem,
    recv_sem,
):
    planes, cols = depth, 4
    tok = xin.shape[0]
    row_len = tok * cols
    place = Plane(planes)
    dp, blk = place.dp, place.blk
    bf16, f32 = jnp.bfloat16, jnp.float32

    row_of, core_of = blk // 2, blk % 2
    near_at = row_of * 2 + (1 - core_of)
    across_at = (1 - row_of) * 2 + core_of
    corner_at = (1 - row_of) * 2 + (1 - core_of)
    near, across = (dp, near_at), (dp, across_at)

    def lane(k):
        return (dp, (blk + k) % cols)

    def lane_from(k):
        return (blk + cols - k) % cols

    lanes = range(1, cols)
    wire = Wire(send_sem, recv_sem, place.inner == 1)
    barrier = pltpu.get_barrier_semaphore()
    peers = [place.side] + [place.at(plane) for plane in place.order[:3]]
    peers = peers + [lane(k) for k in lanes]
    for peer in peers:
        pl.semaphore_signal(barrier, inc=1, device_id=peer, device_id_type=MESH_IDS)

    rows = 24
    width = xin.shape[1]
    lane_ids = lax.broadcasted_iota(jnp.int32, (1, LANES), 1)
    low_half = lane_ids < HALF
    head_width = width // cols
    joined_rows = in_rows[...].astype(f32)
    for j in range(cols):
        starts = [kind * width + j * head_width for kind in range(3)]
        windows = [window_at(joined_rows, start) for start in starts]
        windows.append(
            jnp.where(
                low_half,
                window_at(joined_rows, starts[0] + LANES),
                window_at(joined_rows, starts[1] + LANES - HALF),
            )
        )
        windows.append(jnp.where(low_half, window_at(joined_rows, starts[2] + LANES), 0.0))
        packed = jnp.concatenate(windows, axis=1)
        p_in[j] = jnp.concatenate(
            [packed, jnp.zeros((8, packed.shape[1]), f32)], axis=0
        ).astype(bf16)
    vectors_tab[...] = jnp.zeros_like(vectors_tab)
    for number, vector in enumerate((gain_a, bias_a, gain_b, bias_b)):
        vectors_tab[number : number + 1, 0:rows] = vector[...].astype(f32)
    lower = jnp.concatenate([vectors_tab[...], jnp.zeros((8, width - LANES), f32)], axis=1)
    s_out[blk, dp] = jnp.concatenate([out_rows[...].astype(f32), lower], axis=0).astype(bf16)
    pl.semaphore_wait(barrier, len(peers))

    def to_lanes(source_of, target):
        return [wire.push(source_of((blk + k) % cols), target.at[blk], lane(k)) for k in lanes]

    def from_lanes(slots, target):
        for k, slot in zip(lanes, slots):
            wire.arrive(slot, target.at[lane_from(k)], lane(k))

    def gather_start(source, target):
        return [
            wire.push(source, target.at[blk], across),
            wire.push(source, target.at[blk], near),
        ]

    def gather_relay(slots, target):
        wire.arrive(slots[0], target.at[across_at], across)
        slots.append(wire.push(target.at[across_at], target.at[across_at], near))

    def gather_done(slots, target):
        wire.arrive(slots[1], target.at[near_at], near)
        wire.arrive(slots[2], target.at[corner_at], near)

    def sum_start(part, inbox):
        return [
            wire.push(part.at[corner_at], inbox.at[0], near),
            wire.push(part.at[near_at], inbox.at[1], near),
        ]

    def sum_relay(slots, part, inbox, staged):
        wire.arrive(slots[0], inbox.at[0], near)
        staged[...] = (part[across_at].astype(f32) + inbox[0].astype(f32)).astype(bf16)
        slots.append(wire.push(staged, inbox.at[2], across))

    def sum_done(slots, part, inbox):
        wire.arrive(slots[1], inbox.at[1], near)
        total = part[blk].astype(f32) + inbox[1].astype(f32)
        wire.arrive(slots[2], inbox.at[2], across)
        return total + inbox[2].astype(f32)

    in_slots = to_lanes(lambda to: p_in.at[to], r_in)
    w_down[dp] = p_down[...]
    tail = 0
    out_spread = Spread(wire, place, s_out.at[blk], 0)
    out_spread.start()
    out_spread.start_out()
    out_spread.start_side()
    down_spread = Spread(wire, place, w_down, DT)
    down_spread.start()
    down_spread.start_out()
    down_spread.start_side()
    units = gate_rows.shape[1] // cols
    unit_block = units // (planes * 2)
    for at, weight in ((0, gate_rows), (rows, up_rows)):
        whole = weight[...].astype(f32)
        for j in range(cols):
            packed = jnp.concatenate(
                [
                    gather_lanes(
                        whole,
                        unit_block,
                        n * LANES,
                        lambda ring_at, lane: lane + (cols - 1) * unit_block * ring_at + unit_block * j,
                    )
                    for n in range(units // LANES)
                ],
                axis=1,
            )
            p_mlp[j, at : at + rows] = packed.astype(bf16)
    mlp_slots = to_lanes(lambda to: p_mlp.at[to], r_mlp)
    xs[blk] = xin[...]
    x_slots = gather_start(xin, xs)
    r_in[blk] = p_in[blk]
    r_mlp[blk] = p_mlp[blk]

    lengths = [lens[0, j] for j in range(lens.shape[1])]

    def layout(positions):
        segment = jnp.zeros_like(positions)
        begins = jnp.zeros_like(positions)
        bound = jnp.int32(0)
        for length in lengths:
            bound = bound + length
            passed = positions >= bound
            segment = segment + jnp.where(passed, 1, 0)
            begins = begins + jnp.where(passed, length, 0)
        return segment, positions - begins

    seg_rows, offsets = layout(lax.broadcasted_iota(jnp.int32, (row_len, LANES), 0))
    seg_tab[...] = seg_rows
    seg_key = layout(lax.broadcasted_iota(jnp.int32, (8, row_len), 1))[0][0:1]
    front = lane_ids % HALF < QUART
    angles = offsets.astype(f32) * freq[0:1]
    cos_tab[...] = jnp.cos(angles)
    sin_tab[...] = jnp.where(front, -1.0, 1.0) * jnp.sin(angles)

    def turn(window):
        return jnp.where(
            front, pltpu.roll(window, LANES - QUART, 1), pltpu.roll(window, QUART, 1)
        )

    from_lanes(in_slots, r_in)
    w_in[dp] = jnp.concatenate(
        [r_in[j, 0:rows, :].astype(f32) for j in range(cols)], axis=0
    ).astype(bf16)
    in_spread = Spread(wire, place, w_in, tail)
    in_spread.start()
    in_spread.start_out()
    in_spread.start_side()
    from_lanes(mlp_slots, r_mlp)
    mlp_own = [r_mlp[j].astype(f32) for j in range(cols)]
    w_gate[dp] = jnp.concatenate([part[0:rows] for part in mlp_own], axis=0).astype(bf16)
    w_up[dp] = jnp.concatenate([part[rows:] for part in mlp_own], axis=0).astype(bf16)
    gate_spread = Spread(wire, place, w_gate, tail)
    up_spread = Spread(wire, place, w_up, tail)
    gate_spread.start()
    gate_spread.start_side()
    up_spread.start_side()
    up_spread.start()
    for j in (2, 0, 1):
        out_spread.relay(j)
    in_spread.relay(2)
    in_spread.relay(0)
    down_spread.relay(2)
    in_spread.relay(1)
    down_spread.relay(0)
    down_spread.relay(1)
    gate_spread.start_out()
    up_spread.start_out()
    down_spread.tail()
    gather_relay(x_slots, xs)
    out_spread.settle()
    out_lanes = gather_start(s_out.at[blk], s_out)
    gate_spread.relay(2)
    gather_done(x_slots, xs)
    in_spread.settle()

    group = 2
    chunk = group * tok

    def project(step, carry):
        start = pl.multiple_of(step * chunk, chunk)
        here = pl.ds(start, chunk)
        tokens = xs[pl.ds(step * group, group)].reshape(chunk, width)
        joined = mm(tokens, w_in[...].reshape(width, w_in.shape[2]))
        cosine, sine = cos_tab[here, :], sin_tab[here, :]

        def rotate(number):
            window = joined[:, number * LANES : (number + 1) * LANES]
            return window * cosine + turn(window) * sine

        scale = HALF ** -0.5
        queries = rotate(0).astype(bf16).astype(f32) * scale
        qm[0, here, :] = jnp.where(low_half, queries, 0.0).astype(bf16)
        qm[1, here, :] = jnp.where(low_half, 0.0, queries).astype(bf16)
        kw[0, here, :] = rotate(1).astype(bf16)
        vw[0, here, :] = joined[:, 2 * LANES : 3 * LANES].astype(bf16)
        both = rotate(3)
        qm[2, here, :] = jnp.where(low_half, both.astype(bf16).astype(f32) * scale, 0.0).astype(bf16)
        kw[1, here, :] = jnp.where(low_half, pltpu.roll(both, HALF, 1), 0.0).astype(bf16)
        vw[1, here, :] = joined[:, 4 * LANES : 5 * LANES].astype(bf16)
        return carry

    lax.fori_loop(0, cols // group, project, 0)

    def attend(head):
        window = head // 2

        def step_fn(step, carry):
            here = pl.ds(pl.multiple_of(step * chunk, chunk), chunk)
            scores = mt(qm[head, here, :], kw[window])
            allowed = seg_tab[here, :][:, 0:1] == seg_key
            scores = jnp.where(allowed, scores, NEG)
            top = jnp.max(scores, axis=1, keepdims=True)
            raised = jnp.exp(scores - top)
            total = jnp.sum(raised, axis=1, keepdims=True)
            prob_low = (raised * (1.0 / total)).astype(bf16)
            prob[head, here, :] = prob_low
            mixed = mm(prob_low, vw[window])
            if head == 1:
                mixed = jnp.where(low_half, att[0, here, :], mixed)
            att[window, here, :] = mixed
            return carry

        lax.fori_loop(0, row_len // chunk, step_fn, 0)

    attend(0)
    attend(1)
    attend(2)
    last_segment = lens.shape[1] - 1
    for j in range(cols):
        here = slice(j * tok, (j + 1) * tok)
        kept = seg_tab[here, :] < last_segment
        s_att[j, :, 0:LANES] = jnp.where(kept, att[0, here, :], 0.0).astype(bf16)
        s_att[j, :, LANES : 2 * LANES] = jnp.where(kept, att[1, here, :], 0.0).astype(bf16)
    att_slots = to_lanes(lambda to: s_att.at[to], r_att)
    r_att[blk] = s_att[blk]

    gather_relay(out_lanes, s_out)
    gate_spread.relay(0)
    up_spread.relay(2)
    gate_spread.relay(1)
    gather_done(out_lanes, s_out)
    shards = planes * 2 * cols
    per_quarter = shards // cols
    head_rows = per_quarter * rows
    for quarter in range(cols):
        w_out[quarter, 0:head_rows, :] = jnp.concatenate(
            [
                s_out[s % cols, s // cols, 0:rows, :].astype(f32)
                for s in range(quarter * per_quarter, (quarter + 1) * per_quarter)
            ],
            axis=0,
        ).astype(bf16)
        w_out[quarter, head_rows:, :] = jnp.zeros(
            (w_out.shape[1] - head_rows, width), bf16
        )
    column = lax.broadcasted_iota(jnp.int32, (LANES, width), 1).astype(f32)
    owner = jnp.floor((column + 0.5) * (1.0 / rows))
    inside = column - owner * rows
    unit = (
        inside == lax.broadcasted_iota(jnp.int32, (LANES, width), 0).astype(f32)
    ).astype(bf16)
    tails = jnp.concatenate(
        [
            s_out[s % cols, s // cols, rows : rows + 8, 0:LANES].astype(f32)
            for s in range(shards)
        ],
        axis=0,
    ).astype(bf16)
    shard_ids = lax.broadcasted_iota(jnp.int32, (shards, 8, width), 0).astype(f32)
    shard_hit = (shard_ids == owner[0:1].reshape(1, 1, width)).astype(f32)
    params[...] = jnp.sum(mm(tails, unit).reshape(shards, 8, width) * shard_hit, axis=0)
    gain_one, bias_one = params[0:1, :], params[1:2, :]
    gain_two, bias_two = params[2:3, :], params[3:4, :]

    def normalize(residual):
        centered = residual - jnp.mean(residual, axis=1, keepdims=True)
        variance = jnp.mean(centered * centered, axis=1, keepdims=True)
        spread = lax.rsqrt(variance + EPS)
        return centered * spread, spread

    def normalize_back(grad, normal, spread, gain):
        inner = grad * gain
        mean_inner = jnp.mean(inner, axis=1, keepdims=True)
        mean_both = jnp.mean(inner * normal, axis=1, keepdims=True)
        return (inner - mean_inner - normal * mean_both) * spread

    def column_sum(value):
        return jnp.sum(value, axis=0, keepdims=True)

    from_lanes(att_slots, r_att)
    branch = mm(r_att[0], w_out[0])
    for quarter in range(1, cols):
        branch = branch + mm(r_att[quarter], w_out[quarter])
    normal, spread_one = normalize(xin[...].astype(f32) + branch)
    norm_one[...] = normal
    hidden = normal * gain_one + bias_one
    hid[...] = hidden
    hs[blk] = hidden.astype(bf16)
    hid_slots = gather_start(hs.at[blk], hs)
    up_spread.relay(0)
    up_spread.relay(1)
    down_spread.tail_out()
    for j in range(2):
        down_spread.pass_tail(j)
    gather_relay(hid_slots, hs)
    gate_spread.settle()
    gather_done(hid_slots, hs)
    up_spread.settle()

    wide = 256
    strips = units // wide

    def expand(step, carry):
        here = pl.ds(pl.multiple_of(step * wide, wide), wide)
        tokens = hs[...].reshape(row_len, width)
        gate = mm(tokens, w_gate[:, :, here].reshape(width, wide))
        up = mm(tokens, w_up[:, :, here].reshape(width, wide))
        gate_pre[:, here] = gate
        up_pre[:, here] = up
        act[:, here] = (gate / (1.0 + jnp.exp(-gate)) * up).astype(bf16)
        return carry

    lax.fori_loop(0, strips, expand, 0)
    down_spread.settle()
    down_spread.settle_tail()

    def contract(step, carry):
        here = pl.ds(pl.multiple_of(step * wide, wide), wide)
        mixed = mm(act[...], w_down[:, :, here].reshape(units, wide))
        s_mix[:, :, here] = mixed.reshape(cols, tok, wide).astype(bf16)
        return carry

    lax.fori_loop(0, width // wide, contract, 0)
    mix_slots = sum_start(s_mix, r_mix)
    sum_relay(mix_slots, s_mix, r_mix, t_mix)
    mlp_out = sum_done(mix_slots, s_mix, r_mix)
    normal, spread_two = normalize(hid[...] + mlp_out)
    outputs[...] = (normal * gain_two + bias_two).astype(bf16)
    grad = cot[...].astype(f32)
    second_gain = column_sum(grad * normal)
    second_bias = column_sum(grad)
    d_two = normalize_back(grad, normal, spread_two, gain_two)
    dres_two[...] = d_two
    dms[blk] = d_two.astype(bf16)
    dm_slots = gather_start(dms.at[blk], dms)
    gather_relay(dm_slots, dms)
    gather_done(dm_slots, dms)

    down_sum = Collect(wire, place, sum_down)
    gate_sum = Collect(wire, place, sum_gate)
    up_sum = Collect(wire, place, sum_up)
    in_sum = Collect(wire, place, sum_in)
    out_sum = Collect(wire, place, sum_out)
    half = 4

    def fill_parts(part, left_of, right):
        height = part.shape[2]

        def step_fn(step, carry):
            here = pl.ds(pl.multiple_of(step * half * height, LANES), half * height)
            product = tm(left_of(here), right())
            for j in range(half):
                part[j % 2, step * (half // 2) + j // 2] = product[
                    j * height : (j + 1) * height
                ].astype(bf16)
            return carry

        lax.fori_loop(0, planes * 2 // half, step_fn, 0)

    fill_parts(down_sum.part, lambda here: act[:, here], lambda: dms[...].reshape(row_len, width))
    down_sum.send()

    block = w_down.shape[1]

    def active_grads(step, carry):
        here = pl.ds(pl.multiple_of(step * half * block, LANES), half * block)
        d_active = mt(
            dms[...].reshape(row_len, width),
            w_down[pl.ds(step * half, half)].reshape(half * block, width),
        )
        gate, up = gate_pre[:, here], up_pre[:, here]
        sg = 1.0 / (1.0 + jnp.exp(-gate))
        dgate[:, here] = (d_active * up * sg * (1.0 + gate * (1.0 - sg))).astype(bf16)
        dup[:, here] = (d_active * gate * sg).astype(bf16)
        return carry

    lax.fori_loop(0, planes * 2 // half, active_grads, 0)
    block = w_gate.shape[1]

    def hidden_grads(step, carry):
        here = pl.ds(pl.multiple_of(step * half * block, LANES), half * block)
        those = pl.ds(step * half, half)
        mixed = mt(dgate[...], w_gate[those].reshape(half * block, units)) + mt(
            dup[...], w_up[those].reshape(half * block, units)
        )
        s_dh[:, :, here] = mixed.reshape(cols, tok, half * block).astype(bf16)
        return carry

    lax.fori_loop(0, planes * 2 // half, hidden_grads, 0)
    dh_slots = sum_start(s_dh, r_dh)

    def hidden_rows(here):
        return hs[:, :, here].reshape(row_len, half * block)

    fill_parts(gate_sum.part, hidden_rows, lambda: dgate[...])
    gate_sum.send()
    sum_relay(dh_slots, s_dh, r_dh, t_dh)
    fill_parts(up_sum.part, hidden_rows, lambda: dup[...])
    up_sum.send()
    down_sum.first(1)
    down_sum.first(0)
    d_hidden = dres_two[...] + sum_done(dh_slots, s_dh, r_dh)
    down_sum.first(2)
    normal = norm_one[...]
    first_gain = column_sum(d_hidden * normal)
    first_bias = column_sum(d_hidden)
    d_one = normalize_back(d_hidden, normal, spread_one, gain_one)
    dres_one[...] = d_one
    d_branch = d_one.astype(bf16)
    mine = pl.ds(pl.multiple_of(blk * tok, tok), tok)
    kept = seg_tab[mine, :][:, 0:1] < last_segment
    for quarter in range(cols):
        pulled = mt(d_branch, w_out[quarter]).astype(bf16).astype(f32)
        s_da[quarter] = jnp.where(kept, pulled, 0.0).astype(bf16)
    da_slots = to_lanes(lambda to: s_da.at[to], r_da)
    r_da[blk] = s_da[blk]

    vectors = jnp.concatenate(
        [first_gain, first_bias, second_gain, second_bias, jnp.zeros((4, width), f32)], axis=0
    )
    tails = mt(
        (shard_hit * vectors.reshape(1, 8, width)).reshape(shards * 8, width).astype(bf16), unit
    )
    for quarter in range(cols):
        product = tm(r_att[quarter], d_branch)
        for t in range(per_quarter):
            s = quarter * per_quarter + t
            owner_dp = s // cols
            lower = jnp.concatenate(
                [tails[s * 8 : s * 8 + 8], jnp.zeros((8, width - LANES), f32)], axis=1
            )
            b_out[s % cols, owner_dp % 2, owner_dp // 2] = jnp.concatenate(
                [product[t * rows : (t + 1) * rows], lower], axis=0
            ).astype(bf16)
    out_blk = sum_start(b_out, rb_out)

    sum_relay(out_blk, b_out, rb_out, tb_out)
    down_sum.second_tail(1)
    down_sum.second(1)
    from_lanes(da_slots, r_da)
    def attend_back(head):
        window = head // 2
        fresh = head != 1

        def step_fn(step, carry):
            here = pl.ds(pl.multiple_of(step * chunk, chunk), chunk)
            d_out = r_da[pl.ds(step * group, group), :, window * LANES : (window + 1) * LANES]
            d_out = d_out.reshape(chunk, LANES).astype(f32)
            if head == 0:
                d_out = jnp.where(low_half, d_out, 0.0)
            if head == 1:
                d_out = jnp.where(low_half, 0.0, d_out)
            d_low = d_out.astype(bf16)
            delta = jnp.sum(d_out * att[window, here, :], axis=1, keepdims=True)
            prob_low = prob[head, here, :]
            d_prob = mt(d_low, vw[window])
            d_score = (prob_low.astype(f32) * (d_prob - delta)).astype(bf16)
            d_query = mm(d_score, kw[window]) * (HALF ** -0.5)
            if head == 1:
                d_query = jnp.where(low_half, acc_q[0, here, :], d_query)
            acc_q[window, here, :] = d_query
            d_key = tm(d_score, qm[head, here, :])
            d_value = tm(prob_low, d_low)
            if fresh:

                @pl.when(step == 0)
                def _():
                    acc_k[window] = d_key
                    acc_v[window] = d_value

                @pl.when(step != 0)
                def _():
                    acc_k[window] = acc_k[window] + d_key
                    acc_v[window] = acc_v[window] + d_value
            else:
                acc_k[window] = acc_k[window] + d_key
                acc_v[window] = acc_v[window] + d_value
            return carry

        lax.fori_loop(0, row_len // chunk, step_fn, 0)

    attend_back(0)
    gate_sum.first(1)
    down_sum.second_tail(0)
    down_sum.second(0)
    attend_back(1)
    attend_back(2)

    cosine, sine = cos_tab[...], sin_tab[...]

    def rotate_back(vector):
        vector = vector.astype(bf16).astype(f32)
        return (vector * cosine - turn(vector) * sine).astype(bf16)

    dj[:, 0:LANES] = rotate_back(acc_q[0])
    dj[:, LANES : 2 * LANES] = rotate_back(acc_k[0])
    dj[:, 2 * LANES : 3 * LANES] = acc_v[0].astype(bf16)
    dj[:, 3 * LANES : 4 * LANES] = rotate_back(acc_q[1] + pltpu.roll(acc_k[1], HALF, 1))
    dj[:, 4 * LANES : 5 * LANES] = acc_v[1].astype(bf16)

    gate_sum.first(0)
    down_sum.tail()
    fill_parts(in_sum.part, lambda here: xs[:, :, here].reshape(row_len, half * block), lambda: dj[...])

    def input_grads(step, carry):
        here = pl.ds(pl.multiple_of(step * half * block, LANES), half * block)
        mixed = mt(dj[...], w_in[pl.ds(step * half, half)].reshape(half * block, w_in.shape[2]))
        s_ig[:, :, here] = mixed.reshape(cols, tok, half * block).astype(bf16)
        return carry

    lax.fori_loop(0, planes * 2 // half, input_grads, 0)
    ig_slots = sum_start(s_ig, r_ig)

    gate_sum.second(1)
    gate_sum.first(2)
    sum_relay(ig_slots, s_ig, r_ig, t_ig)
    gate_sum.second(0)
    up_sum.first(1)
    out_sum.part[...] = sum_done(out_blk, b_out, rb_out).astype(bf16)
    in_sum.send()
    out_sum.send()
    up_sum.first(0)
    up_sum.second(1)
    up_sum.first(2)
    f_gate[...] = gate_sum.total()
    up_sum.second(0)
    g_down[...] = down_sum.total()
    grad_in = dres_one[...] + sum_done(ig_slots, s_ig, r_ig)
    input_grad[...] = grad_in.astype(bf16)
    in_sum.first(1)
    up_total = up_sum.total()
    gate_total = f_gate[...]
    for j in range(cols):
        here = slice(j * rows, (j + 1) * rows)
        s_gmlp[j] = jnp.concatenate([gate_total[here], up_total[here]], axis=0).astype(bf16)
    gmlp_slots = to_lanes(lambda to: s_gmlp.at[to], r_gmlp)
    r_gmlp[blk] = s_gmlp[blk]
    in_sum.first(0)
    in_sum.second(1)
    in_sum.first(2)
    in_sum.second(0)
    for j in (1, 0, 2):
        out_sum.first(j)
    out_sum.second(1)
    out_sum.second(0)
    from_lanes(gmlp_slots, r_gmlp)
    g_mlp[...] = r_gmlp[...]
    in_total = in_sum.total()
    for j in range(cols):
        s_gin[j] = jnp.concatenate(
            [in_total[j * rows : (j + 1) * rows], jnp.zeros((8, in_total.shape[1]), f32)], axis=0
        ).astype(bf16)
    gin_slots = to_lanes(lambda to: s_gin.at[to], r_gin)
    r_gin[blk] = s_gin[blk]
    g_out[...] = out_sum.total()
    from_lanes(gin_slots, r_gin)
    g_in[...] = r_gin[...]
    wire.finish()


def unpack(
    rows,
    block,
    outputs,
    input_grad,
    g_in,
    g_mlp,
    g_out,
    g_down,
    outputs_to,
    input_grad_to,
    in_to,
    out_to,
    gate_to,
    up_to,
    down_to,
    *vectors_to,
):
    f32 = jnp.float32
    cols = g_in.shape[0]
    width = outputs.shape[1]
    outputs_to[0] = outputs[...]
    input_grad_to[0] = input_grad[...]
    down_to[...] = g_down[...]
    out_to[...] = g_out[0:rows, :]
    for number, vector_to in enumerate(vectors_to):
        vector_to[...] = g_out[rows + number, 0:rows]
    low_half = lax.broadcasted_iota(jnp.int32, (1, LANES), 1) < HALF
    joined = [g_in[j].astype(f32)[0:rows] for j in range(cols)]
    single_at = ((3, 0), (3, 1), (4, 0))

    def half(kind, number, want):
        owner, part = number // 3, number % 3
        window, at = (kind, part) if part < 2 else single_at[kind]
        value = joined[owner][:, window * LANES : (window + 1) * LANES]
        return value if at == want else pltpu.roll(value, HALF, 1)

    for kind in range(3):
        for n in range(width // LANES):
            at = kind * width + n * LANES
            in_to[:, at : at + LANES] = jnp.where(
                low_half, half(kind, 2 * n, 0), half(kind, 2 * n + 1, 1)
            )
    lanes = lax.broadcasted_iota(jnp.int32, (1, LANES), 1)
    mlp = [g_mlp[j].astype(f32) for j in range(cols)]
    for first_row, target in ((0, gate_to), (rows, up_to)):
        parts = [part[first_row : first_row + rows] for part in mlp]
        for n in range(target.shape[1] // LANES):
            first = n * LANES
            result = None
            for number in range(first // block, (first + LANES - 1) // block + 1):
                ring_at, owner = number // cols, number % cols
                piece = window_at(parts[owner], ring_at * block + first - number * block)
                begin = number * block - first
                result = piece if result is None else jnp.where(lanes < begin, result, piece)
            target[:, first : first + LANES] = result


def fast_shards(
    depth,
    inputs,
    doc_lengths,
    project_in,
    project_out,
    gate_weight,
    up_weight,
    down_weight,
    first_gain,
    first_bias,
    second_gain,
    second_bias,
    cotangent,
):
    cols = 4
    tok, width = inputs.shape[1:]
    rows = project_in.shape[0]
    ff = gate_weight.shape[1]
    ring = depth * 2
    row_len = tok * cols
    units = ff // cols
    block = units // ring
    head_width = width // cols
    in_width = 5 * LANES
    bf16, f32 = jnp.bfloat16, jnp.float32

    lane_ids = np.arange(LANES) % QUART
    freq = jnp.asarray(
        np.broadcast_to(BASE ** (-2.0 * lane_ids / HALF), (8, LANES)).astype(np.float32)
    )

    def scratch(*shape, kind=bf16):
        return pltpu.VMEM(shape, kind)

    def sums(height, across, tail=0):
        main = height - tail
        buffers = [
            scratch(2, depth, height, across),
            scratch(depth, main, across),
            scratch(depth, main, across),
            scratch(4, main, across),
        ]
        if tail:
            buffers = buffers + [
                scratch(4, 2, tail, across),
                scratch(2, 2, tail, across),
                scratch(2, tail, across),
                scratch(tail, across, kind=f32),
            ]
        return tuple(buffers)

    stacked = scratch(cols, tok, width)
    heads = 3
    buffers = [
        stacked,
        scratch(cols, 32, in_width),
        scratch(cols, 2 * rows, units),
        scratch(8, LANES, kind=f32),
        scratch(cols, 32, in_width),
        scratch(cols, 2 * rows, units),
        scratch(cols, ring, 32, width),
        scratch(ring, cols * rows, in_width),
        scratch(ring, cols * rows, units),
        scratch(ring, cols * rows, units),
        scratch(ring, block, width),
        scratch(cols, 2 * LANES, width),
        scratch(8, width, kind=f32),
        scratch(row_len, LANES, kind=f32),
        scratch(row_len, LANES, kind=f32),
        scratch(row_len, LANES, kind=jnp.int32),
        scratch(heads, row_len, LANES),
        scratch(2, row_len, LANES),
        scratch(2, row_len, LANES),
        scratch(heads, row_len, row_len),
        scratch(2, row_len, LANES, kind=f32),
        scratch(cols, tok, 2 * LANES),
        scratch(cols, tok, 2 * LANES),
        scratch(tok, width, kind=f32),
        scratch(tok, width, kind=f32),
        stacked,
        scratch(row_len, units, kind=f32),
        scratch(row_len, units, kind=f32),
        scratch(row_len, units),
        stacked,
        scratch(3, tok, width),
        scratch(tok, width),
        scratch(tok, width, kind=f32),
        stacked,
        scratch(row_len, units),
        scratch(row_len, units),
        stacked,
        scratch(3, tok, width),
        scratch(tok, width),
        scratch(tok, width, kind=f32),
        scratch(cols, tok, 2 * LANES),
        scratch(cols, tok, 2 * LANES),
        scratch(2, row_len, LANES, kind=f32),
        scratch(2, row_len, LANES, kind=f32),
        scratch(2, row_len, LANES, kind=f32),
        scratch(row_len, in_width),
        stacked,
        scratch(3, tok, width),
        scratch(tok, width),
        sums(cols * rows, in_width),
        sums(cols * rows, units),
        sums(cols * rows, units),
        sums(block, width, DT),
        scratch(cols, 2, depth, 32, width),
        scratch(3, 2, depth, 32, width),
        scratch(2, depth, 32, width),
        sums(32, width, 0),
        scratch(cols * rows, units, kind=f32),
        scratch(cols, 2 * rows, units),
        scratch(cols, 2 * rows, units),
        scratch(cols, 32, in_width),
        scratch(cols, 32, in_width),
        pltpu.SemaphoreType.DMA((240,)),
        pltpu.SemaphoreType.DMA((240,)),
    ]
    vmem = pl.BlockSpec(memory_space=pltpu.VMEM)
    tokens = row_len * width
    outputs, input_grad, g_in, g_mlp, g_out, g_down = pl.pallas_call(
        functools.partial(fused, depth),
        out_shape=(
            jax.ShapeDtypeStruct((tok, width), bf16),
            jax.ShapeDtypeStruct((tok, width), bf16),
            jax.ShapeDtypeStruct((cols, 32, in_width), bf16),
            jax.ShapeDtypeStruct((cols, 2 * rows, units), bf16),
            jax.ShapeDtypeStruct((32, width), f32),
            jax.ShapeDtypeStruct((block, width), f32),
        ),
        in_specs=[pl.BlockSpec(memory_space=pltpu.SMEM)] + [vmem] * 12,
        out_specs=(vmem,) * 6,
        scratch_shapes=buffers,
        compiler_params=pltpu.CompilerParams(
            collective_id=0, has_side_effects=True, vmem_limit_bytes=60 * 2**20
        ),
        cost_estimate=pl.CostEstimate(
            flops=6 * tokens * (3 * units + 4 * head_width),
            bytes_accessed=8 * 2**20,
            transcendentals=3 * row_len * row_len,
        ),
        name="layer",
    )(
        doc_lengths,
        freq,
        inputs[0],
        cotangent[0],
        project_in,
        gate_weight,
        up_weight,
        project_out,
        down_weight,
        first_gain[None],
        first_bias[None],
        second_gain[None],
        second_bias[None],
    )

    vector = jax.ShapeDtypeStruct((rows,), f32)
    return pl.pallas_call(
        functools.partial(unpack, rows, block),
        out_shape=(
            jax.ShapeDtypeStruct((1, tok, width), bf16),
            jax.ShapeDtypeStruct((1, tok, width), bf16),
            jax.ShapeDtypeStruct((rows, 3 * width), f32),
            jax.ShapeDtypeStruct((rows, width), f32),
            jax.ShapeDtypeStruct((rows, ff), f32),
            jax.ShapeDtypeStruct((rows, ff), f32),
            jax.ShapeDtypeStruct((block, width), f32),
            vector,
            vector,
            vector,
            vector,
        ),
        in_specs=[vmem] * 6,
        out_specs=(vmem,) * 11,
        name="unpack",
    )(outputs, input_grad, g_in, g_mlp, g_out, g_down)


def pick(sizes):
    def chosen(*args):
        tok, width = args[0].shape[1:]
        ring, cols = sizes["dp"], sizes["blk"]
        fits = (
            ring == 8
            and cols == 4
            and tok == LANES
            and HEADS == 3 * cols
            and width == HEADS * HALF
            and args[2].shape[0] == 24
            and args[4].shape[1] == 4 * width
        )
        if fits:
            return fast_shards(ring // 2, *args)
        return shards(*args)

    return chosen


def solution(mesh):
    placed = (
        P("dp", "blk", None),
        P("dp", None),
        P(("dp", "blk"), None),
        P(("dp", "blk"), None),
        P(("dp", "blk"), None),
        P(("dp", "blk"), None),
        P(("dp", "blk"), None),
        P(("dp", "blk")),
        P(("dp", "blk")),
        P(("dp", "blk")),
        P(("dp", "blk")),
        P("dp", "blk", None),
    )
    return jax.shard_map(
        pick(dict(mesh.shape)),
        mesh=mesh,
        in_specs=placed,
        out_specs=(
            P("dp", "blk", None),
            P("dp", "blk", None),
            P(("dp", "blk"), None),
            P(("dp", "blk"), None),
            P(("dp", "blk"), None),
            P(("dp", "blk"), None),
            P(("dp", "blk"), None),
            P(("dp", "blk")),
            P(("dp", "blk")),
            P(("dp", "blk")),
            P(("dp", "blk")),
        ),
        check_vma=False,
    )
```

```python
import functools

import jax
import jax.numpy as jnp
import numpy as np
from jax import lax
from jax.experimental import pallas as pl
from jax.experimental.pallas import tpu as pltpu
from jax.sharding import PartitionSpec as P

HEADS = 12


NEG = -1e30
EPS = 1e-05
BASE = 1000.0


def doc_layout(lengths_row, positions):
    bounds = jnp.cumsum(lengths_row)
    passed = positions[:, None] >= bounds[None, :]
    segment = jnp.sum(passed.astype(jnp.int32), axis=1)
    begins = jnp.sum(jnp.where(passed, lengths_row[None, :], 0), axis=1)
    return (segment, positions - begins)


def rotary(vectors, offsets):
    half_size = vectors.shape[-1] // 2
    frequency = BASE ** (-2.0 * jnp.arange(half_size, dtype=jnp.float32) / vectors.shape[-1])
    angles = offsets.astype(jnp.float32)[:, None] * frequency[None, :]
    cosine = jnp.concatenate([jnp.cos(angles), jnp.cos(angles)], axis=1)[:, None, :]
    sine_rows = jnp.concatenate([jnp.sin(angles), jnp.sin(angles)], axis=1)[:, None, :]
    first_half = vectors[..., :half_size]
    second_half = vectors[..., half_size:]
    turned = jnp.concatenate([-second_half, first_half], axis=-1)
    return vectors * cosine + turned * sine_rows


def layer_norm(residual, gain_row, bias_row):
    row_mean = jnp.mean(residual, axis=-1, keepdims=True)
    centered = residual - row_mean
    variance = jnp.mean(centered * centered, axis=-1, keepdims=True)
    return centered * lax.rsqrt(variance + EPS) * gain_row + bias_row


def contract_rows(left, right):
    return lax.dot_general(
        left, right, (((0,), (0,)), ((), ())), preferred_element_type=jnp.float32
    )


def contract_cols(left, right):
    return lax.dot_general(
        left, right, (((1,), (1,)), ((), ())), preferred_element_type=jnp.float32
    )


def tile_scores(query_tile, key_tile, seg_query, seg_key, score_scale):
    scores = (
        jnp.einsum("qhd,khd->hqk", query_tile, key_tile, preferred_element_type=jnp.float32)
        * score_scale
    )
    allowed = (seg_query[:, None] == seg_key[None, :])[None, :, :]
    return (jnp.where(allowed, scores, NEG), allowed)


def run_groups(pieces, group, lengths_row, seg_query, carried, tile_fn, extra_shape):
    group_count = pieces[0].shape[0] // group

    def group_step(carried_in, number):
        offset = number * group
        tile_set = tuple(
            (lax.dynamic_slice_in_dim(piece_rows, offset, group, 0) for piece_rows in pieces)
        )
        positions = offset + jnp.arange(group, dtype=jnp.int32)
        seg_key, unused_offsets = doc_layout(lengths_row, positions)
        touches = (seg_key[0] <= seg_query[-1]) & (seg_query[0] <= seg_key[-1])

        def active(state_in):
            return tile_fn(state_in, tile_set, seg_key)

        def skipped(state_in):
            return (state_in, jnp.zeros(extra_shape, jnp.float32))

        return lax.cond(touches, active, skipped, carried_in)

    return lax.scan(group_step, carried, jnp.arange(group_count, dtype=jnp.int32))


def shards(
    inputs,
    doc_lengths,
    project_in,
    project_out,
    gate_weight,
    up_weight,
    down_weight,
    first_gain,
    first_bias,
    second_gain,
    second_bias,
    cotangent,
):
    group = inputs.shape[1]
    width = inputs.shape[2]
    head_count = HEADS
    head_size = width // head_count
    score_scale = head_size ** (-0.5)
    cycle_rank = lax.axis_index("blk")
    positions = cycle_rank * group + jnp.arange(group, dtype=jnp.int32)
    lengths_row = doc_lengths[0]
    seg_query, offsets = doc_layout(lengths_row, positions)
    keep_mask = seg_query < lengths_row.shape[0] - 1
    keep_float = keep_mask.astype(jnp.float32)
    fetched = (
        lax.all_gather(project_in, ("dp", "blk"), axis=0, tiled=True),
        lax.all_gather(project_out, ("dp", "blk"), axis=0, tiled=True),
        lax.all_gather(gate_weight, ("dp", "blk"), axis=0, tiled=True),
        lax.all_gather(up_weight, ("dp", "blk"), axis=0, tiled=True),
        lax.all_gather(down_weight, ("dp", "blk"), axis=0, tiled=True),
        lax.all_gather(first_gain, ("dp", "blk"), axis=0, tiled=True),
        lax.all_gather(first_bias, ("dp", "blk"), axis=0, tiled=True),
        lax.all_gather(second_gain, ("dp", "blk"), axis=0, tiled=True),
        lax.all_gather(second_bias, ("dp", "blk"), axis=0, tiled=True),
    )
    full_in, full_out, full_gate, full_up, full_down = (
        fetched[0],
        fetched[1],
        fetched[2],
        fetched[3],
        fetched[4],
    )
    gain_one = fetched[5].astype(jnp.float32)
    bias_one = fetched[6].astype(jnp.float32)
    gain_two = fetched[7].astype(jnp.float32)
    bias_two = fetched[8].astype(jnp.float32)
    tokens_low = inputs[0]
    tokens_f = tokens_low.astype(jnp.float32)
    joined = jnp.dot(tokens_low, full_in, preferred_element_type=jnp.float32)
    query_raw = joined[:, :width].reshape(group, head_count, head_size)
    key_raw = joined[:, width : 2 * width].reshape(group, head_count, head_size)
    value_low = joined[:, 2 * width :].astype(jnp.bfloat16)
    query_rot, query_pull = jax.vjp(lambda vectors: rotary(vectors, offsets), query_raw)
    key_rot, key_pull = jax.vjp(lambda vectors: rotary(vectors, offsets), key_raw)
    query_low = query_rot.astype(jnp.bfloat16)
    key_low = key_rot.reshape(group, width).astype(jnp.bfloat16)

    def stats_tile(carried, tile_set, seg_key):
        row_top, row_total = carried
        key_tile = tile_set[0].reshape(group, head_count, head_size)
        scores, allowed = tile_scores(query_low, key_tile, seg_query, seg_key, score_scale)
        new_top = jnp.maximum(row_top, jnp.max(scores, axis=2))
        shrink = jnp.exp(row_top - new_top)
        added = jnp.sum(jnp.where(allowed, jnp.exp(scores - new_top[:, :, None]), 0.0), axis=2)
        return ((new_top, row_total * shrink + added), jnp.zeros((1,), jnp.float32))

    init_stats = (
        jnp.full((head_count, group), NEG, jnp.float32),
        jnp.zeros((head_count, group), jnp.float32),
    )
    carried = init_stats
    carried, unused = run_groups(
        (lax.all_gather(key_low, "blk", axis=0, tiled=True),),
        group,
        lengths_row,
        seg_query,
        carried,
        stats_tile,
        (1,),
    )
    row_top, row_total = carried
    log_total = row_top + jnp.log(row_total)

    def output_tile(accum, tile_set, seg_key):
        key_tile = tile_set[0].reshape(group, head_count, head_size)
        value_tile = tile_set[1].reshape(group, head_count, head_size)
        scores, allowed = tile_scores(query_low, key_tile, seg_query, seg_key, score_scale)
        prob_low = jnp.where(allowed, jnp.exp(scores - log_total[:, :, None]), 0.0).astype(
            jnp.bfloat16
        )
        accum = accum + jnp.einsum(
            "hqk,khd->qhd", prob_low, value_tile, preferred_element_type=jnp.float32
        )
        return (accum, jnp.zeros((1,), jnp.float32))

    zero_accum = jnp.zeros((group, head_count, head_size), jnp.float32)
    accum = zero_accum
    accum, unused = run_groups(
        (
            lax.all_gather(key_low, "blk", axis=0, tiled=True),
            lax.all_gather(value_low, "blk", axis=0, tiled=True),
        ),
        group,
        lengths_row,
        seg_query,
        accum,
        output_tile,
        (1,),
    )
    attend_low = (accum * keep_float[:, None, None]).reshape(group, width).astype(jnp.bfloat16)
    branch = jnp.dot(attend_low, full_out, preferred_element_type=jnp.float32)
    residual_one = tokens_f + branch
    hidden, norm_one_pull = jax.vjp(layer_norm, residual_one, gain_one, bias_one)
    hidden_low = hidden.astype(jnp.bfloat16)
    gate_pre = jnp.dot(hidden_low, full_gate, preferred_element_type=jnp.float32)
    up_pre = jnp.dot(hidden_low, full_up, preferred_element_type=jnp.float32)
    activated, swiglu_pull = jax.vjp(
        lambda gate_in, up_in: jax.nn.silu(gate_in) * up_in, gate_pre, up_pre
    )
    active_low = activated.astype(jnp.bfloat16)
    mlp_out = jnp.dot(active_low, full_down, preferred_element_type=jnp.float32)
    outputs_f, norm_two_pull = jax.vjp(layer_norm, hidden + mlp_out, gain_two, bias_two)
    refetched = (
        lax.all_gather(project_in, ("dp", "blk"), axis=0, tiled=True),
        lax.all_gather(project_out, ("dp", "blk"), axis=0, tiled=True),
        lax.all_gather(gate_weight, ("dp", "blk"), axis=0, tiled=True),
        lax.all_gather(up_weight, ("dp", "blk"), axis=0, tiled=True),
        lax.all_gather(down_weight, ("dp", "blk"), axis=0, tiled=True),
    )
    full_in, full_out, full_gate, full_up, full_down = (
        refetched[0],
        refetched[1],
        refetched[2],
        refetched[3],
        refetched[4],
    )
    d_res_two, second_gain_part, second_bias_part = norm_two_pull(cotangent[0].astype(jnp.float32))
    d_mlp_low = d_res_two.astype(jnp.bfloat16)
    down_part = contract_rows(active_low, d_mlp_low)
    d_active = contract_cols(d_mlp_low, full_down)
    d_gate, d_up = swiglu_pull(d_active)
    d_gate_low = d_gate.astype(jnp.bfloat16)
    d_up_low = d_up.astype(jnp.bfloat16)
    gate_part = contract_rows(hidden_low, d_gate_low)
    up_part = contract_rows(hidden_low, d_up_low)
    d_hidden = d_res_two + contract_cols(d_gate_low, full_gate) + contract_cols(d_up_low, full_up)
    d_res_one, first_gain_part, first_bias_part = norm_one_pull(d_hidden)
    d_branch_low = d_res_one.astype(jnp.bfloat16)
    out_part = contract_rows(attend_low, d_branch_low)
    d_attend = contract_cols(d_branch_low, full_out).astype(jnp.bfloat16)
    d_attend_low = (d_attend * keep_mask[:, None].astype(jnp.bfloat16)).reshape(
        group, head_count, head_size
    )
    delta = jnp.einsum("qhd,qhd->hq", d_attend_low.astype(jnp.float32), accum)

    def back_tile(grad_query, tile_set, seg_key):
        key_tile = tile_set[0].reshape(group, head_count, head_size)
        value_tile = tile_set[1].reshape(group, head_count, head_size)
        scores, allowed = tile_scores(query_low, key_tile, seg_query, seg_key, score_scale)
        prob_rows = jnp.where(allowed, jnp.exp(scores - log_total[:, :, None]), 0.0)
        d_probs = jnp.einsum(
            "qhd,khd->hqk", d_attend_low, value_tile, preferred_element_type=jnp.float32
        )
        d_score_low = (prob_rows * (d_probs - delta[:, :, None])).astype(jnp.bfloat16)
        grad_query = (
            grad_query
            + jnp.einsum("hqk,khd->qhd", d_score_low, key_tile, preferred_element_type=jnp.float32)
            * score_scale
        )
        grad_key = (
            jnp.einsum("hqk,qhd->khd", d_score_low, query_low, preferred_element_type=jnp.float32)
            * score_scale
        )
        grad_value = jnp.einsum(
            "hqk,qhd->khd",
            prob_rows.astype(jnp.bfloat16),
            d_attend_low,
            preferred_element_type=jnp.float32,
        )
        return (
            grad_query,
            jnp.concatenate(
                [grad_key.reshape(group, width), grad_value.reshape(group, width)], axis=1
            ),
        )

    grad_query = zero_accum
    grad_query, blocks = run_groups(
        (
            lax.all_gather(key_low, "blk", axis=0, tiled=True),
            lax.all_gather(value_low, "blk", axis=0, tiled=True),
        ),
        group,
        lengths_row,
        seg_query,
        grad_query,
        back_tile,
        (group, 2 * width),
    )
    blocks = blocks.reshape(-1, 2 * width)
    back_result = (grad_query, blocks)
    grad_query = back_result[0]
    owned_pairs = lax.psum_scatter(
        back_result[1].astype(jnp.bfloat16), "blk", scatter_dimension=0, tiled=True
    ).astype(jnp.float32)
    key_sum = owned_pairs[:, :width]
    value_sum = owned_pairs[:, width:]
    d_query_pre = query_pull(grad_query.astype(jnp.bfloat16).astype(jnp.float32))[0]
    d_key_low = key_sum.astype(jnp.bfloat16).astype(jnp.float32)
    d_key_pre = key_pull(d_key_low.reshape(group, head_count, head_size))[0]
    d_value_low = value_sum.astype(jnp.bfloat16).astype(jnp.float32)
    d_joined_low = jnp.concatenate(
        [d_query_pre.reshape(group, width), d_key_pre.reshape(group, width), d_value_low], axis=1
    ).astype(jnp.bfloat16)
    in_part = contract_rows(tokens_low, d_joined_low)
    input_grad = (d_res_one + contract_cols(d_joined_low, full_in)).astype(jnp.bfloat16)
    by_rows = (
        lax.psum_scatter(
            in_part.astype(jnp.bfloat16), "dp", scatter_dimension=0, tiled=True
        ).astype(jnp.float32),
        lax.psum_scatter(
            out_part.astype(jnp.bfloat16), "dp", scatter_dimension=0, tiled=True
        ).astype(jnp.float32),
        lax.psum_scatter(
            gate_part.astype(jnp.bfloat16), "dp", scatter_dimension=0, tiled=True
        ).astype(jnp.float32),
        lax.psum_scatter(
            up_part.astype(jnp.bfloat16), "dp", scatter_dimension=0, tiled=True
        ).astype(jnp.float32),
        lax.psum_scatter(
            down_part.astype(jnp.bfloat16), "dp", scatter_dimension=0, tiled=True
        ).astype(jnp.float32),
        lax.psum_scatter(
            first_gain_part.astype(jnp.bfloat16), "dp", scatter_dimension=0, tiled=True
        ).astype(jnp.float32),
        lax.psum_scatter(
            first_bias_part.astype(jnp.bfloat16), "dp", scatter_dimension=0, tiled=True
        ).astype(jnp.float32),
        lax.psum_scatter(
            second_gain_part.astype(jnp.bfloat16), "dp", scatter_dimension=0, tiled=True
        ).astype(jnp.float32),
        lax.psum_scatter(
            second_bias_part.astype(jnp.bfloat16), "dp", scatter_dimension=0, tiled=True
        ).astype(jnp.float32),
    )
    summed = (
        lax.psum_scatter(
            by_rows[0].astype(jnp.bfloat16), "blk", scatter_dimension=0, tiled=True
        ).astype(jnp.float32),
        lax.psum_scatter(
            by_rows[1].astype(jnp.bfloat16), "blk", scatter_dimension=0, tiled=True
        ).astype(jnp.float32),
        lax.psum_scatter(
            by_rows[2].astype(jnp.bfloat16), "blk", scatter_dimension=0, tiled=True
        ).astype(jnp.float32),
        lax.psum_scatter(
            by_rows[3].astype(jnp.bfloat16), "blk", scatter_dimension=0, tiled=True
        ).astype(jnp.float32),
        lax.psum_scatter(
            by_rows[4].astype(jnp.bfloat16), "blk", scatter_dimension=0, tiled=True
        ).astype(jnp.float32),
        lax.psum_scatter(
            by_rows[5].astype(jnp.bfloat16), "blk", scatter_dimension=0, tiled=True
        ).astype(jnp.float32),
        lax.psum_scatter(
            by_rows[6].astype(jnp.bfloat16), "blk", scatter_dimension=0, tiled=True
        ).astype(jnp.float32),
        lax.psum_scatter(
            by_rows[7].astype(jnp.bfloat16), "blk", scatter_dimension=0, tiled=True
        ).astype(jnp.float32),
        lax.psum_scatter(
            by_rows[8].astype(jnp.bfloat16), "blk", scatter_dimension=0, tiled=True
        ).astype(jnp.float32),
    )
    return (
        outputs_f.astype(jnp.bfloat16)[None],
        input_grad[None],
        summed[0],
        summed[1],
        summed[2],
        summed[3],
        summed[4],
        summed[5],
        summed[6],
        summed[7],
        summed[8],
    )


MESH_IDS = pl.DeviceIdType.MESH
LANES = 128
HALF = 64
QUART = 32
DTF = 48
DTB = 64


def mm(left, right):
    return lax.dot_general(
        left, right, (((1,), (0,)), ((), ())), preferred_element_type=jnp.float32
    )


def mt(left, right):
    return lax.dot_general(
        left, right, (((1,), (1,)), ((), ())), preferred_element_type=jnp.float32
    )


def tm(left, right):
    return lax.dot_general(
        left, right, (((0,), (0,)), ((), ())), preferred_element_type=jnp.float32
    )


def window_at(value, start):
    aligned = min(max(start // LANES * LANES, 0), value.shape[1] - LANES)
    if aligned == start:
        return value[:, aligned : aligned + LANES]
    aligned = min(aligned, value.shape[1] - 2 * LANES)
    two = value[:, aligned : aligned + 2 * LANES]
    return pltpu.roll(two, (aligned - start) % (2 * LANES), 1)[:, :LANES]


def gather_lanes(value, block, first, source):
    lanes = lax.broadcasted_iota(jnp.int32, (1, LANES), 1)
    result = None
    for number in range(first // block, (first + LANES - 1) // block + 1):
        piece = window_at(value, source(number, first))
        begin = number * block - first
        result = piece if result is None else jnp.where(lanes < begin, result, piece)
    return result


class Wire:
    def __init__(self, send_sem, recv_sem, is_inner):
        self.send_sem, self.recv_sem, self.is_inner = send_sem, recv_sem, is_inner
        self.sends, self.slots = 0, 0
        self.sent = {None: [], True: [], False: []}

    def slot(self):
        self.slots += 1
        return self.slots - 1

    def copy(self, src, dst, peer, slot):
        self.sends += 1
        return pltpu.make_async_remote_copy(
            src_ref=src,
            dst_ref=dst,
            send_sem=self.send_sem.at[self.sends - 1],
            recv_sem=self.recv_sem.at[slot],
            device_id=peer,
            device_id_type=MESH_IDS,
        )

    def push(self, src, dst, peer, slot=None, inner=None):
        slot = self.slot() if slot is None else slot
        copy = self.copy(src, dst, peer, slot)
        self.sent[inner].append(copy)
        if inner is None:
            copy.start()
        else:
            pl.when(self.is_inner == inner)(copy.start)
        return slot

    def arrive(self, slot, dst, peer):
        pltpu.make_async_remote_copy(
            src_ref=dst,
            dst_ref=dst,
            send_sem=self.send_sem.at[0],
            recv_sem=self.recv_sem.at[slot],
            device_id=peer,
            device_id_type=MESH_IDS,
        ).wait_recv()

    def finish(self):
        for inner, copies in self.sent.items():

            def drain(copies=copies):
                for copy in copies:
                    copy.wait_send()

            if inner is None:
                drain()
            else:
                pl.when(self.is_inner == inner)(drain)


class Plane:
    def __init__(self, planes):
        dp, self.blk = lax.axis_index("dp"), lax.axis_index("blk")
        self.z, self.x = dp // 2, dp % 2
        self.dp = dp
        self.partner = self.z + 1 - 2 * (self.z % 2)
        self.other = planes // 2 - self.z // (planes // 2)
        self.outer = (planes - 1) * (self.other - 1)
        self.inner = ((self.z + 1) // 2) % 2
        self.order = (self.other, self.outer, self.partner, self.z)
        self.side = (self.z * 2 + (1 - self.x), self.blk)

    def at(self, plane):
        return (plane * 2 + self.x, self.blk)


class Spread:
    def __init__(self, wire, place, target, tail):
        self.wire, self.place, self.target = wire, place, target
        self.height, self.main = target.shape[1], target.shape[1] - tail

    def block(self, plane, column):
        return self.target.at[plane * 2 + column, 0 : self.main]

    def pair(self, plane):
        return self.target.at[pl.ds(plane * 2, 2), self.main : self.height]

    def along(self, own, slots):
        p = self.place
        self.wire.push(own, own, p.at(p.partner), slots[2], inner=False)
        self.wire.push(own, own, p.at(p.other), slots[0] + (1 - p.inner))

    def outward(self, own, slots):
        p = self.place
        self.wire.push(own, own, p.at(p.partner), slots[2], inner=True)

    def start(self):
        p, wire = self.place, self.wire
        self.z_slots = [wire.slot() for _ in range(3)]
        self.along(self.block(p.z, p.x), self.z_slots)

    def start_out(self):
        p = self.place
        self.outward(self.block(p.z, p.x), self.z_slots)

    def start_side(self):
        p, wire = self.place, self.wire
        self.x_slots = [wire.slot() for _ in range(4)]
        own = self.block(p.z, p.x)
        wire.push(own, own, p.side, self.x_slots[3])
        if self.main < self.height:
            rest = self.target.at[p.dp, self.main : self.height]
            self.rest_slot = wire.push(rest, rest, p.side)

    def tail(self):
        p, wire = self.place, self.wire
        rest = self.target.at[p.z * 2 + (1 - p.x), self.main : self.height]
        wire.arrive(self.rest_slot, rest, p.side)
        self.t_slots = [wire.slot() for _ in range(3)]
        self.along(self.pair(p.z), self.t_slots)

    def tail_out(self):
        self.outward(self.pair(self.place.z), self.t_slots)

    def relay(self, j, inner=None):
        p, wire = self.place, self.wire
        block = self.block(p.order[j], p.x)
        onward = wire.copy(block, block, p.side, self.x_slots[j])
        wire.sent[inner].append(onward)
        outward = None
        if j < 2 and inner is not False:
            outward = wire.copy(block, block, p.at(p.partner), self.z_slots[j])
            wire.sent[True].append(outward)

        def run():
            wire.arrive(self.z_slots[j], block, p.side)
            if outward is not None:
                if inner:
                    outward.start()
                else:
                    pl.when(wire.is_inner)(outward.start)
            onward.start()

        if inner is None:
            run()
        else:
            pl.when(wire.is_inner == inner)(run)

    def pass_tail(self, j):
        p, wire = self.place, self.wire
        pair = self.pair(p.order[j])
        copy = wire.copy(pair, pair, p.at(p.partner), self.t_slots[j])
        wire.sent[True].append(copy)

        @pl.when(wire.is_inner)
        def _():
            wire.arrive(self.t_slots[j], pair, p.side)
            copy.start()

    def settle_tail(self):
        p, wire = self.place, self.wire
        wire.arrive(self.t_slots[2], self.pair(p.order[2]), p.side)

        @pl.when(jnp.logical_not(wire.is_inner))
        def _():
            for j in range(2):
                wire.arrive(self.t_slots[j], self.pair(p.order[j]), p.side)

    def settle(self):
        p = self.place
        for j in range(4):
            self.wire.arrive(self.x_slots[j], self.block(p.order[j], 1 - p.x), p.side)


class Collect:
    def __init__(self, wire, place, buffers):
        self.wire, self.place = wire, place
        self.part, self.inbox, self.staged, self.landing = buffers[:4]
        self.height, self.main = self.part.shape[2], self.inbox.shape[1]
        self.split = self.main < self.height
        if self.split:
            self.t_landing, self.t_staged, self.t_cross, self.t_kept = buffers[4:]

    def pair(self, plane):
        return self.part.at[:, plane, self.main : self.height]

    def send_side(self, j):
        p = self.place
        plane = p.order[j]
        self.wire.push(
            self.part.at[1 - p.x, plane, 0 : self.main],
            self.inbox.at[plane],
            p.side,
            self.x_slots[j],
        )

    def send(self, order=(1, 0, 2, 3)):
        p, wire = self.place, self.wire
        self.x_slots = [wire.slot() for _ in range(4)]
        for j in order:
            self.send_side(j)
        self.z_slots = [wire.slot() for _ in range(4)]
        if self.split:
            self.t_slots = [wire.slot() for _ in range(4)]
            for j in (1, 0, 2):
                wire.push(
                    self.pair(p.order[j]),
                    self.t_landing.at[j],
                    p.at(p.partner),
                    self.t_slots[j],
                    inner=None if j == 2 else False,
                )

    def first(self, j):
        p, wire = self.place, self.wire
        plane = p.order[j]
        wire.arrive(self.x_slots[j], self.inbox.at[plane], p.side)
        both = self.part[p.x, plane, 0 : self.main].astype(jnp.float32)
        both = both + self.inbox[plane].astype(jnp.float32)
        self.staged[plane] = both.astype(jnp.bfloat16)
        wire.push(
            self.staged.at[plane],
            self.landing.at[j],
            p.at(p.partner),
            self.z_slots[j],
            inner=None if j == 2 else False,
        )

    def second(self, j):
        p, wire = self.place, self.wire
        plane = p.order[j]
        copy = wire.copy(self.staged.at[plane], self.landing.at[3], p.at(plane), self.z_slots[3])
        wire.sent[True].append(copy)

        @pl.when(wire.is_inner)
        def _():
            wire.arrive(self.z_slots[j], self.landing.at[j], p.side)
            both = self.staged[plane].astype(jnp.float32) + self.landing[j].astype(jnp.float32)
            self.staged[plane] = both.astype(jnp.bfloat16)
            copy.start()

    def second_tail(self, j):
        p, wire = self.place, self.wire
        plane = p.order[j]
        copy = wire.copy(self.t_staged.at[j], self.t_landing.at[3], p.at(plane), self.t_slots[3])
        wire.sent[True].append(copy)

        @pl.when(wire.is_inner)
        def _():
            wire.arrive(self.t_slots[j], self.t_landing.at[j], p.side)
            rest = self.part[:, plane, self.main : self.height].astype(jnp.float32)
            rest = rest + self.t_landing[j].astype(jnp.float32)
            self.t_staged[j] = rest.astype(jnp.bfloat16)
            copy.start()

    def tail(self):
        p, wire = self.place, self.wire
        for j in (2, 3):
            wire.arrive(self.t_slots[j], self.t_landing.at[j], p.side)

        def rest_of(column):
            rest = self.part[column, p.z, self.main : self.height].astype(jnp.float32)
            for j in (2, 3):
                rest = rest + self.t_landing[j, column].astype(jnp.float32)
            return rest

        self.t_kept[...] = rest_of(p.x)
        self.t_cross[0] = rest_of(1 - p.x).astype(jnp.bfloat16)
        self.cross_slot = wire.push(self.t_cross.at[0], self.t_cross.at[1], p.side)

    def total(self):
        p, wire = self.place, self.wire
        wire.arrive(self.x_slots[3], self.inbox.at[p.z], p.side)
        total = self.part[p.x, p.z, 0 : self.main].astype(jnp.float32)
        total = total + self.inbox[p.z].astype(jnp.float32)
        for j in (2, 3):
            wire.arrive(self.z_slots[j], self.landing.at[j], p.side)
            total = total + self.landing[j].astype(jnp.float32)
        if not self.split:
            return total
        wire.arrive(self.cross_slot, self.t_cross.at[1], p.side)
        rest = self.t_kept[...] + self.t_cross[1].astype(jnp.float32)
        return jnp.concatenate([total, rest], axis=0)


def fused(
    depth,
    lens,
    freq,
    xin,
    cot,
    in_rows,
    gate_rows,
    up_rows,
    out_rows,
    p_down,
    gain_a,
    bias_a,
    gain_b,
    bias_b,
    outputs,
    input_grad,
    g_in,
    g_mlp,
    g_out,
    g_down,
    xs,
    p_in,
    p_mlp,
    vectors_tab,
    r_in,
    r_mlp,
    s_out,
    w_in,
    w_gate,
    w_up,
    w_down,
    w_out,
    params,
    cos_tab,
    sin_tab,
    seg_tab,
    qm,
    kw,
    vw,
    prob,
    att,
    s_att,
    r_att,
    norm_one,
    hid,
    hs,
    gate_pre,
    up_pre,
    act,
    s_mix,
    r_mix,
    t_mix,
    dres_two,
    dms,
    dgate,
    dup,
    s_dh,
    r_dh,
    t_dh,
    dres_one,
    s_da,
    r_da,
    acc_q,
    acc_k,
    acc_v,
    dj,
    s_ig,
    r_ig,
    t_ig,
    sum_in,
    sum_gate,
    sum_up,
    sum_down,
    b_out,
    rb_out,
    tb_out,
    sum_out,
    f_gate,
    s_gmlp,
    r_gmlp,
    s_gin,
    r_gin,
    send_sem,
    recv_sem,
):
    planes, cols = depth, 4
    tok = xin.shape[0]
    row_len = tok * cols
    place = Plane(planes)
    dp, blk = place.dp, place.blk
    bf16, f32 = jnp.bfloat16, jnp.float32

    row_of, core_of = blk // 2, blk % 2
    near_at = row_of * 2 + (1 - core_of)
    across_at = (1 - row_of) * 2 + core_of
    corner_at = (1 - row_of) * 2 + (1 - core_of)
    near, across = (dp, near_at), (dp, across_at)

    def lane(k):
        return (dp, (blk + k) % cols)

    def lane_from(k):
        return (blk + cols - k) % cols

    lanes = range(1, cols)
    wire = Wire(send_sem, recv_sem, place.inner == 1)
    barrier = pltpu.get_barrier_semaphore()
    peers = [place.side] + [place.at(plane) for plane in place.order[:3]]
    peers = peers + [lane(k) for k in lanes]
    for peer in peers:
        pl.semaphore_signal(barrier, inc=1, device_id=peer, device_id_type=MESH_IDS)

    rows = 24
    width = xin.shape[1]
    lane_ids = lax.broadcasted_iota(jnp.int32, (1, LANES), 1)
    low_half = lane_ids < HALF
    head_width = width // cols
    joined_rows = in_rows[...].astype(f32)
    for j in range(cols):
        starts = [kind * width + j * head_width for kind in range(3)]
        windows = [window_at(joined_rows, start) for start in starts]
        windows.append(
            jnp.where(
                low_half,
                window_at(joined_rows, starts[0] + LANES),
                window_at(joined_rows, starts[1] + LANES - HALF),
            )
        )
        windows.append(jnp.where(low_half, window_at(joined_rows, starts[2] + LANES), 0.0))
        packed = jnp.concatenate(windows, axis=1)
        p_in[j] = jnp.concatenate(
            [packed, jnp.zeros((8, packed.shape[1]), f32)], axis=0
        ).astype(bf16)
    vectors_tab[...] = jnp.zeros_like(vectors_tab)
    for number, vector in enumerate((gain_a, bias_a, gain_b, bias_b)):
        vectors_tab[number : number + 1, 0:rows] = vector[...].astype(f32)
    lower = jnp.concatenate([vectors_tab[...], jnp.zeros((8, width - LANES), f32)], axis=1)
    s_out[blk, dp] = jnp.concatenate([out_rows[...].astype(f32), lower], axis=0).astype(bf16)
    pl.semaphore_wait(barrier, len(peers))

    def to_lanes(source_of, target):
        return [wire.push(source_of((blk + k) % cols), target.at[blk], lane(k)) for k in lanes]

    def from_lanes(slots, target):
        for k, slot in zip(lanes, slots):
            wire.arrive(slot, target.at[lane_from(k)], lane(k))

    every = pl.ds(0, tok)

    def gather_start(own, target, cut=every):
        return [
            wire.push(own.at[cut], target.at[blk, cut], across),
            wire.push(own.at[cut], target.at[blk, cut], near),
        ]

    def gather_relay(slots, target, cut=every):
        came = target.at[across_at, cut]
        wire.arrive(slots[0], came, across)
        slots.append(wire.push(came, came, near))

    def gather_done(slots, target, cut=every):
        wire.arrive(slots[1], target.at[near_at, cut], near)
        wire.arrive(slots[2], target.at[corner_at, cut], near)

    def sum_start(part, inbox, cut=every):
        return [
            wire.push(part.at[corner_at, cut], inbox.at[0, cut], near),
            wire.push(part.at[near_at, cut], inbox.at[1, cut], near),
        ]

    def sum_relay(slots, part, inbox, staged, cut=every):
        wire.arrive(slots[0], inbox.at[0, cut], near)
        both = part[across_at, cut].astype(f32) + inbox[0, cut].astype(f32)
        staged[cut] = both.astype(bf16)
        slots.append(wire.push(staged.at[cut], inbox.at[2, cut], across))

    def sum_done(slots, part, inbox, cut=every):
        wire.arrive(slots[1], inbox.at[1, cut], near)
        total = part[blk, cut].astype(f32) + inbox[1, cut].astype(f32)
        wire.arrive(slots[2], inbox.at[2, cut], across)
        return total + inbox[2, cut].astype(f32)

    in_slots = to_lanes(lambda to: p_in.at[to], r_in)
    w_down[dp] = p_down[...]
    tail = 0
    out_spread = Spread(wire, place, s_out.at[blk], 0)
    out_spread.start()
    out_spread.start_out()
    out_spread.start_side()
    down_spread = Spread(wire, place, w_down, DTF)
    down_spread.start()
    down_spread.start_out()
    down_spread.start_side()
    units = gate_rows.shape[1] // cols
    unit_block = units // (planes * 2)
    for at, weight in ((0, gate_rows), (rows, up_rows)):
        whole = weight[...].astype(f32)
        for j in range(cols):
            packed = jnp.concatenate(
                [
                    gather_lanes(
                        whole,
                        unit_block,
                        n * LANES,
                        lambda ring_at, lane: lane + (cols - 1) * unit_block * ring_at + unit_block * j,
                    )
                    for n in range(units // LANES)
                ],
                axis=1,
            )
            p_mlp[j, at : at + rows] = packed.astype(bf16)
    mlp_slots = to_lanes(lambda to: p_mlp.at[to], r_mlp)
    xs[blk] = xin[...]
    x_slots = gather_start(xin, xs)
    r_in[blk] = p_in[blk]
    r_mlp[blk] = p_mlp[blk]

    lengths = [lens[0, j] for j in range(lens.shape[1])]

    def layout(positions):
        segment = jnp.zeros_like(positions)
        begins = jnp.zeros_like(positions)
        bound = jnp.int32(0)
        for length in lengths:
            bound = bound + length
            passed = positions >= bound
            segment = segment + jnp.where(passed, 1, 0)
            begins = begins + jnp.where(passed, length, 0)
        return segment, positions - begins

    seg_rows, offsets = layout(lax.broadcasted_iota(jnp.int32, (row_len, LANES), 0))
    seg_tab[...] = seg_rows
    seg_key = layout(lax.broadcasted_iota(jnp.int32, (8, row_len), 1))[0][0:1]
    front = lane_ids % HALF < QUART
    angles = offsets.astype(f32) * freq[0:1]
    cos_tab[...] = jnp.cos(angles)
    sin_tab[...] = jnp.where(front, -1.0, 1.0) * jnp.sin(angles)

    def turn(window):
        return jnp.where(
            front, pltpu.roll(window, LANES - QUART, 1), pltpu.roll(window, QUART, 1)
        )

    from_lanes(in_slots, r_in)
    w_in[dp] = jnp.concatenate(
        [r_in[j, 0:rows, :].astype(f32) for j in range(cols)], axis=0
    ).astype(bf16)
    in_spread = Spread(wire, place, w_in, tail)
    in_spread.start()
    in_spread.start_out()
    in_spread.start_side()
    from_lanes(mlp_slots, r_mlp)
    mlp_own = [r_mlp[j].astype(f32) for j in range(cols)]
    w_gate[dp] = jnp.concatenate([part[0:rows] for part in mlp_own], axis=0).astype(bf16)
    w_up[dp] = jnp.concatenate([part[rows:] for part in mlp_own], axis=0).astype(bf16)
    gate_spread = Spread(wire, place, w_gate, tail)
    up_spread = Spread(wire, place, w_up, tail)
    gate_spread.start()
    gate_spread.start_side()
    up_spread.start()
    for j in (2, 0, 1):
        out_spread.relay(j)
    in_spread.relay(2)
    in_spread.relay(0)
    down_spread.relay(2)
    in_spread.relay(1)
    up_spread.start_side()
    gate_spread.start_out()
    up_spread.start_out()
    down_spread.tail()
    gate_spread.relay(0, inner=True)
    gate_spread.relay(1, inner=True)
    gather_relay(x_slots, xs)
    out_spread.settle()
    shards_here = pl.ds(0, planes * 2)
    out_lanes = gather_start(s_out.at[blk], s_out, shards_here)
    gate_spread.relay(2)
    gather_done(x_slots, xs)
    in_spread.settle()

    group = 2
    chunk = group * tok

    def project(step, carry):
        start = pl.multiple_of(step * chunk, chunk)
        here = pl.ds(start, chunk)
        tokens = xs[pl.ds(step * group, group)].reshape(chunk, width)
        joined = mm(tokens, w_in[...].reshape(width, w_in.shape[2]))
        cosine, sine = cos_tab[here, :], sin_tab[here, :]

        def rotate(number):
            window = joined[:, number * LANES : (number + 1) * LANES]
            return window * cosine + turn(window) * sine

        scale = HALF ** -0.5
        queries = rotate(0).astype(bf16).astype(f32) * scale
        qm[0, here, :] = jnp.where(low_half, queries, 0.0).astype(bf16)
        qm[1, here, :] = jnp.where(low_half, 0.0, queries).astype(bf16)
        kw[0, here, :] = rotate(1).astype(bf16)
        vw[0, here, :] = joined[:, 2 * LANES : 3 * LANES].astype(bf16)
        both = rotate(3)
        qm[2, here, :] = jnp.where(low_half, both.astype(bf16).astype(f32) * scale, 0.0).astype(bf16)
        kw[1, here, :] = jnp.where(low_half, pltpu.roll(both, HALF, 1), 0.0).astype(bf16)
        vw[1, here, :] = joined[:, 4 * LANES : 5 * LANES].astype(bf16)
        return carry

    lax.fori_loop(0, cols // group, project, 0)

    def attend(head):
        window = head // 2

        def step_fn(step, carry):
            here = pl.ds(pl.multiple_of(step * chunk, chunk), chunk)
            scores = mt(qm[head, here, :], kw[window])
            allowed = seg_tab[here, :][:, 0:1] == seg_key
            scores = jnp.where(allowed, scores, NEG)
            top = jnp.max(scores, axis=1, keepdims=True)
            raised = jnp.exp(scores - top)
            total = jnp.sum(raised, axis=1, keepdims=True)
            prob_low = (raised * (1.0 / total)).astype(bf16)
            prob[head, here, :] = prob_low
            mixed = mm(prob_low, vw[window])
            if head == 1:
                mixed = jnp.where(low_half, att[0, here, :], mixed)
            att[window, here, :] = mixed
            return carry

        lax.fori_loop(0, row_len // chunk, step_fn, 0)

    up_spread.relay(0, inner=True)
    attend(0)
    attend(1)
    up_spread.relay(1, inner=True)
    attend(2)
    last_segment = lens.shape[1] - 1
    for j in range(cols):
        here = slice(j * tok, (j + 1) * tok)
        kept = seg_tab[here, :] < last_segment
        s_att[j, :, 0:LANES] = jnp.where(kept, att[0, here, :], 0.0).astype(bf16)
        s_att[j, :, LANES : 2 * LANES] = jnp.where(kept, att[1, here, :], 0.0).astype(bf16)
    att_slots = to_lanes(lambda to: s_att.at[to], r_att)
    r_att[blk] = s_att[blk]

    down_spread.tail_out()
    up_spread.relay(2)
    gather_relay(out_lanes, s_out, shards_here)
    gate_spread.relay(0, inner=False)
    gate_spread.relay(1, inner=False)
    down_spread.relay(0, inner=True)
    down_spread.relay(1, inner=True)
    for j in range(2):
        down_spread.pass_tail(j)
    gather_done(out_lanes, s_out, shards_here)
    shards = planes * 2 * cols
    per_quarter = shards // cols
    head_rows = per_quarter * rows
    for quarter in range(cols):
        w_out[quarter, 0:head_rows, :] = jnp.concatenate(
            [
                s_out[s % cols, s // cols, 0:rows, :].astype(f32)
                for s in range(quarter * per_quarter, (quarter + 1) * per_quarter)
            ],
            axis=0,
        ).astype(bf16)
        w_out[quarter, head_rows:, :] = jnp.zeros(
            (w_out.shape[1] - head_rows, width), bf16
        )
    column = lax.broadcasted_iota(jnp.int32, (LANES, width), 1).astype(f32)
    owner = jnp.floor((column + 0.5) * (1.0 / rows))
    inside = column - owner * rows
    unit = (
        inside == lax.broadcasted_iota(jnp.int32, (LANES, width), 0).astype(f32)
    ).astype(bf16)
    tails = jnp.concatenate(
        [
            s_out[s % cols, s // cols, rows : rows + 8, 0:LANES].astype(f32)
            for s in range(shards)
        ],
        axis=0,
    ).astype(bf16)
    shard_ids = lax.broadcasted_iota(jnp.int32, (shards, 8, width), 0).astype(f32)
    shard_hit = (shard_ids == owner[0:1].reshape(1, 1, width)).astype(f32)
    params[...] = jnp.sum(mm(tails, unit).reshape(shards, 8, width) * shard_hit, axis=0)
    gain_one, bias_one = params[0:1, :], params[1:2, :]
    gain_two, bias_two = params[2:3, :], params[3:4, :]

    def normalize(residual):
        centered = residual - jnp.mean(residual, axis=1, keepdims=True)
        variance = jnp.mean(centered * centered, axis=1, keepdims=True)
        spread = lax.rsqrt(variance + EPS)
        return centered * spread, spread

    def normalize_back(grad, normal, spread, gain):
        inner = grad * gain
        mean_inner = jnp.mean(inner, axis=1, keepdims=True)
        mean_both = jnp.mean(inner * normal, axis=1, keepdims=True)
        return (inner - mean_inner - normal * mean_both) * spread

    def column_sum(value):
        return jnp.sum(value, axis=0, keepdims=True)

    from_lanes(att_slots, r_att)
    branch = mm(r_att[0], w_out[0])
    for quarter in range(1, cols):
        branch = branch + mm(r_att[quarter], w_out[quarter])
    normal, spread_one = normalize(xin[...].astype(f32) + branch)
    norm_one[...] = normal
    hidden = normal * gain_one + bias_one
    hid[...] = hidden
    hs[blk] = hidden.astype(bf16)
    hid_slots = gather_start(hs.at[blk], hs)
    up_spread.relay(0, inner=False)
    up_spread.relay(1, inner=False)
    down_spread.relay(0, inner=False)
    down_spread.relay(1, inner=False)
    gather_relay(hid_slots, hs)
    gate_spread.settle()
    gather_done(hid_slots, hs)

    wide = 256
    strips = units // wide

    def each_strip(body):
        def step_fn(step, carry):
            body(pl.ds(pl.multiple_of(step * wide, wide), wide))
            return carry

        lax.fori_loop(0, strips, step_fn, 0)

    def expand_gate(here):
        tokens = hs[...].reshape(row_len, width)
        gate_pre[:, here] = mm(tokens, w_gate[:, :, here].reshape(width, wide))

    def expand_up(here):
        tokens = hs[...].reshape(row_len, width)
        up = mm(tokens, w_up[:, :, here].reshape(width, wide))
        gate = gate_pre[:, here]
        up_pre[:, here] = up
        act[:, here] = (gate / (1.0 + jnp.exp(-gate)) * up).astype(bf16)

    each_strip(expand_gate)
    up_spread.settle()
    each_strip(expand_up)
    down_spread.settle()
    down_spread.settle_tail()

    def contract(step, carry):
        here = pl.ds(pl.multiple_of(step * wide, wide), wide)
        mixed = mm(act[...], w_down[:, :, here].reshape(units, wide))
        s_mix[:, :, here] = mixed.reshape(cols, tok, wide).astype(bf16)
        return carry

    lax.fori_loop(0, width // wide, contract, 0)
    halves = [pl.ds(0, tok // 2), pl.ds(tok // 2, tok // 2)]
    mix_slots = [sum_start(s_mix, r_mix, cut) for cut in halves]
    for slots, cut in zip(mix_slots, halves):
        sum_relay(slots, s_mix, r_mix, t_mix, cut)
    second_gain, second_bias, dm_slots = 0.0, 0.0, []
    for slots, cut in zip(mix_slots, halves):
        mlp_out = sum_done(slots, s_mix, r_mix, cut)
        normal, spread_two = normalize(hid[cut, :] + mlp_out)
        outputs[cut, :] = (normal * gain_two + bias_two).astype(bf16)
        grad = cot[cut, :].astype(f32)
        second_gain = second_gain + column_sum(grad * normal)
        second_bias = second_bias + column_sum(grad)
        d_two = normalize_back(grad, normal, spread_two, gain_two)
        dres_two[cut, :] = d_two
        dms[blk, cut] = d_two.astype(bf16)
        dm_slots.append(gather_start(dms.at[blk], dms, cut))
    for slots, cut in zip(dm_slots, halves):
        gather_relay(slots, dms, cut)
    for slots, cut in zip(dm_slots, halves):
        gather_done(slots, dms, cut)

    down_sum = Collect(wire, place, sum_down)
    gate_sum = Collect(wire, place, sum_gate)
    up_sum = Collect(wire, place, sum_up)
    in_sum = Collect(wire, place, sum_in)
    out_sum = Collect(wire, place, sum_out)
    half = 4

    def fill_parts(part, left_of, right):
        height = part.shape[2]

        def step_fn(step, carry):
            here = pl.ds(pl.multiple_of(step * half * height, LANES), half * height)
            product = tm(left_of(here), right())
            for j in range(half):
                part[j % 2, step * (half // 2) + j // 2] = product[
                    j * height : (j + 1) * height
                ].astype(bf16)
            return carry

        lax.fori_loop(0, planes * 2 // half, step_fn, 0)

    fill_parts(down_sum.part, lambda here: act[:, here], lambda: dms[...].reshape(row_len, width))
    down_sum.send()

    block = w_down.shape[1]

    def active_grads(step, carry):
        here = pl.ds(pl.multiple_of(step * half * block, LANES), half * block)
        d_active = mt(
            dms[...].reshape(row_len, width),
            w_down[pl.ds(step * half, half)].reshape(half * block, width),
        )
        gate, up = gate_pre[:, here], up_pre[:, here]
        sg = 1.0 / (1.0 + jnp.exp(-gate))
        dgate[:, here] = (d_active * up * sg * (1.0 + gate * (1.0 - sg))).astype(bf16)
        dup[:, here] = (d_active * gate * sg).astype(bf16)
        return carry

    lax.fori_loop(0, planes * 2 // half, active_grads, 0)
    block = w_gate.shape[1]

    def hidden_rows(here):
        return hs[:, :, here].reshape(row_len, half * block)

    fill_parts(gate_sum.part, hidden_rows, lambda: dgate[...])
    gate_sum.send()
    def hidden_grads(step, carry):
        here = pl.ds(pl.multiple_of(step * half * block, LANES), half * block)
        those = pl.ds(step * half, half)
        mixed = mt(dgate[...], w_gate[those].reshape(half * block, units)) + mt(
            dup[...], w_up[those].reshape(half * block, units)
        )
        s_dh[:, :, here] = mixed.reshape(cols, tok, half * block).astype(bf16)
        return carry

    lax.fori_loop(0, planes * 2 // half, hidden_grads, 0)
    dh_slots = sum_start(s_dh, r_dh)

    sum_relay(dh_slots, s_dh, r_dh, t_dh)
    fill_parts(up_sum.part, hidden_rows, lambda: dup[...])
    up_sum.send()
    down_sum.first(1)
    down_sum.first(0)
    d_hidden = dres_two[...] + sum_done(dh_slots, s_dh, r_dh)
    down_sum.first(2)
    normal = norm_one[...]
    first_gain = column_sum(d_hidden * normal)
    first_bias = column_sum(d_hidden)
    d_one = normalize_back(d_hidden, normal, spread_one, gain_one)
    dres_one[...] = d_one
    d_branch = d_one.astype(bf16)
    mine = pl.ds(pl.multiple_of(blk * tok, tok), tok)
    kept = seg_tab[mine, :][:, 0:1] < last_segment
    for quarter in range(cols):
        pulled = mt(d_branch, w_out[quarter]).astype(bf16).astype(f32)
        s_da[quarter] = jnp.where(kept, pulled, 0.0).astype(bf16)
    da_slots = to_lanes(lambda to: s_da.at[to], r_da)
    r_da[blk] = s_da[blk]

    vectors = jnp.concatenate(
        [first_gain, first_bias, second_gain, second_bias, jnp.zeros((4, width), f32)], axis=0
    )
    tails = mt(
        (shard_hit * vectors.reshape(1, 8, width)).reshape(shards * 8, width).astype(bf16), unit
    )
    for quarter in range(cols):
        product = tm(r_att[quarter], d_branch)
        for t in range(per_quarter):
            s = quarter * per_quarter + t
            owner_dp = s // cols
            lower = jnp.concatenate(
                [tails[s * 8 : s * 8 + 8], jnp.zeros((8, width - LANES), f32)], axis=1
            )
            b_out[s % cols, owner_dp % 2, owner_dp // 2] = jnp.concatenate(
                [product[t * rows : (t + 1) * rows], lower], axis=0
            ).astype(bf16)
    both_sides = pl.ds(0, 2)
    out_blk = sum_start(b_out, rb_out, both_sides)

    sum_relay(out_blk, b_out, rb_out, tb_out, both_sides)
    down_sum.second_tail(1)
    down_sum.second(1)
    from_lanes(da_slots, r_da)
    def attend_back(head):
        window = head // 2
        fresh = head != 1

        def step_fn(step, carry):
            here = pl.ds(pl.multiple_of(step * chunk, chunk), chunk)
            d_out = r_da[pl.ds(step * group, group), :, window * LANES : (window + 1) * LANES]
            d_out = d_out.reshape(chunk, LANES).astype(f32)
            if head == 0:
                d_out = jnp.where(low_half, d_out, 0.0)
            if head == 1:
                d_out = jnp.where(low_half, 0.0, d_out)
            d_low = d_out.astype(bf16)
            delta = jnp.sum(d_out * att[window, here, :], axis=1, keepdims=True)
            prob_low = prob[head, here, :]
            d_prob = mt(d_low, vw[window])
            d_score = (prob_low.astype(f32) * (d_prob - delta)).astype(bf16)
            d_query = mm(d_score, kw[window]) * (HALF ** -0.5)
            if head == 1:
                d_query = jnp.where(low_half, acc_q[0, here, :], d_query)
            acc_q[window, here, :] = d_query
            d_key = tm(d_score, qm[head, here, :])
            d_value = tm(prob_low, d_low)
            if fresh:

                @pl.when(step == 0)
                def _():
                    acc_k[window] = d_key
                    acc_v[window] = d_value

                @pl.when(step != 0)
                def _():
                    acc_k[window] = acc_k[window] + d_key
                    acc_v[window] = acc_v[window] + d_value
            else:
                acc_k[window] = acc_k[window] + d_key
                acc_v[window] = acc_v[window] + d_value
            return carry

        lax.fori_loop(0, row_len // chunk, step_fn, 0)

    attend_back(0)
    gate_sum.first(1)
    down_sum.second_tail(0)
    down_sum.second(0)
    attend_back(1)
    attend_back(2)

    cosine, sine = cos_tab[...], sin_tab[...]

    def rotate_back(vector):
        vector = vector.astype(bf16).astype(f32)
        return (vector * cosine - turn(vector) * sine).astype(bf16)

    dj[:, 0:LANES] = rotate_back(acc_q[0])
    dj[:, LANES : 2 * LANES] = rotate_back(acc_k[0])
    dj[:, 2 * LANES : 3 * LANES] = acc_v[0].astype(bf16)
    dj[:, 3 * LANES : 4 * LANES] = rotate_back(acc_q[1] + pltpu.roll(acc_k[1], HALF, 1))
    dj[:, 4 * LANES : 5 * LANES] = acc_v[1].astype(bf16)

    gate_sum.first(0)
    down_sum.tail()
    fill_parts(in_sum.part, lambda here: xs[:, :, here].reshape(row_len, half * block), lambda: dj[...])

    def input_grads(step, carry):
        here = pl.ds(pl.multiple_of(step * half * block, LANES), half * block)
        mixed = mt(dj[...], w_in[pl.ds(step * half, half)].reshape(half * block, w_in.shape[2]))
        s_ig[:, :, here] = mixed.reshape(cols, tok, half * block).astype(bf16)
        return carry

    lax.fori_loop(0, planes * 2 // half, input_grads, 0)
    ig_slots = sum_start(s_ig, r_ig)

    gate_sum.second(1)
    gate_sum.first(2)
    sum_relay(ig_slots, s_ig, r_ig, t_ig)
    gate_sum.second(0)
    up_sum.first(1)
    out_sum.part[...] = sum_done(out_blk, b_out, rb_out, both_sides).astype(bf16)
    in_sum.send((1, 0))
    out_sum.send()
    in_sum.send_side(2)
    in_sum.send_side(3)
    up_sum.first(0)
    up_sum.second(1)
    up_sum.first(2)
    f_gate[...] = gate_sum.total()
    up_sum.second(0)
    g_down[...] = down_sum.total()
    grad_in = dres_one[...] + sum_done(ig_slots, s_ig, r_ig)
    input_grad[...] = grad_in.astype(bf16)
    in_sum.first(1)
    in_sum.first(0)
    up_total = up_sum.total()
    gate_total = f_gate[...]
    for j in range(cols):
        here = slice(j * rows, (j + 1) * rows)
        s_gmlp[j] = jnp.concatenate([gate_total[here], up_total[here]], axis=0).astype(bf16)
    gmlp_slots = to_lanes(lambda to: s_gmlp.at[to], r_gmlp)
    r_gmlp[blk] = s_gmlp[blk]
    in_sum.second(1)
    for j in (1, 0, 2):
        out_sum.first(j)
    in_sum.second(0)
    in_sum.first(2)
    out_sum.second(1)
    out_sum.second(0)
    from_lanes(gmlp_slots, r_gmlp)
    g_mlp[...] = r_gmlp[...]
    in_total = in_sum.total()
    for j in range(cols):
        s_gin[j] = jnp.concatenate(
            [in_total[j * rows : (j + 1) * rows], jnp.zeros((8, in_total.shape[1]), f32)], axis=0
        ).astype(bf16)
    gin_slots = to_lanes(lambda to: s_gin.at[to], r_gin)
    r_gin[blk] = s_gin[blk]
    g_out[...] = out_sum.total()
    from_lanes(gin_slots, r_gin)
    g_in[...] = r_gin[...]
    wire.finish()


def unpack(
    rows,
    block,
    outputs,
    input_grad,
    g_in,
    g_mlp,
    g_out,
    g_down,
    outputs_to,
    input_grad_to,
    in_to,
    out_to,
    gate_to,
    up_to,
    down_to,
    *vectors_to,
):
    f32 = jnp.float32
    cols = g_in.shape[0]
    width = outputs.shape[1]
    outputs_to[0] = outputs[...]
    input_grad_to[0] = input_grad[...]
    down_to[...] = g_down[...]
    out_to[...] = g_out[0:rows, :]
    for number, vector_to in enumerate(vectors_to):
        vector_to[...] = g_out[rows + number, 0:rows]
    low_half = lax.broadcasted_iota(jnp.int32, (1, LANES), 1) < HALF
    joined = [g_in[j].astype(f32)[0:rows] for j in range(cols)]
    single_at = ((3, 0), (3, 1), (4, 0))

    def half(kind, number, want):
        owner, part = number // 3, number % 3
        window, at = (kind, part) if part < 2 else single_at[kind]
        value = joined[owner][:, window * LANES : (window + 1) * LANES]
        return value if at == want else pltpu.roll(value, HALF, 1)

    for kind in range(3):
        for n in range(width // LANES):
            at = kind * width + n * LANES
            in_to[:, at : at + LANES] = jnp.where(
                low_half, half(kind, 2 * n, 0), half(kind, 2 * n + 1, 1)
            )
    lanes = lax.broadcasted_iota(jnp.int32, (1, LANES), 1)
    mlp = [g_mlp[j].astype(f32) for j in range(cols)]
    for first_row, target in ((0, gate_to), (rows, up_to)):
        parts = [part[first_row : first_row + rows] for part in mlp]
        for n in range(target.shape[1] // LANES):
            first = n * LANES
            result = None
            for number in range(first // block, (first + LANES - 1) // block + 1):
                ring_at, owner = number // cols, number % cols
                piece = window_at(parts[owner], ring_at * block + first - number * block)
                begin = number * block - first
                result = piece if result is None else jnp.where(lanes < begin, result, piece)
            target[:, first : first + LANES] = result


def fast_shards(
    depth,
    inputs,
    doc_lengths,
    project_in,
    project_out,
    gate_weight,
    up_weight,
    down_weight,
    first_gain,
    first_bias,
    second_gain,
    second_bias,
    cotangent,
):
    cols = 4
    tok, width = inputs.shape[1:]
    rows = project_in.shape[0]
    ff = gate_weight.shape[1]
    ring = depth * 2
    row_len = tok * cols
    units = ff // cols
    block = units // ring
    head_width = width // cols
    in_width = 5 * LANES
    bf16, f32 = jnp.bfloat16, jnp.float32

    lane_ids = np.arange(LANES) % QUART
    freq = jnp.asarray(
        np.broadcast_to(BASE ** (-2.0 * lane_ids / HALF), (8, LANES)).astype(np.float32)
    )

    def scratch(*shape, kind=bf16):
        return pltpu.VMEM(shape, kind)

    def sums(height, across, tail=0):
        main = height - tail
        buffers = [
            scratch(2, depth, height, across),
            scratch(depth, main, across),
            scratch(depth, main, across),
            scratch(4, main, across),
        ]
        if tail:
            buffers = buffers + [
                scratch(4, 2, tail, across),
                scratch(2, 2, tail, across),
                scratch(2, tail, across),
                scratch(tail, across, kind=f32),
            ]
        return tuple(buffers)

    stacked = scratch(cols, tok, width)
    heads = 3
    buffers = [
        stacked,
        scratch(cols, 32, in_width),
        scratch(cols, 2 * rows, units),
        scratch(8, LANES, kind=f32),
        scratch(cols, 32, in_width),
        scratch(cols, 2 * rows, units),
        scratch(cols, ring, 32, width),
        scratch(ring, cols * rows, in_width),
        scratch(ring, cols * rows, units),
        scratch(ring, cols * rows, units),
        scratch(ring, block, width),
        scratch(cols, 2 * LANES, width),
        scratch(8, width, kind=f32),
        scratch(row_len, LANES, kind=f32),
        scratch(row_len, LANES, kind=f32),
        scratch(row_len, LANES, kind=jnp.int32),
        scratch(heads, row_len, LANES),
        scratch(2, row_len, LANES),
        scratch(2, row_len, LANES),
        scratch(heads, row_len, row_len),
        scratch(2, row_len, LANES, kind=f32),
        scratch(cols, tok, 2 * LANES),
        scratch(cols, tok, 2 * LANES),
        scratch(tok, width, kind=f32),
        scratch(tok, width, kind=f32),
        stacked,
        scratch(row_len, units, kind=f32),
        scratch(row_len, units, kind=f32),
        scratch(row_len, units),
        stacked,
        scratch(3, tok, width),
        scratch(tok, width),
        scratch(tok, width, kind=f32),
        stacked,
        scratch(row_len, units),
        scratch(row_len, units),
        stacked,
        scratch(3, tok, width),
        scratch(tok, width),
        scratch(tok, width, kind=f32),
        scratch(cols, tok, 2 * LANES),
        scratch(cols, tok, 2 * LANES),
        scratch(2, row_len, LANES, kind=f32),
        scratch(2, row_len, LANES, kind=f32),
        scratch(2, row_len, LANES, kind=f32),
        scratch(row_len, in_width),
        stacked,
        scratch(3, tok, width),
        scratch(tok, width),
        sums(cols * rows, in_width),
        sums(cols * rows, units),
        sums(cols * rows, units),
        sums(block, width, DTB),
        scratch(cols, 2, depth, 32, width),
        scratch(3, 2, depth, 32, width),
        scratch(2, depth, 32, width),
        sums(32, width, 0),
        scratch(cols * rows, units, kind=f32),
        scratch(cols, 2 * rows, units),
        scratch(cols, 2 * rows, units),
        scratch(cols, 32, in_width),
        scratch(cols, 32, in_width),
        pltpu.SemaphoreType.DMA((240,)),
        pltpu.SemaphoreType.DMA((240,)),
    ]
    vmem = pl.BlockSpec(memory_space=pltpu.VMEM)
    tokens = row_len * width
    outputs, input_grad, g_in, g_mlp, g_out, g_down = pl.pallas_call(
        functools.partial(fused, depth),
        out_shape=(
            jax.ShapeDtypeStruct((tok, width), bf16),
            jax.ShapeDtypeStruct((tok, width), bf16),
            jax.ShapeDtypeStruct((cols, 32, in_width), bf16),
            jax.ShapeDtypeStruct((cols, 2 * rows, units), bf16),
            jax.ShapeDtypeStruct((32, width), f32),
            jax.ShapeDtypeStruct((block, width), f32),
        ),
        in_specs=[pl.BlockSpec(memory_space=pltpu.SMEM)] + [vmem] * 12,
        out_specs=(vmem,) * 6,
        scratch_shapes=buffers,
        compiler_params=pltpu.CompilerParams(
            collective_id=0, has_side_effects=True, vmem_limit_bytes=60 * 2**20
        ),
        cost_estimate=pl.CostEstimate(
            flops=6 * tokens * (3 * units + 4 * head_width),
            bytes_accessed=8 * 2**20,
            transcendentals=3 * row_len * row_len,
        ),
        name="layer",
    )(
        doc_lengths,
        freq,
        inputs[0],
        cotangent[0],
        project_in,
        gate_weight,
        up_weight,
        project_out,
        down_weight,
        first_gain[None],
        first_bias[None],
        second_gain[None],
        second_bias[None],
    )

    vector = jax.ShapeDtypeStruct((rows,), f32)
    return pl.pallas_call(
        functools.partial(unpack, rows, block),
        out_shape=(
            jax.ShapeDtypeStruct((1, tok, width), bf16),
            jax.ShapeDtypeStruct((1, tok, width), bf16),
            jax.ShapeDtypeStruct((rows, 3 * width), f32),
            jax.ShapeDtypeStruct((rows, width), f32),
            jax.ShapeDtypeStruct((rows, ff), f32),
            jax.ShapeDtypeStruct((rows, ff), f32),
            jax.ShapeDtypeStruct((block, width), f32),
            vector,
            vector,
            vector,
            vector,
        ),
        in_specs=[vmem] * 6,
        out_specs=(vmem,) * 11,
        name="unpack",
    )(outputs, input_grad, g_in, g_mlp, g_out, g_down)


def pick(sizes):
    def chosen(*args):
        tok, width = args[0].shape[1:]
        ring, cols = sizes["dp"], sizes["blk"]
        fits = (
            ring == 8
            and cols == 4
            and tok == LANES
            and HEADS == 3 * cols
            and width == HEADS * HALF
            and args[2].shape[0] == 24
            and args[4].shape[1] == 4 * width
        )
        if fits:
            return fast_shards(ring // 2, *args)
        return shards(*args)

    return chosen


def solution(mesh):
    placed = (
        P("dp", "blk", None),
        P("dp", None),
        P(("dp", "blk"), None),
        P(("dp", "blk"), None),
        P(("dp", "blk"), None),
        P(("dp", "blk"), None),
        P(("dp", "blk"), None),
        P(("dp", "blk")),
        P(("dp", "blk")),
        P(("dp", "blk")),
        P(("dp", "blk")),
        P("dp", "blk", None),
    )
    return jax.shard_map(
        pick(dict(mesh.shape)),
        mesh=mesh,
        in_specs=placed,
        out_specs=(
            P("dp", "blk", None),
            P("dp", "blk", None),
            P(("dp", "blk"), None),
            P(("dp", "blk"), None),
            P(("dp", "blk"), None),
            P(("dp", "blk"), None),
            P(("dp", "blk"), None),
            P(("dp", "blk")),
            P(("dp", "blk")),
            P(("dp", "blk")),
            P(("dp", "blk")),
        ),
        check_vma=False,
    )
```

```python
import functools

import jax
import jax.numpy as jnp
import numpy as np
from jax import lax
from jax.experimental import pallas as pl
from jax.experimental.pallas import tpu as pltpu
from jax.sharding import PartitionSpec as P

HEADS = 12


NEG = -1e30
EPS = 1e-05
BASE = 1000.0


def doc_layout(lengths_row, positions):
    bounds = jnp.cumsum(lengths_row)
    passed = positions[:, None] >= bounds[None, :]
    segment = jnp.sum(passed.astype(jnp.int32), axis=1)
    begins = jnp.sum(jnp.where(passed, lengths_row[None, :], 0), axis=1)
    return (segment, positions - begins)


def rotary(vectors, offsets):
    half_size = vectors.shape[-1] // 2
    frequency = BASE ** (-2.0 * jnp.arange(half_size, dtype=jnp.float32) / vectors.shape[-1])
    angles = offsets.astype(jnp.float32)[:, None] * frequency[None, :]
    cosine = jnp.concatenate([jnp.cos(angles), jnp.cos(angles)], axis=1)[:, None, :]
    sine_rows = jnp.concatenate([jnp.sin(angles), jnp.sin(angles)], axis=1)[:, None, :]
    first_half = vectors[..., :half_size]
    second_half = vectors[..., half_size:]
    turned = jnp.concatenate([-second_half, first_half], axis=-1)
    return vectors * cosine + turned * sine_rows


def layer_norm(residual, gain_row, bias_row):
    row_mean = jnp.mean(residual, axis=-1, keepdims=True)
    centered = residual - row_mean
    variance = jnp.mean(centered * centered, axis=-1, keepdims=True)
    return centered * lax.rsqrt(variance + EPS) * gain_row + bias_row


def contract_rows(left, right):
    return lax.dot_general(
        left, right, (((0,), (0,)), ((), ())), preferred_element_type=jnp.float32
    )


def contract_cols(left, right):
    return lax.dot_general(
        left, right, (((1,), (1,)), ((), ())), preferred_element_type=jnp.float32
    )


def tile_scores(query_tile, key_tile, seg_query, seg_key, score_scale):
    scores = (
        jnp.einsum("qhd,khd->hqk", query_tile, key_tile, preferred_element_type=jnp.float32)
        * score_scale
    )
    allowed = (seg_query[:, None] == seg_key[None, :])[None, :, :]
    return (jnp.where(allowed, scores, NEG), allowed)


def run_groups(pieces, group, lengths_row, seg_query, carried, tile_fn, extra_shape):
    group_count = pieces[0].shape[0] // group

    def group_step(carried_in, number):
        offset = number * group
        tile_set = tuple(
            (lax.dynamic_slice_in_dim(piece_rows, offset, group, 0) for piece_rows in pieces)
        )
        positions = offset + jnp.arange(group, dtype=jnp.int32)
        seg_key, unused_offsets = doc_layout(lengths_row, positions)
        touches = (seg_key[0] <= seg_query[-1]) & (seg_query[0] <= seg_key[-1])

        def active(state_in):
            return tile_fn(state_in, tile_set, seg_key)

        def skipped(state_in):
            return (state_in, jnp.zeros(extra_shape, jnp.float32))

        return lax.cond(touches, active, skipped, carried_in)

    return lax.scan(group_step, carried, jnp.arange(group_count, dtype=jnp.int32))


def shards(
    inputs,
    doc_lengths,
    project_in,
    project_out,
    gate_weight,
    up_weight,
    down_weight,
    first_gain,
    first_bias,
    second_gain,
    second_bias,
    cotangent,
):
    group = inputs.shape[1]
    width = inputs.shape[2]
    head_count = HEADS
    head_size = width // head_count
    score_scale = head_size ** (-0.5)
    cycle_rank = lax.axis_index("blk")
    positions = cycle_rank * group + jnp.arange(group, dtype=jnp.int32)
    lengths_row = doc_lengths[0]
    seg_query, offsets = doc_layout(lengths_row, positions)
    keep_mask = seg_query < lengths_row.shape[0] - 1
    keep_float = keep_mask.astype(jnp.float32)
    fetched = (
        lax.all_gather(project_in, ("dp", "blk"), axis=0, tiled=True),
        lax.all_gather(project_out, ("dp", "blk"), axis=0, tiled=True),
        lax.all_gather(gate_weight, ("dp", "blk"), axis=0, tiled=True),
        lax.all_gather(up_weight, ("dp", "blk"), axis=0, tiled=True),
        lax.all_gather(down_weight, ("dp", "blk"), axis=0, tiled=True),
        lax.all_gather(first_gain, ("dp", "blk"), axis=0, tiled=True),
        lax.all_gather(first_bias, ("dp", "blk"), axis=0, tiled=True),
        lax.all_gather(second_gain, ("dp", "blk"), axis=0, tiled=True),
        lax.all_gather(second_bias, ("dp", "blk"), axis=0, tiled=True),
    )
    full_in, full_out, full_gate, full_up, full_down = (
        fetched[0],
        fetched[1],
        fetched[2],
        fetched[3],
        fetched[4],
    )
    gain_one = fetched[5].astype(jnp.float32)
    bias_one = fetched[6].astype(jnp.float32)
    gain_two = fetched[7].astype(jnp.float32)
    bias_two = fetched[8].astype(jnp.float32)
    tokens_low = inputs[0]
    tokens_f = tokens_low.astype(jnp.float32)
    joined = jnp.dot(tokens_low, full_in, preferred_element_type=jnp.float32)
    query_raw = joined[:, :width].reshape(group, head_count, head_size)
    key_raw = joined[:, width : 2 * width].reshape(group, head_count, head_size)
    value_low = joined[:, 2 * width :].astype(jnp.bfloat16)
    query_rot, query_pull = jax.vjp(lambda vectors: rotary(vectors, offsets), query_raw)
    key_rot, key_pull = jax.vjp(lambda vectors: rotary(vectors, offsets), key_raw)
    query_low = query_rot.astype(jnp.bfloat16)
    key_low = key_rot.reshape(group, width).astype(jnp.bfloat16)

    def stats_tile(carried, tile_set, seg_key):
        row_top, row_total = carried
        key_tile = tile_set[0].reshape(group, head_count, head_size)
        scores, allowed = tile_scores(query_low, key_tile, seg_query, seg_key, score_scale)
        new_top = jnp.maximum(row_top, jnp.max(scores, axis=2))
        shrink = jnp.exp(row_top - new_top)
        added = jnp.sum(jnp.where(allowed, jnp.exp(scores - new_top[:, :, None]), 0.0), axis=2)
        return ((new_top, row_total * shrink + added), jnp.zeros((1,), jnp.float32))

    init_stats = (
        jnp.full((head_count, group), NEG, jnp.float32),
        jnp.zeros((head_count, group), jnp.float32),
    )
    carried = init_stats
    carried, unused = run_groups(
        (lax.all_gather(key_low, "blk", axis=0, tiled=True),),
        group,
        lengths_row,
        seg_query,
        carried,
        stats_tile,
        (1,),
    )
    row_top, row_total = carried
    log_total = row_top + jnp.log(row_total)

    def output_tile(accum, tile_set, seg_key):
        key_tile = tile_set[0].reshape(group, head_count, head_size)
        value_tile = tile_set[1].reshape(group, head_count, head_size)
        scores, allowed = tile_scores(query_low, key_tile, seg_query, seg_key, score_scale)
        prob_low = jnp.where(allowed, jnp.exp(scores - log_total[:, :, None]), 0.0).astype(
            jnp.bfloat16
        )
        accum = accum + jnp.einsum(
            "hqk,khd->qhd", prob_low, value_tile, preferred_element_type=jnp.float32
        )
        return (accum, jnp.zeros((1,), jnp.float32))

    zero_accum = jnp.zeros((group, head_count, head_size), jnp.float32)
    accum = zero_accum
    accum, unused = run_groups(
        (
            lax.all_gather(key_low, "blk", axis=0, tiled=True),
            lax.all_gather(value_low, "blk", axis=0, tiled=True),
        ),
        group,
        lengths_row,
        seg_query,
        accum,
        output_tile,
        (1,),
    )
    attend_low = (accum * keep_float[:, None, None]).reshape(group, width).astype(jnp.bfloat16)
    branch = jnp.dot(attend_low, full_out, preferred_element_type=jnp.float32)
    residual_one = tokens_f + branch
    hidden, norm_one_pull = jax.vjp(layer_norm, residual_one, gain_one, bias_one)
    hidden_low = hidden.astype(jnp.bfloat16)
    gate_pre = jnp.dot(hidden_low, full_gate, preferred_element_type=jnp.float32)
    up_pre = jnp.dot(hidden_low, full_up, preferred_element_type=jnp.float32)
    activated, swiglu_pull = jax.vjp(
        lambda gate_in, up_in: jax.nn.silu(gate_in) * up_in, gate_pre, up_pre
    )
    active_low = activated.astype(jnp.bfloat16)
    mlp_out = jnp.dot(active_low, full_down, preferred_element_type=jnp.float32)
    outputs_f, norm_two_pull = jax.vjp(layer_norm, hidden + mlp_out, gain_two, bias_two)
    refetched = (
        lax.all_gather(project_in, ("dp", "blk"), axis=0, tiled=True),
        lax.all_gather(project_out, ("dp", "blk"), axis=0, tiled=True),
        lax.all_gather(gate_weight, ("dp", "blk"), axis=0, tiled=True),
        lax.all_gather(up_weight, ("dp", "blk"), axis=0, tiled=True),
        lax.all_gather(down_weight, ("dp", "blk"), axis=0, tiled=True),
    )
    full_in, full_out, full_gate, full_up, full_down = (
        refetched[0],
        refetched[1],
        refetched[2],
        refetched[3],
        refetched[4],
    )
    d_res_two, second_gain_part, second_bias_part = norm_two_pull(cotangent[0].astype(jnp.float32))
    d_mlp_low = d_res_two.astype(jnp.bfloat16)
    down_part = contract_rows(active_low, d_mlp_low)
    d_active = contract_cols(d_mlp_low, full_down)
    d_gate, d_up = swiglu_pull(d_active)
    d_gate_low = d_gate.astype(jnp.bfloat16)
    d_up_low = d_up.astype(jnp.bfloat16)
    gate_part = contract_rows(hidden_low, d_gate_low)
    up_part = contract_rows(hidden_low, d_up_low)
    d_hidden = d_res_two + contract_cols(d_gate_low, full_gate) + contract_cols(d_up_low, full_up)
    d_res_one, first_gain_part, first_bias_part = norm_one_pull(d_hidden)
    d_branch_low = d_res_one.astype(jnp.bfloat16)
    out_part = contract_rows(attend_low, d_branch_low)
    d_attend = contract_cols(d_branch_low, full_out).astype(jnp.bfloat16)
    d_attend_low = (d_attend * keep_mask[:, None].astype(jnp.bfloat16)).reshape(
        group, head_count, head_size
    )
    delta = jnp.einsum("qhd,qhd->hq", d_attend_low.astype(jnp.float32), accum)

    def back_tile(grad_query, tile_set, seg_key):
        key_tile = tile_set[0].reshape(group, head_count, head_size)
        value_tile = tile_set[1].reshape(group, head_count, head_size)
        scores, allowed = tile_scores(query_low, key_tile, seg_query, seg_key, score_scale)
        prob_rows = jnp.where(allowed, jnp.exp(scores - log_total[:, :, None]), 0.0)
        d_probs = jnp.einsum(
            "qhd,khd->hqk", d_attend_low, value_tile, preferred_element_type=jnp.float32
        )
        d_score_low = (prob_rows * (d_probs - delta[:, :, None])).astype(jnp.bfloat16)
        grad_query = (
            grad_query
            + jnp.einsum("hqk,khd->qhd", d_score_low, key_tile, preferred_element_type=jnp.float32)
            * score_scale
        )
        grad_key = (
            jnp.einsum("hqk,qhd->khd", d_score_low, query_low, preferred_element_type=jnp.float32)
            * score_scale
        )
        grad_value = jnp.einsum(
            "hqk,qhd->khd",
            prob_rows.astype(jnp.bfloat16),
            d_attend_low,
            preferred_element_type=jnp.float32,
        )
        return (
            grad_query,
            jnp.concatenate(
                [grad_key.reshape(group, width), grad_value.reshape(group, width)], axis=1
            ),
        )

    grad_query = zero_accum
    grad_query, blocks = run_groups(
        (
            lax.all_gather(key_low, "blk", axis=0, tiled=True),
            lax.all_gather(value_low, "blk", axis=0, tiled=True),
        ),
        group,
        lengths_row,
        seg_query,
        grad_query,
        back_tile,
        (group, 2 * width),
    )
    blocks = blocks.reshape(-1, 2 * width)
    back_result = (grad_query, blocks)
    grad_query = back_result[0]
    owned_pairs = lax.psum_scatter(
        back_result[1].astype(jnp.bfloat16), "blk", scatter_dimension=0, tiled=True
    ).astype(jnp.float32)
    key_sum = owned_pairs[:, :width]
    value_sum = owned_pairs[:, width:]
    d_query_pre = query_pull(grad_query.astype(jnp.bfloat16).astype(jnp.float32))[0]
    d_key_low = key_sum.astype(jnp.bfloat16).astype(jnp.float32)
    d_key_pre = key_pull(d_key_low.reshape(group, head_count, head_size))[0]
    d_value_low = value_sum.astype(jnp.bfloat16).astype(jnp.float32)
    d_joined_low = jnp.concatenate(
        [d_query_pre.reshape(group, width), d_key_pre.reshape(group, width), d_value_low], axis=1
    ).astype(jnp.bfloat16)
    in_part = contract_rows(tokens_low, d_joined_low)
    input_grad = (d_res_one + contract_cols(d_joined_low, full_in)).astype(jnp.bfloat16)
    by_rows = (
        lax.psum_scatter(
            in_part.astype(jnp.bfloat16), "dp", scatter_dimension=0, tiled=True
        ).astype(jnp.float32),
        lax.psum_scatter(
            out_part.astype(jnp.bfloat16), "dp", scatter_dimension=0, tiled=True
        ).astype(jnp.float32),
        lax.psum_scatter(
            gate_part.astype(jnp.bfloat16), "dp", scatter_dimension=0, tiled=True
        ).astype(jnp.float32),
        lax.psum_scatter(
            up_part.astype(jnp.bfloat16), "dp", scatter_dimension=0, tiled=True
        ).astype(jnp.float32),
        lax.psum_scatter(
            down_part.astype(jnp.bfloat16), "dp", scatter_dimension=0, tiled=True
        ).astype(jnp.float32),
        lax.psum_scatter(
            first_gain_part.astype(jnp.bfloat16), "dp", scatter_dimension=0, tiled=True
        ).astype(jnp.float32),
        lax.psum_scatter(
            first_bias_part.astype(jnp.bfloat16), "dp", scatter_dimension=0, tiled=True
        ).astype(jnp.float32),
        lax.psum_scatter(
            second_gain_part.astype(jnp.bfloat16), "dp", scatter_dimension=0, tiled=True
        ).astype(jnp.float32),
        lax.psum_scatter(
            second_bias_part.astype(jnp.bfloat16), "dp", scatter_dimension=0, tiled=True
        ).astype(jnp.float32),
    )
    summed = (
        lax.psum_scatter(
            by_rows[0].astype(jnp.bfloat16), "blk", scatter_dimension=0, tiled=True
        ).astype(jnp.float32),
        lax.psum_scatter(
            by_rows[1].astype(jnp.bfloat16), "blk", scatter_dimension=0, tiled=True
        ).astype(jnp.float32),
        lax.psum_scatter(
            by_rows[2].astype(jnp.bfloat16), "blk", scatter_dimension=0, tiled=True
        ).astype(jnp.float32),
        lax.psum_scatter(
            by_rows[3].astype(jnp.bfloat16), "blk", scatter_dimension=0, tiled=True
        ).astype(jnp.float32),
        lax.psum_scatter(
            by_rows[4].astype(jnp.bfloat16), "blk", scatter_dimension=0, tiled=True
        ).astype(jnp.float32),
        lax.psum_scatter(
            by_rows[5].astype(jnp.bfloat16), "blk", scatter_dimension=0, tiled=True
        ).astype(jnp.float32),
        lax.psum_scatter(
            by_rows[6].astype(jnp.bfloat16), "blk", scatter_dimension=0, tiled=True
        ).astype(jnp.float32),
        lax.psum_scatter(
            by_rows[7].astype(jnp.bfloat16), "blk", scatter_dimension=0, tiled=True
        ).astype(jnp.float32),
        lax.psum_scatter(
            by_rows[8].astype(jnp.bfloat16), "blk", scatter_dimension=0, tiled=True
        ).astype(jnp.float32),
    )
    return (
        outputs_f.astype(jnp.bfloat16)[None],
        input_grad[None],
        summed[0],
        summed[1],
        summed[2],
        summed[3],
        summed[4],
        summed[5],
        summed[6],
        summed[7],
        summed[8],
    )


MESH_IDS = pl.DeviceIdType.MESH
LANES = 128
HALF = 64
QUART = 32
DTF = 48
DTB = 64


def mm(left, right):
    return lax.dot_general(
        left, right, (((1,), (0,)), ((), ())), preferred_element_type=jnp.float32
    )


def mt(left, right):
    return lax.dot_general(
        left, right, (((1,), (1,)), ((), ())), preferred_element_type=jnp.float32
    )


def tm(left, right):
    return lax.dot_general(
        left, right, (((0,), (0,)), ((), ())), preferred_element_type=jnp.float32
    )


def window_at(value, start):
    aligned = min(max(start // LANES * LANES, 0), value.shape[1] - LANES)
    if aligned == start:
        return value[:, aligned : aligned + LANES]
    aligned = min(aligned, value.shape[1] - 2 * LANES)
    two = value[:, aligned : aligned + 2 * LANES]
    return pltpu.roll(two, (aligned - start) % (2 * LANES), 1)[:, :LANES]


def gather_lanes(value, block, first, source):
    lanes = lax.broadcasted_iota(jnp.int32, (1, LANES), 1)
    result = None
    for number in range(first // block, (first + LANES - 1) // block + 1):
        piece = window_at(value, source(number, first))
        begin = number * block - first
        result = piece if result is None else jnp.where(lanes < begin, result, piece)
    return result


class Wire:
    def __init__(self, send_sem, recv_sem, is_inner):
        self.send_sem, self.recv_sem, self.is_inner = send_sem, recv_sem, is_inner
        self.sends, self.slots = 0, 0
        self.sent = {None: [], True: [], False: []}

    def slot(self):
        self.slots += 1
        return self.slots - 1

    def copy(self, src, dst, peer, slot):
        self.sends += 1
        return pltpu.make_async_remote_copy(
            src_ref=src,
            dst_ref=dst,
            send_sem=self.send_sem.at[self.sends - 1],
            recv_sem=self.recv_sem.at[slot],
            device_id=peer,
            device_id_type=MESH_IDS,
        )

    def push(self, src, dst, peer, slot=None, inner=None):
        slot = self.slot() if slot is None else slot
        copy = self.copy(src, dst, peer, slot)
        self.sent[inner].append(copy)
        if inner is None:
            copy.start()
        else:
            pl.when(self.is_inner == inner)(copy.start)
        return slot

    def arrive(self, slot, dst, peer):
        pltpu.make_async_remote_copy(
            src_ref=dst,
            dst_ref=dst,
            send_sem=self.send_sem.at[0],
            recv_sem=self.recv_sem.at[slot],
            device_id=peer,
            device_id_type=MESH_IDS,
        ).wait_recv()

    def finish(self):
        for inner, copies in self.sent.items():

            def drain(copies=copies):
                for copy in copies:
                    copy.wait_send()

            if inner is None:
                drain()
            else:
                pl.when(self.is_inner == inner)(drain)


class Plane:
    def __init__(self, planes):
        dp, self.blk = lax.axis_index("dp"), lax.axis_index("blk")
        self.z, self.x = dp // 2, dp % 2
        self.dp = dp
        self.partner = self.z + 1 - 2 * (self.z % 2)
        self.other = planes // 2 - self.z // (planes // 2)
        self.outer = (planes - 1) * (self.other - 1)
        self.inner = ((self.z + 1) // 2) % 2
        self.order = (self.other, self.outer, self.partner, self.z)
        self.side = (self.z * 2 + (1 - self.x), self.blk)

    def at(self, plane):
        return (plane * 2 + self.x, self.blk)


class Spread:
    def __init__(self, wire, place, target, tail):
        self.wire, self.place, self.target = wire, place, target
        self.height, self.main = target.shape[1], target.shape[1] - tail

    def block(self, plane, column):
        return self.target.at[plane * 2 + column, 0 : self.main]

    def pair(self, plane):
        return self.target.at[pl.ds(plane * 2, 2), self.main : self.height]

    def along(self, own, slots):
        p = self.place
        self.wire.push(own, own, p.at(p.partner), slots[2], inner=False)
        self.wire.push(own, own, p.at(p.other), slots[0] + (1 - p.inner))

    def outward(self, own, slots):
        p = self.place
        self.wire.push(own, own, p.at(p.partner), slots[2], inner=True)

    def start(self):
        p, wire = self.place, self.wire
        self.z_slots = [wire.slot() for _ in range(3)]
        self.along(self.block(p.z, p.x), self.z_slots)

    def start_out(self):
        p = self.place
        self.outward(self.block(p.z, p.x), self.z_slots)

    def start_side(self):
        p, wire = self.place, self.wire
        self.x_slots = [wire.slot() for _ in range(4)]
        own = self.block(p.z, p.x)
        wire.push(own, own, p.side, self.x_slots[3])
        if self.main < self.height:
            rest = self.target.at[p.dp, self.main : self.height]
            self.rest_slot = wire.push(rest, rest, p.side)

    def tail(self):
        p, wire = self.place, self.wire
        rest = self.target.at[p.z * 2 + (1 - p.x), self.main : self.height]
        wire.arrive(self.rest_slot, rest, p.side)
        self.t_slots = [wire.slot() for _ in range(3)]
        self.along(self.pair(p.z), self.t_slots)

    def tail_out(self):
        self.outward(self.pair(self.place.z), self.t_slots)

    def relay(self, j, inner=None):
        p, wire = self.place, self.wire
        block = self.block(p.order[j], p.x)
        onward = wire.copy(block, block, p.side, self.x_slots[j])
        wire.sent[inner].append(onward)
        outward = None
        if j < 2 and inner is not False:
            outward = wire.copy(block, block, p.at(p.partner), self.z_slots[j])
            wire.sent[True].append(outward)

        def run():
            wire.arrive(self.z_slots[j], block, p.side)
            if outward is not None:
                if inner:
                    outward.start()
                else:
                    pl.when(wire.is_inner)(outward.start)
            onward.start()

        if inner is None:
            run()
        else:
            pl.when(wire.is_inner == inner)(run)

    def pass_tail(self, j):
        p, wire = self.place, self.wire
        pair = self.pair(p.order[j])
        copy = wire.copy(pair, pair, p.at(p.partner), self.t_slots[j])
        wire.sent[True].append(copy)

        @pl.when(wire.is_inner)
        def _():
            wire.arrive(self.t_slots[j], pair, p.side)
            copy.start()

    def settle_tail(self):
        p, wire = self.place, self.wire
        wire.arrive(self.t_slots[2], self.pair(p.order[2]), p.side)

        @pl.when(jnp.logical_not(wire.is_inner))
        def _():
            for j in range(2):
                wire.arrive(self.t_slots[j], self.pair(p.order[j]), p.side)

    def settle(self):
        p = self.place
        for j in range(4):
            self.wire.arrive(self.x_slots[j], self.block(p.order[j], 1 - p.x), p.side)


class Collect:
    def __init__(self, wire, place, buffers):
        self.wire, self.place = wire, place
        self.part, self.inbox, self.staged, self.landing = buffers[:4]
        self.height, self.main = self.part.shape[2], self.inbox.shape[1]
        self.split = self.main < self.height
        if self.split:
            self.t_landing, self.t_staged, self.t_cross, self.t_kept = buffers[4:]

    def pair(self, plane):
        return self.part.at[:, plane, self.main : self.height]

    def send_side(self, j):
        p = self.place
        plane = p.order[j]
        self.wire.push(
            self.part.at[1 - p.x, plane, 0 : self.main],
            self.inbox.at[plane],
            p.side,
            self.x_slots[j],
        )

    def send(self, order=(1, 0, 2, 3)):
        p, wire = self.place, self.wire
        self.x_slots = [wire.slot() for _ in range(4)]
        for j in order:
            self.send_side(j)
        self.z_slots = [wire.slot() for _ in range(4)]
        if self.split:
            self.t_slots = [wire.slot() for _ in range(4)]
            for j in (1, 0, 2):
                wire.push(
                    self.pair(p.order[j]),
                    self.t_landing.at[j],
                    p.at(p.partner),
                    self.t_slots[j],
                    inner=None if j == 2 else False,
                )

    def first(self, j):
        p, wire = self.place, self.wire
        plane = p.order[j]
        wire.arrive(self.x_slots[j], self.inbox.at[plane], p.side)
        both = self.part[p.x, plane, 0 : self.main].astype(jnp.float32)
        both = both + self.inbox[plane].astype(jnp.float32)
        self.staged[plane] = both.astype(jnp.bfloat16)
        wire.push(
            self.staged.at[plane],
            self.landing.at[j],
            p.at(p.partner),
            self.z_slots[j],
            inner=None if j == 2 else False,
        )

    def second(self, j):
        p, wire = self.place, self.wire
        plane = p.order[j]
        copy = wire.copy(self.staged.at[plane], self.landing.at[3], p.at(plane), self.z_slots[3])
        wire.sent[True].append(copy)

        @pl.when(wire.is_inner)
        def _():
            wire.arrive(self.z_slots[j], self.landing.at[j], p.side)
            both = self.staged[plane].astype(jnp.float32) + self.landing[j].astype(jnp.float32)
            self.staged[plane] = both.astype(jnp.bfloat16)
            copy.start()

    def second_tail(self, j):
        p, wire = self.place, self.wire
        plane = p.order[j]
        copy = wire.copy(self.t_staged.at[j], self.t_landing.at[3], p.at(plane), self.t_slots[3])
        wire.sent[True].append(copy)

        @pl.when(wire.is_inner)
        def _():
            wire.arrive(self.t_slots[j], self.t_landing.at[j], p.side)
            rest = self.part[:, plane, self.main : self.height].astype(jnp.float32)
            rest = rest + self.t_landing[j].astype(jnp.float32)
            self.t_staged[j] = rest.astype(jnp.bfloat16)
            copy.start()

    def tail(self):
        p, wire = self.place, self.wire
        for j in (2, 3):
            wire.arrive(self.t_slots[j], self.t_landing.at[j], p.side)

        def rest_of(column):
            rest = self.part[column, p.z, self.main : self.height].astype(jnp.float32)
            for j in (2, 3):
                rest = rest + self.t_landing[j, column].astype(jnp.float32)
            return rest

        self.t_kept[...] = rest_of(p.x)
        self.t_cross[0] = rest_of(1 - p.x).astype(jnp.bfloat16)
        self.cross_slot = wire.push(self.t_cross.at[0], self.t_cross.at[1], p.side)

    def total(self):
        p, wire = self.place, self.wire
        wire.arrive(self.x_slots[3], self.inbox.at[p.z], p.side)
        total = self.part[p.x, p.z, 0 : self.main].astype(jnp.float32)
        total = total + self.inbox[p.z].astype(jnp.float32)
        for j in (2, 3):
            wire.arrive(self.z_slots[j], self.landing.at[j], p.side)
            total = total + self.landing[j].astype(jnp.float32)
        if not self.split:
            return total
        wire.arrive(self.cross_slot, self.t_cross.at[1], p.side)
        rest = self.t_kept[...] + self.t_cross[1].astype(jnp.float32)
        return jnp.concatenate([total, rest], axis=0)


def fused(
    depth,
    lens,
    freq,
    xin,
    cot,
    in_rows,
    gate_rows,
    up_rows,
    out_rows,
    p_down,
    gain_a,
    bias_a,
    gain_b,
    bias_b,
    outputs,
    input_grad,
    g_in,
    g_mlp,
    g_out,
    g_down,
    xs,
    p_in,
    p_mlp,
    vectors_tab,
    r_in,
    r_mlp,
    s_out,
    w_in,
    w_gate,
    w_up,
    w_down,
    w_out,
    params,
    cos_tab,
    sin_tab,
    seg_tab,
    qm,
    kw,
    vw,
    prob,
    att,
    s_att,
    r_att,
    norm_one,
    hid,
    hs,
    gate_pre,
    up_pre,
    act,
    s_mix,
    r_mix,
    t_mix,
    dres_two,
    dms,
    dgate,
    dup,
    s_dh,
    r_dh,
    t_dh,
    dres_one,
    s_da,
    r_da,
    acc_q,
    acc_k,
    acc_v,
    dj,
    s_ig,
    r_ig,
    t_ig,
    sum_in,
    sum_gate,
    sum_up,
    sum_down,
    b_out,
    rb_out,
    tb_out,
    sum_out,
    f_gate,
    s_gmlp,
    r_gmlp,
    s_gin,
    r_gin,
    send_sem,
    recv_sem,
):
    planes, cols = depth, 4
    tok = xin.shape[0]
    row_len = tok * cols
    place = Plane(planes)
    dp, blk = place.dp, place.blk
    bf16, f32 = jnp.bfloat16, jnp.float32

    row_of, core_of = blk // 2, blk % 2
    near_at = row_of * 2 + (1 - core_of)
    across_at = (1 - row_of) * 2 + core_of
    corner_at = (1 - row_of) * 2 + (1 - core_of)
    near, across = (dp, near_at), (dp, across_at)

    def lane(k):
        return (dp, (blk + k) % cols)

    def lane_from(k):
        return (blk + cols - k) % cols

    lanes = range(1, cols)
    wire = Wire(send_sem, recv_sem, place.inner == 1)
    barrier = pltpu.get_barrier_semaphore()
    peers = [place.side, place.at(place.partner), place.at(place.other)]
    peers = peers + [lane(k) for k in lanes]
    for peer in peers:
        pl.semaphore_signal(barrier, inc=1, device_id=peer, device_id_type=MESH_IDS)
    far = place.at(place.outer)

    @pl.when(place.inner == 1)
    def _():
        pl.semaphore_signal(barrier, inc=1, device_id=far, device_id_type=MESH_IDS)


    rows = 24
    width = xin.shape[1]
    lane_ids = lax.broadcasted_iota(jnp.int32, (1, LANES), 1)
    low_half = lane_ids < HALF
    head_width = width // cols
    vectors_tab[...] = jnp.zeros_like(vectors_tab)
    for number, vector in enumerate((gain_a, bias_a, gain_b, bias_b)):
        vectors_tab[number : number + 1, 0:rows] = vector[...].astype(f32)
    free_lane = lax.broadcasted_iota(jnp.int32, (8, LANES), 0) + HALF
    to_lane = jnp.where(
        free_lane == lax.broadcasted_iota(jnp.int32, (8, LANES), 1), 1.0, 0.0
    ).astype(bf16)
    vector_columns = tm(vectors_tab[...].astype(bf16), to_lane)[0:rows]
    joined_rows = in_rows[...].astype(f32)
    for j in range(cols):
        starts = [kind * width + j * head_width for kind in range(3)]
        windows = [window_at(joined_rows, start) for start in starts]
        windows.append(
            jnp.where(
                low_half,
                window_at(joined_rows, starts[0] + LANES),
                window_at(joined_rows, starts[1] + LANES - HALF),
            )
        )
        windows.append(
            jnp.where(low_half, window_at(joined_rows, starts[2] + LANES), vector_columns)
        )
        packed = jnp.concatenate(windows, axis=1)
        p_in[j] = jnp.concatenate(
            [packed, jnp.zeros((8, packed.shape[1]), f32)], axis=0
        ).astype(bf16)
    halved = [out_rows[:, n * width // 2 : (n + 1) * width // 2].astype(f32) for n in range(2)]
    s_out[blk, dp] = jnp.concatenate(halved, axis=0).astype(bf16)
    pl.semaphore_wait(barrier, len(peers) + place.inner)

    def to_lanes(source_of, target):
        return [wire.push(source_of((blk + k) % cols), target.at[blk], lane(k)) for k in lanes]

    def from_lanes(slots, target):
        for k, slot in zip(lanes, slots):
            wire.arrive(slot, target.at[lane_from(k)], lane(k))

    every = pl.ds(0, tok)

    def gather_start(own, target, cut=every):
        return [
            wire.push(own.at[cut], target.at[blk, cut], across),
            wire.push(own.at[cut], target.at[blk, cut], near),
        ]

    def gather_relay(slots, target, cut=every):
        came = target.at[across_at, cut]
        wire.arrive(slots[0], came, across)
        slots.append(wire.push(came, came, near))

    def gather_done(slots, target, cut=every):
        wire.arrive(slots[1], target.at[near_at, cut], near)
        wire.arrive(slots[2], target.at[corner_at, cut], near)

    def sum_start(part, inbox, cut=every):
        return [
            wire.push(part.at[corner_at, cut], inbox.at[0, cut], near),
            wire.push(part.at[near_at, cut], inbox.at[1, cut], near),
        ]

    def sum_relay(slots, part, inbox, staged, cut=every):
        wire.arrive(slots[0], inbox.at[0, cut], near)
        both = part[across_at, cut].astype(f32) + inbox[0, cut].astype(f32)
        staged[cut] = both.astype(bf16)
        slots.append(wire.push(staged.at[cut], inbox.at[2, cut], across))

    def sum_done(slots, part, inbox, cut=every):
        wire.arrive(slots[1], inbox.at[1, cut], near)
        total = part[blk, cut].astype(f32) + inbox[1, cut].astype(f32)
        wire.arrive(slots[2], inbox.at[2, cut], across)
        return total + inbox[2, cut].astype(f32)

    in_slots = to_lanes(lambda to: p_in.at[to], r_in)
    w_down[dp] = p_down[...]
    tail = 0
    out_spread = Spread(wire, place, s_out.at[blk], 0)
    out_spread.start()
    out_spread.start_out()
    out_spread.start_side()
    down_spread = Spread(wire, place, w_down, DTF)
    down_spread.start()
    down_spread.start_out()
    down_spread.start_side()
    units = gate_rows.shape[1] // cols
    unit_block = units // (planes * 2)
    for at, weight in ((0, gate_rows), (rows, up_rows)):
        whole = weight[...].astype(f32)
        for j in range(cols):
            packed = jnp.concatenate(
                [
                    gather_lanes(
                        whole,
                        unit_block,
                        n * LANES,
                        lambda ring_at, lane: lane + (cols - 1) * unit_block * ring_at + unit_block * j,
                    )
                    for n in range(units // LANES)
                ],
                axis=1,
            )
            p_mlp[j, at : at + rows] = packed.astype(bf16)
    mlp_slots = to_lanes(lambda to: p_mlp.at[to], r_mlp)
    xs[blk] = xin[...]
    x_slots = gather_start(xin, xs)
    r_in[blk] = p_in[blk]
    r_mlp[blk] = p_mlp[blk]

    lengths = [lens[0, j] for j in range(lens.shape[1])]

    def layout(positions):
        segment = jnp.zeros_like(positions)
        begins = jnp.zeros_like(positions)
        bound = jnp.int32(0)
        for length in lengths:
            bound = bound + length
            passed = positions >= bound
            segment = segment + jnp.where(passed, 1, 0)
            begins = begins + jnp.where(passed, length, 0)
        return segment, positions - begins

    seg_rows, offsets = layout(lax.broadcasted_iota(jnp.int32, (row_len, LANES), 0))
    seg_tab[...] = seg_rows
    seg_key = layout(lax.broadcasted_iota(jnp.int32, (8, row_len), 1))[0][0:1]
    front = lane_ids % HALF < QUART
    angles = offsets.astype(f32) * freq[0:1]
    cos_tab[...] = jnp.cos(angles)
    sin_tab[...] = jnp.where(front, -1.0, 1.0) * jnp.sin(angles)

    def turn(window):
        return jnp.where(
            front, pltpu.roll(window, LANES - QUART, 1), pltpu.roll(window, QUART, 1)
        )

    from_lanes(in_slots, r_in)
    w_in[dp] = jnp.concatenate(
        [r_in[j, 0:rows, :].astype(f32) for j in range(cols)], axis=0
    ).astype(bf16)
    in_spread = Spread(wire, place, w_in, tail)
    in_spread.start()
    in_spread.start_out()
    in_spread.start_side()
    from_lanes(mlp_slots, r_mlp)
    mlp_own = [r_mlp[j].astype(f32) for j in range(cols)]
    w_gate[dp] = jnp.concatenate([part[0:rows] for part in mlp_own], axis=0).astype(bf16)
    w_up[dp] = jnp.concatenate([part[rows:] for part in mlp_own], axis=0).astype(bf16)
    gate_spread = Spread(wire, place, w_gate, tail)
    up_spread = Spread(wire, place, w_up, tail)
    gate_spread.start()
    gate_spread.start_side()
    up_spread.start()
    for j in (2, 0, 1):
        out_spread.relay(j)
    in_spread.relay(2)
    in_spread.relay(0)
    down_spread.relay(2)
    in_spread.relay(1)
    up_spread.start_side()
    gate_spread.start_out()
    up_spread.start_out()
    down_spread.tail()
    gate_spread.relay(0, inner=True)
    gate_spread.relay(1, inner=True)
    gather_relay(x_slots, xs)
    out_spread.settle()
    shards_here = pl.ds(0, planes * 2)
    out_lanes = gather_start(s_out.at[blk], s_out, shards_here)
    gate_spread.relay(2)
    up_spread.relay(2)
    gather_done(x_slots, xs)
    in_spread.settle()

    group = 2
    chunk = group * tok

    def project(step, carry):
        start = pl.multiple_of(step * chunk, chunk)
        here = pl.ds(start, chunk)
        tokens = xs[pl.ds(step * group, group)].reshape(chunk, width)
        joined = mm(tokens, w_in[...].reshape(width, w_in.shape[2]))
        cosine, sine = cos_tab[here, :], sin_tab[here, :]

        def rotate(number):
            window = joined[:, number * LANES : (number + 1) * LANES]
            return window * cosine + turn(window) * sine

        scale = HALF ** -0.5
        queries = rotate(0).astype(bf16).astype(f32) * scale
        qm[0, here, :] = jnp.where(low_half, queries, 0.0).astype(bf16)
        qm[1, here, :] = jnp.where(low_half, 0.0, queries).astype(bf16)
        kw[0, here, :] = rotate(1).astype(bf16)
        vw[0, here, :] = joined[:, 2 * LANES : 3 * LANES].astype(bf16)
        both = rotate(3)
        qm[2, here, :] = jnp.where(low_half, both.astype(bf16).astype(f32) * scale, 0.0).astype(bf16)
        kw[1, here, :] = jnp.where(low_half, pltpu.roll(both, HALF, 1), 0.0).astype(bf16)
        vw[1, here, :] = joined[:, 4 * LANES : 5 * LANES].astype(bf16)
        return carry

    lax.fori_loop(0, cols // group, project, 0)

    def attend(head):
        window = head // 2

        def step_fn(step, carry):
            here = pl.ds(pl.multiple_of(step * chunk, chunk), chunk)
            scores = mt(qm[head, here, :], kw[window])
            allowed = seg_tab[here, :][:, 0:1] == seg_key
            scores = jnp.where(allowed, scores, NEG)
            top = jnp.max(scores, axis=1, keepdims=True)
            raised = jnp.exp(scores - top)
            total = jnp.sum(raised, axis=1, keepdims=True)
            prob_low = (raised * (1.0 / total)).astype(bf16)
            prob[head, here, :] = prob_low
            mixed = mm(prob_low, vw[window])
            if head == 1:
                mixed = jnp.where(low_half, att[0, here, :], mixed)
            att[window, here, :] = mixed
            return carry

        lax.fori_loop(0, row_len // chunk, step_fn, 0)

    up_spread.relay(0, inner=True)
    attend(0)
    attend(1)
    up_spread.relay(1, inner=True)
    attend(2)
    last_segment = lens.shape[1] - 1
    for j in range(cols):
        here = slice(j * tok, (j + 1) * tok)
        kept = seg_tab[here, :] < last_segment
        s_att[j, :, 0:LANES] = jnp.where(kept, att[0, here, :], 0.0).astype(bf16)
        s_att[j, :, LANES : 2 * LANES] = jnp.where(kept, att[1, here, :], 0.0).astype(bf16)
    att_slots = to_lanes(lambda to: s_att.at[to], r_att)
    r_att[blk] = s_att[blk]

    down_spread.tail_out()
    gather_relay(out_lanes, s_out, shards_here)
    gate_spread.relay(0, inner=False)
    gate_spread.relay(1, inner=False)
    down_spread.relay(0, inner=True)
    down_spread.relay(1, inner=True)
    for j in range(2):
        down_spread.pass_tail(j)
    gather_done(out_lanes, s_out, shards_here)
    shards = planes * 2 * cols
    per_quarter = shards // cols
    head_rows = per_quarter * rows
    for quarter in range(cols):
        slots = [
            s_out[s % cols, s // cols].astype(f32)
            for s in range(quarter * per_quarter, (quarter + 1) * per_quarter)
        ]
        w_out[quarter, 0:head_rows, :] = jnp.concatenate(
            [
                jnp.concatenate([slot[n * rows : (n + 1) * rows] for slot in slots], axis=0)
                for n in range(2)
            ],
            axis=1,
        ).astype(bf16)
        w_out[quarter, head_rows:, :] = jnp.zeros(
            (w_out.shape[1] - head_rows, width), bf16
        )
    last_window = w_in[:, :, 4 * LANES : 5 * LANES].reshape(width, LANES)
    params[...] = mt(to_lane, last_window)
    gain_one, bias_one = params[0:1, :], params[1:2, :]
    gain_two, bias_two = params[2:3, :], params[3:4, :]

    def normalize(residual):
        centered = residual - jnp.mean(residual, axis=1, keepdims=True)
        variance = jnp.mean(centered * centered, axis=1, keepdims=True)
        spread = lax.rsqrt(variance + EPS)
        return centered * spread, spread

    def normalize_back(grad, normal, spread, gain):
        inner = grad * gain
        mean_inner = jnp.mean(inner, axis=1, keepdims=True)
        mean_both = jnp.mean(inner * normal, axis=1, keepdims=True)
        return (inner - mean_inner - normal * mean_both) * spread

    def column_sum(value):
        return jnp.sum(value, axis=0, keepdims=True)

    from_lanes(att_slots, r_att)
    branch = mm(r_att[0], w_out[0])
    for quarter in range(1, cols):
        branch = branch + mm(r_att[quarter], w_out[quarter])
    normal, spread_one = normalize(xin[...].astype(f32) + branch)
    norm_one[...] = normal
    hidden = normal * gain_one + bias_one
    hid[...] = hidden
    hs[blk] = hidden.astype(bf16)
    hid_slots = gather_start(hs.at[blk], hs)
    up_spread.relay(0, inner=False)
    up_spread.relay(1, inner=False)
    down_spread.relay(0, inner=False)
    down_spread.relay(1, inner=False)
    gather_relay(hid_slots, hs)
    gate_spread.settle()
    gather_done(hid_slots, hs)

    wide = 256
    strips = units // wide

    def each_strip(body):
        def step_fn(step, carry):
            body(pl.ds(pl.multiple_of(step * wide, wide), wide))
            return carry

        lax.fori_loop(0, strips, step_fn, 0)

    def expand_gate(here):
        tokens = hs[...].reshape(row_len, width)
        gate_pre[:, here] = mm(tokens, w_gate[:, :, here].reshape(width, wide))

    def expand_up(here):
        tokens = hs[...].reshape(row_len, width)
        up = mm(tokens, w_up[:, :, here].reshape(width, wide))
        gate = gate_pre[:, here]
        up_pre[:, here] = up
        act[:, here] = (gate / (1.0 + jnp.exp(-gate)) * up).astype(bf16)

    each_strip(expand_gate)
    up_spread.settle()
    each_strip(expand_up)
    down_spread.settle()
    down_spread.settle_tail()

    def contract(step, carry):
        here = pl.ds(pl.multiple_of(step * wide, wide), wide)
        mixed = mm(act[...], w_down[:, :, here].reshape(units, wide))
        s_mix[:, :, here] = mixed.reshape(cols, tok, wide).astype(bf16)
        return carry

    lax.fori_loop(0, width // wide, contract, 0)
    pieces = 4
    halves = [pl.ds(n * tok // pieces, tok // pieces) for n in range(pieces)]
    mix_slots = [sum_start(s_mix, r_mix, cut) for cut in halves]
    for slots, cut in zip(mix_slots, halves):
        sum_relay(slots, s_mix, r_mix, t_mix, cut)
    second_gain, second_bias, dm_slots = 0.0, 0.0, []
    for slots, cut in zip(mix_slots, halves):
        mlp_out = sum_done(slots, s_mix, r_mix, cut)
        normal, spread_two = normalize(hid[cut, :] + mlp_out)
        outputs[cut, :] = (normal * gain_two + bias_two).astype(bf16)
        grad = cot[cut, :].astype(f32)
        second_gain = second_gain + column_sum(grad * normal)
        second_bias = second_bias + column_sum(grad)
        d_two = normalize_back(grad, normal, spread_two, gain_two)
        dres_two[cut, :] = d_two
        dms[blk, cut] = d_two.astype(bf16)
        dm_slots.append(gather_start(dms.at[blk], dms, cut))
    for slots, cut in zip(dm_slots, halves):
        gather_relay(slots, dms, cut)
    for slots, cut in zip(dm_slots, halves):
        gather_done(slots, dms, cut)

    down_sum = Collect(wire, place, sum_down)
    gate_sum = Collect(wire, place, sum_gate)
    up_sum = Collect(wire, place, sum_up)
    in_sum = Collect(wire, place, sum_in)
    out_sum = Collect(wire, place, sum_out)
    half = 4

    def fill_parts(part, left_of, right, more=lambda product, here: product):
        height = part.shape[2]

        def step_fn(step, carry):
            here = pl.ds(pl.multiple_of(step * half * height, LANES), half * height)
            product = more(tm(left_of(here), right()), here)
            for j in range(half):
                part[j % 2, step * (half // 2) + j // 2] = product[
                    j * height : (j + 1) * height
                ].astype(bf16)
            return carry

        lax.fori_loop(0, planes * 2 // half, step_fn, 0)

    fill_parts(down_sum.part, lambda here: act[:, here], lambda: dms[...].reshape(row_len, width))
    down_sum.send()

    block = w_down.shape[1]

    def active_grads(step, carry):
        here = pl.ds(pl.multiple_of(step * half * block, LANES), half * block)
        d_active = mt(
            dms[...].reshape(row_len, width),
            w_down[pl.ds(step * half, half)].reshape(half * block, width),
        )
        gate, up = gate_pre[:, here], up_pre[:, here]
        sg = 1.0 / (1.0 + jnp.exp(-gate))
        dgate[:, here] = (d_active * up * sg * (1.0 + gate * (1.0 - sg))).astype(bf16)
        dup[:, here] = (d_active * gate * sg).astype(bf16)
        return carry

    lax.fori_loop(0, planes * 2 // half, active_grads, 0)
    block = w_gate.shape[1]

    def hidden_rows(here):
        return hs[:, :, here].reshape(row_len, half * block)

    fill_parts(gate_sum.part, hidden_rows, lambda: dgate[...])
    gate_sum.send()
    def hidden_grads(step, carry):
        here = pl.ds(pl.multiple_of(step * half * block, LANES), half * block)
        those = pl.ds(step * half, half)
        mixed = mt(dgate[...], w_gate[those].reshape(half * block, units)) + mt(
            dup[...], w_up[those].reshape(half * block, units)
        )
        s_dh[:, :, here] = mixed.reshape(cols, tok, half * block).astype(bf16)
        return carry

    lax.fori_loop(0, planes * 2 // half, hidden_grads, 0)
    dh_slots = sum_start(s_dh, r_dh)

    sum_relay(dh_slots, s_dh, r_dh, t_dh)
    fill_parts(up_sum.part, hidden_rows, lambda: dup[...])
    up_sum.send()
    down_sum.first(1)
    down_sum.first(0)
    d_hidden = dres_two[...] + sum_done(dh_slots, s_dh, r_dh)
    down_sum.first(2)
    normal = norm_one[...]
    first_gain = column_sum(d_hidden * normal)
    first_bias = column_sum(d_hidden)
    d_one = normalize_back(d_hidden, normal, spread_one, gain_one)
    dres_one[...] = d_one
    d_branch = d_one.astype(bf16)
    mine = pl.ds(pl.multiple_of(blk * tok, tok), tok)
    kept = seg_tab[mine, :][:, 0:1] < last_segment
    for quarter in range(cols):
        pulled = mt(d_branch, w_out[quarter]).astype(bf16).astype(f32)
        s_da[quarter] = jnp.where(kept, pulled, 0.0).astype(bf16)
    da_slots = to_lanes(lambda to: s_da.at[to], r_da)
    r_da[blk] = s_da[blk]

    params[...] = jnp.concatenate(
        [first_gain, first_bias, second_gain, second_bias, jnp.zeros((4, width), f32)], axis=0
    )
    for quarter in range(cols):
        product = tm(r_att[quarter], d_branch)
        for t in range(per_quarter):
            s = quarter * per_quarter + t
            owner_dp = s // cols
            mine_rows = product[t * rows : (t + 1) * rows]
            halved = [mine_rows[:, n * width // 2 : (n + 1) * width // 2] for n in range(2)]
            b_out[s % cols, owner_dp % 2, owner_dp // 2] = jnp.concatenate(
                halved, axis=0
            ).astype(bf16)
    both_sides = pl.ds(0, 2)
    out_blk = sum_start(b_out, rb_out, both_sides)

    gate_sum.first(1)
    sum_relay(out_blk, b_out, rb_out, tb_out, both_sides)
    down_sum.second_tail(1)
    down_sum.second(1)
    gate_sum.first(0)
    from_lanes(da_slots, r_da)
    def attend_back(head):
        window = head // 2
        fresh = head != 1

        def step_fn(step, carry):
            here = pl.ds(pl.multiple_of(step * chunk, chunk), chunk)
            d_out = r_da[pl.ds(step * group, group), :, window * LANES : (window + 1) * LANES]
            d_out = d_out.reshape(chunk, LANES).astype(f32)
            if head == 0:
                d_out = jnp.where(low_half, d_out, 0.0)
            if head == 1:
                d_out = jnp.where(low_half, 0.0, d_out)
            d_low = d_out.astype(bf16)
            delta = jnp.sum(d_out * att[window, here, :], axis=1, keepdims=True)
            prob_low = prob[head, here, :]
            d_prob = mt(d_low, vw[window])
            d_score = (prob_low.astype(f32) * (d_prob - delta)).astype(bf16)
            d_query = mm(d_score, kw[window]) * (HALF ** -0.5)
            if head == 1:
                d_query = jnp.where(low_half, acc_q[0, here, :], d_query)
            acc_q[window, here, :] = d_query
            d_key = tm(d_score, qm[head, here, :])
            d_value = tm(prob_low, d_low)
            if fresh:

                @pl.when(step == 0)
                def _():
                    acc_k[window] = d_key
                    acc_v[window] = d_value

                @pl.when(step != 0)
                def _():
                    acc_k[window] = acc_k[window] + d_key
                    acc_v[window] = acc_v[window] + d_value
            else:
                acc_k[window] = acc_k[window] + d_key
                acc_v[window] = acc_v[window] + d_value
            return carry

        lax.fori_loop(0, row_len // chunk, step_fn, 0)

    attend_back(0)
    gate_sum.first(2)
    down_sum.second_tail(0)
    down_sum.second(0)
    attend_back(1)
    attend_back(2)

    cosine, sine = cos_tab[...], sin_tab[...]

    def rotate_back(vector):
        vector = vector.astype(bf16).astype(f32)
        return (vector * cosine - turn(vector) * sine).astype(bf16)

    dj[:, 0:LANES] = rotate_back(acc_q[0])
    dj[:, LANES : 2 * LANES] = rotate_back(acc_k[0])
    dj[:, 2 * LANES : 3 * LANES] = acc_v[0].astype(bf16)
    dj[:, 3 * LANES : 4 * LANES] = rotate_back(acc_q[1] + pltpu.roll(acc_k[1], HALF, 1))
    dj[:, 4 * LANES : 5 * LANES] = acc_v[1].astype(bf16)

    up_sum.first(1)

    def with_vectors(product, here):
        columns = tm(params[:, here].astype(bf16), to_lane)
        last = product[:, 4 * LANES :] + columns
        return jnp.concatenate([product[:, : 4 * LANES], last], axis=1)

    fill_parts(
        in_sum.part,
        lambda here: xs[:, :, here].reshape(row_len, half * block),
        lambda: dj[...],
        with_vectors,
    )

    def input_grads(step, carry):
        here = pl.ds(pl.multiple_of(step * half * block, LANES), half * block)
        mixed = mt(dj[...], w_in[pl.ds(step * half, half)].reshape(half * block, w_in.shape[2]))
        s_ig[:, :, here] = mixed.reshape(cols, tok, half * block).astype(bf16)
        return carry

    lax.fori_loop(0, planes * 2 // half, input_grads, 0)
    ig_slots = sum_start(s_ig, r_ig)

    gate_sum.second(1)
    sum_relay(ig_slots, s_ig, r_ig, t_ig)
    up_sum.first(0)
    gate_sum.second(0)
    out_sum.part[...] = sum_done(out_blk, b_out, rb_out, both_sides).astype(bf16)
    in_sum.send((1, 0, 2))
    out_sum.send((1, 0, 2))
    in_sum.send_side(3)
    out_sum.send_side(3)
    down_sum.tail()
    up_sum.second(1)
    up_sum.first(2)
    f_gate[...] = gate_sum.total()
    up_sum.second(0)
    grad_in = dres_one[...] + sum_done(ig_slots, s_ig, r_ig)
    input_grad[...] = grad_in.astype(bf16)
    in_sum.first(1)
    in_sum.first(0)
    up_total = up_sum.total()
    gate_total = f_gate[...]
    for j in range(cols):
        here = slice(j * rows, (j + 1) * rows)
        s_gmlp[j] = jnp.concatenate([gate_total[here], up_total[here]], axis=0).astype(bf16)
    gmlp_slots = to_lanes(lambda to: s_gmlp.at[to], r_gmlp)
    r_gmlp[blk] = s_gmlp[blk]
    in_sum.second(1)
    in_sum.first(2)
    in_sum.second(0)
    for j in (1, 0, 2):
        out_sum.first(j)
    out_sum.second(1)
    out_sum.second(0)
    from_lanes(gmlp_slots, r_gmlp)
    g_mlp[...] = r_gmlp[...]
    in_total = in_sum.total()
    for j in range(cols):
        s_gin[j] = jnp.concatenate(
            [in_total[j * rows : (j + 1) * rows], jnp.zeros((8, in_total.shape[1]), f32)], axis=0
        ).astype(bf16)
    gin_slots = to_lanes(lambda to: s_gin.at[to], r_gin)
    r_gin[blk] = s_gin[blk]
    g_out[...] = out_sum.total()
    g_down[...] = down_sum.total()
    from_lanes(gin_slots, r_gin)
    g_in[...] = r_gin[...]
    wire.finish()


def unpack(
    rows,
    block,
    outputs,
    input_grad,
    g_in,
    g_mlp,
    g_out,
    g_down,
    outputs_to,
    input_grad_to,
    in_to,
    out_to,
    gate_to,
    up_to,
    down_to,
    *vectors_to,
):
    f32 = jnp.float32
    cols = g_in.shape[0]
    width = outputs.shape[1]
    outputs_to[0] = outputs[...]
    input_grad_to[0] = input_grad[...]
    down_to[...] = g_down[...]
    for n in range(2):
        out_to[:, n * width // 2 : (n + 1) * width // 2] = g_out[n * rows : (n + 1) * rows, :]
    low_half = lax.broadcasted_iota(jnp.int32, (1, LANES), 1) < HALF
    joined = [g_in[j].astype(f32)[0:rows] for j in range(cols)]
    vectors = joined[0][:, 4 * LANES :]
    for j in range(1, cols):
        vectors = vectors + joined[j][:, 4 * LANES :]
    vectors = jnp.concatenate([vectors, jnp.zeros((LANES - rows, LANES), f32)], axis=0).T
    for number, vector_to in enumerate(vectors_to):
        vector_to[...] = vectors[HALF + number, 0:rows]
    single_at = ((3, 0), (3, 1), (4, 0))

    def half(kind, number, want):
        owner, part = number // 3, number % 3
        window, at = (kind, part) if part < 2 else single_at[kind]
        value = joined[owner][:, window * LANES : (window + 1) * LANES]
        return value if at == want else pltpu.roll(value, HALF, 1)

    for kind in range(3):
        for n in range(width // LANES):
            at = kind * width + n * LANES
            in_to[:, at : at + LANES] = jnp.where(
                low_half, half(kind, 2 * n, 0), half(kind, 2 * n + 1, 1)
            )
    lanes = lax.broadcasted_iota(jnp.int32, (1, LANES), 1)
    mlp = [g_mlp[j].astype(f32) for j in range(cols)]
    for first_row, target in ((0, gate_to), (rows, up_to)):
        parts = [part[first_row : first_row + rows] for part in mlp]
        for n in range(target.shape[1] // LANES):
            first = n * LANES
            result = None
            for number in range(first // block, (first + LANES - 1) // block + 1):
                ring_at, owner = number // cols, number % cols
                piece = window_at(parts[owner], ring_at * block + first - number * block)
                begin = number * block - first
                result = piece if result is None else jnp.where(lanes < begin, result, piece)
            target[:, first : first + LANES] = result


def fast_shards(
    depth,
    inputs,
    doc_lengths,
    project_in,
    project_out,
    gate_weight,
    up_weight,
    down_weight,
    first_gain,
    first_bias,
    second_gain,
    second_bias,
    cotangent,
):
    cols = 4
    tok, width = inputs.shape[1:]
    rows = project_in.shape[0]
    ff = gate_weight.shape[1]
    ring = depth * 2
    row_len = tok * cols
    units = ff // cols
    block = units // ring
    head_width = width // cols
    in_width = 5 * LANES
    bf16, f32 = jnp.bfloat16, jnp.float32

    lane_ids = np.arange(LANES) % QUART
    freq = jnp.asarray(
        np.broadcast_to(BASE ** (-2.0 * lane_ids / HALF), (8, LANES)).astype(np.float32)
    )

    def scratch(*shape, kind=bf16):
        return pltpu.VMEM(shape, kind)

    def sums(height, across, tail=0):
        main = height - tail
        buffers = [
            scratch(2, depth, height, across),
            scratch(depth, main, across),
            scratch(depth, main, across),
            scratch(4, main, across),
        ]
        if tail:
            buffers = buffers + [
                scratch(4, 2, tail, across),
                scratch(2, 2, tail, across),
                scratch(2, tail, across),
                scratch(tail, across, kind=f32),
            ]
        return tuple(buffers)

    stacked = scratch(cols, tok, width)
    heads = 3
    buffers = [
        stacked,
        scratch(cols, 32, in_width),
        scratch(cols, 2 * rows, units),
        scratch(8, LANES, kind=f32),
        scratch(cols, 32, in_width),
        scratch(cols, 2 * rows, units),
        scratch(cols, ring, 2 * rows, width // 2),
        scratch(ring, cols * rows, in_width),
        scratch(ring, cols * rows, units),
        scratch(ring, cols * rows, units),
        scratch(ring, block, width),
        scratch(cols, 2 * LANES, width),
        scratch(8, width, kind=f32),
        scratch(row_len, LANES, kind=f32),
        scratch(row_len, LANES, kind=f32),
        scratch(row_len, LANES, kind=jnp.int32),
        scratch(heads, row_len, LANES),
        scratch(2, row_len, LANES),
        scratch(2, row_len, LANES),
        scratch(heads, row_len, row_len),
        scratch(2, row_len, LANES, kind=f32),
        scratch(cols, tok, 2 * LANES),
        scratch(cols, tok, 2 * LANES),
        scratch(tok, width, kind=f32),
        scratch(tok, width, kind=f32),
        stacked,
        scratch(row_len, units, kind=f32),
        scratch(row_len, units, kind=f32),
        scratch(row_len, units),
        stacked,
        scratch(3, tok, width),
        scratch(tok, width),
        scratch(tok, width, kind=f32),
        stacked,
        scratch(row_len, units),
        scratch(row_len, units),
        stacked,
        scratch(3, tok, width),
        scratch(tok, width),
        scratch(tok, width, kind=f32),
        scratch(cols, tok, 2 * LANES),
        scratch(cols, tok, 2 * LANES),
        scratch(2, row_len, LANES, kind=f32),
        scratch(2, row_len, LANES, kind=f32),
        scratch(2, row_len, LANES, kind=f32),
        scratch(row_len, in_width),
        stacked,
        scratch(3, tok, width),
        scratch(tok, width),
        sums(cols * rows, in_width),
        sums(cols * rows, units),
        sums(cols * rows, units),
        sums(block, width, DTB),
        scratch(cols, 2, depth, 2 * rows, width // 2),
        scratch(3, 2, depth, 2 * rows, width // 2),
        scratch(2, depth, 2 * rows, width // 2),
        sums(2 * rows, width // 2, 0),
        scratch(cols * rows, units, kind=f32),
        scratch(cols, 2 * rows, units),
        scratch(cols, 2 * rows, units),
        scratch(cols, 32, in_width),
        scratch(cols, 32, in_width),
        pltpu.SemaphoreType.DMA((240,)),
        pltpu.SemaphoreType.DMA((240,)),
    ]
    vmem = pl.BlockSpec(memory_space=pltpu.VMEM)
    tokens = row_len * width
    outputs, input_grad, g_in, g_mlp, g_out, g_down = pl.pallas_call(
        functools.partial(fused, depth),
        out_shape=(
            jax.ShapeDtypeStruct((tok, width), bf16),
            jax.ShapeDtypeStruct((tok, width), bf16),
            jax.ShapeDtypeStruct((cols, 32, in_width), bf16),
            jax.ShapeDtypeStruct((cols, 2 * rows, units), bf16),
            jax.ShapeDtypeStruct((2 * rows, width // 2), f32),
            jax.ShapeDtypeStruct((block, width), f32),
        ),
        in_specs=[pl.BlockSpec(memory_space=pltpu.SMEM)] + [vmem] * 12,
        out_specs=(vmem,) * 6,
        scratch_shapes=buffers,
        compiler_params=pltpu.CompilerParams(
            collective_id=0, has_side_effects=True, vmem_limit_bytes=60 * 2**20
        ),
        cost_estimate=pl.CostEstimate(
            flops=6 * tokens * (3 * units + 4 * head_width),
            bytes_accessed=8 * 2**20,
            transcendentals=3 * row_len * row_len,
        ),
        name="layer",
    )(
        doc_lengths,
        freq,
        inputs[0],
        cotangent[0],
        project_in,
        gate_weight,
        up_weight,
        project_out,
        down_weight,
        first_gain[None],
        first_bias[None],
        second_gain[None],
        second_bias[None],
    )

    vector = jax.ShapeDtypeStruct((rows,), f32)
    return pl.pallas_call(
        functools.partial(unpack, rows, block),
        out_shape=(
            jax.ShapeDtypeStruct((1, tok, width), bf16),
            jax.ShapeDtypeStruct((1, tok, width), bf16),
            jax.ShapeDtypeStruct((rows, 3 * width), f32),
            jax.ShapeDtypeStruct((rows, width), f32),
            jax.ShapeDtypeStruct((rows, ff), f32),
            jax.ShapeDtypeStruct((rows, ff), f32),
            jax.ShapeDtypeStruct((block, width), f32),
            vector,
            vector,
            vector,
            vector,
        ),
        in_specs=[vmem] * 6,
        out_specs=(vmem,) * 11,
        name="unpack",
    )(outputs, input_grad, g_in, g_mlp, g_out, g_down)


def pick(sizes):
    def chosen(*args):
        tok, width = args[0].shape[1:]
        ring, cols = sizes["dp"], sizes["blk"]
        fits = (
            ring == 8
            and cols == 4
            and tok == LANES
            and HEADS == 3 * cols
            and width == HEADS * HALF
            and args[2].shape[0] == 24
            and args[4].shape[1] == 4 * width
        )
        if fits:
            return fast_shards(ring // 2, *args)
        return shards(*args)

    return chosen


def solution(mesh):
    placed = (
        P("dp", "blk", None),
        P("dp", None),
        P(("dp", "blk"), None),
        P(("dp", "blk"), None),
        P(("dp", "blk"), None),
        P(("dp", "blk"), None),
        P(("dp", "blk"), None),
        P(("dp", "blk")),
        P(("dp", "blk")),
        P(("dp", "blk")),
        P(("dp", "blk")),
        P("dp", "blk", None),
    )
    return jax.shard_map(
        pick(dict(mesh.shape)),
        mesh=mesh,
        in_specs=placed,
        out_specs=(
            P("dp", "blk", None),
            P("dp", "blk", None),
            P(("dp", "blk"), None),
            P(("dp", "blk"), None),
            P(("dp", "blk"), None),
            P(("dp", "blk"), None),
            P(("dp", "blk"), None),
            P(("dp", "blk")),
            P(("dp", "blk")),
            P(("dp", "blk")),
            P(("dp", "blk")),
        ),
        check_vma=False,
    )
```

```python
import functools

import jax
import jax.numpy as jnp
import numpy as np
from jax import lax
from jax.experimental import pallas as pl
from jax.experimental.pallas import tpu as pltpu
from jax.sharding import PartitionSpec as P

HEADS = 12


NEG = -1e30
EPS = 1e-05
BASE = 1000.0


def doc_layout(lengths_row, positions):
    bounds = jnp.cumsum(lengths_row)
    passed = positions[:, None] >= bounds[None, :]
    segment = jnp.sum(passed.astype(jnp.int32), axis=1)
    begins = jnp.sum(jnp.where(passed, lengths_row[None, :], 0), axis=1)
    return (segment, positions - begins)


def rotary(vectors, offsets):
    half_size = vectors.shape[-1] // 2
    frequency = BASE ** (-2.0 * jnp.arange(half_size, dtype=jnp.float32) / vectors.shape[-1])
    angles = offsets.astype(jnp.float32)[:, None] * frequency[None, :]
    cosine = jnp.concatenate([jnp.cos(angles), jnp.cos(angles)], axis=1)[:, None, :]
    sine_rows = jnp.concatenate([jnp.sin(angles), jnp.sin(angles)], axis=1)[:, None, :]
    first_half = vectors[..., :half_size]
    second_half = vectors[..., half_size:]
    turned = jnp.concatenate([-second_half, first_half], axis=-1)
    return vectors * cosine + turned * sine_rows


def layer_norm(residual, gain_row, bias_row):
    row_mean = jnp.mean(residual, axis=-1, keepdims=True)
    centered = residual - row_mean
    variance = jnp.mean(centered * centered, axis=-1, keepdims=True)
    return centered * lax.rsqrt(variance + EPS) * gain_row + bias_row


def contract_rows(left, right):
    return lax.dot_general(
        left, right, (((0,), (0,)), ((), ())), preferred_element_type=jnp.float32
    )


def contract_cols(left, right):
    return lax.dot_general(
        left, right, (((1,), (1,)), ((), ())), preferred_element_type=jnp.float32
    )


def tile_scores(query_tile, key_tile, seg_query, seg_key, score_scale):
    scores = (
        jnp.einsum("qhd,khd->hqk", query_tile, key_tile, preferred_element_type=jnp.float32)
        * score_scale
    )
    allowed = (seg_query[:, None] == seg_key[None, :])[None, :, :]
    return (jnp.where(allowed, scores, NEG), allowed)


def run_groups(pieces, group, lengths_row, seg_query, carried, tile_fn, extra_shape):
    group_count = pieces[0].shape[0] // group

    def group_step(carried_in, number):
        offset = number * group
        tile_set = tuple(
            (lax.dynamic_slice_in_dim(piece_rows, offset, group, 0) for piece_rows in pieces)
        )
        positions = offset + jnp.arange(group, dtype=jnp.int32)
        seg_key, unused_offsets = doc_layout(lengths_row, positions)
        touches = (seg_key[0] <= seg_query[-1]) & (seg_query[0] <= seg_key[-1])

        def active(state_in):
            return tile_fn(state_in, tile_set, seg_key)

        def skipped(state_in):
            return (state_in, jnp.zeros(extra_shape, jnp.float32))

        return lax.cond(touches, active, skipped, carried_in)

    return lax.scan(group_step, carried, jnp.arange(group_count, dtype=jnp.int32))


def shards(
    inputs,
    doc_lengths,
    project_in,
    project_out,
    gate_weight,
    up_weight,
    down_weight,
    first_gain,
    first_bias,
    second_gain,
    second_bias,
    cotangent,
):
    group = inputs.shape[1]
    width = inputs.shape[2]
    head_count = HEADS
    head_size = width // head_count
    score_scale = head_size ** (-0.5)
    cycle_rank = lax.axis_index("blk")
    positions = cycle_rank * group + jnp.arange(group, dtype=jnp.int32)
    lengths_row = doc_lengths[0]
    seg_query, offsets = doc_layout(lengths_row, positions)
    keep_mask = seg_query < lengths_row.shape[0] - 1
    keep_float = keep_mask.astype(jnp.float32)
    fetched = (
        lax.all_gather(project_in, ("dp", "blk"), axis=0, tiled=True),
        lax.all_gather(project_out, ("dp", "blk"), axis=0, tiled=True),
        lax.all_gather(gate_weight, ("dp", "blk"), axis=0, tiled=True),
        lax.all_gather(up_weight, ("dp", "blk"), axis=0, tiled=True),
        lax.all_gather(down_weight, ("dp", "blk"), axis=0, tiled=True),
        lax.all_gather(first_gain, ("dp", "blk"), axis=0, tiled=True),
        lax.all_gather(first_bias, ("dp", "blk"), axis=0, tiled=True),
        lax.all_gather(second_gain, ("dp", "blk"), axis=0, tiled=True),
        lax.all_gather(second_bias, ("dp", "blk"), axis=0, tiled=True),
    )
    full_in, full_out, full_gate, full_up, full_down = (
        fetched[0],
        fetched[1],
        fetched[2],
        fetched[3],
        fetched[4],
    )
    gain_one = fetched[5].astype(jnp.float32)
    bias_one = fetched[6].astype(jnp.float32)
    gain_two = fetched[7].astype(jnp.float32)
    bias_two = fetched[8].astype(jnp.float32)
    tokens_low = inputs[0]
    tokens_f = tokens_low.astype(jnp.float32)
    joined = jnp.dot(tokens_low, full_in, preferred_element_type=jnp.float32)
    query_raw = joined[:, :width].reshape(group, head_count, head_size)
    key_raw = joined[:, width : 2 * width].reshape(group, head_count, head_size)
    value_low = joined[:, 2 * width :].astype(jnp.bfloat16)
    query_rot, query_pull = jax.vjp(lambda vectors: rotary(vectors, offsets), query_raw)
    key_rot, key_pull = jax.vjp(lambda vectors: rotary(vectors, offsets), key_raw)
    query_low = query_rot.astype(jnp.bfloat16)
    key_low = key_rot.reshape(group, width).astype(jnp.bfloat16)

    def stats_tile(carried, tile_set, seg_key):
        row_top, row_total = carried
        key_tile = tile_set[0].reshape(group, head_count, head_size)
        scores, allowed = tile_scores(query_low, key_tile, seg_query, seg_key, score_scale)
        new_top = jnp.maximum(row_top, jnp.max(scores, axis=2))
        shrink = jnp.exp(row_top - new_top)
        added = jnp.sum(jnp.where(allowed, jnp.exp(scores - new_top[:, :, None]), 0.0), axis=2)
        return ((new_top, row_total * shrink + added), jnp.zeros((1,), jnp.float32))

    init_stats = (
        jnp.full((head_count, group), NEG, jnp.float32),
        jnp.zeros((head_count, group), jnp.float32),
    )
    carried = init_stats
    carried, unused = run_groups(
        (lax.all_gather(key_low, "blk", axis=0, tiled=True),),
        group,
        lengths_row,
        seg_query,
        carried,
        stats_tile,
        (1,),
    )
    row_top, row_total = carried
    log_total = row_top + jnp.log(row_total)

    def output_tile(accum, tile_set, seg_key):
        key_tile = tile_set[0].reshape(group, head_count, head_size)
        value_tile = tile_set[1].reshape(group, head_count, head_size)
        scores, allowed = tile_scores(query_low, key_tile, seg_query, seg_key, score_scale)
        prob_low = jnp.where(allowed, jnp.exp(scores - log_total[:, :, None]), 0.0).astype(
            jnp.bfloat16
        )
        accum = accum + jnp.einsum(
            "hqk,khd->qhd", prob_low, value_tile, preferred_element_type=jnp.float32
        )
        return (accum, jnp.zeros((1,), jnp.float32))

    zero_accum = jnp.zeros((group, head_count, head_size), jnp.float32)
    accum = zero_accum
    accum, unused = run_groups(
        (
            lax.all_gather(key_low, "blk", axis=0, tiled=True),
            lax.all_gather(value_low, "blk", axis=0, tiled=True),
        ),
        group,
        lengths_row,
        seg_query,
        accum,
        output_tile,
        (1,),
    )
    attend_low = (accum * keep_float[:, None, None]).reshape(group, width).astype(jnp.bfloat16)
    branch = jnp.dot(attend_low, full_out, preferred_element_type=jnp.float32)
    residual_one = tokens_f + branch
    hidden, norm_one_pull = jax.vjp(layer_norm, residual_one, gain_one, bias_one)
    hidden_low = hidden.astype(jnp.bfloat16)
    gate_pre = jnp.dot(hidden_low, full_gate, preferred_element_type=jnp.float32)
    up_pre = jnp.dot(hidden_low, full_up, preferred_element_type=jnp.float32)
    activated, swiglu_pull = jax.vjp(
        lambda gate_in, up_in: jax.nn.silu(gate_in) * up_in, gate_pre, up_pre
    )
    active_low = activated.astype(jnp.bfloat16)
    mlp_out = jnp.dot(active_low, full_down, preferred_element_type=jnp.float32)
    outputs_f, norm_two_pull = jax.vjp(layer_norm, hidden + mlp_out, gain_two, bias_two)
    refetched = (
        lax.all_gather(project_in, ("dp", "blk"), axis=0, tiled=True),
        lax.all_gather(project_out, ("dp", "blk"), axis=0, tiled=True),
        lax.all_gather(gate_weight, ("dp", "blk"), axis=0, tiled=True),
        lax.all_gather(up_weight, ("dp", "blk"), axis=0, tiled=True),
        lax.all_gather(down_weight, ("dp", "blk"), axis=0, tiled=True),
    )
    full_in, full_out, full_gate, full_up, full_down = (
        refetched[0],
        refetched[1],
        refetched[2],
        refetched[3],
        refetched[4],
    )
    d_res_two, second_gain_part, second_bias_part = norm_two_pull(cotangent[0].astype(jnp.float32))
    d_mlp_low = d_res_two.astype(jnp.bfloat16)
    down_part = contract_rows(active_low, d_mlp_low)
    d_active = contract_cols(d_mlp_low, full_down)
    d_gate, d_up = swiglu_pull(d_active)
    d_gate_low = d_gate.astype(jnp.bfloat16)
    d_up_low = d_up.astype(jnp.bfloat16)
    gate_part = contract_rows(hidden_low, d_gate_low)
    up_part = contract_rows(hidden_low, d_up_low)
    d_hidden = d_res_two + contract_cols(d_gate_low, full_gate) + contract_cols(d_up_low, full_up)
    d_res_one, first_gain_part, first_bias_part = norm_one_pull(d_hidden)
    d_branch_low = d_res_one.astype(jnp.bfloat16)
    out_part = contract_rows(attend_low, d_branch_low)
    d_attend = contract_cols(d_branch_low, full_out).astype(jnp.bfloat16)
    d_attend_low = (d_attend * keep_mask[:, None].astype(jnp.bfloat16)).reshape(
        group, head_count, head_size
    )
    delta = jnp.einsum("qhd,qhd->hq", d_attend_low.astype(jnp.float32), accum)

    def back_tile(grad_query, tile_set, seg_key):
        key_tile = tile_set[0].reshape(group, head_count, head_size)
        value_tile = tile_set[1].reshape(group, head_count, head_size)
        scores, allowed = tile_scores(query_low, key_tile, seg_query, seg_key, score_scale)
        prob_rows = jnp.where(allowed, jnp.exp(scores - log_total[:, :, None]), 0.0)
        d_probs = jnp.einsum(
            "qhd,khd->hqk", d_attend_low, value_tile, preferred_element_type=jnp.float32
        )
        d_score_low = (prob_rows * (d_probs - delta[:, :, None])).astype(jnp.bfloat16)
        grad_query = (
            grad_query
            + jnp.einsum("hqk,khd->qhd", d_score_low, key_tile, preferred_element_type=jnp.float32)
            * score_scale
        )
        grad_key = (
            jnp.einsum("hqk,qhd->khd", d_score_low, query_low, preferred_element_type=jnp.float32)
            * score_scale
        )
        grad_value = jnp.einsum(
            "hqk,qhd->khd",
            prob_rows.astype(jnp.bfloat16),
            d_attend_low,
            preferred_element_type=jnp.float32,
        )
        return (
            grad_query,
            jnp.concatenate(
                [grad_key.reshape(group, width), grad_value.reshape(group, width)], axis=1
            ),
        )

    grad_query = zero_accum
    grad_query, blocks = run_groups(
        (
            lax.all_gather(key_low, "blk", axis=0, tiled=True),
            lax.all_gather(value_low, "blk", axis=0, tiled=True),
        ),
        group,
        lengths_row,
        seg_query,
        grad_query,
        back_tile,
        (group, 2 * width),
    )
    blocks = blocks.reshape(-1, 2 * width)
    back_result = (grad_query, blocks)
    grad_query = back_result[0]
    owned_pairs = lax.psum_scatter(
        back_result[1].astype(jnp.bfloat16), "blk", scatter_dimension=0, tiled=True
    ).astype(jnp.float32)
    key_sum = owned_pairs[:, :width]
    value_sum = owned_pairs[:, width:]
    d_query_pre = query_pull(grad_query.astype(jnp.bfloat16).astype(jnp.float32))[0]
    d_key_low = key_sum.astype(jnp.bfloat16).astype(jnp.float32)
    d_key_pre = key_pull(d_key_low.reshape(group, head_count, head_size))[0]
    d_value_low = value_sum.astype(jnp.bfloat16).astype(jnp.float32)
    d_joined_low = jnp.concatenate(
        [d_query_pre.reshape(group, width), d_key_pre.reshape(group, width), d_value_low], axis=1
    ).astype(jnp.bfloat16)
    in_part = contract_rows(tokens_low, d_joined_low)
    input_grad = (d_res_one + contract_cols(d_joined_low, full_in)).astype(jnp.bfloat16)
    by_rows = (
        lax.psum_scatter(
            in_part.astype(jnp.bfloat16), "dp", scatter_dimension=0, tiled=True
        ).astype(jnp.float32),
        lax.psum_scatter(
            out_part.astype(jnp.bfloat16), "dp", scatter_dimension=0, tiled=True
        ).astype(jnp.float32),
        lax.psum_scatter(
            gate_part.astype(jnp.bfloat16), "dp", scatter_dimension=0, tiled=True
        ).astype(jnp.float32),
        lax.psum_scatter(
            up_part.astype(jnp.bfloat16), "dp", scatter_dimension=0, tiled=True
        ).astype(jnp.float32),
        lax.psum_scatter(
            down_part.astype(jnp.bfloat16), "dp", scatter_dimension=0, tiled=True
        ).astype(jnp.float32),
        lax.psum_scatter(
            first_gain_part.astype(jnp.bfloat16), "dp", scatter_dimension=0, tiled=True
        ).astype(jnp.float32),
        lax.psum_scatter(
            first_bias_part.astype(jnp.bfloat16), "dp", scatter_dimension=0, tiled=True
        ).astype(jnp.float32),
        lax.psum_scatter(
            second_gain_part.astype(jnp.bfloat16), "dp", scatter_dimension=0, tiled=True
        ).astype(jnp.float32),
        lax.psum_scatter(
            second_bias_part.astype(jnp.bfloat16), "dp", scatter_dimension=0, tiled=True
        ).astype(jnp.float32),
    )
    summed = (
        lax.psum_scatter(
            by_rows[0].astype(jnp.bfloat16), "blk", scatter_dimension=0, tiled=True
        ).astype(jnp.float32),
        lax.psum_scatter(
            by_rows[1].astype(jnp.bfloat16), "blk", scatter_dimension=0, tiled=True
        ).astype(jnp.float32),
        lax.psum_scatter(
            by_rows[2].astype(jnp.bfloat16), "blk", scatter_dimension=0, tiled=True
        ).astype(jnp.float32),
        lax.psum_scatter(
            by_rows[3].astype(jnp.bfloat16), "blk", scatter_dimension=0, tiled=True
        ).astype(jnp.float32),
        lax.psum_scatter(
            by_rows[4].astype(jnp.bfloat16), "blk", scatter_dimension=0, tiled=True
        ).astype(jnp.float32),
        lax.psum_scatter(
            by_rows[5].astype(jnp.bfloat16), "blk", scatter_dimension=0, tiled=True
        ).astype(jnp.float32),
        lax.psum_scatter(
            by_rows[6].astype(jnp.bfloat16), "blk", scatter_dimension=0, tiled=True
        ).astype(jnp.float32),
        lax.psum_scatter(
            by_rows[7].astype(jnp.bfloat16), "blk", scatter_dimension=0, tiled=True
        ).astype(jnp.float32),
        lax.psum_scatter(
            by_rows[8].astype(jnp.bfloat16), "blk", scatter_dimension=0, tiled=True
        ).astype(jnp.float32),
    )
    return (
        outputs_f.astype(jnp.bfloat16)[None],
        input_grad[None],
        summed[0],
        summed[1],
        summed[2],
        summed[3],
        summed[4],
        summed[5],
        summed[6],
        summed[7],
        summed[8],
    )


MESH_IDS = pl.DeviceIdType.MESH
LANES = 128
HALF = 64
QUART = 32
DTF = 64
DTB = 64


def mm(left, right):
    return lax.dot_general(
        left, right, (((1,), (0,)), ((), ())), preferred_element_type=jnp.float32
    )


def mt(left, right):
    return lax.dot_general(
        left, right, (((1,), (1,)), ((), ())), preferred_element_type=jnp.float32
    )


def tm(left, right):
    return lax.dot_general(
        left, right, (((0,), (0,)), ((), ())), preferred_element_type=jnp.float32
    )


def window_at(value, start):
    aligned = min(max(start // LANES * LANES, 0), value.shape[1] - LANES)
    if aligned == start:
        return value[:, aligned : aligned + LANES]
    aligned = min(aligned, value.shape[1] - 2 * LANES)
    two = value[:, aligned : aligned + 2 * LANES]
    return pltpu.roll(two, (aligned - start) % (2 * LANES), 1)[:, :LANES]


def gather_lanes(value, block, first, source):
    lanes = lax.broadcasted_iota(jnp.int32, (1, LANES), 1)
    result = None
    for number in range(first // block, (first + LANES - 1) // block + 1):
        piece = window_at(value, source(number, first))
        begin = number * block - first
        result = piece if result is None else jnp.where(lanes < begin, result, piece)
    return result


class Wire:
    def __init__(self, send_sem, recv_sem, is_inner):
        self.send_sem, self.recv_sem, self.is_inner = send_sem, recv_sem, is_inner
        self.sends, self.slots = 0, 0
        self.sent = {None: [], True: [], False: []}

    def slot(self):
        self.slots += 1
        return self.slots - 1

    def copy(self, src, dst, peer, slot):
        self.sends += 1
        return pltpu.make_async_remote_copy(
            src_ref=src,
            dst_ref=dst,
            send_sem=self.send_sem.at[self.sends - 1],
            recv_sem=self.recv_sem.at[slot],
            device_id=peer,
            device_id_type=MESH_IDS,
        )

    def push(self, src, dst, peer, slot=None, inner=None):
        slot = self.slot() if slot is None else slot
        copy = self.copy(src, dst, peer, slot)
        self.sent[inner].append(copy)
        if inner is None:
            copy.start()
        else:
            pl.when(self.is_inner == inner)(copy.start)
        return slot

    def arrive(self, slot, dst, peer):
        pltpu.make_async_remote_copy(
            src_ref=dst,
            dst_ref=dst,
            send_sem=self.send_sem.at[0],
            recv_sem=self.recv_sem.at[slot],
            device_id=peer,
            device_id_type=MESH_IDS,
        ).wait_recv()

    def finish(self):
        for inner, copies in self.sent.items():

            def drain(copies=copies):
                for copy in copies:
                    copy.wait_send()

            if inner is None:
                drain()
            else:
                pl.when(self.is_inner == inner)(drain)


class Plane:
    def __init__(self, planes):
        dp, self.blk = lax.axis_index("dp"), lax.axis_index("blk")
        self.z, self.x = dp // 2, dp % 2
        self.dp = dp
        self.partner = self.z + 1 - 2 * (self.z % 2)
        self.other = planes // 2 - self.z // (planes // 2)
        self.outer = (planes - 1) * (self.other - 1)
        self.inner = ((self.z + 1) // 2) % 2
        self.order = (self.other, self.outer, self.partner, self.z)
        self.side = (self.z * 2 + (1 - self.x), self.blk)

    def at(self, plane):
        return (plane * 2 + self.x, self.blk)


class Spread:
    def __init__(self, wire, place, target, tail):
        self.wire, self.place, self.target = wire, place, target
        self.height, self.main = target.shape[1], target.shape[1] - tail

    def block(self, plane, column):
        return self.target.at[plane * 2 + column, 0 : self.main]

    def pair(self, plane):
        return self.target.at[pl.ds(plane * 2, 2), self.main : self.height]

    def along(self, own, slots):
        p = self.place
        self.wire.push(own, own, p.at(p.partner), slots[2], inner=False)
        self.wire.push(own, own, p.at(p.other), slots[0] + (1 - p.inner))

    def outward(self, own, slots):
        p = self.place
        self.wire.push(own, own, p.at(p.partner), slots[2], inner=True)

    def start(self):
        p, wire = self.place, self.wire
        self.z_slots = [wire.slot() for _ in range(3)]
        self.along(self.block(p.z, p.x), self.z_slots)

    def start_out(self):
        p = self.place
        self.outward(self.block(p.z, p.x), self.z_slots)

    def start_side(self):
        p, wire = self.place, self.wire
        self.x_slots = [wire.slot() for _ in range(4)]
        own = self.block(p.z, p.x)
        wire.push(own, own, p.side, self.x_slots[3])
        if self.main < self.height:
            rest = self.target.at[p.dp, self.main : self.height]
            self.rest_slot = wire.push(rest, rest, p.side)

    def tail(self):
        p, wire = self.place, self.wire
        rest = self.target.at[p.z * 2 + (1 - p.x), self.main : self.height]
        wire.arrive(self.rest_slot, rest, p.side)
        self.t_slots = [wire.slot() for _ in range(3)]
        self.along(self.pair(p.z), self.t_slots)

    def tail_out(self):
        self.outward(self.pair(self.place.z), self.t_slots)

    def relay(self, j, inner=None):
        p, wire = self.place, self.wire
        block = self.block(p.order[j], p.x)
        onward = wire.copy(block, block, p.side, self.x_slots[j])
        wire.sent[inner].append(onward)
        outward = None
        if j < 2 and inner is not False:
            outward = wire.copy(block, block, p.at(p.partner), self.z_slots[j])
            wire.sent[True].append(outward)

        def run():
            wire.arrive(self.z_slots[j], block, p.side)
            if outward is not None:
                if inner:
                    outward.start()
                else:
                    pl.when(wire.is_inner)(outward.start)
            onward.start()

        if inner is None:
            run()
        else:
            pl.when(wire.is_inner == inner)(run)

    def pass_tail(self, j):
        p, wire = self.place, self.wire
        pair = self.pair(p.order[j])
        copy = wire.copy(pair, pair, p.at(p.partner), self.t_slots[j])
        wire.sent[True].append(copy)

        @pl.when(wire.is_inner)
        def _():
            wire.arrive(self.t_slots[j], pair, p.side)
            copy.start()

    def settle_tail(self):
        p, wire = self.place, self.wire
        wire.arrive(self.t_slots[2], self.pair(p.order[2]), p.side)

        @pl.when(jnp.logical_not(wire.is_inner))
        def _():
            for j in range(2):
                wire.arrive(self.t_slots[j], self.pair(p.order[j]), p.side)

    def settle(self):
        p = self.place
        for j in range(4):
            self.wire.arrive(self.x_slots[j], self.block(p.order[j], 1 - p.x), p.side)


class Collect:
    def __init__(self, wire, place, buffers):
        self.wire, self.place = wire, place
        self.part, self.inbox, self.staged, self.landing = buffers[:4]
        self.height, self.main = self.part.shape[2], self.inbox.shape[1]
        self.split = self.main < self.height
        if self.split:
            self.t_landing, self.t_staged, self.t_cross, self.t_kept = buffers[4:]

    def pair(self, plane):
        return self.part.at[:, plane, self.main : self.height]

    def send_side(self, j):
        p = self.place
        plane = p.order[j]
        self.wire.push(
            self.part.at[1 - p.x, plane, 0 : self.main],
            self.inbox.at[plane],
            p.side,
            self.x_slots[j],
        )

    def send(self, order=(1, 0, 2, 3)):
        p, wire = self.place, self.wire
        self.x_slots = [wire.slot() for _ in range(4)]
        for j in order:
            self.send_side(j)
        self.z_slots = [wire.slot() for _ in range(4)]
        if self.split:
            self.t_slots = [wire.slot() for _ in range(4)]
            for j in (1, 0, 2):
                wire.push(
                    self.pair(p.order[j]),
                    self.t_landing.at[j],
                    p.at(p.partner),
                    self.t_slots[j],
                    inner=None if j == 2 else False,
                )

    def first(self, j):
        p, wire = self.place, self.wire
        plane = p.order[j]
        wire.arrive(self.x_slots[j], self.inbox.at[plane], p.side)
        both = self.part[p.x, plane, 0 : self.main].astype(jnp.float32)
        both = both + self.inbox[plane].astype(jnp.float32)
        self.staged[plane] = both.astype(jnp.bfloat16)
        wire.push(
            self.staged.at[plane],
            self.landing.at[j],
            p.at(p.partner),
            self.z_slots[j],
            inner=None if j == 2 else False,
        )

    def second(self, j):
        p, wire = self.place, self.wire
        plane = p.order[j]
        copy = wire.copy(self.staged.at[plane], self.landing.at[3], p.at(plane), self.z_slots[3])
        wire.sent[True].append(copy)

        @pl.when(wire.is_inner)
        def _():
            wire.arrive(self.z_slots[j], self.landing.at[j], p.side)
            both = self.staged[plane].astype(jnp.float32) + self.landing[j].astype(jnp.float32)
            self.staged[plane] = both.astype(jnp.bfloat16)
            copy.start()

    def second_tail(self, j):
        p, wire = self.place, self.wire
        plane = p.order[j]
        copy = wire.copy(self.t_staged.at[j], self.t_landing.at[3], p.at(plane), self.t_slots[3])
        wire.sent[True].append(copy)

        @pl.when(wire.is_inner)
        def _():
            wire.arrive(self.t_slots[j], self.t_landing.at[j], p.side)
            rest = self.part[:, plane, self.main : self.height].astype(jnp.float32)
            rest = rest + self.t_landing[j].astype(jnp.float32)
            self.t_staged[j] = rest.astype(jnp.bfloat16)
            copy.start()

    def tail(self):
        p, wire = self.place, self.wire
        for j in (2, 3):
            wire.arrive(self.t_slots[j], self.t_landing.at[j], p.side)

        def rest_of(column):
            rest = self.part[column, p.z, self.main : self.height].astype(jnp.float32)
            for j in (2, 3):
                rest = rest + self.t_landing[j, column].astype(jnp.float32)
            return rest

        self.t_kept[...] = rest_of(p.x)
        self.t_cross[0] = rest_of(1 - p.x).astype(jnp.bfloat16)
        self.cross_slot = wire.push(self.t_cross.at[0], self.t_cross.at[1], p.side)

    def total(self):
        p, wire = self.place, self.wire
        wire.arrive(self.x_slots[3], self.inbox.at[p.z], p.side)
        total = self.part[p.x, p.z, 0 : self.main].astype(jnp.float32)
        total = total + self.inbox[p.z].astype(jnp.float32)
        for j in (2, 3):
            wire.arrive(self.z_slots[j], self.landing.at[j], p.side)
            total = total + self.landing[j].astype(jnp.float32)
        if not self.split:
            return total
        wire.arrive(self.cross_slot, self.t_cross.at[1], p.side)
        rest = self.t_kept[...] + self.t_cross[1].astype(jnp.float32)
        return jnp.concatenate([total, rest], axis=0)


def fused(
    depth,
    lens,
    freq,
    xin_at,
    cot_at,
    in_at,
    gate_at,
    up_at,
    out_at,
    down_at,
    gain_a,
    bias_a,
    gain_b,
    bias_b,
    outputs_to,
    input_grad_to,
    g_in_to,
    g_mlp_to,
    g_out_to,
    g_down_to,
    cot,
    in_rows,
    gate_rows,
    up_rows,
    out_rows,
    outputs,
    input_grad,
    g_out,
    g_down,
    local_sem,
    xs,
    p_in,
    p_mlp,
    vectors_tab,
    r_in,
    r_mlp,
    s_out,
    w_in,
    w_gate,
    w_up,
    w_down,
    w_out,
    params,
    cos_tab,
    sin_tab,
    seg_tab,
    qm,
    kw,
    vw,
    prob,
    att,
    s_att,
    r_att,
    norm_one,
    hid,
    hs,
    gate_pre,
    up_pre,
    act,
    s_mix,
    r_mix,
    t_mix,
    dres_two,
    dms,
    dgate,
    dup,
    s_dh,
    r_dh,
    t_dh,
    dres_one,
    s_da,
    r_da,
    acc_q,
    acc_k,
    acc_v,
    dj,
    s_ig,
    r_ig,
    t_ig,
    sum_in,
    sum_gate,
    sum_up,
    sum_down,
    b_out,
    rb_out,
    tb_out,
    sum_out,
    f_gate,
    s_gmlp,
    r_gmlp,
    s_gin,
    r_gin,
    send_sem,
    recv_sem,
):
    planes, cols = depth, 4
    tok = xin_at.shape[0]
    row_len = tok * cols
    place = Plane(planes)
    dp, blk = place.dp, place.blk
    bf16, f32 = jnp.bfloat16, jnp.float32

    row_of, core_of = blk // 2, blk % 2
    near_at = row_of * 2 + (1 - core_of)
    across_at = (1 - row_of) * 2 + core_of
    corner_at = (1 - row_of) * 2 + (1 - core_of)
    near, across = (dp, near_at), (dp, across_at)

    def lane(k):
        return (dp, (blk + k) % cols)

    def lane_from(k):
        return (blk + cols - k) % cols

    lanes = range(1, cols)
    local = []

    def move(source, target):
        copy = pltpu.make_async_copy(source, target, local_sem.at[len(local)])
        local.append(copy)
        copy.start()
        return copy

    xin = xs.at[blk]
    in_load = move(in_at, in_rows)
    out_load = move(out_at, out_rows)
    down_load = move(down_at, w_down.at[dp])
    x_load = move(xin_at, xin)
    gate_load = move(gate_at, gate_rows)
    up_load = move(up_at, up_rows)
    cot_load = move(cot_at, cot)
    wire = Wire(send_sem, recv_sem, place.inner == 1)
    barrier = pltpu.get_barrier_semaphore()
    peers = [place.side, place.at(place.partner), place.at(place.other)]
    peers = peers + [lane(k) for k in lanes]
    for peer in peers:
        pl.semaphore_signal(barrier, inc=1, device_id=peer, device_id_type=MESH_IDS)
    far = place.at(place.outer)

    @pl.when(place.inner == 1)
    def _():
        pl.semaphore_signal(barrier, inc=1, device_id=far, device_id_type=MESH_IDS)


    rows = 24
    width = xin_at.shape[1]
    lane_ids = lax.broadcasted_iota(jnp.int32, (1, LANES), 1)
    low_half = lane_ids < HALF
    head_width = width // cols
    vectors_tab[...] = jnp.zeros_like(vectors_tab)
    for number, vector in enumerate((gain_a, bias_a, gain_b, bias_b)):
        vectors_tab[number : number + 1, 0:rows] = vector[...].astype(f32)
    free_lane = lax.broadcasted_iota(jnp.int32, (8, LANES), 0) + HALF
    to_lane = jnp.where(
        free_lane == lax.broadcasted_iota(jnp.int32, (8, LANES), 1), 1.0, 0.0
    ).astype(bf16)
    vector_columns = tm(vectors_tab[...].astype(bf16), to_lane)[0:rows]
    in_load.wait()
    joined_rows = in_rows[...].astype(f32)
    for j in range(cols):
        starts = [kind * width + j * head_width for kind in range(3)]
        windows = [window_at(joined_rows, start) for start in starts]
        windows.append(
            jnp.where(
                low_half,
                window_at(joined_rows, starts[0] + LANES),
                window_at(joined_rows, starts[1] + LANES - HALF),
            )
        )
        windows.append(
            jnp.where(low_half, window_at(joined_rows, starts[2] + LANES), vector_columns)
        )
        packed = jnp.concatenate(windows, axis=1)
        p_in[j] = jnp.concatenate(
            [packed, jnp.zeros((8, packed.shape[1]), f32)], axis=0
        ).astype(bf16)
    out_load.wait()
    halved = [out_rows[:, n * width // 2 : (n + 1) * width // 2].astype(f32) for n in range(2)]
    s_out[blk, dp] = jnp.concatenate(halved, axis=0).astype(bf16)
    pl.semaphore_wait(barrier, len(peers) + place.inner)

    def to_lanes(source_of, target):
        return [wire.push(source_of((blk + k) % cols), target.at[blk], lane(k)) for k in lanes]

    def from_lanes(slots, target):
        for k, slot in zip(lanes, slots):
            wire.arrive(slot, target.at[lane_from(k)], lane(k))

    every = pl.ds(0, tok)

    def gather_start(own, target, cut=every):
        return [
            wire.push(own.at[cut], target.at[blk, cut], across),
            wire.push(own.at[cut], target.at[blk, cut], near),
        ]

    def gather_relay(slots, target, cut=every):
        came = target.at[across_at, cut]
        wire.arrive(slots[0], came, across)
        slots.append(wire.push(came, came, near))

    def gather_done(slots, target, cut=every):
        wire.arrive(slots[1], target.at[near_at, cut], near)
        wire.arrive(slots[2], target.at[corner_at, cut], near)

    def sum_start(part, inbox, cut=every):
        return [
            wire.push(part.at[corner_at, cut], inbox.at[0, cut], near),
            wire.push(part.at[near_at, cut], inbox.at[1, cut], near),
        ]

    def sum_relay(slots, part, inbox, staged, cut=every):
        wire.arrive(slots[0], inbox.at[0, cut], near)
        both = part[across_at, cut].astype(f32) + inbox[0, cut].astype(f32)
        staged[cut] = both.astype(bf16)
        slots.append(wire.push(staged.at[cut], inbox.at[2, cut], across))

    def sum_done(slots, part, inbox, cut=every):
        wire.arrive(slots[1], inbox.at[1, cut], near)
        total = part[blk, cut].astype(f32) + inbox[1, cut].astype(f32)
        wire.arrive(slots[2], inbox.at[2, cut], across)
        return total + inbox[2, cut].astype(f32)

    in_slots = to_lanes(lambda to: p_in.at[to], r_in)
    down_load.wait()
    tail = 0
    out_spread = Spread(wire, place, s_out.at[blk], 0)
    out_spread.start()
    out_spread.start_out()
    out_spread.start_side()
    down_spread = Spread(wire, place, w_down, DTF)
    down_spread.start()
    down_spread.start_out()
    down_spread.start_side()
    gate_load.wait()
    up_load.wait()
    units = gate_rows.shape[1] // cols
    unit_block = units // (planes * 2)
    for at, weight in ((0, gate_rows), (rows, up_rows)):
        whole = weight[...].astype(f32)
        for j in range(cols):
            packed = jnp.concatenate(
                [
                    gather_lanes(
                        whole,
                        unit_block,
                        n * LANES,
                        lambda ring_at, lane: lane + (cols - 1) * unit_block * ring_at + unit_block * j,
                    )
                    for n in range(units // LANES)
                ],
                axis=1,
            )
            p_mlp[j, at : at + rows] = packed.astype(bf16)
    mlp_slots = to_lanes(lambda to: p_mlp.at[to], r_mlp)
    x_load.wait()
    x_slots = gather_start(xin, xs)
    r_in[blk] = p_in[blk]
    r_mlp[blk] = p_mlp[blk]

    lengths = [lens[0, j] for j in range(lens.shape[1])]

    def layout(positions):
        segment = jnp.zeros_like(positions)
        begins = jnp.zeros_like(positions)
        bound = jnp.int32(0)
        for length in lengths:
            bound = bound + length
            passed = positions >= bound
            segment = segment + jnp.where(passed, 1, 0)
            begins = begins + jnp.where(passed, length, 0)
        return segment, positions - begins

    seg_rows, offsets = layout(lax.broadcasted_iota(jnp.int32, (row_len, LANES), 0))
    seg_tab[...] = seg_rows
    seg_key = layout(lax.broadcasted_iota(jnp.int32, (8, row_len), 1))[0][0:1]
    front = lane_ids % HALF < QUART
    angles = offsets.astype(f32) * freq[0:1]
    cos_tab[...] = jnp.cos(angles)
    sin_tab[...] = jnp.where(front, -1.0, 1.0) * jnp.sin(angles)

    def turn(window):
        return jnp.where(
            front, pltpu.roll(window, LANES - QUART, 1), pltpu.roll(window, QUART, 1)
        )

    from_lanes(in_slots, r_in)
    w_in[dp] = jnp.concatenate(
        [r_in[j, 0:rows, :].astype(f32) for j in range(cols)], axis=0
    ).astype(bf16)
    in_spread = Spread(wire, place, w_in, tail)
    in_spread.start()
    in_spread.start_out()
    in_spread.start_side()
    from_lanes(mlp_slots, r_mlp)
    mlp_own = [r_mlp[j].astype(f32) for j in range(cols)]
    w_gate[dp] = jnp.concatenate([part[0:rows] for part in mlp_own], axis=0).astype(bf16)
    w_up[dp] = jnp.concatenate([part[rows:] for part in mlp_own], axis=0).astype(bf16)
    gate_spread = Spread(wire, place, w_gate, tail)
    up_spread = Spread(wire, place, w_up, tail)
    gate_spread.start()
    gate_spread.start_side()
    up_spread.start()
    out_spread.relay(2)
    for spread in (out_spread, down_spread):
        spread.relay(0, inner=True)
        spread.relay(1, inner=True)
    in_spread.relay(2)
    out_spread.relay(0, inner=False)
    out_spread.relay(1, inner=False)
    in_spread.relay(0)
    down_spread.relay(2)
    in_spread.relay(1)
    up_spread.start_side()
    gate_spread.start_out()
    up_spread.start_out()
    down_spread.tail()
    gate_spread.relay(0, inner=True)
    gate_spread.relay(1, inner=True)
    gather_relay(x_slots, xs)
    out_spread.settle()
    shards_here = pl.ds(0, planes * 2)
    out_lanes = gather_start(s_out.at[blk], s_out, shards_here)
    gate_spread.relay(2)
    up_spread.relay(2)
    gather_done(x_slots, xs)
    in_spread.settle()

    group = 2
    chunk = group * tok

    def project(step, carry):
        start = pl.multiple_of(step * chunk, chunk)
        here = pl.ds(start, chunk)
        tokens = xs[pl.ds(step * group, group)].reshape(chunk, width)
        joined = mm(tokens, w_in[...].reshape(width, w_in.shape[2]))
        cosine, sine = cos_tab[here, :], sin_tab[here, :]

        def rotate(number):
            window = joined[:, number * LANES : (number + 1) * LANES]
            return window * cosine + turn(window) * sine

        scale = HALF ** -0.5
        queries = rotate(0).astype(bf16).astype(f32) * scale
        qm[0, here, :] = jnp.where(low_half, queries, 0.0).astype(bf16)
        qm[1, here, :] = jnp.where(low_half, 0.0, queries).astype(bf16)
        kw[0, here, :] = rotate(1).astype(bf16)
        vw[0, here, :] = joined[:, 2 * LANES : 3 * LANES].astype(bf16)
        both = rotate(3)
        qm[2, here, :] = jnp.where(low_half, both.astype(bf16).astype(f32) * scale, 0.0).astype(bf16)
        kw[1, here, :] = jnp.where(low_half, pltpu.roll(both, HALF, 1), 0.0).astype(bf16)
        vw[1, here, :] = joined[:, 4 * LANES : 5 * LANES].astype(bf16)
        return carry

    lax.fori_loop(0, cols // group, project, 0)

    def attend(head):
        window = head // 2

        def step_fn(step, carry):
            here = pl.ds(pl.multiple_of(step * chunk, chunk), chunk)
            scores = mt(qm[head, here, :], kw[window])
            allowed = seg_tab[here, :][:, 0:1] == seg_key
            scores = jnp.where(allowed, scores, NEG)
            top = jnp.max(scores, axis=1, keepdims=True)
            raised = jnp.exp(scores - top)
            total = jnp.sum(raised, axis=1, keepdims=True)
            prob_low = (raised * (1.0 / total)).astype(bf16)
            prob[head, here, :] = prob_low
            mixed = mm(prob_low, vw[window])
            if head == 1:
                mixed = jnp.where(low_half, att[0, here, :], mixed)
            att[window, here, :] = mixed
            return carry

        lax.fori_loop(0, row_len // chunk, step_fn, 0)

    up_spread.relay(0, inner=True)
    attend(0)
    attend(1)
    up_spread.relay(1, inner=True)
    attend(2)
    last_segment = lens.shape[1] - 1
    for j in range(cols):
        here = slice(j * tok, (j + 1) * tok)
        kept = seg_tab[here, :] < last_segment
        s_att[j, :, 0:LANES] = jnp.where(kept, att[0, here, :], 0.0).astype(bf16)
        s_att[j, :, LANES : 2 * LANES] = jnp.where(kept, att[1, here, :], 0.0).astype(bf16)
    att_slots = to_lanes(lambda to: s_att.at[to], r_att)
    r_att[blk] = s_att[blk]

    down_spread.tail_out()
    gather_relay(out_lanes, s_out, shards_here)
    gate_spread.relay(0, inner=False)
    gate_spread.relay(1, inner=False)
    for j in range(2):
        down_spread.pass_tail(j)
    gather_done(out_lanes, s_out, shards_here)
    shards = planes * 2 * cols
    per_quarter = shards // cols
    head_rows = per_quarter * rows
    for quarter in range(cols):
        slots = [
            s_out[s % cols, s // cols].astype(f32)
            for s in range(quarter * per_quarter, (quarter + 1) * per_quarter)
        ]
        w_out[quarter, 0:head_rows, :] = jnp.concatenate(
            [
                jnp.concatenate([slot[n * rows : (n + 1) * rows] for slot in slots], axis=0)
                for n in range(2)
            ],
            axis=1,
        ).astype(bf16)
        w_out[quarter, head_rows:, :] = jnp.zeros(
            (w_out.shape[1] - head_rows, width), bf16
        )
    last_window = w_in[:, :, 4 * LANES : 5 * LANES].reshape(width, LANES)
    params[...] = mt(to_lane, last_window)
    gain_one, bias_one = params[0:1, :], params[1:2, :]
    gain_two, bias_two = params[2:3, :], params[3:4, :]

    def normalize(residual):
        centered = residual - jnp.mean(residual, axis=1, keepdims=True)
        variance = jnp.mean(centered * centered, axis=1, keepdims=True)
        spread = lax.rsqrt(variance + EPS)
        return centered * spread, spread

    def normalize_back(grad, normal, spread, gain):
        inner = grad * gain
        mean_inner = jnp.mean(inner, axis=1, keepdims=True)
        mean_both = jnp.mean(inner * normal, axis=1, keepdims=True)
        return (inner - mean_inner - normal * mean_both) * spread

    def column_sum(value):
        return jnp.sum(value, axis=0, keepdims=True)

    from_lanes(att_slots, r_att)
    branch = mm(r_att[0], w_out[0])
    for quarter in range(1, cols):
        branch = branch + mm(r_att[quarter], w_out[quarter])
    normal, spread_one = normalize(xin[...].astype(f32) + branch)
    norm_one[...] = normal
    hidden = normal * gain_one + bias_one
    hid[...] = hidden
    hs[blk] = hidden.astype(bf16)
    hid_slots = gather_start(hs.at[blk], hs)
    up_spread.relay(0, inner=False)
    up_spread.relay(1, inner=False)
    down_spread.relay(0, inner=False)
    down_spread.relay(1, inner=False)
    gather_relay(hid_slots, hs)
    gate_spread.settle()
    gather_done(hid_slots, hs)

    wide = 256
    strips = units // wide

    def each_strip(body):
        def step_fn(step, carry):
            body(pl.ds(pl.multiple_of(step * wide, wide), wide))
            return carry

        lax.fori_loop(0, strips, step_fn, 0)

    def expand_gate(here):
        tokens = hs[...].reshape(row_len, width)
        gate_pre[:, here] = mm(tokens, w_gate[:, :, here].reshape(width, wide))

    def expand_up(here):
        tokens = hs[...].reshape(row_len, width)
        up = mm(tokens, w_up[:, :, here].reshape(width, wide))
        gate = gate_pre[:, here]
        up_pre[:, here] = up
        act[:, here] = (gate / (1.0 + jnp.exp(-gate)) * up).astype(bf16)

    each_strip(expand_gate)
    up_spread.settle()
    each_strip(expand_up)
    down_spread.settle()
    down_spread.settle_tail()

    def contract(step, carry):
        here = pl.ds(pl.multiple_of(step * wide, wide), wide)
        mixed = mm(act[...], w_down[:, :, here].reshape(units, wide))
        s_mix[:, :, here] = mixed.reshape(cols, tok, wide).astype(bf16)
        return carry

    lax.fori_loop(0, width // wide, contract, 0)
    pieces = 4
    cot_load.wait()
    halves = [pl.ds(n * tok // pieces, tok // pieces) for n in range(pieces)]
    mix_slots = [sum_start(s_mix, r_mix, cut) for cut in halves]
    for slots, cut in zip(mix_slots, halves):
        sum_relay(slots, s_mix, r_mix, t_mix, cut)
    second_gain, second_bias, dm_slots = 0.0, 0.0, []
    for slots, cut in zip(mix_slots, halves):
        mlp_out = sum_done(slots, s_mix, r_mix, cut)
        normal, spread_two = normalize(hid[cut, :] + mlp_out)
        outputs[cut, :] = (normal * gain_two + bias_two).astype(bf16)
        grad = cot[cut, :].astype(f32)
        second_gain = second_gain + column_sum(grad * normal)
        second_bias = second_bias + column_sum(grad)
        d_two = normalize_back(grad, normal, spread_two, gain_two)
        dres_two[cut, :] = d_two
        dms[blk, cut] = d_two.astype(bf16)
        dm_slots.append(gather_start(dms.at[blk], dms, cut))
    writes = [move(outputs, outputs_to)]
    for slots, cut in zip(dm_slots, halves):
        gather_relay(slots, dms, cut)
    for slots, cut in zip(dm_slots, halves):
        gather_done(slots, dms, cut)

    down_sum = Collect(wire, place, sum_down)
    gate_sum = Collect(wire, place, sum_gate)
    up_sum = Collect(wire, place, sum_up)
    in_sum = Collect(wire, place, sum_in)
    out_sum = Collect(wire, place, sum_out)
    half = 4

    def fill_parts(part, left_of, right, more=lambda product, here: product):
        height = part.shape[2]

        def step_fn(step, carry):
            here = pl.ds(pl.multiple_of(step * half * height, LANES), half * height)
            product = more(tm(left_of(here), right()), here)
            for j in range(half):
                part[j % 2, step * (half // 2) + j // 2] = product[
                    j * height : (j + 1) * height
                ].astype(bf16)
            return carry

        lax.fori_loop(0, planes * 2 // half, step_fn, 0)

    fill_parts(down_sum.part, lambda here: act[:, here], lambda: dms[...].reshape(row_len, width))
    down_sum.send()

    block = w_down.shape[1]

    def active_grads(step, carry):
        here = pl.ds(pl.multiple_of(step * half * block, LANES), half * block)
        d_active = mt(
            dms[...].reshape(row_len, width),
            w_down[pl.ds(step * half, half)].reshape(half * block, width),
        )
        gate, up = gate_pre[:, here], up_pre[:, here]
        sg = 1.0 / (1.0 + jnp.exp(-gate))
        dgate[:, here] = (d_active * up * sg * (1.0 + gate * (1.0 - sg))).astype(bf16)
        dup[:, here] = (d_active * gate * sg).astype(bf16)
        return carry

    lax.fori_loop(0, planes * 2 // half, active_grads, 0)
    block = w_gate.shape[1]

    def hidden_rows(here):
        return hs[:, :, here].reshape(row_len, half * block)

    fill_parts(gate_sum.part, hidden_rows, lambda: dgate[...])
    gate_sum.send()
    def hidden_grads(step, carry):
        here = pl.ds(pl.multiple_of(step * half * block, LANES), half * block)
        those = pl.ds(step * half, half)
        mixed = mt(dgate[...], w_gate[those].reshape(half * block, units)) + mt(
            dup[...], w_up[those].reshape(half * block, units)
        )
        s_dh[:, :, here] = mixed.reshape(cols, tok, half * block).astype(bf16)
        return carry

    lax.fori_loop(0, planes * 2 // half, hidden_grads, 0)
    dh_slots = sum_start(s_dh, r_dh)

    sum_relay(dh_slots, s_dh, r_dh, t_dh)
    fill_parts(up_sum.part, hidden_rows, lambda: dup[...])
    up_sum.send()
    down_sum.first(1)
    down_sum.first(0)
    d_hidden = dres_two[...] + sum_done(dh_slots, s_dh, r_dh)
    down_sum.first(2)
    normal = norm_one[...]
    first_gain = column_sum(d_hidden * normal)
    first_bias = column_sum(d_hidden)
    d_one = normalize_back(d_hidden, normal, spread_one, gain_one)
    dres_one[...] = d_one
    d_branch = d_one.astype(bf16)
    mine = pl.ds(pl.multiple_of(blk * tok, tok), tok)
    kept = seg_tab[mine, :][:, 0:1] < last_segment
    for quarter in range(cols):
        pulled = mt(d_branch, w_out[quarter]).astype(bf16).astype(f32)
        s_da[quarter] = jnp.where(kept, pulled, 0.0).astype(bf16)
    da_slots = to_lanes(lambda to: s_da.at[to], r_da)
    r_da[blk] = s_da[blk]

    params[...] = jnp.concatenate(
        [first_gain, first_bias, second_gain, second_bias, jnp.zeros((4, width), f32)], axis=0
    )
    for quarter in range(cols):
        product = tm(r_att[quarter], d_branch)
        for t in range(per_quarter):
            s = quarter * per_quarter + t
            owner_dp = s // cols
            mine_rows = product[t * rows : (t + 1) * rows]
            halved = [mine_rows[:, n * width // 2 : (n + 1) * width // 2] for n in range(2)]
            b_out[s % cols, owner_dp % 2, owner_dp // 2] = jnp.concatenate(
                halved, axis=0
            ).astype(bf16)
    both_sides = pl.ds(0, 2)
    out_blk = sum_start(b_out, rb_out, both_sides)

    gate_sum.first(1)
    sum_relay(out_blk, b_out, rb_out, tb_out, both_sides)
    down_sum.second_tail(1)
    down_sum.second(1)
    gate_sum.first(0)
    from_lanes(da_slots, r_da)
    def attend_back(head):
        window = head // 2
        fresh = head != 1

        def step_fn(step, carry):
            here = pl.ds(pl.multiple_of(step * chunk, chunk), chunk)
            d_out = r_da[pl.ds(step * group, group), :, window * LANES : (window + 1) * LANES]
            d_out = d_out.reshape(chunk, LANES).astype(f32)
            if head == 0:
                d_out = jnp.where(low_half, d_out, 0.0)
            if head == 1:
                d_out = jnp.where(low_half, 0.0, d_out)
            d_low = d_out.astype(bf16)
            delta = jnp.sum(d_out * att[window, here, :], axis=1, keepdims=True)
            prob_low = prob[head, here, :]
            d_prob = mt(d_low, vw[window])
            d_score = (prob_low.astype(f32) * (d_prob - delta)).astype(bf16)
            d_query = mm(d_score, kw[window]) * (HALF ** -0.5)
            if head == 1:
                d_query = jnp.where(low_half, acc_q[0, here, :], d_query)
            acc_q[window, here, :] = d_query
            d_key = tm(d_score, qm[head, here, :])
            d_value = tm(prob_low, d_low)
            if fresh:

                @pl.when(step == 0)
                def _():
                    acc_k[window] = d_key
                    acc_v[window] = d_value

                @pl.when(step != 0)
                def _():
                    acc_k[window] = acc_k[window] + d_key
                    acc_v[window] = acc_v[window] + d_value
            else:
                acc_k[window] = acc_k[window] + d_key
                acc_v[window] = acc_v[window] + d_value
            return carry

        lax.fori_loop(0, row_len // chunk, step_fn, 0)

    attend_back(0)
    gate_sum.first(2)
    down_sum.second_tail(0)
    down_sum.second(0)
    attend_back(1)
    attend_back(2)

    cosine, sine = cos_tab[...], sin_tab[...]

    def rotate_back(vector):
        vector = vector.astype(bf16).astype(f32)
        return (vector * cosine - turn(vector) * sine).astype(bf16)

    dj[:, 0:LANES] = rotate_back(acc_q[0])
    dj[:, LANES : 2 * LANES] = rotate_back(acc_k[0])
    dj[:, 2 * LANES : 3 * LANES] = acc_v[0].astype(bf16)
    dj[:, 3 * LANES : 4 * LANES] = rotate_back(acc_q[1] + pltpu.roll(acc_k[1], HALF, 1))
    dj[:, 4 * LANES : 5 * LANES] = acc_v[1].astype(bf16)

    up_sum.first(1)

    def with_vectors(product, here):
        columns = tm(params[:, here].astype(bf16), to_lane)
        last = product[:, 4 * LANES :] + columns
        return jnp.concatenate([product[:, : 4 * LANES], last], axis=1)

    fill_parts(
        in_sum.part,
        lambda here: xs[:, :, here].reshape(row_len, half * block),
        lambda: dj[...],
        with_vectors,
    )

    def input_grads(step, carry):
        here = pl.ds(pl.multiple_of(step * half * block, LANES), half * block)
        mixed = mt(dj[...], w_in[pl.ds(step * half, half)].reshape(half * block, w_in.shape[2]))
        s_ig[:, :, here] = mixed.reshape(cols, tok, half * block).astype(bf16)
        return carry

    lax.fori_loop(0, planes * 2 // half, input_grads, 0)
    ig_slots = sum_start(s_ig, r_ig)

    gate_sum.second(1)
    sum_relay(ig_slots, s_ig, r_ig, t_ig)
    up_sum.first(0)
    gate_sum.second(0)
    out_sum.part[...] = sum_done(out_blk, b_out, rb_out, both_sides).astype(bf16)
    in_sum.send((1, 0, 2))
    out_sum.send((1, 0, 2))
    in_sum.send_side(3)
    out_sum.send_side(3)
    down_sum.tail()
    up_sum.second(1)
    up_sum.first(2)
    f_gate[...] = gate_sum.total()
    up_sum.second(0)
    grad_in = dres_one[...] + sum_done(ig_slots, s_ig, r_ig)
    input_grad[...] = grad_in.astype(bf16)
    writes.append(move(input_grad, input_grad_to))
    in_sum.first(1)
    in_sum.first(0)
    up_total = up_sum.total()
    gate_total = f_gate[...]
    for j in range(cols):
        here = slice(j * rows, (j + 1) * rows)
        s_gmlp[j] = jnp.concatenate([gate_total[here], up_total[here]], axis=0).astype(bf16)
    gmlp_slots = to_lanes(lambda to: s_gmlp.at[to], r_gmlp)
    r_gmlp[blk] = s_gmlp[blk]
    in_sum.second(1)
    in_sum.first(2)
    in_sum.second(0)
    for j in (1, 0, 2):
        out_sum.first(j)
    out_sum.second(1)
    out_sum.second(0)
    from_lanes(gmlp_slots, r_gmlp)
    writes.append(move(r_gmlp, g_mlp_to))
    in_total = in_sum.total()
    for j in range(cols):
        s_gin[j] = jnp.concatenate(
            [in_total[j * rows : (j + 1) * rows], jnp.zeros((8, in_total.shape[1]), f32)], axis=0
        ).astype(bf16)
    gin_slots = to_lanes(lambda to: s_gin.at[to], r_gin)
    r_gin[blk] = s_gin[blk]
    g_out[...] = out_sum.total()
    writes.append(move(g_out, g_out_to))
    g_down[...] = down_sum.total()
    writes.append(move(g_down, g_down_to))
    from_lanes(gin_slots, r_gin)
    writes.append(move(r_gin, g_in_to))
    wire.finish()
    for write in writes:
        write.wait()


def unpack(
    rows,
    block,
    outputs,
    input_grad,
    g_in,
    g_mlp,
    g_out,
    g_down,
    outputs_to,
    input_grad_to,
    in_to,
    out_to,
    gate_to,
    up_to,
    down_to,
    *vectors_to,
):
    f32 = jnp.float32
    cols = g_in.shape[0]
    width = outputs.shape[1]
    outputs_to[0] = outputs[...]
    input_grad_to[0] = input_grad[...]
    down_to[...] = g_down[...]
    for n in range(2):
        out_to[:, n * width // 2 : (n + 1) * width // 2] = g_out[n * rows : (n + 1) * rows, :]
    low_half = lax.broadcasted_iota(jnp.int32, (1, LANES), 1) < HALF
    joined = [g_in[j].astype(f32)[0:rows] for j in range(cols)]
    vectors = joined[0][:, 4 * LANES :]
    for j in range(1, cols):
        vectors = vectors + joined[j][:, 4 * LANES :]
    vectors = jnp.concatenate([vectors, jnp.zeros((LANES - rows, LANES), f32)], axis=0).T
    for number, vector_to in enumerate(vectors_to):
        vector_to[...] = vectors[HALF + number, 0:rows]
    single_at = ((3, 0), (3, 1), (4, 0))

    def half(kind, number, want):
        owner, part = number // 3, number % 3
        window, at = (kind, part) if part < 2 else single_at[kind]
        value = joined[owner][:, window * LANES : (window + 1) * LANES]
        return value if at == want else pltpu.roll(value, HALF, 1)

    for kind in range(3):
        for n in range(width // LANES):
            at = kind * width + n * LANES
            in_to[:, at : at + LANES] = jnp.where(
                low_half, half(kind, 2 * n, 0), half(kind, 2 * n + 1, 1)
            )
    lanes = lax.broadcasted_iota(jnp.int32, (1, LANES), 1)
    mlp = [g_mlp[j].astype(f32) for j in range(cols)]
    for first_row, target in ((0, gate_to), (rows, up_to)):
        parts = [part[first_row : first_row + rows] for part in mlp]
        for n in range(target.shape[1] // LANES):
            first = n * LANES
            result = None
            for number in range(first // block, (first + LANES - 1) // block + 1):
                ring_at, owner = number // cols, number % cols
                piece = window_at(parts[owner], ring_at * block + first - number * block)
                begin = number * block - first
                result = piece if result is None else jnp.where(lanes < begin, result, piece)
            target[:, first : first + LANES] = result


def fast_shards(
    depth,
    inputs,
    doc_lengths,
    project_in,
    project_out,
    gate_weight,
    up_weight,
    down_weight,
    first_gain,
    first_bias,
    second_gain,
    second_bias,
    cotangent,
):
    cols = 4
    tok, width = inputs.shape[1:]
    rows = project_in.shape[0]
    ff = gate_weight.shape[1]
    ring = depth * 2
    row_len = tok * cols
    units = ff // cols
    block = units // ring
    head_width = width // cols
    in_width = 5 * LANES
    bf16, f32 = jnp.bfloat16, jnp.float32

    lane_ids = np.arange(LANES) % QUART
    freq = jnp.asarray(
        np.broadcast_to(BASE ** (-2.0 * lane_ids / HALF), (8, LANES)).astype(np.float32)
    )

    def scratch(*shape, kind=bf16):
        return pltpu.VMEM(shape, kind)

    def sums(height, across, tail=0):
        main = height - tail
        buffers = [
            scratch(2, depth, height, across),
            scratch(depth, main, across),
            scratch(depth, main, across),
            scratch(4, main, across),
        ]
        if tail:
            buffers = buffers + [
                scratch(4, 2, tail, across),
                scratch(2, 2, tail, across),
                scratch(2, tail, across),
                scratch(tail, across, kind=f32),
            ]
        return tuple(buffers)

    stacked = scratch(cols, tok, width)
    heads = 3
    buffers = [
        scratch(tok, width),
        scratch(rows, 3 * width),
        scratch(rows, ff),
        scratch(rows, ff),
        scratch(rows, width),
        scratch(tok, width),
        scratch(tok, width),
        scratch(2 * rows, width // 2, kind=f32),
        scratch(block, width, kind=f32),
        pltpu.SemaphoreType.DMA((16,)),
        stacked,
        scratch(cols, 32, in_width),
        scratch(cols, 2 * rows, units),
        scratch(8, LANES, kind=f32),
        scratch(cols, 32, in_width),
        scratch(cols, 2 * rows, units),
        scratch(cols, ring, 2 * rows, width // 2),
        scratch(ring, cols * rows, in_width),
        scratch(ring, cols * rows, units),
        scratch(ring, cols * rows, units),
        scratch(ring, block, width),
        scratch(cols, 2 * LANES, width),
        scratch(8, width, kind=f32),
        scratch(row_len, LANES, kind=f32),
        scratch(row_len, LANES, kind=f32),
        scratch(row_len, LANES, kind=jnp.int32),
        scratch(heads, row_len, LANES),
        scratch(2, row_len, LANES),
        scratch(2, row_len, LANES),
        scratch(heads, row_len, row_len),
        scratch(2, row_len, LANES, kind=f32),
        scratch(cols, tok, 2 * LANES),
        scratch(cols, tok, 2 * LANES),
        scratch(tok, width, kind=f32),
        scratch(tok, width, kind=f32),
        stacked,
        scratch(row_len, units, kind=f32),
        scratch(row_len, units, kind=f32),
        scratch(row_len, units),
        stacked,
        scratch(3, tok, width),
        scratch(tok, width),
        scratch(tok, width, kind=f32),
        stacked,
        scratch(row_len, units),
        scratch(row_len, units),
        stacked,
        scratch(3, tok, width),
        scratch(tok, width),
        scratch(tok, width, kind=f32),
        scratch(cols, tok, 2 * LANES),
        scratch(cols, tok, 2 * LANES),
        scratch(2, row_len, LANES, kind=f32),
        scratch(2, row_len, LANES, kind=f32),
        scratch(2, row_len, LANES, kind=f32),
        scratch(row_len, in_width),
        stacked,
        scratch(3, tok, width),
        scratch(tok, width),
        sums(cols * rows, in_width),
        sums(cols * rows, units),
        sums(cols * rows, units),
        sums(block, width, DTB),
        scratch(cols, 2, depth, 2 * rows, width // 2),
        scratch(3, 2, depth, 2 * rows, width // 2),
        scratch(2, depth, 2 * rows, width // 2),
        sums(2 * rows, width // 2, 0),
        scratch(cols * rows, units, kind=f32),
        scratch(cols, 2 * rows, units),
        scratch(cols, 2 * rows, units),
        scratch(cols, 32, in_width),
        scratch(cols, 32, in_width),
        pltpu.SemaphoreType.DMA((240,)),
        pltpu.SemaphoreType.DMA((240,)),
    ]
    vmem = pl.BlockSpec(memory_space=pltpu.VMEM)
    anywhere = pl.BlockSpec(memory_space=pl.ANY)
    tokens = row_len * width
    outputs, input_grad, g_in, g_mlp, g_out, g_down = pl.pallas_call(
        functools.partial(fused, depth),
        out_shape=(
            jax.ShapeDtypeStruct((tok, width), bf16),
            jax.ShapeDtypeStruct((tok, width), bf16),
            jax.ShapeDtypeStruct((cols, 32, in_width), bf16),
            jax.ShapeDtypeStruct((cols, 2 * rows, units), bf16),
            jax.ShapeDtypeStruct((2 * rows, width // 2), f32),
            jax.ShapeDtypeStruct((block, width), f32),
        ),
        in_specs=[pl.BlockSpec(memory_space=pltpu.SMEM), vmem] + [anywhere] * 7 + [vmem] * 4,
        out_specs=(anywhere,) * 6,
        scratch_shapes=buffers,
        compiler_params=pltpu.CompilerParams(
            collective_id=0, has_side_effects=True, vmem_limit_bytes=60 * 2**20
        ),
        cost_estimate=pl.CostEstimate(
            flops=6 * tokens * (3 * units + 4 * head_width),
            bytes_accessed=8 * 2**20,
            transcendentals=3 * row_len * row_len,
        ),
        name="layer",
    )(
        doc_lengths,
        freq,
        inputs[0],
        cotangent[0],
        project_in,
        gate_weight,
        up_weight,
        project_out,
        down_weight,
        first_gain[None],
        first_bias[None],
        second_gain[None],
        second_bias[None],
    )

    vector = jax.ShapeDtypeStruct((rows,), f32)
    return pl.pallas_call(
        functools.partial(unpack, rows, block),
        out_shape=(
            jax.ShapeDtypeStruct((1, tok, width), bf16),
            jax.ShapeDtypeStruct((1, tok, width), bf16),
            jax.ShapeDtypeStruct((rows, 3 * width), f32),
            jax.ShapeDtypeStruct((rows, width), f32),
            jax.ShapeDtypeStruct((rows, ff), f32),
            jax.ShapeDtypeStruct((rows, ff), f32),
            jax.ShapeDtypeStruct((block, width), f32),
            vector,
            vector,
            vector,
            vector,
        ),
        in_specs=[vmem] * 6,
        out_specs=(vmem,) * 11,
        name="unpack",
    )(outputs, input_grad, g_in, g_mlp, g_out, g_down)


def pick(sizes):
    def chosen(*args):
        tok, width = args[0].shape[1:]
        ring, cols = sizes["dp"], sizes["blk"]
        fits = (
            ring == 8
            and cols == 4
            and tok == LANES
            and HEADS == 3 * cols
            and width == HEADS * HALF
            and args[2].shape[0] == 24
            and args[4].shape[1] == 4 * width
        )
        if fits:
            return fast_shards(ring // 2, *args)
        return shards(*args)

    return chosen


def solution(mesh):
    placed = (
        P("dp", "blk", None),
        P("dp", None),
        P(("dp", "blk"), None),
        P(("dp", "blk"), None),
        P(("dp", "blk"), None),
        P(("dp", "blk"), None),
        P(("dp", "blk"), None),
        P(("dp", "blk")),
        P(("dp", "blk")),
        P(("dp", "blk")),
        P(("dp", "blk")),
        P("dp", "blk", None),
    )
    return jax.shard_map(
        pick(dict(mesh.shape)),
        mesh=mesh,
        in_specs=placed,
        out_specs=(
            P("dp", "blk", None),
            P("dp", "blk", None),
            P(("dp", "blk"), None),
            P(("dp", "blk"), None),
            P(("dp", "blk"), None),
            P(("dp", "blk"), None),
            P(("dp", "blk"), None),
            P(("dp", "blk")),
            P(("dp", "blk")),
            P(("dp", "blk")),
            P(("dp", "blk")),
        ),
        check_vma=False,
    )
```

```python
import functools

import jax
import jax.numpy as jnp
import numpy as np
from jax import lax
from jax.experimental import pallas as pl
from jax.experimental.pallas import tpu as pltpu
from jax.sharding import PartitionSpec as P

HEADS = 12


NEG = -1e30
EPS = 1e-05
BASE = 1000.0


def doc_layout(lengths_row, positions):
    bounds = jnp.cumsum(lengths_row)
    passed = positions[:, None] >= bounds[None, :]
    segment = jnp.sum(passed.astype(jnp.int32), axis=1)
    begins = jnp.sum(jnp.where(passed, lengths_row[None, :], 0), axis=1)
    return (segment, positions - begins)


def rotary(vectors, offsets):
    half_size = vectors.shape[-1] // 2
    frequency = BASE ** (-2.0 * jnp.arange(half_size, dtype=jnp.float32) / vectors.shape[-1])
    angles = offsets.astype(jnp.float32)[:, None] * frequency[None, :]
    cosine = jnp.concatenate([jnp.cos(angles), jnp.cos(angles)], axis=1)[:, None, :]
    sine_rows = jnp.concatenate([jnp.sin(angles), jnp.sin(angles)], axis=1)[:, None, :]
    first_half = vectors[..., :half_size]
    second_half = vectors[..., half_size:]
    turned = jnp.concatenate([-second_half, first_half], axis=-1)
    return vectors * cosine + turned * sine_rows


def layer_norm(residual, gain_row, bias_row):
    row_mean = jnp.mean(residual, axis=-1, keepdims=True)
    centered = residual - row_mean
    variance = jnp.mean(centered * centered, axis=-1, keepdims=True)
    return centered * lax.rsqrt(variance + EPS) * gain_row + bias_row


def contract_rows(left, right):
    return lax.dot_general(
        left, right, (((0,), (0,)), ((), ())), preferred_element_type=jnp.float32
    )


def contract_cols(left, right):
    return lax.dot_general(
        left, right, (((1,), (1,)), ((), ())), preferred_element_type=jnp.float32
    )


def tile_scores(query_tile, key_tile, seg_query, seg_key, score_scale):
    scores = (
        jnp.einsum("qhd,khd->hqk", query_tile, key_tile, preferred_element_type=jnp.float32)
        * score_scale
    )
    allowed = (seg_query[:, None] == seg_key[None, :])[None, :, :]
    return (jnp.where(allowed, scores, NEG), allowed)


def run_groups(pieces, group, lengths_row, seg_query, carried, tile_fn, extra_shape):
    group_count = pieces[0].shape[0] // group

    def group_step(carried_in, number):
        offset = number * group
        tile_set = tuple(
            (lax.dynamic_slice_in_dim(piece_rows, offset, group, 0) for piece_rows in pieces)
        )
        positions = offset + jnp.arange(group, dtype=jnp.int32)
        seg_key, unused_offsets = doc_layout(lengths_row, positions)
        touches = (seg_key[0] <= seg_query[-1]) & (seg_query[0] <= seg_key[-1])

        def active(state_in):
            return tile_fn(state_in, tile_set, seg_key)

        def skipped(state_in):
            return (state_in, jnp.zeros(extra_shape, jnp.float32))

        return lax.cond(touches, active, skipped, carried_in)

    return lax.scan(group_step, carried, jnp.arange(group_count, dtype=jnp.int32))


def shards(
    inputs,
    doc_lengths,
    project_in,
    project_out,
    gate_weight,
    up_weight,
    down_weight,
    first_gain,
    first_bias,
    second_gain,
    second_bias,
    cotangent,
):
    group = inputs.shape[1]
    width = inputs.shape[2]
    head_count = HEADS
    head_size = width // head_count
    score_scale = head_size ** (-0.5)
    cycle_rank = lax.axis_index("blk")
    positions = cycle_rank * group + jnp.arange(group, dtype=jnp.int32)
    lengths_row = doc_lengths[0]
    seg_query, offsets = doc_layout(lengths_row, positions)
    keep_mask = seg_query < lengths_row.shape[0] - 1
    keep_float = keep_mask.astype(jnp.float32)
    fetched = (
        lax.all_gather(project_in, ("dp", "blk"), axis=0, tiled=True),
        lax.all_gather(project_out, ("dp", "blk"), axis=0, tiled=True),
        lax.all_gather(gate_weight, ("dp", "blk"), axis=0, tiled=True),
        lax.all_gather(up_weight, ("dp", "blk"), axis=0, tiled=True),
        lax.all_gather(down_weight, ("dp", "blk"), axis=0, tiled=True),
        lax.all_gather(first_gain, ("dp", "blk"), axis=0, tiled=True),
        lax.all_gather(first_bias, ("dp", "blk"), axis=0, tiled=True),
        lax.all_gather(second_gain, ("dp", "blk"), axis=0, tiled=True),
        lax.all_gather(second_bias, ("dp", "blk"), axis=0, tiled=True),
    )
    full_in, full_out, full_gate, full_up, full_down = (
        fetched[0],
        fetched[1],
        fetched[2],
        fetched[3],
        fetched[4],
    )
    gain_one = fetched[5].astype(jnp.float32)
    bias_one = fetched[6].astype(jnp.float32)
    gain_two = fetched[7].astype(jnp.float32)
    bias_two = fetched[8].astype(jnp.float32)
    tokens_low = inputs[0]
    tokens_f = tokens_low.astype(jnp.float32)
    joined = jnp.dot(tokens_low, full_in, preferred_element_type=jnp.float32)
    query_raw = joined[:, :width].reshape(group, head_count, head_size)
    key_raw = joined[:, width : 2 * width].reshape(group, head_count, head_size)
    value_low = joined[:, 2 * width :].astype(jnp.bfloat16)
    query_rot, query_pull = jax.vjp(lambda vectors: rotary(vectors, offsets), query_raw)
    key_rot, key_pull = jax.vjp(lambda vectors: rotary(vectors, offsets), key_raw)
    query_low = query_rot.astype(jnp.bfloat16)
    key_low = key_rot.reshape(group, width).astype(jnp.bfloat16)

    def stats_tile(carried, tile_set, seg_key):
        row_top, row_total = carried
        key_tile = tile_set[0].reshape(group, head_count, head_size)
        scores, allowed = tile_scores(query_low, key_tile, seg_query, seg_key, score_scale)
        new_top = jnp.maximum(row_top, jnp.max(scores, axis=2))
        shrink = jnp.exp(row_top - new_top)
        added = jnp.sum(jnp.where(allowed, jnp.exp(scores - new_top[:, :, None]), 0.0), axis=2)
        return ((new_top, row_total * shrink + added), jnp.zeros((1,), jnp.float32))

    init_stats = (
        jnp.full((head_count, group), NEG, jnp.float32),
        jnp.zeros((head_count, group), jnp.float32),
    )
    carried = init_stats
    carried, unused = run_groups(
        (lax.all_gather(key_low, "blk", axis=0, tiled=True),),
        group,
        lengths_row,
        seg_query,
        carried,
        stats_tile,
        (1,),
    )
    row_top, row_total = carried
    log_total = row_top + jnp.log(row_total)

    def output_tile(accum, tile_set, seg_key):
        key_tile = tile_set[0].reshape(group, head_count, head_size)
        value_tile = tile_set[1].reshape(group, head_count, head_size)
        scores, allowed = tile_scores(query_low, key_tile, seg_query, seg_key, score_scale)
        prob_low = jnp.where(allowed, jnp.exp(scores - log_total[:, :, None]), 0.0).astype(
            jnp.bfloat16
        )
        accum = accum + jnp.einsum(
            "hqk,khd->qhd", prob_low, value_tile, preferred_element_type=jnp.float32
        )
        return (accum, jnp.zeros((1,), jnp.float32))

    zero_accum = jnp.zeros((group, head_count, head_size), jnp.float32)
    accum = zero_accum
    accum, unused = run_groups(
        (
            lax.all_gather(key_low, "blk", axis=0, tiled=True),
            lax.all_gather(value_low, "blk", axis=0, tiled=True),
        ),
        group,
        lengths_row,
        seg_query,
        accum,
        output_tile,
        (1,),
    )
    attend_low = (accum * keep_float[:, None, None]).reshape(group, width).astype(jnp.bfloat16)
    branch = jnp.dot(attend_low, full_out, preferred_element_type=jnp.float32)
    residual_one = tokens_f + branch
    hidden, norm_one_pull = jax.vjp(layer_norm, residual_one, gain_one, bias_one)
    hidden_low = hidden.astype(jnp.bfloat16)
    gate_pre = jnp.dot(hidden_low, full_gate, preferred_element_type=jnp.float32)
    up_pre = jnp.dot(hidden_low, full_up, preferred_element_type=jnp.float32)
    activated, swiglu_pull = jax.vjp(
        lambda gate_in, up_in: jax.nn.silu(gate_in) * up_in, gate_pre, up_pre
    )
    active_low = activated.astype(jnp.bfloat16)
    mlp_out = jnp.dot(active_low, full_down, preferred_element_type=jnp.float32)
    outputs_f, norm_two_pull = jax.vjp(layer_norm, hidden + mlp_out, gain_two, bias_two)
    refetched = (
        lax.all_gather(project_in, ("dp", "blk"), axis=0, tiled=True),
        lax.all_gather(project_out, ("dp", "blk"), axis=0, tiled=True),
        lax.all_gather(gate_weight, ("dp", "blk"), axis=0, tiled=True),
        lax.all_gather(up_weight, ("dp", "blk"), axis=0, tiled=True),
        lax.all_gather(down_weight, ("dp", "blk"), axis=0, tiled=True),
    )
    full_in, full_out, full_gate, full_up, full_down = (
        refetched[0],
        refetched[1],
        refetched[2],
        refetched[3],
        refetched[4],
    )
    d_res_two, second_gain_part, second_bias_part = norm_two_pull(cotangent[0].astype(jnp.float32))
    d_mlp_low = d_res_two.astype(jnp.bfloat16)
    down_part = contract_rows(active_low, d_mlp_low)
    d_active = contract_cols(d_mlp_low, full_down)
    d_gate, d_up = swiglu_pull(d_active)
    d_gate_low = d_gate.astype(jnp.bfloat16)
    d_up_low = d_up.astype(jnp.bfloat16)
    gate_part = contract_rows(hidden_low, d_gate_low)
    up_part = contract_rows(hidden_low, d_up_low)
    d_hidden = d_res_two + contract_cols(d_gate_low, full_gate) + contract_cols(d_up_low, full_up)
    d_res_one, first_gain_part, first_bias_part = norm_one_pull(d_hidden)
    d_branch_low = d_res_one.astype(jnp.bfloat16)
    out_part = contract_rows(attend_low, d_branch_low)
    d_attend = contract_cols(d_branch_low, full_out).astype(jnp.bfloat16)
    d_attend_low = (d_attend * keep_mask[:, None].astype(jnp.bfloat16)).reshape(
        group, head_count, head_size
    )
    delta = jnp.einsum("qhd,qhd->hq", d_attend_low.astype(jnp.float32), accum)

    def back_tile(grad_query, tile_set, seg_key):
        key_tile = tile_set[0].reshape(group, head_count, head_size)
        value_tile = tile_set[1].reshape(group, head_count, head_size)
        scores, allowed = tile_scores(query_low, key_tile, seg_query, seg_key, score_scale)
        prob_rows = jnp.where(allowed, jnp.exp(scores - log_total[:, :, None]), 0.0)
        d_probs = jnp.einsum(
            "qhd,khd->hqk", d_attend_low, value_tile, preferred_element_type=jnp.float32
        )
        d_score_low = (prob_rows * (d_probs - delta[:, :, None])).astype(jnp.bfloat16)
        grad_query = (
            grad_query
            + jnp.einsum("hqk,khd->qhd", d_score_low, key_tile, preferred_element_type=jnp.float32)
            * score_scale
        )
        grad_key = (
            jnp.einsum("hqk,qhd->khd", d_score_low, query_low, preferred_element_type=jnp.float32)
            * score_scale
        )
        grad_value = jnp.einsum(
            "hqk,qhd->khd",
            prob_rows.astype(jnp.bfloat16),
            d_attend_low,
            preferred_element_type=jnp.float32,
        )
        return (
            grad_query,
            jnp.concatenate(
                [grad_key.reshape(group, width), grad_value.reshape(group, width)], axis=1
            ),
        )

    grad_query = zero_accum
    grad_query, blocks = run_groups(
        (
            lax.all_gather(key_low, "blk", axis=0, tiled=True),
            lax.all_gather(value_low, "blk", axis=0, tiled=True),
        ),
        group,
        lengths_row,
        seg_query,
        grad_query,
        back_tile,
        (group, 2 * width),
    )
    blocks = blocks.reshape(-1, 2 * width)
    back_result = (grad_query, blocks)
    grad_query = back_result[0]
    owned_pairs = lax.psum_scatter(
        back_result[1].astype(jnp.bfloat16), "blk", scatter_dimension=0, tiled=True
    ).astype(jnp.float32)
    key_sum = owned_pairs[:, :width]
    value_sum = owned_pairs[:, width:]
    d_query_pre = query_pull(grad_query.astype(jnp.bfloat16).astype(jnp.float32))[0]
    d_key_low = key_sum.astype(jnp.bfloat16).astype(jnp.float32)
    d_key_pre = key_pull(d_key_low.reshape(group, head_count, head_size))[0]
    d_value_low = value_sum.astype(jnp.bfloat16).astype(jnp.float32)
    d_joined_low = jnp.concatenate(
        [d_query_pre.reshape(group, width), d_key_pre.reshape(group, width), d_value_low], axis=1
    ).astype(jnp.bfloat16)
    in_part = contract_rows(tokens_low, d_joined_low)
    input_grad = (d_res_one + contract_cols(d_joined_low, full_in)).astype(jnp.bfloat16)
    by_rows = (
        lax.psum_scatter(
            in_part.astype(jnp.bfloat16), "dp", scatter_dimension=0, tiled=True
        ).astype(jnp.float32),
        lax.psum_scatter(
            out_part.astype(jnp.bfloat16), "dp", scatter_dimension=0, tiled=True
        ).astype(jnp.float32),
        lax.psum_scatter(
            gate_part.astype(jnp.bfloat16), "dp", scatter_dimension=0, tiled=True
        ).astype(jnp.float32),
        lax.psum_scatter(
            up_part.astype(jnp.bfloat16), "dp", scatter_dimension=0, tiled=True
        ).astype(jnp.float32),
        lax.psum_scatter(
            down_part.astype(jnp.bfloat16), "dp", scatter_dimension=0, tiled=True
        ).astype(jnp.float32),
        lax.psum_scatter(
            first_gain_part.astype(jnp.bfloat16), "dp", scatter_dimension=0, tiled=True
        ).astype(jnp.float32),
        lax.psum_scatter(
            first_bias_part.astype(jnp.bfloat16), "dp", scatter_dimension=0, tiled=True
        ).astype(jnp.float32),
        lax.psum_scatter(
            second_gain_part.astype(jnp.bfloat16), "dp", scatter_dimension=0, tiled=True
        ).astype(jnp.float32),
        lax.psum_scatter(
            second_bias_part.astype(jnp.bfloat16), "dp", scatter_dimension=0, tiled=True
        ).astype(jnp.float32),
    )
    summed = (
        lax.psum_scatter(
            by_rows[0].astype(jnp.bfloat16), "blk", scatter_dimension=0, tiled=True
        ).astype(jnp.float32),
        lax.psum_scatter(
            by_rows[1].astype(jnp.bfloat16), "blk", scatter_dimension=0, tiled=True
        ).astype(jnp.float32),
        lax.psum_scatter(
            by_rows[2].astype(jnp.bfloat16), "blk", scatter_dimension=0, tiled=True
        ).astype(jnp.float32),
        lax.psum_scatter(
            by_rows[3].astype(jnp.bfloat16), "blk", scatter_dimension=0, tiled=True
        ).astype(jnp.float32),
        lax.psum_scatter(
            by_rows[4].astype(jnp.bfloat16), "blk", scatter_dimension=0, tiled=True
        ).astype(jnp.float32),
        lax.psum_scatter(
            by_rows[5].astype(jnp.bfloat16), "blk", scatter_dimension=0, tiled=True
        ).astype(jnp.float32),
        lax.psum_scatter(
            by_rows[6].astype(jnp.bfloat16), "blk", scatter_dimension=0, tiled=True
        ).astype(jnp.float32),
        lax.psum_scatter(
            by_rows[7].astype(jnp.bfloat16), "blk", scatter_dimension=0, tiled=True
        ).astype(jnp.float32),
        lax.psum_scatter(
            by_rows[8].astype(jnp.bfloat16), "blk", scatter_dimension=0, tiled=True
        ).astype(jnp.float32),
    )
    return (
        outputs_f.astype(jnp.bfloat16)[None],
        input_grad[None],
        summed[0],
        summed[1],
        summed[2],
        summed[3],
        summed[4],
        summed[5],
        summed[6],
        summed[7],
        summed[8],
    )


MESH_IDS = pl.DeviceIdType.MESH
LANES = 128
HALF = 64
QUART = 32
DTF = 64
DTB = 64


def mm(left, right):
    return lax.dot_general(
        left, right, (((1,), (0,)), ((), ())), preferred_element_type=jnp.float32
    )


def mt(left, right):
    return lax.dot_general(
        left, right, (((1,), (1,)), ((), ())), preferred_element_type=jnp.float32
    )


def tm(left, right):
    return lax.dot_general(
        left, right, (((0,), (0,)), ((), ())), preferred_element_type=jnp.float32
    )


def window_at(value, start):
    aligned = min(max(start // LANES * LANES, 0), value.shape[1] - LANES)
    if aligned == start:
        return value[:, aligned : aligned + LANES]
    aligned = min(aligned, value.shape[1] - 2 * LANES)
    two = value[:, aligned : aligned + 2 * LANES]
    return pltpu.roll(two, (aligned - start) % (2 * LANES), 1)[:, :LANES]


def gather_lanes(value, block, first, source):
    lanes = lax.broadcasted_iota(jnp.int32, (1, LANES), 1)
    result = None
    for number in range(first // block, (first + LANES - 1) // block + 1):
        piece = window_at(value, source(number, first))
        begin = number * block - first
        result = piece if result is None else jnp.where(lanes < begin, result, piece)
    return result


class Wire:
    def __init__(self, send_sem, recv_sem, is_inner):
        self.send_sem, self.recv_sem, self.is_inner = send_sem, recv_sem, is_inner
        self.sends, self.slots = 0, 0
        self.sent = {None: [], True: [], False: []}

    def slot(self):
        self.slots += 1
        return self.slots - 1

    def copy(self, src, dst, peer, slot):
        self.sends += 1
        return pltpu.make_async_remote_copy(
            src_ref=src,
            dst_ref=dst,
            send_sem=self.send_sem.at[self.sends - 1],
            recv_sem=self.recv_sem.at[slot],
            device_id=peer,
            device_id_type=MESH_IDS,
        )

    def push(self, src, dst, peer, slot=None, inner=None):
        slot = self.slot() if slot is None else slot
        copy = self.copy(src, dst, peer, slot)
        self.sent[inner].append(copy)
        if inner is None:
            copy.start()
        else:
            pl.when(self.is_inner == inner)(copy.start)
        return slot

    def arrive(self, slot, dst, peer):
        pltpu.make_async_remote_copy(
            src_ref=dst,
            dst_ref=dst,
            send_sem=self.send_sem.at[0],
            recv_sem=self.recv_sem.at[slot],
            device_id=peer,
            device_id_type=MESH_IDS,
        ).wait_recv()

    def finish(self):
        for inner, copies in self.sent.items():

            def drain(copies=copies):
                for copy in copies:
                    copy.wait_send()

            if inner is None:
                drain()
            else:
                pl.when(self.is_inner == inner)(drain)


class Plane:
    def __init__(self, planes):
        dp, self.blk = lax.axis_index("dp"), lax.axis_index("blk")
        self.z, self.x = dp // 2, dp % 2
        self.dp = dp
        self.partner = self.z + 1 - 2 * (self.z % 2)
        self.other = planes // 2 - self.z // (planes // 2)
        self.outer = (planes - 1) * (self.other - 1)
        self.inner = ((self.z + 1) // 2) % 2
        self.order = (self.other, self.outer, self.partner, self.z)
        self.side = (self.z * 2 + (1 - self.x), self.blk)

    def at(self, plane):
        return (plane * 2 + self.x, self.blk)


class Spread:
    def __init__(self, wire, place, target, tail):
        self.wire, self.place, self.target = wire, place, target
        self.height, self.main = target.shape[1], target.shape[1] - tail

    def block(self, plane, column):
        return self.target.at[plane * 2 + column, 0 : self.main]

    def pair(self, plane):
        return self.target.at[pl.ds(plane * 2, 2), self.main : self.height]

    def along(self, own, slots):
        p = self.place
        self.wire.push(own, own, p.at(p.partner), slots[2], inner=False)
        self.wire.push(own, own, p.at(p.other), slots[0] + (1 - p.inner))

    def outward(self, own, slots):
        p = self.place
        self.wire.push(own, own, p.at(p.partner), slots[2], inner=True)

    def start(self):
        p, wire = self.place, self.wire
        self.z_slots = [wire.slot() for _ in range(3)]
        self.along(self.block(p.z, p.x), self.z_slots)

    def start_out(self):
        p = self.place
        self.outward(self.block(p.z, p.x), self.z_slots)

    def start_side(self):
        p, wire = self.place, self.wire
        self.x_slots = [wire.slot() for _ in range(4)]
        own = self.block(p.z, p.x)
        wire.push(own, own, p.side, self.x_slots[3])
        if self.main < self.height:
            self.out_slots = []
            self.rest_slot = wire.push(self.rest(p.x), self.rest(p.x), p.side)

    def tail(self):
        p, wire = self.place, self.wire
        rest = self.target.at[p.z * 2 + (1 - p.x), self.main : self.height]
        wire.arrive(self.rest_slot, rest, p.side)
        self.t_slots = [wire.slot() for _ in range(3)]
        self.along(self.pair(p.z), self.t_slots)

    def rest(self, column):
        p = self.place
        return self.target.at[p.z * 2 + column, self.main : self.height]

    def tail_out(self, own):
        p, wire = self.place, self.wire
        rest = self.rest(p.x if own else 1 - p.x)
        self.out_slots.append(wire.push(rest, rest, p.at(p.partner), inner=True))

    def relay(self, j, inner=None):
        p, wire = self.place, self.wire
        block = self.block(p.order[j], p.x)
        onward = wire.copy(block, block, p.side, self.x_slots[j])
        wire.sent[inner].append(onward)
        outward = None
        if j < 2 and inner is not False:
            outward = wire.copy(block, block, p.at(p.partner), self.z_slots[j])
            wire.sent[True].append(outward)

        def run():
            wire.arrive(self.z_slots[j], block, p.side)
            if outward is not None:
                if inner:
                    outward.start()
                else:
                    pl.when(wire.is_inner)(outward.start)
            onward.start()

        if inner is None:
            run()
        else:
            pl.when(wire.is_inner == inner)(run)

    def pass_tail(self, j):
        p, wire = self.place, self.wire
        pair = self.pair(p.order[j])
        copy = wire.copy(pair, pair, p.at(p.partner), self.t_slots[j])
        wire.sent[True].append(copy)

        @pl.when(wire.is_inner)
        def _():
            wire.arrive(self.t_slots[j], pair, p.side)
            copy.start()

    def settle_tail(self):
        p, wire = self.place, self.wire

        @pl.when(wire.is_inner)
        def _():
            wire.arrive(self.t_slots[2], self.pair(p.order[2]), p.side)

        @pl.when(jnp.logical_not(wire.is_inner))
        def _():
            for j in range(2):
                wire.arrive(self.t_slots[j], self.pair(p.order[j]), p.side)
            for slot, column in zip(self.out_slots, (p.x, 1 - p.x)):
                came = self.target.at[p.partner * 2 + column, self.main : self.height]
                wire.arrive(slot, came, p.side)

    def settle(self):
        p = self.place
        for j in range(4):
            self.wire.arrive(self.x_slots[j], self.block(p.order[j], 1 - p.x), p.side)


class Collect:
    def __init__(self, wire, place, buffers):
        self.wire, self.place = wire, place
        self.part, self.inbox, self.staged, self.landing = buffers[:4]
        self.height, self.main = self.part.shape[2], self.inbox.shape[1]
        self.split = self.main < self.height
        if self.split:
            self.t_landing, self.t_staged, self.t_cross, self.t_kept = buffers[4:]

    def pair(self, plane):
        return self.part.at[:, plane, self.main : self.height]

    def send_side(self, j):
        p = self.place
        plane = p.order[j]
        self.wire.push(
            self.part.at[1 - p.x, plane, 0 : self.main],
            self.inbox.at[plane],
            p.side,
            self.x_slots[j],
        )

    def send(self, order=(1, 0, 2, 3)):
        p, wire = self.place, self.wire
        self.x_slots = [wire.slot() for _ in range(4)]
        for j in order:
            self.send_side(j)
        self.z_slots = [wire.slot() for _ in range(4)]
        if self.split:
            self.t_slots = [wire.slot() for _ in range(4)]
            for j in (1, 0, 2):
                wire.push(
                    self.pair(p.order[j]),
                    self.t_landing.at[j],
                    p.at(p.partner),
                    self.t_slots[j],
                    inner=None if j == 2 else False,
                )

    def first(self, j):
        p, wire = self.place, self.wire
        plane = p.order[j]
        wire.arrive(self.x_slots[j], self.inbox.at[plane], p.side)
        both = self.part[p.x, plane, 0 : self.main].astype(jnp.float32)
        both = both + self.inbox[plane].astype(jnp.float32)
        self.staged[plane] = both.astype(jnp.bfloat16)
        wire.push(
            self.staged.at[plane],
            self.landing.at[j],
            p.at(p.partner),
            self.z_slots[j],
            inner=None if j == 2 else False,
        )

    def second(self, j):
        p, wire = self.place, self.wire
        plane = p.order[j]
        copy = wire.copy(self.staged.at[plane], self.landing.at[3], p.at(plane), self.z_slots[3])
        wire.sent[True].append(copy)

        @pl.when(wire.is_inner)
        def _():
            wire.arrive(self.z_slots[j], self.landing.at[j], p.side)
            both = self.staged[plane].astype(jnp.float32) + self.landing[j].astype(jnp.float32)
            self.staged[plane] = both.astype(jnp.bfloat16)
            copy.start()

    def second_tail(self, j):
        p, wire = self.place, self.wire
        plane = p.order[j]
        copy = wire.copy(self.t_staged.at[j], self.t_landing.at[3], p.at(plane), self.t_slots[3])
        wire.sent[True].append(copy)

        @pl.when(wire.is_inner)
        def _():
            wire.arrive(self.t_slots[j], self.t_landing.at[j], p.side)
            rest = self.part[:, plane, self.main : self.height].astype(jnp.float32)
            rest = rest + self.t_landing[j].astype(jnp.float32)
            self.t_staged[j] = rest.astype(jnp.bfloat16)
            copy.start()

    def tail(self):
        p, wire = self.place, self.wire
        for j in (2, 3):
            wire.arrive(self.t_slots[j], self.t_landing.at[j], p.side)

        def rest_of(column):
            rest = self.part[column, p.z, self.main : self.height].astype(jnp.float32)
            for j in (2, 3):
                rest = rest + self.t_landing[j, column].astype(jnp.float32)
            return rest

        self.t_kept[...] = rest_of(p.x)
        self.t_cross[0] = rest_of(1 - p.x).astype(jnp.bfloat16)
        self.cross_slot = wire.push(self.t_cross.at[0], self.t_cross.at[1], p.side)

    def total(self):
        p, wire = self.place, self.wire
        wire.arrive(self.x_slots[3], self.inbox.at[p.z], p.side)
        total = self.part[p.x, p.z, 0 : self.main].astype(jnp.float32)
        total = total + self.inbox[p.z].astype(jnp.float32)
        for j in (2, 3):
            wire.arrive(self.z_slots[j], self.landing.at[j], p.side)
            total = total + self.landing[j].astype(jnp.float32)
        if not self.split:
            return total
        wire.arrive(self.cross_slot, self.t_cross.at[1], p.side)
        rest = self.t_kept[...] + self.t_cross[1].astype(jnp.float32)
        return jnp.concatenate([total, rest], axis=0)


def fused(
    depth,
    lens,
    freq,
    xin_at,
    cot_at,
    in_at,
    gate_at,
    up_at,
    out_at,
    down_at,
    gain_a,
    bias_a,
    gain_b,
    bias_b,
    outputs_to,
    input_grad_to,
    g_in_to,
    g_mlp_to,
    g_out_to,
    g_down_to,
    cot,
    in_rows,
    gate_rows,
    up_rows,
    out_rows,
    outputs,
    input_grad,
    g_out,
    g_down,
    local_sem,
    xs,
    p_in,
    p_mlp,
    vectors_tab,
    r_in,
    r_mlp,
    s_out,
    w_in,
    w_value,
    w_gate,
    w_up,
    w_down,
    w_out,
    params,
    cos_tab,
    sin_tab,
    seg_tab,
    qm,
    kw,
    vw,
    prob,
    att,
    s_att,
    r_att,
    norm_one,
    hid,
    hs,
    gate_pre,
    up_pre,
    act,
    s_mix,
    r_mix,
    t_mix,
    dres_two,
    dms,
    dgate,
    dup,
    s_dh,
    r_dh,
    t_dh,
    dres_one,
    s_da,
    r_da,
    acc_q,
    acc_k,
    acc_v,
    dj,
    s_ig,
    r_ig,
    t_ig,
    sum_in,
    sum_gate,
    sum_up,
    sum_down,
    b_out,
    rb_out,
    tb_out,
    sum_out,
    f_gate,
    s_gmlp,
    r_gmlp,
    s_gin,
    r_gin,
    send_sem,
    recv_sem,
):
    planes, cols = depth, 4
    tok = xin_at.shape[0]
    row_len = tok * cols
    place = Plane(planes)
    dp, blk = place.dp, place.blk
    bf16, f32 = jnp.bfloat16, jnp.float32

    row_of, core_of = blk // 2, blk % 2
    near_at = row_of * 2 + (1 - core_of)
    across_at = (1 - row_of) * 2 + core_of
    corner_at = (1 - row_of) * 2 + (1 - core_of)
    near, across = (dp, near_at), (dp, across_at)

    def lane(k):
        return (dp, (blk + k) % cols)

    def lane_from(k):
        return (blk + cols - k) % cols

    lanes = range(1, cols)
    local = []

    def move(source, target):
        copy = pltpu.make_async_copy(source, target, local_sem.at[len(local)])
        local.append(copy)
        copy.start()
        return copy

    xin = xs.at[blk]
    in_load = move(in_at, in_rows)
    out_load = move(out_at, out_rows)
    down_load = move(down_at, w_down.at[dp])
    x_load = move(xin_at, xin)
    gate_load = move(gate_at, gate_rows)
    up_load = move(up_at, up_rows)
    cot_load = move(cot_at, cot)
    wire = Wire(send_sem, recv_sem, place.inner == 1)
    barrier = pltpu.get_barrier_semaphore()
    peers = [place.side, place.at(place.partner), place.at(place.other)]
    peers = peers + [lane(k) for k in lanes]
    for peer in peers:
        pl.semaphore_signal(barrier, inc=1, device_id=peer, device_id_type=MESH_IDS)
    far = place.at(place.outer)

    @pl.when(place.inner == 1)
    def _():
        pl.semaphore_signal(barrier, inc=1, device_id=far, device_id_type=MESH_IDS)


    rows = 24
    width = xin_at.shape[1]
    lane_ids = lax.broadcasted_iota(jnp.int32, (1, LANES), 1)
    low_half = lane_ids < HALF
    head_width = width // cols
    vectors_tab[...] = jnp.zeros_like(vectors_tab)
    for number, vector in enumerate((gain_a, bias_a, gain_b, bias_b)):
        vectors_tab[number : number + 1, 0:rows] = vector[...].astype(f32)
    free_lane = lax.broadcasted_iota(jnp.int32, (8, LANES), 0) + HALF
    to_lane = jnp.where(
        free_lane == lax.broadcasted_iota(jnp.int32, (8, LANES), 1), 1.0, 0.0
    ).astype(bf16)
    vector_columns = tm(vectors_tab[...].astype(bf16), to_lane)[0:rows]
    in_load.wait()
    joined_rows = in_rows[...].astype(f32)
    for j in range(cols):
        starts = [kind * width + j * head_width for kind in range(3)]
        windows = [window_at(joined_rows, start) for start in starts]
        windows.append(
            jnp.where(
                low_half,
                window_at(joined_rows, starts[0] + LANES),
                window_at(joined_rows, starts[1] + LANES - HALF),
            )
        )
        windows.append(
            jnp.where(low_half, window_at(joined_rows, starts[2] + LANES), vector_columns)
        )
        packed = jnp.concatenate(windows, axis=1)
        p_in[j] = jnp.concatenate(
            [packed, jnp.zeros((8, packed.shape[1]), f32)], axis=0
        ).astype(bf16)
    out_load.wait()
    halved = [out_rows[:, n * width // 2 : (n + 1) * width // 2].astype(f32) for n in range(2)]
    s_out[blk, dp] = jnp.concatenate(halved, axis=0).astype(bf16)
    pl.semaphore_wait(barrier, len(peers) + place.inner)

    def to_lanes(source_of, target):
        return [wire.push(source_of((blk + k) % cols), target.at[blk], lane(k)) for k in lanes]

    def from_lanes(slots, target):
        for k, slot in zip(lanes, slots):
            wire.arrive(slot, target.at[lane_from(k)], lane(k))

    every = pl.ds(0, tok)

    def gather_start(own, target, cut=every):
        return [
            wire.push(own.at[cut], target.at[blk, cut], across),
            wire.push(own.at[cut], target.at[blk, cut], near),
        ]

    def gather_relay(slots, target, cut=every):
        came = target.at[across_at, cut]
        wire.arrive(slots[0], came, across)
        slots.append(wire.push(came, came, near))

    def gather_done(slots, target, cut=every):
        wire.arrive(slots[1], target.at[near_at, cut], near)
        wire.arrive(slots[2], target.at[corner_at, cut], near)

    def sum_start(part, inbox, cut=every):
        return [
            wire.push(part.at[corner_at, cut], inbox.at[0, cut], near),
            wire.push(part.at[near_at, cut], inbox.at[1, cut], near),
        ]

    def sum_relay(slots, part, inbox, staged, cut=every):
        wire.arrive(slots[0], inbox.at[0, cut], near)
        both = part[across_at, cut].astype(f32) + inbox[0, cut].astype(f32)
        staged[cut] = both.astype(bf16)
        slots.append(wire.push(staged.at[cut], inbox.at[2, cut], across))

    def sum_done(slots, part, inbox, cut=every):
        wire.arrive(slots[1], inbox.at[1, cut], near)
        total = part[blk, cut].astype(f32) + inbox[1, cut].astype(f32)
        wire.arrive(slots[2], inbox.at[2, cut], across)
        return total + inbox[2, cut].astype(f32)

    in_slots = to_lanes(lambda to: p_in.at[to], r_in)
    down_load.wait()
    tail = 0
    out_spread = Spread(wire, place, s_out.at[blk], 0)
    out_spread.start()
    out_spread.start_out()
    out_spread.start_side()
    down_spread = Spread(wire, place, w_down, DTF)
    down_spread.start()
    down_spread.start_out()
    down_spread.start_side()
    down_spread.tail_out(True)
    gate_load.wait()
    up_load.wait()
    units = gate_rows.shape[1] // cols
    unit_block = units // (planes * 2)
    for at, weight in ((0, gate_rows), (rows, up_rows)):
        whole = weight[...].astype(f32)
        for j in range(cols):
            packed = jnp.concatenate(
                [
                    gather_lanes(
                        whole,
                        unit_block,
                        n * LANES,
                        lambda ring_at, lane: lane + (cols - 1) * unit_block * ring_at + unit_block * j,
                    )
                    for n in range(units // LANES)
                ],
                axis=1,
            )
            p_mlp[j, at : at + rows] = packed.astype(bf16)
    mlp_slots = to_lanes(lambda to: p_mlp.at[to], r_mlp)
    x_load.wait()
    x_slots = gather_start(xin, xs)
    r_in[blk] = p_in[blk]
    r_mlp[blk] = p_mlp[blk]

    lengths = [lens[0, j] for j in range(lens.shape[1])]

    def layout(positions):
        segment = jnp.zeros_like(positions)
        begins = jnp.zeros_like(positions)
        bound = jnp.int32(0)
        for length in lengths:
            bound = bound + length
            passed = positions >= bound
            segment = segment + jnp.where(passed, 1, 0)
            begins = begins + jnp.where(passed, length, 0)
        return segment, positions - begins

    seg_rows, offsets = layout(lax.broadcasted_iota(jnp.int32, (row_len, LANES), 0))
    seg_tab[...] = seg_rows
    seg_key = layout(lax.broadcasted_iota(jnp.int32, (8, row_len), 1))[0][0:1]
    front = lane_ids % HALF < QUART
    angles = offsets.astype(f32) * freq[0:1]
    cos_tab[...] = jnp.cos(angles)
    sin_tab[...] = jnp.where(front, -1.0, 1.0) * jnp.sin(angles)

    def turn(window):
        return jnp.where(
            front, pltpu.roll(window, LANES - QUART, 1), pltpu.roll(window, QUART, 1)
        )

    from_lanes(in_slots, r_in)
    own_rows = cols * rows
    fold_rows = own_rows // 2
    heads_width = 4 * LANES

    def folded(last, tile):
        fold = jnp.where(low_half, last[0:fold_rows], pltpu.roll(last[fold_rows:], HALF, 1))
        chunks = [fold[n * 16 : (n + 1) * 16] for n in range(3)]
        chunks.append(jnp.concatenate([tile, jnp.zeros((8, LANES), f32)], axis=0))
        return jnp.concatenate(chunks, axis=1)

    def unfolded(below):
        fold = jnp.concatenate([below[:, n * LANES : (n + 1) * LANES] for n in range(3)], axis=0)
        return jnp.concatenate([fold, pltpu.roll(fold, HALF, 1)], axis=0), below[0:8, 3 * LANES :]

    gathered = jnp.concatenate(
        [r_in[j, 0:rows, :].astype(f32) for j in range(cols)], axis=0
    )
    last = gathered[:, heads_width:]
    padded = jnp.concatenate([last, jnp.zeros((LANES - own_rows, LANES), f32)], axis=0)
    w_in[dp] = jnp.concatenate(
        [gathered[:, :heads_width], folded(last, mt(to_lane, padded.astype(bf16)))], axis=0
    ).astype(bf16)
    in_spread = Spread(wire, place, w_in, tail)
    in_spread.start()
    in_spread.start_out()
    in_spread.start_side()
    from_lanes(mlp_slots, r_mlp)
    mlp_own = [r_mlp[j].astype(f32) for j in range(cols)]
    w_gate[dp] = jnp.concatenate([part[0:rows] for part in mlp_own], axis=0).astype(bf16)
    w_up[dp] = jnp.concatenate([part[rows:] for part in mlp_own], axis=0).astype(bf16)
    gate_spread = Spread(wire, place, w_gate, tail)
    up_spread = Spread(wire, place, w_up, tail)
    gate_spread.start()
    gate_spread.start_side()
    up_spread.start()
    out_spread.relay(2)
    for spread in (out_spread, down_spread):
        spread.relay(0, inner=True)
        spread.relay(1, inner=True)
    in_spread.relay(2)
    out_spread.relay(0, inner=False)
    out_spread.relay(1, inner=False)
    in_spread.relay(0)
    down_spread.relay(2)
    in_spread.relay(1)
    up_spread.start_side()
    gate_spread.start_out()
    up_spread.start_out()
    down_spread.tail()
    gate_spread.relay(0, inner=True)
    gate_spread.relay(1, inner=True)
    gather_relay(x_slots, xs)
    out_spread.settle()
    shards_here = pl.ds(0, planes * 2)
    out_lanes = gather_start(s_out.at[blk], s_out, shards_here)
    gate_spread.relay(2)
    up_spread.relay(2)
    gather_done(x_slots, xs)
    in_spread.settle()

    group = 2
    chunk = group * tok

    tiles = []
    for d in range(planes * 2):
        values, tile = unfolded(w_in[d, own_rows:, :].astype(f32))
        w_value[d] = jnp.where(low_half, values, 0.0).astype(bf16)
        tiles.append(tile)

    def project(step, carry):
        start = pl.multiple_of(step * chunk, chunk)
        here = pl.ds(start, chunk)
        tokens = xs[pl.ds(step * group, group)].reshape(chunk, width)
        joined = mm(tokens, w_in[:, 0:own_rows, :].reshape(width, heads_width))
        cosine, sine = cos_tab[here, :], sin_tab[here, :]

        def rotate(number):
            window = joined[:, number * LANES : (number + 1) * LANES]
            return window * cosine + turn(window) * sine

        scale = HALF ** -0.5
        queries = rotate(0).astype(bf16).astype(f32) * scale
        qm[0, here, :] = jnp.where(low_half, queries, 0.0).astype(bf16)
        qm[1, here, :] = jnp.where(low_half, 0.0, queries).astype(bf16)
        kw[0, here, :] = rotate(1).astype(bf16)
        vw[0, here, :] = joined[:, 2 * LANES : 3 * LANES].astype(bf16)
        both = rotate(3)
        qm[2, here, :] = jnp.where(low_half, both.astype(bf16).astype(f32) * scale, 0.0).astype(bf16)
        kw[1, here, :] = jnp.where(low_half, pltpu.roll(both, HALF, 1), 0.0).astype(bf16)
        vw[1, here, :] = mm(tokens, w_value[...].reshape(width, LANES)).astype(bf16)
        return carry

    lax.fori_loop(0, cols // group, project, 0)

    def attend(head):
        window = head // 2

        def step_fn(step, carry):
            here = pl.ds(pl.multiple_of(step * chunk, chunk), chunk)
            scores = mt(qm[head, here, :], kw[window])
            allowed = seg_tab[here, :][:, 0:1] == seg_key
            scores = jnp.where(allowed, scores, NEG)
            top = jnp.max(scores, axis=1, keepdims=True)
            raised = jnp.exp(scores - top)
            total = jnp.sum(raised, axis=1, keepdims=True)
            prob_low = (raised * (1.0 / total)).astype(bf16)
            prob[head, here, :] = prob_low
            mixed = mm(prob_low, vw[window])
            if head == 1:
                mixed = jnp.where(low_half, att[0, here, :], mixed)
            att[window, here, :] = mixed
            return carry

        lax.fori_loop(0, row_len // chunk, step_fn, 0)

    up_spread.relay(0, inner=True)
    attend(0)
    attend(1)
    up_spread.relay(1, inner=True)
    attend(2)
    last_segment = lens.shape[1] - 1
    for j in range(cols):
        here = slice(j * tok, (j + 1) * tok)
        kept = seg_tab[here, :] < last_segment
        s_att[j, :, 0:LANES] = jnp.where(kept, att[0, here, :], 0.0).astype(bf16)
        s_att[j, :, LANES : 2 * LANES] = jnp.where(kept, att[1, here, :], 0.0).astype(bf16)
    att_slots = to_lanes(lambda to: s_att.at[to], r_att)
    r_att[blk] = s_att[blk]

    down_spread.tail_out(False)
    gather_relay(out_lanes, s_out, shards_here)
    gate_spread.relay(0, inner=False)
    gate_spread.relay(1, inner=False)
    for j in range(2):
        down_spread.pass_tail(j)
    gather_done(out_lanes, s_out, shards_here)
    shards = planes * 2 * cols
    per_quarter = shards // cols
    head_rows = per_quarter * rows
    for quarter in range(cols):
        slots = [
            s_out[s % cols, s // cols].astype(f32)
            for s in range(quarter * per_quarter, (quarter + 1) * per_quarter)
        ]
        w_out[quarter, 0:head_rows, :] = jnp.concatenate(
            [
                jnp.concatenate([slot[n * rows : (n + 1) * rows] for slot in slots], axis=0)
                for n in range(2)
            ],
            axis=1,
        ).astype(bf16)
        w_out[quarter, head_rows:, :] = jnp.zeros(
            (w_out.shape[1] - head_rows, width), bf16
        )
    for n in range(width // LANES):
        first = n * LANES
        result = None
        for d in range(first // own_rows, (first + LANES - 1) // own_rows + 1):
            begin = d * own_rows - first
            piece = pltpu.roll(tiles[d], begin % LANES, 1)
            result = piece if result is None else jnp.where(lane_ids < begin, result, piece)
        params[:, first : first + LANES] = result
    gain_one, bias_one = params[0:1, :], params[1:2, :]
    gain_two, bias_two = params[2:3, :], params[3:4, :]

    def normalize(residual):
        centered = residual - jnp.mean(residual, axis=1, keepdims=True)
        variance = jnp.mean(centered * centered, axis=1, keepdims=True)
        spread = lax.rsqrt(variance + EPS)
        return centered * spread, spread

    def normalize_back(grad, normal, spread, gain):
        inner = grad * gain
        mean_inner = jnp.mean(inner, axis=1, keepdims=True)
        mean_both = jnp.mean(inner * normal, axis=1, keepdims=True)
        return (inner - mean_inner - normal * mean_both) * spread

    def column_sum(value):
        return jnp.sum(value, axis=0, keepdims=True)

    from_lanes(att_slots, r_att)
    branch = mm(r_att[0], w_out[0])
    for quarter in range(1, cols):
        branch = branch + mm(r_att[quarter], w_out[quarter])
    normal, spread_one = normalize(xin[...].astype(f32) + branch)
    norm_one[...] = normal
    hidden = normal * gain_one + bias_one
    hid[...] = hidden
    hs[blk] = hidden.astype(bf16)
    hid_slots = gather_start(hs.at[blk], hs)
    up_spread.relay(0, inner=False)
    up_spread.relay(1, inner=False)
    down_spread.relay(0, inner=False)
    down_spread.relay(1, inner=False)
    gather_relay(hid_slots, hs)
    gate_spread.settle()
    gather_done(hid_slots, hs)

    wide = 256
    strips = units // wide

    def each_strip(body):
        def step_fn(step, carry):
            body(pl.ds(pl.multiple_of(step * wide, wide), wide))
            return carry

        lax.fori_loop(0, strips, step_fn, 0)

    def expand_gate(here):
        tokens = hs[...].reshape(row_len, width)
        gate_pre[:, here] = mm(tokens, w_gate[:, :, here].reshape(width, wide))

    def expand_up(here):
        tokens = hs[...].reshape(row_len, width)
        up = mm(tokens, w_up[:, :, here].reshape(width, wide))
        gate = gate_pre[:, here]
        up_pre[:, here] = up
        act[:, here] = (gate / (1.0 + jnp.exp(-gate)) * up).astype(bf16)

    each_strip(expand_gate)
    up_spread.settle()
    each_strip(expand_up)
    down_spread.settle()
    down_spread.settle_tail()

    def contract(step, carry):
        here = pl.ds(pl.multiple_of(step * wide, wide), wide)
        mixed = mm(act[...], w_down[:, :, here].reshape(units, wide))
        s_mix[:, :, here] = mixed.reshape(cols, tok, wide).astype(bf16)
        return carry

    lax.fori_loop(0, width // wide, contract, 0)
    pieces = 4
    cot_load.wait()
    halves = [pl.ds(n * tok // pieces, tok // pieces) for n in range(pieces)]
    mix_slots = [sum_start(s_mix, r_mix, cut) for cut in halves]
    for slots, cut in zip(mix_slots, halves):
        sum_relay(slots, s_mix, r_mix, t_mix, cut)
    second_gain, second_bias, dm_slots = 0.0, 0.0, []
    for slots, cut in zip(mix_slots, halves):
        mlp_out = sum_done(slots, s_mix, r_mix, cut)
        normal, spread_two = normalize(hid[cut, :] + mlp_out)
        outputs[cut, :] = (normal * gain_two + bias_two).astype(bf16)
        grad = cot[cut, :].astype(f32)
        second_gain = second_gain + column_sum(grad * normal)
        second_bias = second_bias + column_sum(grad)
        d_two = normalize_back(grad, normal, spread_two, gain_two)
        dres_two[cut, :] = d_two
        dms[blk, cut] = d_two.astype(bf16)
        dm_slots.append(gather_start(dms.at[blk], dms, cut))
    writes = [move(outputs, outputs_to)]
    for slots, cut in zip(dm_slots, halves):
        gather_relay(slots, dms, cut)
    for slots, cut in zip(dm_slots, halves):
        gather_done(slots, dms, cut)

    down_sum = Collect(wire, place, sum_down)
    gate_sum = Collect(wire, place, sum_gate)
    up_sum = Collect(wire, place, sum_up)
    in_sum = Collect(wire, place, sum_in)
    out_sum = Collect(wire, place, sum_out)
    half = 4

    def fill_parts(part, left_of, right, more=lambda product, here: product):
        height = part.shape[2]

        def step_fn(step, carry):
            here = pl.ds(pl.multiple_of(step * half * height, LANES), half * height)
            product = more(tm(left_of(here), right()), here)
            for j in range(half):
                part[j % 2, step * (half // 2) + j // 2] = product[
                    j * height : (j + 1) * height
                ].astype(bf16)
            return carry

        lax.fori_loop(0, planes * 2 // half, step_fn, 0)

    fill_parts(down_sum.part, lambda here: act[:, here], lambda: dms[...].reshape(row_len, width))
    down_sum.send()

    block = w_down.shape[1]

    def active_grads(step, carry):
        here = pl.ds(pl.multiple_of(step * half * block, LANES), half * block)
        d_active = mt(
            dms[...].reshape(row_len, width),
            w_down[pl.ds(step * half, half)].reshape(half * block, width),
        )
        gate, up = gate_pre[:, here], up_pre[:, here]
        sg = 1.0 / (1.0 + jnp.exp(-gate))
        dgate[:, here] = (d_active * up * sg * (1.0 + gate * (1.0 - sg))).astype(bf16)
        dup[:, here] = (d_active * gate * sg).astype(bf16)
        return carry

    lax.fori_loop(0, planes * 2 // half, active_grads, 0)
    block = w_gate.shape[1]

    def hidden_rows(here):
        return hs[:, :, here].reshape(row_len, half * block)

    fill_parts(gate_sum.part, hidden_rows, lambda: dgate[...])
    gate_sum.send()
    def hidden_grads(step, carry):
        here = pl.ds(pl.multiple_of(step * half * block, LANES), half * block)
        those = pl.ds(step * half, half)
        mixed = mt(dgate[...], w_gate[those].reshape(half * block, units)) + mt(
            dup[...], w_up[those].reshape(half * block, units)
        )
        s_dh[:, :, here] = mixed.reshape(cols, tok, half * block).astype(bf16)
        return carry

    lax.fori_loop(0, planes * 2 // half, hidden_grads, 0)
    dh_slots = sum_start(s_dh, r_dh)

    sum_relay(dh_slots, s_dh, r_dh, t_dh)
    fill_parts(up_sum.part, hidden_rows, lambda: dup[...])
    up_sum.send()
    down_sum.first(1)
    down_sum.first(0)
    d_hidden = dres_two[...] + sum_done(dh_slots, s_dh, r_dh)
    down_sum.first(2)
    normal = norm_one[...]
    first_gain = column_sum(d_hidden * normal)
    first_bias = column_sum(d_hidden)
    d_one = normalize_back(d_hidden, normal, spread_one, gain_one)
    dres_one[...] = d_one
    d_branch = d_one.astype(bf16)
    mine = pl.ds(pl.multiple_of(blk * tok, tok), tok)
    kept = seg_tab[mine, :][:, 0:1] < last_segment
    for quarter in range(cols):
        pulled = mt(d_branch, w_out[quarter]).astype(bf16).astype(f32)
        s_da[quarter] = jnp.where(kept, pulled, 0.0).astype(bf16)
    da_slots = to_lanes(lambda to: s_da.at[to], r_da)
    r_da[blk] = s_da[blk]

    params[...] = jnp.concatenate(
        [first_gain, first_bias, second_gain, second_bias, jnp.zeros((4, width), f32)], axis=0
    )
    for quarter in range(cols):
        product = tm(r_att[quarter], d_branch)
        for t in range(per_quarter):
            s = quarter * per_quarter + t
            owner_dp = s // cols
            mine_rows = product[t * rows : (t + 1) * rows]
            halved = [mine_rows[:, n * width // 2 : (n + 1) * width // 2] for n in range(2)]
            b_out[s % cols, owner_dp % 2, owner_dp // 2] = jnp.concatenate(
                halved, axis=0
            ).astype(bf16)
    both_sides = pl.ds(0, 2)
    out_blk = sum_start(b_out, rb_out, both_sides)

    gate_sum.first(1)
    sum_relay(out_blk, b_out, rb_out, tb_out, both_sides)
    down_sum.second_tail(1)
    down_sum.second(1)
    gate_sum.first(0)
    from_lanes(da_slots, r_da)
    def attend_back(head):
        window = head // 2
        fresh = head != 1

        def step_fn(step, carry):
            here = pl.ds(pl.multiple_of(step * chunk, chunk), chunk)
            d_out = r_da[pl.ds(step * group, group), :, window * LANES : (window + 1) * LANES]
            d_out = d_out.reshape(chunk, LANES).astype(f32)
            if head == 0:
                d_out = jnp.where(low_half, d_out, 0.0)
            if head == 1:
                d_out = jnp.where(low_half, 0.0, d_out)
            d_low = d_out.astype(bf16)
            delta = jnp.sum(d_out * att[window, here, :], axis=1, keepdims=True)
            prob_low = prob[head, here, :]
            d_prob = mt(d_low, vw[window])
            d_score = (prob_low.astype(f32) * (d_prob - delta)).astype(bf16)
            d_query = mm(d_score, kw[window]) * (HALF ** -0.5)
            if head == 1:
                d_query = jnp.where(low_half, acc_q[0, here, :], d_query)
            acc_q[window, here, :] = d_query
            d_key = tm(d_score, qm[head, here, :])
            d_value = tm(prob_low, d_low)
            if fresh:

                @pl.when(step == 0)
                def _():
                    acc_k[window] = d_key
                    acc_v[window] = d_value

                @pl.when(step != 0)
                def _():
                    acc_k[window] = acc_k[window] + d_key
                    acc_v[window] = acc_v[window] + d_value
            else:
                acc_k[window] = acc_k[window] + d_key
                acc_v[window] = acc_v[window] + d_value
            return carry

        lax.fori_loop(0, row_len // chunk, step_fn, 0)

    attend_back(0)
    gate_sum.first(2)
    down_sum.second_tail(0)
    down_sum.second(0)
    attend_back(1)
    attend_back(2)

    cosine, sine = cos_tab[...], sin_tab[...]

    def rotate_back(vector):
        vector = vector.astype(bf16).astype(f32)
        return (vector * cosine - turn(vector) * sine).astype(bf16)

    dj[:, 0:LANES] = rotate_back(acc_q[0])
    dj[:, LANES : 2 * LANES] = rotate_back(acc_k[0])
    dj[:, 2 * LANES : 3 * LANES] = acc_v[0].astype(bf16)
    dj[:, 3 * LANES : 4 * LANES] = rotate_back(acc_q[1] + pltpu.roll(acc_k[1], HALF, 1))
    dj[:, 4 * LANES : 5 * LANES] = acc_v[1].astype(bf16)

    up_sum.first(1)

    def input_parts(step, carry):
        here = pl.ds(pl.multiple_of(step * half * own_rows, LANES), half * own_rows)
        product = tm(xs[:, :, here].reshape(row_len, half * own_rows), dj[...])
        vectors = params[:, here]
        for j in range(half):
            mine_rows = product[j * own_rows : (j + 1) * own_rows]
            tile = jnp.where(lane_ids < own_rows, window_at(vectors, j * own_rows), 0.0)
            in_sum.part[j % 2, step * (half // 2) + j // 2] = jnp.concatenate(
                [mine_rows[:, :heads_width], folded(mine_rows[:, heads_width:], tile)], axis=0
            ).astype(bf16)
        return carry

    lax.fori_loop(0, planes * 2 // half, input_parts, 0)

    def input_grads(step, carry):
        here = pl.ds(pl.multiple_of(step * half * block, LANES), half * block)
        those = pl.ds(step * half, half)
        mixed = mt(dj[:, 0:heads_width], w_in[those, 0:own_rows].reshape(half * block, heads_width))
        mixed = mixed + mt(dj[:, heads_width:], w_value[those].reshape(half * block, LANES))
        s_ig[:, :, here] = mixed.reshape(cols, tok, half * block).astype(bf16)
        return carry

    lax.fori_loop(0, planes * 2 // half, input_grads, 0)
    ig_slots = sum_start(s_ig, r_ig)

    gate_sum.second(1)
    sum_relay(ig_slots, s_ig, r_ig, t_ig)
    up_sum.first(0)
    gate_sum.second(0)
    out_sum.part[...] = sum_done(out_blk, b_out, rb_out, both_sides).astype(bf16)
    in_sum.send((1, 0, 2))
    in_sum.send_side(3)
    out_sum.send((1, 0, 2))
    out_sum.send_side(3)
    down_sum.tail()
    up_sum.second(1)
    up_sum.first(2)
    f_gate[...] = gate_sum.total()
    up_sum.second(0)
    grad_in = dres_one[...] + sum_done(ig_slots, s_ig, r_ig)
    input_grad[...] = grad_in.astype(bf16)
    writes.append(move(input_grad, input_grad_to))
    in_sum.first(1)
    in_sum.first(0)
    up_total = up_sum.total()
    gate_total = f_gate[...]
    for j in range(cols):
        here = slice(j * rows, (j + 1) * rows)
        s_gmlp[j] = jnp.concatenate([gate_total[here], up_total[here]], axis=0).astype(bf16)
    gmlp_slots = to_lanes(lambda to: s_gmlp.at[to], r_gmlp)
    r_gmlp[blk] = s_gmlp[blk]
    in_sum.second(1)
    in_sum.first(2)
    in_sum.second(0)
    for j in (1, 0, 2):
        out_sum.first(j)
    out_sum.second(1)
    out_sum.second(0)
    from_lanes(gmlp_slots, r_gmlp)
    writes.append(move(r_gmlp, g_mlp_to))
    in_total = in_sum.total()
    values, tile = unfolded(in_total[own_rows:])
    columns = tm(tile.astype(bf16), to_lane)[0:own_rows]
    in_total = jnp.concatenate(
        [in_total[0:own_rows], jnp.where(low_half, values, columns)], axis=1
    )
    for j in range(cols):
        s_gin[j] = jnp.concatenate(
            [in_total[j * rows : (j + 1) * rows], jnp.zeros((8, in_total.shape[1]), f32)], axis=0
        ).astype(bf16)
    gin_slots = to_lanes(lambda to: s_gin.at[to], r_gin)
    r_gin[blk] = s_gin[blk]
    g_out[...] = out_sum.total()
    writes.append(move(g_out, g_out_to))
    g_down[...] = down_sum.total()
    writes.append(move(g_down, g_down_to))
    from_lanes(gin_slots, r_gin)
    writes.append(move(r_gin, g_in_to))
    wire.finish()
    for write in writes:
        write.wait()


def unpack(
    rows,
    block,
    outputs,
    input_grad,
    g_in,
    g_mlp,
    g_out,
    g_down,
    outputs_to,
    input_grad_to,
    in_to,
    out_to,
    gate_to,
    up_to,
    down_to,
    *vectors_to,
):
    f32 = jnp.float32
    cols = g_in.shape[0]
    width = outputs.shape[1]
    outputs_to[0] = outputs[...]
    input_grad_to[0] = input_grad[...]
    down_to[...] = g_down[...]
    for n in range(2):
        out_to[:, n * width // 2 : (n + 1) * width // 2] = g_out[n * rows : (n + 1) * rows, :]
    low_half = lax.broadcasted_iota(jnp.int32, (1, LANES), 1) < HALF
    joined = [g_in[j].astype(f32)[0:rows] for j in range(cols)]
    vectors = joined[0][:, 4 * LANES :]
    for j in range(1, cols):
        vectors = vectors + joined[j][:, 4 * LANES :]
    vectors = jnp.concatenate([vectors, jnp.zeros((LANES - rows, LANES), f32)], axis=0).T
    for number, vector_to in enumerate(vectors_to):
        vector_to[...] = vectors[HALF + number, 0:rows]
    single_at = ((3, 0), (3, 1), (4, 0))

    def half(kind, number, want):
        owner, part = number // 3, number % 3
        window, at = (kind, part) if part < 2 else single_at[kind]
        value = joined[owner][:, window * LANES : (window + 1) * LANES]
        return value if at == want else pltpu.roll(value, HALF, 1)

    for kind in range(3):
        for n in range(width // LANES):
            at = kind * width + n * LANES
            in_to[:, at : at + LANES] = jnp.where(
                low_half, half(kind, 2 * n, 0), half(kind, 2 * n + 1, 1)
            )
    lanes = lax.broadcasted_iota(jnp.int32, (1, LANES), 1)
    mlp = [g_mlp[j].astype(f32) for j in range(cols)]
    for first_row, target in ((0, gate_to), (rows, up_to)):
        parts = [part[first_row : first_row + rows] for part in mlp]
        for n in range(target.shape[1] // LANES):
            first = n * LANES
            result = None
            for number in range(first // block, (first + LANES - 1) // block + 1):
                ring_at, owner = number // cols, number % cols
                piece = window_at(parts[owner], ring_at * block + first - number * block)
                begin = number * block - first
                result = piece if result is None else jnp.where(lanes < begin, result, piece)
            target[:, first : first + LANES] = result


def fast_shards(
    depth,
    inputs,
    doc_lengths,
    project_in,
    project_out,
    gate_weight,
    up_weight,
    down_weight,
    first_gain,
    first_bias,
    second_gain,
    second_bias,
    cotangent,
):
    cols = 4
    tok, width = inputs.shape[1:]
    rows = project_in.shape[0]
    ff = gate_weight.shape[1]
    ring = depth * 2
    row_len = tok * cols
    units = ff // cols
    block = units // ring
    head_width = width // cols
    in_width = 5 * LANES
    bf16, f32 = jnp.bfloat16, jnp.float32

    lane_ids = np.arange(LANES) % QUART
    freq = jnp.asarray(
        np.broadcast_to(BASE ** (-2.0 * lane_ids / HALF), (8, LANES)).astype(np.float32)
    )

    def scratch(*shape, kind=bf16):
        return pltpu.VMEM(shape, kind)

    def sums(height, across, tail=0):
        main = height - tail
        buffers = [
            scratch(2, depth, height, across),
            scratch(depth, main, across),
            scratch(depth, main, across),
            scratch(4, main, across),
        ]
        if tail:
            buffers = buffers + [
                scratch(4, 2, tail, across),
                scratch(2, 2, tail, across),
                scratch(2, tail, across),
                scratch(tail, across, kind=f32),
            ]
        return tuple(buffers)

    stacked = scratch(cols, tok, width)
    heads = 3
    buffers = [
        scratch(tok, width),
        scratch(rows, 3 * width),
        scratch(rows, ff),
        scratch(rows, ff),
        scratch(rows, width),
        scratch(tok, width),
        scratch(tok, width),
        scratch(2 * rows, width // 2, kind=f32),
        scratch(block, width, kind=f32),
        pltpu.SemaphoreType.DMA((16,)),
        stacked,
        scratch(cols, 32, in_width),
        scratch(cols, 2 * rows, units),
        scratch(8, LANES, kind=f32),
        scratch(cols, 32, in_width),
        scratch(cols, 2 * rows, units),
        scratch(cols, ring, 2 * rows, width // 2),
        scratch(ring, cols * rows + 16, 4 * LANES),
        scratch(ring, cols * rows, LANES),
        scratch(ring, cols * rows, units),
        scratch(ring, cols * rows, units),
        scratch(ring, block, width),
        scratch(cols, 2 * LANES, width),
        scratch(8, width, kind=f32),
        scratch(row_len, LANES, kind=f32),
        scratch(row_len, LANES, kind=f32),
        scratch(row_len, LANES, kind=jnp.int32),
        scratch(heads, row_len, LANES),
        scratch(2, row_len, LANES),
        scratch(2, row_len, LANES),
        scratch(heads, row_len, row_len),
        scratch(2, row_len, LANES, kind=f32),
        scratch(cols, tok, 2 * LANES),
        scratch(cols, tok, 2 * LANES),
        scratch(tok, width, kind=f32),
        scratch(tok, width, kind=f32),
        stacked,
        scratch(row_len, units, kind=f32),
        scratch(row_len, units, kind=f32),
        scratch(row_len, units),
        stacked,
        scratch(3, tok, width),
        scratch(tok, width),
        scratch(tok, width, kind=f32),
        stacked,
        scratch(row_len, units),
        scratch(row_len, units),
        stacked,
        scratch(3, tok, width),
        scratch(tok, width),
        scratch(tok, width, kind=f32),
        scratch(cols, tok, 2 * LANES),
        scratch(cols, tok, 2 * LANES),
        scratch(2, row_len, LANES, kind=f32),
        scratch(2, row_len, LANES, kind=f32),
        scratch(2, row_len, LANES, kind=f32),
        scratch(row_len, in_width),
        stacked,
        scratch(3, tok, width),
        scratch(tok, width),
        sums(cols * rows + 16, 4 * LANES),
        sums(cols * rows, units),
        sums(cols * rows, units),
        sums(block, width, DTB),
        scratch(cols, 2, depth, 2 * rows, width // 2),
        scratch(3, 2, depth, 2 * rows, width // 2),
        scratch(2, depth, 2 * rows, width // 2),
        sums(2 * rows, width // 2, 0),
        scratch(cols * rows, units, kind=f32),
        scratch(cols, 2 * rows, units),
        scratch(cols, 2 * rows, units),
        scratch(cols, 32, in_width),
        scratch(cols, 32, in_width),
        pltpu.SemaphoreType.DMA((240,)),
        pltpu.SemaphoreType.DMA((240,)),
    ]
    vmem = pl.BlockSpec(memory_space=pltpu.VMEM)
    anywhere = pl.BlockSpec(memory_space=pl.ANY)
    tokens = row_len * width
    outputs, input_grad, g_in, g_mlp, g_out, g_down = pl.pallas_call(
        functools.partial(fused, depth),
        out_shape=(
            jax.ShapeDtypeStruct((tok, width), bf16),
            jax.ShapeDtypeStruct((tok, width), bf16),
            jax.ShapeDtypeStruct((cols, 32, in_width), bf16),
            jax.ShapeDtypeStruct((cols, 2 * rows, units), bf16),
            jax.ShapeDtypeStruct((2 * rows, width // 2), f32),
            jax.ShapeDtypeStruct((block, width), f32),
        ),
        in_specs=[pl.BlockSpec(memory_space=pltpu.SMEM), vmem] + [anywhere] * 7 + [vmem] * 4,
        out_specs=(anywhere,) * 6,
        scratch_shapes=buffers,
        compiler_params=pltpu.CompilerParams(
            collective_id=0, has_side_effects=True, vmem_limit_bytes=60 * 2**20
        ),
        cost_estimate=pl.CostEstimate(
            flops=6 * tokens * (3 * units + 4 * head_width),
            bytes_accessed=8 * 2**20,
            transcendentals=3 * row_len * row_len,
        ),
        name="layer",
    )(
        doc_lengths,
        freq,
        inputs[0],
        cotangent[0],
        project_in,
        gate_weight,
        up_weight,
        project_out,
        down_weight,
        first_gain[None],
        first_bias[None],
        second_gain[None],
        second_bias[None],
    )

    vector = jax.ShapeDtypeStruct((rows,), f32)
    return pl.pallas_call(
        functools.partial(unpack, rows, block),
        out_shape=(
            jax.ShapeDtypeStruct((1, tok, width), bf16),
            jax.ShapeDtypeStruct((1, tok, width), bf16),
            jax.ShapeDtypeStruct((rows, 3 * width), f32),
            jax.ShapeDtypeStruct((rows, width), f32),
            jax.ShapeDtypeStruct((rows, ff), f32),
            jax.ShapeDtypeStruct((rows, ff), f32),
            jax.ShapeDtypeStruct((block, width), f32),
            vector,
            vector,
            vector,
            vector,
        ),
        in_specs=[vmem] * 6,
        out_specs=(vmem,) * 11,
        name="unpack",
    )(outputs, input_grad, g_in, g_mlp, g_out, g_down)


def pick(sizes):
    def chosen(*args):
        tok, width = args[0].shape[1:]
        ring, cols = sizes["dp"], sizes["blk"]
        fits = (
            ring == 8
            and cols == 4
            and tok == LANES
            and HEADS == 3 * cols
            and width == HEADS * HALF
            and args[2].shape[0] == 24
            and args[4].shape[1] == 4 * width
        )
        if fits:
            return fast_shards(ring // 2, *args)
        return shards(*args)

    return chosen


def solution(mesh):
    placed = (
        P("dp", "blk", None),
        P("dp", None),
        P(("dp", "blk"), None),
        P(("dp", "blk"), None),
        P(("dp", "blk"), None),
        P(("dp", "blk"), None),
        P(("dp", "blk"), None),
        P(("dp", "blk")),
        P(("dp", "blk")),
        P(("dp", "blk")),
        P(("dp", "blk")),
        P("dp", "blk", None),
    )
    return jax.shard_map(
        pick(dict(mesh.shape)),
        mesh=mesh,
        in_specs=placed,
        out_specs=(
            P("dp", "blk", None),
            P("dp", "blk", None),
            P(("dp", "blk"), None),
            P(("dp", "blk"), None),
            P(("dp", "blk"), None),
            P(("dp", "blk"), None),
            P(("dp", "blk"), None),
            P(("dp", "blk")),
            P(("dp", "blk")),
            P(("dp", "blk")),
            P(("dp", "blk")),
        ),
        check_vma=False,
    )
```

```python
import functools

import jax
import jax.numpy as jnp
import numpy as np
from jax import lax
from jax.experimental import pallas as pl
from jax.experimental.pallas import tpu as pltpu
from jax.sharding import PartitionSpec as P

HEADS = 12


NEG = -1e30
EPS = 1e-05
BASE = 1000.0


def doc_layout(lengths_row, positions):
    bounds = jnp.cumsum(lengths_row)
    passed = positions[:, None] >= bounds[None, :]
    segment = jnp.sum(passed.astype(jnp.int32), axis=1)
    begins = jnp.sum(jnp.where(passed, lengths_row[None, :], 0), axis=1)
    return (segment, positions - begins)


def rotary(vectors, offsets):
    half_size = vectors.shape[-1] // 2
    frequency = BASE ** (-2.0 * jnp.arange(half_size, dtype=jnp.float32) / vectors.shape[-1])
    angles = offsets.astype(jnp.float32)[:, None] * frequency[None, :]
    cosine = jnp.concatenate([jnp.cos(angles), jnp.cos(angles)], axis=1)[:, None, :]
    sine_rows = jnp.concatenate([jnp.sin(angles), jnp.sin(angles)], axis=1)[:, None, :]
    first_half = vectors[..., :half_size]
    second_half = vectors[..., half_size:]
    turned = jnp.concatenate([-second_half, first_half], axis=-1)
    return vectors * cosine + turned * sine_rows


def layer_norm(residual, gain_row, bias_row):
    row_mean = jnp.mean(residual, axis=-1, keepdims=True)
    centered = residual - row_mean
    variance = jnp.mean(centered * centered, axis=-1, keepdims=True)
    return centered * lax.rsqrt(variance + EPS) * gain_row + bias_row


def contract_rows(left, right):
    return lax.dot_general(
        left, right, (((0,), (0,)), ((), ())), preferred_element_type=jnp.float32
    )


def contract_cols(left, right):
    return lax.dot_general(
        left, right, (((1,), (1,)), ((), ())), preferred_element_type=jnp.float32
    )


def tile_scores(query_tile, key_tile, seg_query, seg_key, score_scale):
    scores = (
        jnp.einsum("qhd,khd->hqk", query_tile, key_tile, preferred_element_type=jnp.float32)
        * score_scale
    )
    allowed = (seg_query[:, None] == seg_key[None, :])[None, :, :]
    return (jnp.where(allowed, scores, NEG), allowed)


def run_groups(pieces, group, lengths_row, seg_query, carried, tile_fn, extra_shape):
    group_count = pieces[0].shape[0] // group

    def group_step(carried_in, number):
        offset = number * group
        tile_set = tuple(
            (lax.dynamic_slice_in_dim(piece_rows, offset, group, 0) for piece_rows in pieces)
        )
        positions = offset + jnp.arange(group, dtype=jnp.int32)
        seg_key, unused_offsets = doc_layout(lengths_row, positions)
        touches = (seg_key[0] <= seg_query[-1]) & (seg_query[0] <= seg_key[-1])

        def active(state_in):
            return tile_fn(state_in, tile_set, seg_key)

        def skipped(state_in):
            return (state_in, jnp.zeros(extra_shape, jnp.float32))

        return lax.cond(touches, active, skipped, carried_in)

    return lax.scan(group_step, carried, jnp.arange(group_count, dtype=jnp.int32))


def shards(
    inputs,
    doc_lengths,
    project_in,
    project_out,
    gate_weight,
    up_weight,
    down_weight,
    first_gain,
    first_bias,
    second_gain,
    second_bias,
    cotangent,
):
    group = inputs.shape[1]
    width = inputs.shape[2]
    head_count = HEADS
    head_size = width // head_count
    score_scale = head_size ** (-0.5)
    cycle_rank = lax.axis_index("blk")
    positions = cycle_rank * group + jnp.arange(group, dtype=jnp.int32)
    lengths_row = doc_lengths[0]
    seg_query, offsets = doc_layout(lengths_row, positions)
    keep_mask = seg_query < lengths_row.shape[0] - 1
    keep_float = keep_mask.astype(jnp.float32)
    fetched = (
        lax.all_gather(project_in, ("dp", "blk"), axis=0, tiled=True),
        lax.all_gather(project_out, ("dp", "blk"), axis=0, tiled=True),
        lax.all_gather(gate_weight, ("dp", "blk"), axis=0, tiled=True),
        lax.all_gather(up_weight, ("dp", "blk"), axis=0, tiled=True),
        lax.all_gather(down_weight, ("dp", "blk"), axis=0, tiled=True),
        lax.all_gather(first_gain, ("dp", "blk"), axis=0, tiled=True),
        lax.all_gather(first_bias, ("dp", "blk"), axis=0, tiled=True),
        lax.all_gather(second_gain, ("dp", "blk"), axis=0, tiled=True),
        lax.all_gather(second_bias, ("dp", "blk"), axis=0, tiled=True),
    )
    full_in, full_out, full_gate, full_up, full_down = (
        fetched[0],
        fetched[1],
        fetched[2],
        fetched[3],
        fetched[4],
    )
    gain_one = fetched[5].astype(jnp.float32)
    bias_one = fetched[6].astype(jnp.float32)
    gain_two = fetched[7].astype(jnp.float32)
    bias_two = fetched[8].astype(jnp.float32)
    tokens_low = inputs[0]
    tokens_f = tokens_low.astype(jnp.float32)
    joined = jnp.dot(tokens_low, full_in, preferred_element_type=jnp.float32)
    query_raw = joined[:, :width].reshape(group, head_count, head_size)
    key_raw = joined[:, width : 2 * width].reshape(group, head_count, head_size)
    value_low = joined[:, 2 * width :].astype(jnp.bfloat16)
    query_rot, query_pull = jax.vjp(lambda vectors: rotary(vectors, offsets), query_raw)
    key_rot, key_pull = jax.vjp(lambda vectors: rotary(vectors, offsets), key_raw)
    query_low = query_rot.astype(jnp.bfloat16)
    key_low = key_rot.reshape(group, width).astype(jnp.bfloat16)

    def stats_tile(carried, tile_set, seg_key):
        row_top, row_total = carried
        key_tile = tile_set[0].reshape(group, head_count, head_size)
        scores, allowed = tile_scores(query_low, key_tile, seg_query, seg_key, score_scale)
        new_top = jnp.maximum(row_top, jnp.max(scores, axis=2))
        shrink = jnp.exp(row_top - new_top)
        added = jnp.sum(jnp.where(allowed, jnp.exp(scores - new_top[:, :, None]), 0.0), axis=2)
        return ((new_top, row_total * shrink + added), jnp.zeros((1,), jnp.float32))

    init_stats = (
        jnp.full((head_count, group), NEG, jnp.float32),
        jnp.zeros((head_count, group), jnp.float32),
    )
    carried = init_stats
    carried, unused = run_groups(
        (lax.all_gather(key_low, "blk", axis=0, tiled=True),),
        group,
        lengths_row,
        seg_query,
        carried,
        stats_tile,
        (1,),
    )
    row_top, row_total = carried
    log_total = row_top + jnp.log(row_total)

    def output_tile(accum, tile_set, seg_key):
        key_tile = tile_set[0].reshape(group, head_count, head_size)
        value_tile = tile_set[1].reshape(group, head_count, head_size)
        scores, allowed = tile_scores(query_low, key_tile, seg_query, seg_key, score_scale)
        prob_low = jnp.where(allowed, jnp.exp(scores - log_total[:, :, None]), 0.0).astype(
            jnp.bfloat16
        )
        accum = accum + jnp.einsum(
            "hqk,khd->qhd", prob_low, value_tile, preferred_element_type=jnp.float32
        )
        return (accum, jnp.zeros((1,), jnp.float32))

    zero_accum = jnp.zeros((group, head_count, head_size), jnp.float32)
    accum = zero_accum
    accum, unused = run_groups(
        (
            lax.all_gather(key_low, "blk", axis=0, tiled=True),
            lax.all_gather(value_low, "blk", axis=0, tiled=True),
        ),
        group,
        lengths_row,
        seg_query,
        accum,
        output_tile,
        (1,),
    )
    attend_low = (accum * keep_float[:, None, None]).reshape(group, width).astype(jnp.bfloat16)
    branch = jnp.dot(attend_low, full_out, preferred_element_type=jnp.float32)
    residual_one = tokens_f + branch
    hidden, norm_one_pull = jax.vjp(layer_norm, residual_one, gain_one, bias_one)
    hidden_low = hidden.astype(jnp.bfloat16)
    gate_pre = jnp.dot(hidden_low, full_gate, preferred_element_type=jnp.float32)
    up_pre = jnp.dot(hidden_low, full_up, preferred_element_type=jnp.float32)
    activated, swiglu_pull = jax.vjp(
        lambda gate_in, up_in: jax.nn.silu(gate_in) * up_in, gate_pre, up_pre
    )
    active_low = activated.astype(jnp.bfloat16)
    mlp_out = jnp.dot(active_low, full_down, preferred_element_type=jnp.float32)
    outputs_f, norm_two_pull = jax.vjp(layer_norm, hidden + mlp_out, gain_two, bias_two)
    refetched = (
        lax.all_gather(project_in, ("dp", "blk"), axis=0, tiled=True),
        lax.all_gather(project_out, ("dp", "blk"), axis=0, tiled=True),
        lax.all_gather(gate_weight, ("dp", "blk"), axis=0, tiled=True),
        lax.all_gather(up_weight, ("dp", "blk"), axis=0, tiled=True),
        lax.all_gather(down_weight, ("dp", "blk"), axis=0, tiled=True),
    )
    full_in, full_out, full_gate, full_up, full_down = (
        refetched[0],
        refetched[1],
        refetched[2],
        refetched[3],
        refetched[4],
    )
    d_res_two, second_gain_part, second_bias_part = norm_two_pull(cotangent[0].astype(jnp.float32))
    d_mlp_low = d_res_two.astype(jnp.bfloat16)
    down_part = contract_rows(active_low, d_mlp_low)
    d_active = contract_cols(d_mlp_low, full_down)
    d_gate, d_up = swiglu_pull(d_active)
    d_gate_low = d_gate.astype(jnp.bfloat16)
    d_up_low = d_up.astype(jnp.bfloat16)
    gate_part = contract_rows(hidden_low, d_gate_low)
    up_part = contract_rows(hidden_low, d_up_low)
    d_hidden = d_res_two + contract_cols(d_gate_low, full_gate) + contract_cols(d_up_low, full_up)
    d_res_one, first_gain_part, first_bias_part = norm_one_pull(d_hidden)
    d_branch_low = d_res_one.astype(jnp.bfloat16)
    out_part = contract_rows(attend_low, d_branch_low)
    d_attend = contract_cols(d_branch_low, full_out).astype(jnp.bfloat16)
    d_attend_low = (d_attend * keep_mask[:, None].astype(jnp.bfloat16)).reshape(
        group, head_count, head_size
    )
    delta = jnp.einsum("qhd,qhd->hq", d_attend_low.astype(jnp.float32), accum)

    def back_tile(grad_query, tile_set, seg_key):
        key_tile = tile_set[0].reshape(group, head_count, head_size)
        value_tile = tile_set[1].reshape(group, head_count, head_size)
        scores, allowed = tile_scores(query_low, key_tile, seg_query, seg_key, score_scale)
        prob_rows = jnp.where(allowed, jnp.exp(scores - log_total[:, :, None]), 0.0)
        d_probs = jnp.einsum(
            "qhd,khd->hqk", d_attend_low, value_tile, preferred_element_type=jnp.float32
        )
        d_score_low = (prob_rows * (d_probs - delta[:, :, None])).astype(jnp.bfloat16)
        grad_query = (
            grad_query
            + jnp.einsum("hqk,khd->qhd", d_score_low, key_tile, preferred_element_type=jnp.float32)
            * score_scale
        )
        grad_key = (
            jnp.einsum("hqk,qhd->khd", d_score_low, query_low, preferred_element_type=jnp.float32)
            * score_scale
        )
        grad_value = jnp.einsum(
            "hqk,qhd->khd",
            prob_rows.astype(jnp.bfloat16),
            d_attend_low,
            preferred_element_type=jnp.float32,
        )
        return (
            grad_query,
            jnp.concatenate(
                [grad_key.reshape(group, width), grad_value.reshape(group, width)], axis=1
            ),
        )

    grad_query = zero_accum
    grad_query, blocks = run_groups(
        (
            lax.all_gather(key_low, "blk", axis=0, tiled=True),
            lax.all_gather(value_low, "blk", axis=0, tiled=True),
        ),
        group,
        lengths_row,
        seg_query,
        grad_query,
        back_tile,
        (group, 2 * width),
    )
    blocks = blocks.reshape(-1, 2 * width)
    back_result = (grad_query, blocks)
    grad_query = back_result[0]
    owned_pairs = lax.psum_scatter(
        back_result[1].astype(jnp.bfloat16), "blk", scatter_dimension=0, tiled=True
    ).astype(jnp.float32)
    key_sum = owned_pairs[:, :width]
    value_sum = owned_pairs[:, width:]
    d_query_pre = query_pull(grad_query.astype(jnp.bfloat16).astype(jnp.float32))[0]
    d_key_low = key_sum.astype(jnp.bfloat16).astype(jnp.float32)
    d_key_pre = key_pull(d_key_low.reshape(group, head_count, head_size))[0]
    d_value_low = value_sum.astype(jnp.bfloat16).astype(jnp.float32)
    d_joined_low = jnp.concatenate(
        [d_query_pre.reshape(group, width), d_key_pre.reshape(group, width), d_value_low], axis=1
    ).astype(jnp.bfloat16)
    in_part = contract_rows(tokens_low, d_joined_low)
    input_grad = (d_res_one + contract_cols(d_joined_low, full_in)).astype(jnp.bfloat16)
    by_rows = (
        lax.psum_scatter(
            in_part.astype(jnp.bfloat16), "dp", scatter_dimension=0, tiled=True
        ).astype(jnp.float32),
        lax.psum_scatter(
            out_part.astype(jnp.bfloat16), "dp", scatter_dimension=0, tiled=True
        ).astype(jnp.float32),
        lax.psum_scatter(
            gate_part.astype(jnp.bfloat16), "dp", scatter_dimension=0, tiled=True
        ).astype(jnp.float32),
        lax.psum_scatter(
            up_part.astype(jnp.bfloat16), "dp", scatter_dimension=0, tiled=True
        ).astype(jnp.float32),
        lax.psum_scatter(
            down_part.astype(jnp.bfloat16), "dp", scatter_dimension=0, tiled=True
        ).astype(jnp.float32),
        lax.psum_scatter(
            first_gain_part.astype(jnp.bfloat16), "dp", scatter_dimension=0, tiled=True
        ).astype(jnp.float32),
        lax.psum_scatter(
            first_bias_part.astype(jnp.bfloat16), "dp", scatter_dimension=0, tiled=True
        ).astype(jnp.float32),
        lax.psum_scatter(
            second_gain_part.astype(jnp.bfloat16), "dp", scatter_dimension=0, tiled=True
        ).astype(jnp.float32),
        lax.psum_scatter(
            second_bias_part.astype(jnp.bfloat16), "dp", scatter_dimension=0, tiled=True
        ).astype(jnp.float32),
    )
    summed = (
        lax.psum_scatter(
            by_rows[0].astype(jnp.bfloat16), "blk", scatter_dimension=0, tiled=True
        ).astype(jnp.float32),
        lax.psum_scatter(
            by_rows[1].astype(jnp.bfloat16), "blk", scatter_dimension=0, tiled=True
        ).astype(jnp.float32),
        lax.psum_scatter(
            by_rows[2].astype(jnp.bfloat16), "blk", scatter_dimension=0, tiled=True
        ).astype(jnp.float32),
        lax.psum_scatter(
            by_rows[3].astype(jnp.bfloat16), "blk", scatter_dimension=0, tiled=True
        ).astype(jnp.float32),
        lax.psum_scatter(
            by_rows[4].astype(jnp.bfloat16), "blk", scatter_dimension=0, tiled=True
        ).astype(jnp.float32),
        lax.psum_scatter(
            by_rows[5].astype(jnp.bfloat16), "blk", scatter_dimension=0, tiled=True
        ).astype(jnp.float32),
        lax.psum_scatter(
            by_rows[6].astype(jnp.bfloat16), "blk", scatter_dimension=0, tiled=True
        ).astype(jnp.float32),
        lax.psum_scatter(
            by_rows[7].astype(jnp.bfloat16), "blk", scatter_dimension=0, tiled=True
        ).astype(jnp.float32),
        lax.psum_scatter(
            by_rows[8].astype(jnp.bfloat16), "blk", scatter_dimension=0, tiled=True
        ).astype(jnp.float32),
    )
    return (
        outputs_f.astype(jnp.bfloat16)[None],
        input_grad[None],
        summed[0],
        summed[1],
        summed[2],
        summed[3],
        summed[4],
        summed[5],
        summed[6],
        summed[7],
        summed[8],
    )


MESH_IDS = pl.DeviceIdType.MESH
LANES = 128
HALF = 64
QUART = 32
DTF = 64
DTB = 64


def mm(left, right):
    return lax.dot_general(
        left, right, (((1,), (0,)), ((), ())), preferred_element_type=jnp.float32
    )


def mt(left, right):
    return lax.dot_general(
        left, right, (((1,), (1,)), ((), ())), preferred_element_type=jnp.float32
    )


def tm(left, right):
    return lax.dot_general(
        left, right, (((0,), (0,)), ((), ())), preferred_element_type=jnp.float32
    )


def window_at(value, start):
    aligned = min(max(start // LANES * LANES, 0), value.shape[1] - LANES)
    if aligned == start:
        return value[:, aligned : aligned + LANES]
    aligned = min(aligned, value.shape[1] - 2 * LANES)
    two = value[:, aligned : aligned + 2 * LANES]
    return pltpu.roll(two, (aligned - start) % (2 * LANES), 1)[:, :LANES]


def gather_lanes(value, block, first, source):
    lanes = lax.broadcasted_iota(jnp.int32, (1, LANES), 1)
    result = None
    for number in range(first // block, (first + LANES - 1) // block + 1):
        piece = window_at(value, source(number, first))
        begin = number * block - first
        result = piece if result is None else jnp.where(lanes < begin, result, piece)
    return result


class Wire:
    def __init__(self, send_sem, recv_sem, is_inner):
        self.send_sem, self.recv_sem, self.is_inner = send_sem, recv_sem, is_inner
        self.sends, self.slots = 0, 0
        self.sent = {None: [], True: [], False: []}

    def slot(self):
        self.slots += 1
        return self.slots - 1

    def copy(self, src, dst, peer, slot):
        self.sends += 1
        return pltpu.make_async_remote_copy(
            src_ref=src,
            dst_ref=dst,
            send_sem=self.send_sem.at[self.sends - 1],
            recv_sem=self.recv_sem.at[slot],
            device_id=peer,
            device_id_type=MESH_IDS,
        )

    def push(self, src, dst, peer, slot=None, inner=None):
        slot = self.slot() if slot is None else slot
        copy = self.copy(src, dst, peer, slot)
        self.sent[inner].append(copy)
        if inner is None:
            copy.start()
        else:
            pl.when(self.is_inner == inner)(copy.start)
        return slot

    def arrive(self, slot, dst, peer):
        pltpu.make_async_remote_copy(
            src_ref=dst,
            dst_ref=dst,
            send_sem=self.send_sem.at[0],
            recv_sem=self.recv_sem.at[slot],
            device_id=peer,
            device_id_type=MESH_IDS,
        ).wait_recv()

    def finish(self):
        for inner, copies in self.sent.items():

            def drain(copies=copies):
                for copy in copies:
                    copy.wait_send()

            if inner is None:
                drain()
            else:
                pl.when(self.is_inner == inner)(drain)


class Plane:
    def __init__(self, planes):
        dp, self.blk = lax.axis_index("dp"), lax.axis_index("blk")
        self.z, self.x = dp // 2, dp % 2
        self.dp = dp
        self.partner = self.z + 1 - 2 * (self.z % 2)
        self.other = planes // 2 - self.z // (planes // 2)
        self.outer = (planes - 1) * (self.other - 1)
        self.inner = ((self.z + 1) // 2) % 2
        self.order = (self.other, self.outer, self.partner, self.z)
        self.side = (self.z * 2 + (1 - self.x), self.blk)

    def at(self, plane):
        return (plane * 2 + self.x, self.blk)


class Spread:
    def __init__(self, wire, place, target, tail):
        self.wire, self.place, self.target = wire, place, target
        self.height, self.main = target.shape[1], target.shape[1] - tail

    def block(self, plane, column):
        return self.target.at[plane * 2 + column, 0 : self.main]

    def pair(self, plane):
        return self.target.at[pl.ds(plane * 2, 2), self.main : self.height]

    def along(self, own, slots):
        p = self.place
        self.wire.push(own, own, p.at(p.partner), slots[2], inner=False)
        self.wire.push(own, own, p.at(p.other), slots[0] + (1 - p.inner))

    def outward(self, own, slots):
        p = self.place
        self.wire.push(own, own, p.at(p.partner), slots[2], inner=True)

    def start(self):
        p, wire = self.place, self.wire
        self.z_slots = [wire.slot() for _ in range(3)]
        self.along(self.block(p.z, p.x), self.z_slots)

    def start_out(self):
        p = self.place
        self.outward(self.block(p.z, p.x), self.z_slots)

    def start_side(self):
        p, wire = self.place, self.wire
        self.x_slots = [wire.slot() for _ in range(4)]
        own = self.block(p.z, p.x)
        wire.push(own, own, p.side, self.x_slots[3])
        if self.main < self.height:
            self.out_slots = []
            self.rest_slot = wire.push(self.rest(p.x), self.rest(p.x), p.side)

    def tail(self):
        p, wire = self.place, self.wire
        rest = self.target.at[p.z * 2 + (1 - p.x), self.main : self.height]
        wire.arrive(self.rest_slot, rest, p.side)
        self.t_slots = [wire.slot() for _ in range(3)]
        self.along(self.pair(p.z), self.t_slots)

    def rest(self, column):
        p = self.place
        return self.target.at[p.z * 2 + column, self.main : self.height]

    def tail_out(self, own):
        p, wire = self.place, self.wire
        rest = self.rest(p.x if own else 1 - p.x)
        self.out_slots.append(wire.push(rest, rest, p.at(p.partner), inner=True))

    def relay(self, j, inner=None):
        p, wire = self.place, self.wire
        block = self.block(p.order[j], p.x)
        onward = wire.copy(block, block, p.side, self.x_slots[j])
        wire.sent[inner].append(onward)
        outward = None
        if j < 2 and inner is not False:
            outward = wire.copy(block, block, p.at(p.partner), self.z_slots[j])
            wire.sent[True].append(outward)

        def run():
            wire.arrive(self.z_slots[j], block, p.side)
            if outward is not None:
                if inner:
                    outward.start()
                else:
                    pl.when(wire.is_inner)(outward.start)
            onward.start()

        if inner is None:
            run()
        else:
            pl.when(wire.is_inner == inner)(run)

    def pass_tail(self, j):
        p, wire = self.place, self.wire
        pair = self.pair(p.order[j])
        copy = wire.copy(pair, pair, p.at(p.partner), self.t_slots[j])
        wire.sent[True].append(copy)

        @pl.when(wire.is_inner)
        def _():
            wire.arrive(self.t_slots[j], pair, p.side)
            copy.start()

    def settle_tail(self):
        p, wire = self.place, self.wire

        @pl.when(wire.is_inner)
        def _():
            wire.arrive(self.t_slots[2], self.pair(p.order[2]), p.side)

        @pl.when(jnp.logical_not(wire.is_inner))
        def _():
            for j in range(2):
                wire.arrive(self.t_slots[j], self.pair(p.order[j]), p.side)
            for slot, column in zip(self.out_slots, (p.x, 1 - p.x)):
                came = self.target.at[p.partner * 2 + column, self.main : self.height]
                wire.arrive(slot, came, p.side)

    def settle(self):
        p = self.place
        for j in range(4):
            self.wire.arrive(self.x_slots[j], self.block(p.order[j], 1 - p.x), p.side)


class Collect:
    def __init__(self, wire, place, buffers):
        self.wire, self.place = wire, place
        self.part, self.inbox, self.staged, self.landing = buffers[:4]
        self.height, self.main = self.part.shape[2], self.inbox.shape[1]
        self.split = self.main < self.height
        self.x_slots = [wire.slot() for _ in range(4)]
        self.z_slots = [wire.slot() for _ in range(4)]
        if self.split:
            self.t_landing, self.t_staged, self.t_cross, self.t_kept = buffers[4:]
            self.t_slots = [wire.slot() for _ in range(4)]

    def pair(self, plane):
        return self.part.at[:, plane, self.main : self.height]

    def send_side(self, j):
        p = self.place
        plane = p.order[j]
        self.wire.push(
            self.part.at[1 - p.x, plane, 0 : self.main],
            self.inbox.at[plane],
            p.side,
            self.x_slots[j],
        )

    def send(self, order=(1, 0, 2, 3)):
        for j in order:
            self.send_side(j)

    def send_tails(self):
        p = self.place
        for j in (1, 0, 2):
            self.wire.push(
                self.pair(p.order[j]),
                self.t_landing.at[j],
                p.at(p.partner),
                self.t_slots[j],
                inner=None if j == 2 else False,
            )

    def first(self, j):
        p, wire = self.place, self.wire
        plane = p.order[j]
        wire.arrive(self.x_slots[j], self.inbox.at[plane], p.side)
        both = self.part[p.x, plane, 0 : self.main].astype(jnp.float32)
        both = both + self.inbox[plane].astype(jnp.float32)
        self.staged[plane] = both.astype(jnp.bfloat16)
        wire.push(
            self.staged.at[plane],
            self.landing.at[j],
            p.at(p.partner),
            self.z_slots[j],
            inner=None if j == 2 else False,
        )

    def second(self, j):
        p, wire = self.place, self.wire
        plane = p.order[j]
        copy = wire.copy(self.staged.at[plane], self.landing.at[3], p.at(plane), self.z_slots[3])
        wire.sent[True].append(copy)

        @pl.when(wire.is_inner)
        def _():
            wire.arrive(self.z_slots[j], self.landing.at[j], p.side)
            both = self.staged[plane].astype(jnp.float32) + self.landing[j].astype(jnp.float32)
            self.staged[plane] = both.astype(jnp.bfloat16)
            copy.start()

    def second_tail(self, j):
        p, wire = self.place, self.wire
        plane = p.order[j]
        copy = wire.copy(self.t_staged.at[j], self.t_landing.at[3], p.at(plane), self.t_slots[3])
        wire.sent[True].append(copy)

        @pl.when(wire.is_inner)
        def _():
            wire.arrive(self.t_slots[j], self.t_landing.at[j], p.side)
            rest = self.part[:, plane, self.main : self.height].astype(jnp.float32)
            rest = rest + self.t_landing[j].astype(jnp.float32)
            self.t_staged[j] = rest.astype(jnp.bfloat16)
            copy.start()

    def tail(self):
        p, wire = self.place, self.wire
        for j in (2, 3):
            wire.arrive(self.t_slots[j], self.t_landing.at[j], p.side)

        def rest_of(column):
            rest = self.part[column, p.z, self.main : self.height].astype(jnp.float32)
            for j in (2, 3):
                rest = rest + self.t_landing[j, column].astype(jnp.float32)
            return rest

        self.t_kept[...] = rest_of(p.x)
        self.t_cross[0] = rest_of(1 - p.x).astype(jnp.bfloat16)
        self.cross_slot = wire.push(self.t_cross.at[0], self.t_cross.at[1], p.side)

    def total(self):
        p, wire = self.place, self.wire
        wire.arrive(self.x_slots[3], self.inbox.at[p.z], p.side)
        total = self.part[p.x, p.z, 0 : self.main].astype(jnp.float32)
        total = total + self.inbox[p.z].astype(jnp.float32)
        for j in (2, 3):
            wire.arrive(self.z_slots[j], self.landing.at[j], p.side)
            total = total + self.landing[j].astype(jnp.float32)
        if not self.split:
            return total
        wire.arrive(self.cross_slot, self.t_cross.at[1], p.side)
        rest = self.t_kept[...] + self.t_cross[1].astype(jnp.float32)
        return jnp.concatenate([total, rest], axis=0)


def fused(
    depth,
    lens,
    freq,
    xin_at,
    cot_at,
    in_at,
    gate_at,
    up_at,
    out_at,
    down_at,
    gain_a,
    bias_a,
    gain_b,
    bias_b,
    outputs_to,
    input_grad_to,
    g_in_to,
    g_mlp_to,
    g_out_to,
    g_down_to,
    cot,
    in_rows,
    gate_rows,
    up_rows,
    out_rows,
    outputs,
    input_grad,
    g_out,
    g_down,
    local_sem,
    xs,
    p_in,
    p_mlp,
    vectors_tab,
    r_in,
    r_mlp,
    s_out,
    w_in,
    w_value,
    w_gate,
    w_up,
    w_down,
    w_out,
    params,
    cos_tab,
    sin_tab,
    seg_tab,
    qm,
    kw,
    vw,
    prob,
    att,
    s_att,
    r_att,
    norm_one,
    hid,
    hs,
    gate_pre,
    up_pre,
    act,
    act_t,
    hs_t,
    s_mix,
    r_mix,
    t_mix,
    dres_two,
    dms,
    dgate,
    dup,
    s_dh,
    r_dh,
    t_dh,
    dres_one,
    s_da,
    r_da,
    acc_q,
    acc_k,
    acc_v,
    dj,
    s_ig,
    r_ig,
    t_ig,
    sum_in,
    sum_gate,
    sum_up,
    sum_down,
    b_out,
    rb_out,
    tb_out,
    sum_out,
    f_gate,
    s_gmlp,
    r_gmlp,
    s_gin,
    r_gin,
    send_sem,
    recv_sem,
):
    planes, cols = depth, 4
    tok = xin_at.shape[0]
    row_len = tok * cols
    place = Plane(planes)
    dp, blk = place.dp, place.blk
    bf16, f32 = jnp.bfloat16, jnp.float32

    row_of, core_of = blk // 2, blk % 2
    near_at = row_of * 2 + (1 - core_of)
    across_at = (1 - row_of) * 2 + core_of
    corner_at = (1 - row_of) * 2 + (1 - core_of)
    near, across = (dp, near_at), (dp, across_at)

    def lane(k):
        return (dp, (blk + k) % cols)

    def lane_from(k):
        return (blk + cols - k) % cols

    lanes = range(1, cols)
    local = []

    def move(source, target):
        copy = pltpu.make_async_copy(source, target, local_sem.at[len(local)])
        local.append(copy)
        copy.start()
        return copy

    xin = xs.at[blk]
    in_load = move(in_at, in_rows)
    out_load = move(out_at, out_rows)
    down_load = move(down_at, w_down.at[dp])
    x_load = move(xin_at, xin)
    gate_load = move(gate_at, gate_rows)
    up_load = move(up_at, up_rows)
    cot_load = move(cot_at, cot)
    wire = Wire(send_sem, recv_sem, place.inner == 1)
    barrier = pltpu.get_barrier_semaphore()
    peers = [place.side, place.at(place.partner), place.at(place.other)]
    peers = peers + [lane(k) for k in lanes]
    for peer in peers:
        pl.semaphore_signal(barrier, inc=1, device_id=peer, device_id_type=MESH_IDS)
    far = place.at(place.outer)

    @pl.when(place.inner == 1)
    def _():
        pl.semaphore_signal(barrier, inc=1, device_id=far, device_id_type=MESH_IDS)


    rows = 24
    width = xin_at.shape[1]
    lane_ids = lax.broadcasted_iota(jnp.int32, (1, LANES), 1)
    low_half = lane_ids < HALF
    head_width = width // cols
    vectors_tab[...] = jnp.zeros_like(vectors_tab)
    for number, vector in enumerate((gain_a, bias_a, gain_b, bias_b)):
        vectors_tab[number : number + 1, 0:rows] = vector[...].astype(f32)
    free_lane = lax.broadcasted_iota(jnp.int32, (8, LANES), 0) + HALF
    to_lane = jnp.where(
        free_lane == lax.broadcasted_iota(jnp.int32, (8, LANES), 1), 1.0, 0.0
    ).astype(bf16)
    vector_columns = tm(vectors_tab[...].astype(bf16), to_lane)[0:rows]
    in_load.wait()
    joined_rows = in_rows[...].astype(f32)
    for j in range(cols):
        starts = [kind * width + j * head_width for kind in range(3)]
        windows = [window_at(joined_rows, start) for start in starts]
        windows.append(
            jnp.where(
                low_half,
                window_at(joined_rows, starts[0] + LANES),
                window_at(joined_rows, starts[1] + LANES - HALF),
            )
        )
        windows.append(
            jnp.where(low_half, window_at(joined_rows, starts[2] + LANES), vector_columns)
        )
        packed = jnp.concatenate(windows, axis=1)
        p_in[j] = jnp.concatenate(
            [packed, jnp.zeros((8, packed.shape[1]), f32)], axis=0
        ).astype(bf16)
    out_load.wait()
    halved = [out_rows[:, n * width // 2 : (n + 1) * width // 2].astype(f32) for n in range(2)]
    s_out[blk, dp] = jnp.concatenate(halved, axis=0).astype(bf16)
    pl.semaphore_wait(barrier, len(peers) + place.inner)

    def to_lanes(source_of, target):
        return [wire.push(source_of((blk + k) % cols), target.at[blk], lane(k)) for k in lanes]

    def from_lanes(slots, target):
        for k, slot in zip(lanes, slots):
            wire.arrive(slot, target.at[lane_from(k)], lane(k))

    every = pl.ds(0, tok)

    def gather_start(own, target, cut=every):
        return [
            wire.push(own.at[cut], target.at[blk, cut], across),
            wire.push(own.at[cut], target.at[blk, cut], near),
        ]

    def gather_relay(slots, target, cut=every):
        came = target.at[across_at, cut]
        wire.arrive(slots[0], came, across)
        slots.append(wire.push(came, came, near))

    def gather_done(slots, target, cut=every):
        wire.arrive(slots[1], target.at[near_at, cut], near)
        wire.arrive(slots[2], target.at[corner_at, cut], near)

    def sum_start(part, inbox, cut=every):
        return [
            wire.push(part.at[corner_at, cut], inbox.at[0, cut], near),
            wire.push(part.at[near_at, cut], inbox.at[1, cut], near),
        ]

    def sum_relay(slots, part, inbox, staged, cut=every):
        wire.arrive(slots[0], inbox.at[0, cut], near)
        both = part[across_at, cut].astype(f32) + inbox[0, cut].astype(f32)
        staged[cut] = both.astype(bf16)
        slots.append(wire.push(staged.at[cut], inbox.at[2, cut], across))

    def sum_done(slots, part, inbox, cut=every):
        wire.arrive(slots[1], inbox.at[1, cut], near)
        total = part[blk, cut].astype(f32) + inbox[1, cut].astype(f32)
        wire.arrive(slots[2], inbox.at[2, cut], across)
        return total + inbox[2, cut].astype(f32)

    in_slots = to_lanes(lambda to: p_in.at[to], r_in)
    down_load.wait()
    tail = 0
    out_spread = Spread(wire, place, s_out.at[blk], 0)
    out_spread.start()
    out_spread.start_out()
    out_spread.start_side()
    down_spread = Spread(wire, place, w_down, DTF)
    down_spread.start()
    down_spread.start_out()
    down_spread.start_side()
    down_spread.tail_out(True)
    gate_load.wait()
    up_load.wait()
    units = gate_rows.shape[1] // cols
    unit_block = units // (planes * 2)
    for at, weight in ((0, gate_rows), (rows, up_rows)):
        whole = weight[...].astype(f32)
        for j in range(cols):
            packed = jnp.concatenate(
                [
                    gather_lanes(
                        whole,
                        unit_block,
                        n * LANES,
                        lambda ring_at, lane: lane + (cols - 1) * unit_block * ring_at + unit_block * j,
                    )
                    for n in range(units // LANES)
                ],
                axis=1,
            )
            p_mlp[j, at : at + rows] = packed.astype(bf16)
    mlp_slots = to_lanes(lambda to: p_mlp.at[to], r_mlp)
    x_load.wait()
    x_slots = gather_start(xin, xs)
    r_in[blk] = p_in[blk]
    r_mlp[blk] = p_mlp[blk]

    lengths = [lens[0, j] for j in range(lens.shape[1])]

    def layout(positions):
        segment = jnp.zeros_like(positions)
        begins = jnp.zeros_like(positions)
        bound = jnp.int32(0)
        for length in lengths:
            bound = bound + length
            passed = positions >= bound
            segment = segment + jnp.where(passed, 1, 0)
            begins = begins + jnp.where(passed, length, 0)
        return segment, positions - begins

    seg_rows, offsets = layout(lax.broadcasted_iota(jnp.int32, (row_len, LANES), 0))
    seg_tab[...] = seg_rows
    seg_key = layout(lax.broadcasted_iota(jnp.int32, (8, row_len), 1))[0][0:1]
    front = lane_ids % HALF < QUART
    angles = offsets.astype(f32) * freq[0:1]
    cos_tab[...] = jnp.cos(angles)
    sin_tab[...] = jnp.where(front, -1.0, 1.0) * jnp.sin(angles)

    def turn(window):
        return jnp.where(
            front, pltpu.roll(window, LANES - QUART, 1), pltpu.roll(window, QUART, 1)
        )

    from_lanes(in_slots, r_in)
    own_rows = cols * rows
    fold_rows = own_rows // 2
    heads_width = 4 * LANES

    def folded(last, tile):
        fold = jnp.where(low_half, last[0:fold_rows], pltpu.roll(last[fold_rows:], HALF, 1))
        chunks = [fold[n * 16 : (n + 1) * 16] for n in range(3)]
        chunks.append(jnp.concatenate([tile, jnp.zeros((8, LANES), f32)], axis=0))
        return jnp.concatenate(chunks, axis=1)

    def unfolded(below):
        fold = jnp.concatenate([below[:, n * LANES : (n + 1) * LANES] for n in range(3)], axis=0)
        return jnp.concatenate([fold, pltpu.roll(fold, HALF, 1)], axis=0), below[0:8, 3 * LANES :]

    gathered = jnp.concatenate(
        [r_in[j, 0:rows, :].astype(f32) for j in range(cols)], axis=0
    )
    last = gathered[:, heads_width:]
    padded = jnp.concatenate([last, jnp.zeros((LANES - own_rows, LANES), f32)], axis=0)
    w_in[dp] = jnp.concatenate(
        [gathered[:, :heads_width], folded(last, mt(to_lane, padded.astype(bf16)))], axis=0
    ).astype(bf16)
    in_spread = Spread(wire, place, w_in, tail)
    in_spread.start()
    in_spread.start_out()
    in_spread.start_side()
    from_lanes(mlp_slots, r_mlp)
    mlp_own = [r_mlp[j].astype(f32) for j in range(cols)]
    w_gate[dp] = jnp.concatenate([part[0:rows] for part in mlp_own], axis=0).astype(bf16)
    w_up[dp] = jnp.concatenate([part[rows:] for part in mlp_own], axis=0).astype(bf16)
    gate_spread = Spread(wire, place, w_gate, tail)
    up_spread = Spread(wire, place, w_up, tail)
    gate_spread.start()
    gate_spread.start_side()
    up_spread.start()
    out_spread.relay(2)
    for spread in (out_spread, down_spread):
        spread.relay(0, inner=True)
        spread.relay(1, inner=True)
    in_spread.relay(2)
    out_spread.relay(0, inner=False)
    out_spread.relay(1, inner=False)
    in_spread.relay(0)
    down_spread.relay(2)
    in_spread.relay(1)
    up_spread.start_side()
    gate_spread.start_out()
    up_spread.start_out()
    down_spread.tail()
    gate_spread.relay(0, inner=True)
    gate_spread.relay(1, inner=True)
    gather_relay(x_slots, xs)
    out_spread.settle()
    shards_here = pl.ds(0, planes * 2)
    out_lanes = gather_start(s_out.at[blk], s_out, shards_here)
    gate_spread.relay(2)
    up_spread.relay(2)
    gather_done(x_slots, xs)
    in_spread.settle()

    group = 2
    chunk = group * tok

    tiles = []
    for d in range(planes * 2):
        values, tile = unfolded(w_in[d, own_rows:, :].astype(f32))
        w_value[d] = jnp.where(low_half, values, 0.0).astype(bf16)
        tiles.append(tile)

    def project(step, carry):
        start = pl.multiple_of(step * chunk, chunk)
        here = pl.ds(start, chunk)
        tokens = xs[pl.ds(step * group, group)].reshape(chunk, width)
        joined = mm(tokens, w_in[:, 0:own_rows, :].reshape(width, heads_width))
        cosine, sine = cos_tab[here, :], sin_tab[here, :]

        def rotate(number):
            window = joined[:, number * LANES : (number + 1) * LANES]
            return window * cosine + turn(window) * sine

        scale = HALF ** -0.5
        queries = rotate(0).astype(bf16).astype(f32) * scale
        qm[0, here, :] = jnp.where(low_half, queries, 0.0).astype(bf16)
        qm[1, here, :] = jnp.where(low_half, 0.0, queries).astype(bf16)
        kw[0, here, :] = rotate(1).astype(bf16)
        vw[0, here, :] = joined[:, 2 * LANES : 3 * LANES].astype(bf16)
        both = rotate(3)
        qm[2, here, :] = jnp.where(low_half, both.astype(bf16).astype(f32) * scale, 0.0).astype(bf16)
        kw[1, here, :] = jnp.where(low_half, pltpu.roll(both, HALF, 1), 0.0).astype(bf16)
        vw[1, here, :] = mm(tokens, w_value[...].reshape(width, LANES)).astype(bf16)
        return carry

    lax.fori_loop(0, cols // group, project, 0)

    def attend(head):
        window = head // 2

        def step_fn(step, carry):
            here = pl.ds(pl.multiple_of(step * chunk, chunk), chunk)
            scores = mt(qm[head, here, :], kw[window])
            allowed = seg_tab[here, :][:, 0:1] == seg_key
            scores = jnp.where(allowed, scores, NEG)
            top = jnp.max(scores, axis=1, keepdims=True)
            raised = jnp.exp(scores - top)
            total = jnp.sum(raised, axis=1, keepdims=True)
            prob_low = (raised * (1.0 / total)).astype(bf16)
            prob[head, here, :] = prob_low
            mixed = mm(prob_low, vw[window])
            if head == 1:
                mixed = jnp.where(low_half, att[0, here, :], mixed)
            att[window, here, :] = mixed
            return carry

        lax.fori_loop(0, row_len // chunk, step_fn, 0)

    up_spread.relay(0, inner=True)
    attend(0)
    attend(1)
    up_spread.relay(1, inner=True)
    attend(2)
    last_segment = lens.shape[1] - 1
    for j in range(cols):
        here = slice(j * tok, (j + 1) * tok)
        kept = seg_tab[here, :] < last_segment
        s_att[j, :, 0:LANES] = jnp.where(kept, att[0, here, :], 0.0).astype(bf16)
        s_att[j, :, LANES : 2 * LANES] = jnp.where(kept, att[1, here, :], 0.0).astype(bf16)
    att_slots = to_lanes(lambda to: s_att.at[to], r_att)
    r_att[blk] = s_att[blk]

    down_spread.tail_out(False)
    gather_relay(out_lanes, s_out, shards_here)
    gate_spread.relay(0, inner=False)
    gate_spread.relay(1, inner=False)
    for j in range(2):
        down_spread.pass_tail(j)
    gather_done(out_lanes, s_out, shards_here)
    shards = planes * 2 * cols
    per_quarter = shards // cols
    head_rows = per_quarter * rows
    for quarter in range(cols):
        slots = [
            s_out[s % cols, s // cols].astype(f32)
            for s in range(quarter * per_quarter, (quarter + 1) * per_quarter)
        ]
        w_out[quarter, 0:head_rows, :] = jnp.concatenate(
            [
                jnp.concatenate([slot[n * rows : (n + 1) * rows] for slot in slots], axis=0)
                for n in range(2)
            ],
            axis=1,
        ).astype(bf16)
        w_out[quarter, head_rows:, :] = jnp.zeros(
            (w_out.shape[1] - head_rows, width), bf16
        )
    for n in range(width // LANES):
        first = n * LANES
        result = None
        for d in range(first // own_rows, (first + LANES - 1) // own_rows + 1):
            begin = d * own_rows - first
            piece = pltpu.roll(tiles[d], begin % LANES, 1)
            result = piece if result is None else jnp.where(lane_ids < begin, result, piece)
        params[:, first : first + LANES] = result
    gain_one, bias_one = params[0:1, :], params[1:2, :]
    gain_two, bias_two = params[2:3, :], params[3:4, :]

    def normalize(residual):
        centered = residual - jnp.mean(residual, axis=1, keepdims=True)
        variance = jnp.mean(centered * centered, axis=1, keepdims=True)
        spread = lax.rsqrt(variance + EPS)
        return centered * spread, spread

    def normalize_back(grad, normal, spread, gain):
        inner = grad * gain
        mean_inner = jnp.mean(inner, axis=1, keepdims=True)
        mean_both = jnp.mean(inner * normal, axis=1, keepdims=True)
        return (inner - mean_inner - normal * mean_both) * spread

    def column_sum(value):
        return jnp.sum(value, axis=0, keepdims=True)

    from_lanes(att_slots, r_att)
    branch = mm(r_att[0], w_out[0])
    for quarter in range(1, cols):
        branch = branch + mm(r_att[quarter], w_out[quarter])
    normal, spread_one = normalize(xin[...].astype(f32) + branch)
    norm_one[...] = normal
    hidden = normal * gain_one + bias_one
    hid[...] = hidden
    hs[blk] = hidden.astype(bf16)
    hid_slots = gather_start(hs.at[blk], hs)
    up_spread.relay(0, inner=False)
    up_spread.relay(1, inner=False)
    down_spread.relay(0, inner=False)
    down_spread.relay(1, inner=False)
    gather_relay(hid_slots, hs)
    gate_spread.settle()
    gather_done(hid_slots, hs)

    wide = 256
    strips = units // wide

    def each_strip(body):
        def step_fn(step, carry):
            body(pl.ds(pl.multiple_of(step * wide, wide), wide))
            return carry

        lax.fori_loop(0, strips, step_fn, 0)

    def expand_gate(here):
        tokens = hs[...].reshape(row_len, width)
        gate_pre[:, here] = mm(tokens, w_gate[:, :, here].reshape(width, wide))

    def expand_up(here):
        tokens = hs[...].reshape(row_len, width)
        up = mm(tokens, w_up[:, :, here].reshape(width, wide))
        gate = gate_pre[:, here]
        up_pre[:, here] = up
        act[:, here] = (gate / (1.0 + jnp.exp(-gate)) * up).astype(bf16)

    each_strip(expand_gate)
    hs_t[...] = hs[...].reshape(row_len, width).T
    up_spread.settle()
    each_strip(expand_up)
    down_spread.settle()
    down_spread.settle_tail()

    def contract(step, carry):
        here = pl.ds(pl.multiple_of(step * wide, wide), wide)
        mixed = mm(act[...], w_down[:, :, here].reshape(units, wide))
        s_mix[:, :, here] = mixed.reshape(cols, tok, wide).astype(bf16)
        return carry

    lax.fori_loop(0, width // wide, contract, 0)
    pieces = 4
    cot_load.wait()
    halves = [pl.ds(n * tok // pieces, tok // pieces) for n in range(pieces)]
    mix_slots = [sum_start(s_mix, r_mix, cut) for cut in halves]
    for slots, cut in zip(mix_slots, halves):
        sum_relay(slots, s_mix, r_mix, t_mix, cut)
    act_t[...] = act[...].T
    second_gain, second_bias, dm_slots = 0.0, 0.0, []
    for slots, cut in zip(mix_slots, halves):
        mlp_out = sum_done(slots, s_mix, r_mix, cut)
        normal, spread_two = normalize(hid[cut, :] + mlp_out)
        outputs[cut, :] = (normal * gain_two + bias_two).astype(bf16)
        grad = cot[cut, :].astype(f32)
        second_gain = second_gain + column_sum(grad * normal)
        second_bias = second_bias + column_sum(grad)
        d_two = normalize_back(grad, normal, spread_two, gain_two)
        dres_two[cut, :] = d_two
        dms[blk, cut] = d_two.astype(bf16)
        dm_slots.append(gather_start(dms.at[blk], dms, cut))
    writes = [move(outputs, outputs_to)]
    for slots, cut in zip(dm_slots, halves):
        gather_relay(slots, dms, cut)
    for slots, cut in zip(dm_slots, halves):
        gather_done(slots, dms, cut)

    down_sum = Collect(wire, place, sum_down)
    gate_sum = Collect(wire, place, sum_gate)
    up_sum = Collect(wire, place, sum_up)
    in_sum = Collect(wire, place, sum_in)
    out_sum = Collect(wire, place, sum_out)
    half = 4

    def fill_parts(part, left_of, right, more=lambda product, here: product):
        height = part.shape[2]

        def step_fn(step, carry):
            here = pl.ds(pl.multiple_of(step * half * height, LANES), half * height)
            product = more(mm(left_of(here), right()), here)
            for j in range(half):
                part[j % 2, step * (half // 2) + j // 2] = product[
                    j * height : (j + 1) * height
                ].astype(bf16)
            return carry

        lax.fori_loop(0, planes * 2 // half, step_fn, 0)

    fill_parts(down_sum.part, lambda here: act_t[here, :], lambda: dms[...].reshape(row_len, width))
    down_sum.send((1, 0,))
    down_sum.send_tails()

    block = w_down.shape[1]

    def active_grads(step, carry):
        here = pl.ds(pl.multiple_of(step * half * block, LANES), half * block)
        d_active = mt(
            dms[...].reshape(row_len, width),
            w_down[pl.ds(step * half, half)].reshape(half * block, width),
        )
        gate, up = gate_pre[:, here], up_pre[:, here]
        sg = 1.0 / (1.0 + jnp.exp(-gate))
        dgate[:, here] = (d_active * up * sg * (1.0 + gate * (1.0 - sg))).astype(bf16)
        dup[:, here] = (d_active * gate * sg).astype(bf16)
        return carry

    lax.fori_loop(0, planes * 2 // half, active_grads, 0)
    block = w_gate.shape[1]

    def hidden_rows(here):
        return hs_t[here, :]

    fill_parts(gate_sum.part, hidden_rows, lambda: dgate[...])
    gate_sum.send()
    def hidden_grads(step, carry):
        here = pl.ds(pl.multiple_of(step * half * block, LANES), half * block)
        those = pl.ds(step * half, half)
        mixed = mt(dgate[...], w_gate[those].reshape(half * block, units)) + mt(
            dup[...], w_up[those].reshape(half * block, units)
        )
        s_dh[:, :, here] = mixed.reshape(cols, tok, half * block).astype(bf16)
        return carry

    lax.fori_loop(0, planes * 2 // half, hidden_grads, 0)
    dh_slots = sum_start(s_dh, r_dh)

    sum_relay(dh_slots, s_dh, r_dh, t_dh)
    fill_parts(up_sum.part, hidden_rows, lambda: dup[...])
    up_sum.send((1, 0))
    down_sum.first(1)
    down_sum.first(0)
    d_hidden = dres_two[...] + sum_done(dh_slots, s_dh, r_dh)
    normal = norm_one[...]
    first_gain = column_sum(d_hidden * normal)
    first_bias = column_sum(d_hidden)
    d_one = normalize_back(d_hidden, normal, spread_one, gain_one)
    dres_one[...] = d_one
    d_branch = d_one.astype(bf16)
    mine = pl.ds(pl.multiple_of(blk * tok, tok), tok)
    kept = seg_tab[mine, :][:, 0:1] < last_segment
    for quarter in range(cols):
        pulled = mt(d_branch, w_out[quarter]).astype(bf16).astype(f32)
        s_da[quarter] = jnp.where(kept, pulled, 0.0).astype(bf16)
    da_slots = to_lanes(lambda to: s_da.at[to], r_da)
    r_da[blk] = s_da[blk]

    params[...] = jnp.concatenate(
        [first_gain, first_bias, second_gain, second_bias, jnp.zeros((4, width), f32)], axis=0
    )
    for quarter in range(cols):
        product = tm(r_att[quarter], d_branch)
        for t in range(per_quarter):
            s = quarter * per_quarter + t
            owner_dp = s // cols
            mine_rows = product[t * rows : (t + 1) * rows]
            halved = [mine_rows[:, n * width // 2 : (n + 1) * width // 2] for n in range(2)]
            b_out[s % cols, owner_dp % 2, owner_dp // 2] = jnp.concatenate(
                halved, axis=0
            ).astype(bf16)
    both_sides = pl.ds(0, 2)
    out_blk = sum_start(b_out, rb_out, both_sides)

    gate_sum.first(1)
    sum_relay(out_blk, b_out, rb_out, tb_out, both_sides)
    down_sum.second_tail(1)
    down_sum.second(1)
    gate_sum.first(0)
    from_lanes(da_slots, r_da)
    def attend_back(head):
        window = head // 2
        fresh = head != 1

        def step_fn(step, carry):
            here = pl.ds(pl.multiple_of(step * chunk, chunk), chunk)
            d_out = r_da[pl.ds(step * group, group), :, window * LANES : (window + 1) * LANES]
            d_out = d_out.reshape(chunk, LANES).astype(f32)
            if head == 0:
                d_out = jnp.where(low_half, d_out, 0.0)
            if head == 1:
                d_out = jnp.where(low_half, 0.0, d_out)
            d_low = d_out.astype(bf16)
            delta = jnp.sum(d_out * att[window, here, :], axis=1, keepdims=True)
            prob_low = prob[head, here, :]
            d_prob = mt(d_low, vw[window])
            d_score = (prob_low.astype(f32) * (d_prob - delta)).astype(bf16)
            d_query = mm(d_score, kw[window]) * (HALF ** -0.5)
            if head == 1:
                d_query = jnp.where(low_half, acc_q[0, here, :], d_query)
            acc_q[window, here, :] = d_query
            d_key = tm(d_score, qm[head, here, :])
            d_value = tm(prob_low, d_low)
            if fresh:

                @pl.when(step == 0)
                def _():
                    acc_k[window] = d_key
                    acc_v[window] = d_value

                @pl.when(step != 0)
                def _():
                    acc_k[window] = acc_k[window] + d_key
                    acc_v[window] = acc_v[window] + d_value
            else:
                acc_k[window] = acc_k[window] + d_key
                acc_v[window] = acc_v[window] + d_value
            return carry

        lax.fori_loop(0, row_len // chunk, step_fn, 0)

    attend_back(0)
    gate_sum.first(2)
    down_sum.second_tail(0)
    down_sum.second(0)
    attend_back(1)
    attend_back(2)

    cosine, sine = cos_tab[...], sin_tab[...]

    def rotate_back(vector):
        vector = vector.astype(bf16).astype(f32)
        return (vector * cosine - turn(vector) * sine).astype(bf16)

    dj[:, 0:LANES] = rotate_back(acc_q[0])
    dj[:, LANES : 2 * LANES] = rotate_back(acc_k[0])
    dj[:, 2 * LANES : 3 * LANES] = acc_v[0].astype(bf16)
    dj[:, 3 * LANES : 4 * LANES] = rotate_back(acc_q[1] + pltpu.roll(acc_k[1], HALF, 1))
    dj[:, 4 * LANES : 5 * LANES] = acc_v[1].astype(bf16)


    def input_parts(step, carry):
        here = pl.ds(pl.multiple_of(step * half * own_rows, LANES), half * own_rows)
        product = tm(xs[:, :, here].reshape(row_len, half * own_rows), dj[...])
        vectors = params[:, here]
        for j in range(half):
            mine_rows = product[j * own_rows : (j + 1) * own_rows]
            tile = jnp.where(lane_ids < own_rows, window_at(vectors, j * own_rows), 0.0)
            in_sum.part[j % 2, step * (half // 2) + j // 2] = jnp.concatenate(
                [mine_rows[:, :heads_width], folded(mine_rows[:, heads_width:], tile)], axis=0
            ).astype(bf16)
        return carry

    lax.fori_loop(0, planes * 2 // half, input_parts, 0)

    in_sum.send((1, 0))
    def input_grads(step, carry):
        here = pl.ds(pl.multiple_of(step * half * block, LANES), half * block)
        those = pl.ds(step * half, half)
        mixed = mt(dj[:, 0:heads_width], w_in[those, 0:own_rows].reshape(half * block, heads_width))
        mixed = mixed + mt(dj[:, heads_width:], w_value[those].reshape(half * block, LANES))
        s_ig[:, :, here] = mixed.reshape(cols, tok, half * block).astype(bf16)
        return carry

    lax.fori_loop(0, planes * 2 // half, input_grads, 0)
    ig_slots = sum_start(s_ig, r_ig)

    up_sum.first(1)
    gate_sum.second(1)
    sum_relay(ig_slots, s_ig, r_ig, t_ig)
    out_sum.part[...] = sum_done(out_blk, b_out, rb_out, both_sides).astype(bf16)
    out_sum.send((1, 0,))
    up_sum.send((2,))
    in_sum.send((2,))
    up_sum.send((3,))
    in_sum.send((3,))
    down_sum.send((2,))
    out_sum.send((2,))
    out_sum.send((3,))
    down_sum.send((3,))
    down_sum.tail()
    up_sum.first(0)
    gate_sum.second(0)
    in_sum.first(1)
    up_sum.second(1)
    in_sum.first(0)
    out_sum.first(1)
    out_sum.first(0)
    up_sum.second(0)
    f_gate[...] = gate_sum.total()
    in_sum.second(1)
    up_sum.first(2)
    grad_in = dres_one[...] + sum_done(ig_slots, s_ig, r_ig)
    input_grad[...] = grad_in.astype(bf16)
    writes.append(move(input_grad, input_grad_to))
    in_sum.second(0)
    out_sum.second(1)
    out_sum.second(0)
    in_sum.first(2)
    up_total = up_sum.total()
    gate_total = f_gate[...]
    for j in range(cols):
        here = slice(j * rows, (j + 1) * rows)
        s_gmlp[j] = jnp.concatenate([gate_total[here], up_total[here]], axis=0).astype(bf16)
    gmlp_slots = to_lanes(lambda to: s_gmlp.at[to], r_gmlp)
    r_gmlp[blk] = s_gmlp[blk]
    out_sum.first(2)
    down_sum.first(2)
    in_total = in_sum.total()
    values, tile = unfolded(in_total[own_rows:])
    columns = tm(tile.astype(bf16), to_lane)[0:own_rows]
    in_total = jnp.concatenate(
        [in_total[0:own_rows], jnp.where(low_half, values, columns)], axis=1
    )
    for j in range(cols):
        s_gin[j] = jnp.concatenate(
            [in_total[j * rows : (j + 1) * rows], jnp.zeros((8, in_total.shape[1]), f32)], axis=0
        ).astype(bf16)
    gin_slots = to_lanes(lambda to: s_gin.at[to], r_gin)
    r_gin[blk] = s_gin[blk]
    g_out[...] = out_sum.total()
    writes.append(move(g_out, g_out_to))
    g_down[...] = down_sum.total()
    writes.append(move(g_down, g_down_to))
    from_lanes(gmlp_slots, r_gmlp)
    writes.append(move(r_gmlp, g_mlp_to))
    from_lanes(gin_slots, r_gin)
    writes.append(move(r_gin, g_in_to))
    wire.finish()
    for write in writes:
        write.wait()


def unpack(
    rows,
    block,
    outputs,
    input_grad,
    g_in,
    g_mlp,
    g_out,
    g_down,
    outputs_to,
    input_grad_to,
    in_to,
    out_to,
    gate_to,
    up_to,
    down_to,
    *vectors_to,
):
    f32 = jnp.float32
    cols = g_in.shape[0]
    width = outputs.shape[1]
    outputs_to[0] = outputs[...]
    input_grad_to[0] = input_grad[...]
    down_to[...] = g_down[...]
    for n in range(2):
        out_to[:, n * width // 2 : (n + 1) * width // 2] = g_out[n * rows : (n + 1) * rows, :]
    low_half = lax.broadcasted_iota(jnp.int32, (1, LANES), 1) < HALF
    joined = [g_in[j].astype(f32)[0:rows] for j in range(cols)]
    vectors = joined[0][:, 4 * LANES :]
    for j in range(1, cols):
        vectors = vectors + joined[j][:, 4 * LANES :]
    vectors = jnp.concatenate([vectors, jnp.zeros((LANES - rows, LANES), f32)], axis=0).T
    for number, vector_to in enumerate(vectors_to):
        vector_to[...] = vectors[HALF + number, 0:rows]
    single_at = ((3, 0), (3, 1), (4, 0))

    def half(kind, number, want):
        owner, part = number // 3, number % 3
        window, at = (kind, part) if part < 2 else single_at[kind]
        value = joined[owner][:, window * LANES : (window + 1) * LANES]
        return value if at == want else pltpu.roll(value, HALF, 1)

    for kind in range(3):
        for n in range(width // LANES):
            at = kind * width + n * LANES
            in_to[:, at : at + LANES] = jnp.where(
                low_half, half(kind, 2 * n, 0), half(kind, 2 * n + 1, 1)
            )
    lanes = lax.broadcasted_iota(jnp.int32, (1, LANES), 1)
    mlp = [g_mlp[j].astype(f32) for j in range(cols)]
    for first_row, target in ((0, gate_to), (rows, up_to)):
        parts = [part[first_row : first_row + rows] for part in mlp]
        for n in range(target.shape[1] // LANES):
            first = n * LANES
            result = None
            for number in range(first // block, (first + LANES - 1) // block + 1):
                ring_at, owner = number // cols, number % cols
                piece = window_at(parts[owner], ring_at * block + first - number * block)
                begin = number * block - first
                result = piece if result is None else jnp.where(lanes < begin, result, piece)
            target[:, first : first + LANES] = result


def fast_shards(
    depth,
    inputs,
    doc_lengths,
    project_in,
    project_out,
    gate_weight,
    up_weight,
    down_weight,
    first_gain,
    first_bias,
    second_gain,
    second_bias,
    cotangent,
):
    cols = 4
    tok, width = inputs.shape[1:]
    rows = project_in.shape[0]
    ff = gate_weight.shape[1]
    ring = depth * 2
    row_len = tok * cols
    units = ff // cols
    block = units // ring
    head_width = width // cols
    in_width = 5 * LANES
    bf16, f32 = jnp.bfloat16, jnp.float32

    lane_ids = np.arange(LANES) % QUART
    freq = jnp.asarray(
        np.broadcast_to(BASE ** (-2.0 * lane_ids / HALF), (8, LANES)).astype(np.float32)
    )

    def scratch(*shape, kind=bf16):
        return pltpu.VMEM(shape, kind)

    def sums(height, across, tail=0):
        main = height - tail
        buffers = [
            scratch(2, depth, height, across),
            scratch(depth, main, across),
            scratch(depth, main, across),
            scratch(4, main, across),
        ]
        if tail:
            buffers = buffers + [
                scratch(4, 2, tail, across),
                scratch(2, 2, tail, across),
                scratch(2, tail, across),
                scratch(tail, across, kind=f32),
            ]
        return tuple(buffers)

    stacked = scratch(cols, tok, width)
    heads = 3
    buffers = [
        scratch(tok, width),
        scratch(rows, 3 * width),
        scratch(rows, ff),
        scratch(rows, ff),
        scratch(rows, width),
        scratch(tok, width),
        scratch(tok, width),
        scratch(2 * rows, width // 2, kind=f32),
        scratch(block, width, kind=f32),
        pltpu.SemaphoreType.DMA((16,)),
        stacked,
        scratch(cols, 32, in_width),
        scratch(cols, 2 * rows, units),
        scratch(8, LANES, kind=f32),
        scratch(cols, 32, in_width),
        scratch(cols, 2 * rows, units),
        scratch(cols, ring, 2 * rows, width // 2),
        scratch(ring, cols * rows + 16, 4 * LANES),
        scratch(ring, cols * rows, LANES),
        scratch(ring, cols * rows, units),
        scratch(ring, cols * rows, units),
        scratch(ring, block, width),
        scratch(cols, 2 * LANES, width),
        scratch(8, width, kind=f32),
        scratch(row_len, LANES, kind=f32),
        scratch(row_len, LANES, kind=f32),
        scratch(row_len, LANES, kind=jnp.int32),
        scratch(heads, row_len, LANES),
        scratch(2, row_len, LANES),
        scratch(2, row_len, LANES),
        scratch(heads, row_len, row_len),
        scratch(2, row_len, LANES, kind=f32),
        scratch(cols, tok, 2 * LANES),
        scratch(cols, tok, 2 * LANES),
        scratch(tok, width, kind=f32),
        scratch(tok, width, kind=f32),
        stacked,
        scratch(row_len, units, kind=f32),
        scratch(row_len, units, kind=f32),
        scratch(row_len, units),
        scratch(units, row_len),
        scratch(width, row_len),
        stacked,
        scratch(3, tok, width),
        scratch(tok, width),
        scratch(tok, width, kind=f32),
        stacked,
        scratch(row_len, units),
        scratch(row_len, units),
        stacked,
        scratch(3, tok, width),
        scratch(tok, width),
        scratch(tok, width, kind=f32),
        scratch(cols, tok, 2 * LANES),
        scratch(cols, tok, 2 * LANES),
        scratch(2, row_len, LANES, kind=f32),
        scratch(2, row_len, LANES, kind=f32),
        scratch(2, row_len, LANES, kind=f32),
        scratch(row_len, in_width),
        stacked,
        scratch(3, tok, width),
        scratch(tok, width),
        sums(cols * rows + 16, 4 * LANES),
        sums(cols * rows, units),
        sums(cols * rows, units),
        sums(block, width, DTB),
        scratch(cols, 2, depth, 2 * rows, width // 2),
        scratch(3, 2, depth, 2 * rows, width // 2),
        scratch(2, depth, 2 * rows, width // 2),
        sums(2 * rows, width // 2, 0),
        scratch(cols * rows, units, kind=f32),
        scratch(cols, 2 * rows, units),
        scratch(cols, 2 * rows, units),
        scratch(cols, 32, in_width),
        scratch(cols, 32, in_width),
        pltpu.SemaphoreType.DMA((240,)),
        pltpu.SemaphoreType.DMA((240,)),
    ]
    vmem = pl.BlockSpec(memory_space=pltpu.VMEM)
    anywhere = pl.BlockSpec(memory_space=pl.ANY)
    tokens = row_len * width
    outputs, input_grad, g_in, g_mlp, g_out, g_down = pl.pallas_call(
        functools.partial(fused, depth),
        out_shape=(
            jax.ShapeDtypeStruct((tok, width), bf16),
            jax.ShapeDtypeStruct((tok, width), bf16),
            jax.ShapeDtypeStruct((cols, 32, in_width), bf16),
            jax.ShapeDtypeStruct((cols, 2 * rows, units), bf16),
            jax.ShapeDtypeStruct((2 * rows, width // 2), f32),
            jax.ShapeDtypeStruct((block, width), f32),
        ),
        in_specs=[pl.BlockSpec(memory_space=pltpu.SMEM), vmem] + [anywhere] * 7 + [vmem] * 4,
        out_specs=(anywhere,) * 6,
        scratch_shapes=buffers,
        compiler_params=pltpu.CompilerParams(
            collective_id=0, has_side_effects=True, vmem_limit_bytes=60 * 2**20
        ),
        cost_estimate=pl.CostEstimate(
            flops=6 * tokens * (3 * units + 4 * head_width),
            bytes_accessed=8 * 2**20,
            transcendentals=3 * row_len * row_len,
        ),
        name="layer",
    )(
        doc_lengths,
        freq,
        inputs[0],
        cotangent[0],
        project_in,
        gate_weight,
        up_weight,
        project_out,
        down_weight,
        first_gain[None],
        first_bias[None],
        second_gain[None],
        second_bias[None],
    )

    vector = jax.ShapeDtypeStruct((rows,), f32)
    return pl.pallas_call(
        functools.partial(unpack, rows, block),
        out_shape=(
            jax.ShapeDtypeStruct((1, tok, width), bf16),
            jax.ShapeDtypeStruct((1, tok, width), bf16),
            jax.ShapeDtypeStruct((rows, 3 * width), f32),
            jax.ShapeDtypeStruct((rows, width), f32),
            jax.ShapeDtypeStruct((rows, ff), f32),
            jax.ShapeDtypeStruct((rows, ff), f32),
            jax.ShapeDtypeStruct((block, width), f32),
            vector,
            vector,
            vector,
            vector,
        ),
        in_specs=[vmem] * 6,
        out_specs=(vmem,) * 11,
        name="unpack",
    )(outputs, input_grad, g_in, g_mlp, g_out, g_down)


def pick(sizes):
    def chosen(*args):
        tok, width = args[0].shape[1:]
        ring, cols = sizes["dp"], sizes["blk"]
        fits = (
            ring == 8
            and cols == 4
            and tok == LANES
            and HEADS == 3 * cols
            and width == HEADS * HALF
            and args[2].shape[0] == 24
            and args[4].shape[1] == 4 * width
        )
        if fits:
            return fast_shards(ring // 2, *args)
        return shards(*args)

    return chosen


def solution(mesh):
    placed = (
        P("dp", "blk", None),
        P("dp", None),
        P(("dp", "blk"), None),
        P(("dp", "blk"), None),
        P(("dp", "blk"), None),
        P(("dp", "blk"), None),
        P(("dp", "blk"), None),
        P(("dp", "blk")),
        P(("dp", "blk")),
        P(("dp", "blk")),
        P(("dp", "blk")),
        P("dp", "blk", None),
    )
    return jax.shard_map(
        pick(dict(mesh.shape)),
        mesh=mesh,
        in_specs=placed,
        out_specs=(
            P("dp", "blk", None),
            P("dp", "blk", None),
            P(("dp", "blk"), None),
            P(("dp", "blk"), None),
            P(("dp", "blk"), None),
            P(("dp", "blk"), None),
            P(("dp", "blk"), None),
            P(("dp", "blk")),
            P(("dp", "blk")),
            P(("dp", "blk")),
            P(("dp", "blk")),
        ),
        check_vma=False,
    )
```

```python
import functools

import jax
import jax.numpy as jnp
import numpy as np
from jax import lax
from jax.experimental import pallas as pl
from jax.experimental.pallas import tpu as pltpu
from jax.sharding import PartitionSpec as P

HEADS = 12


NEG = -1e30
EPS = 1e-05
BASE = 1000.0


def doc_layout(lengths_row, positions):
    bounds = jnp.cumsum(lengths_row)
    passed = positions[:, None] >= bounds[None, :]
    segment = jnp.sum(passed.astype(jnp.int32), axis=1)
    begins = jnp.sum(jnp.where(passed, lengths_row[None, :], 0), axis=1)
    return (segment, positions - begins)


def rotary(vectors, offsets):
    half_size = vectors.shape[-1] // 2
    frequency = BASE ** (-2.0 * jnp.arange(half_size, dtype=jnp.float32) / vectors.shape[-1])
    angles = offsets.astype(jnp.float32)[:, None] * frequency[None, :]
    cosine = jnp.concatenate([jnp.cos(angles), jnp.cos(angles)], axis=1)[:, None, :]
    sine_rows = jnp.concatenate([jnp.sin(angles), jnp.sin(angles)], axis=1)[:, None, :]
    first_half = vectors[..., :half_size]
    second_half = vectors[..., half_size:]
    turned = jnp.concatenate([-second_half, first_half], axis=-1)
    return vectors * cosine + turned * sine_rows


def layer_norm(residual, gain_row, bias_row):
    row_mean = jnp.mean(residual, axis=-1, keepdims=True)
    centered = residual - row_mean
    variance = jnp.mean(centered * centered, axis=-1, keepdims=True)
    return centered * lax.rsqrt(variance + EPS) * gain_row + bias_row


def contract_rows(left, right):
    return lax.dot_general(
        left, right, (((0,), (0,)), ((), ())), preferred_element_type=jnp.float32
    )


def contract_cols(left, right):
    return lax.dot_general(
        left, right, (((1,), (1,)), ((), ())), preferred_element_type=jnp.float32
    )


def tile_scores(query_tile, key_tile, seg_query, seg_key, score_scale):
    scores = (
        jnp.einsum("qhd,khd->hqk", query_tile, key_tile, preferred_element_type=jnp.float32)
        * score_scale
    )
    allowed = (seg_query[:, None] == seg_key[None, :])[None, :, :]
    return (jnp.where(allowed, scores, NEG), allowed)


def run_groups(pieces, group, lengths_row, seg_query, carried, tile_fn, extra_shape):
    group_count = pieces[0].shape[0] // group

    def group_step(carried_in, number):
        offset = number * group
        tile_set = tuple(
            (lax.dynamic_slice_in_dim(piece_rows, offset, group, 0) for piece_rows in pieces)
        )
        positions = offset + jnp.arange(group, dtype=jnp.int32)
        seg_key, unused_offsets = doc_layout(lengths_row, positions)
        touches = (seg_key[0] <= seg_query[-1]) & (seg_query[0] <= seg_key[-1])

        def active(state_in):
            return tile_fn(state_in, tile_set, seg_key)

        def skipped(state_in):
            return (state_in, jnp.zeros(extra_shape, jnp.float32))

        return lax.cond(touches, active, skipped, carried_in)

    return lax.scan(group_step, carried, jnp.arange(group_count, dtype=jnp.int32))


def shards(
    inputs,
    doc_lengths,
    project_in,
    project_out,
    gate_weight,
    up_weight,
    down_weight,
    first_gain,
    first_bias,
    second_gain,
    second_bias,
    cotangent,
):
    group = inputs.shape[1]
    width = inputs.shape[2]
    head_count = HEADS
    head_size = width // head_count
    score_scale = head_size ** (-0.5)
    cycle_rank = lax.axis_index("blk")
    positions = cycle_rank * group + jnp.arange(group, dtype=jnp.int32)
    lengths_row = doc_lengths[0]
    seg_query, offsets = doc_layout(lengths_row, positions)
    keep_mask = seg_query < lengths_row.shape[0] - 1
    keep_float = keep_mask.astype(jnp.float32)
    fetched = (
        lax.all_gather(project_in, ("dp", "blk"), axis=0, tiled=True),
        lax.all_gather(project_out, ("dp", "blk"), axis=0, tiled=True),
        lax.all_gather(gate_weight, ("dp", "blk"), axis=0, tiled=True),
        lax.all_gather(up_weight, ("dp", "blk"), axis=0, tiled=True),
        lax.all_gather(down_weight, ("dp", "blk"), axis=0, tiled=True),
        lax.all_gather(first_gain, ("dp", "blk"), axis=0, tiled=True),
        lax.all_gather(first_bias, ("dp", "blk"), axis=0, tiled=True),
        lax.all_gather(second_gain, ("dp", "blk"), axis=0, tiled=True),
        lax.all_gather(second_bias, ("dp", "blk"), axis=0, tiled=True),
    )
    full_in, full_out, full_gate, full_up, full_down = (
        fetched[0],
        fetched[1],
        fetched[2],
        fetched[3],
        fetched[4],
    )
    gain_one = fetched[5].astype(jnp.float32)
    bias_one = fetched[6].astype(jnp.float32)
    gain_two = fetched[7].astype(jnp.float32)
    bias_two = fetched[8].astype(jnp.float32)
    tokens_low = inputs[0]
    tokens_f = tokens_low.astype(jnp.float32)
    joined = jnp.dot(tokens_low, full_in, preferred_element_type=jnp.float32)
    query_raw = joined[:, :width].reshape(group, head_count, head_size)
    key_raw = joined[:, width : 2 * width].reshape(group, head_count, head_size)
    value_low = joined[:, 2 * width :].astype(jnp.bfloat16)
    query_rot, query_pull = jax.vjp(lambda vectors: rotary(vectors, offsets), query_raw)
    key_rot, key_pull = jax.vjp(lambda vectors: rotary(vectors, offsets), key_raw)
    query_low = query_rot.astype(jnp.bfloat16)
    key_low = key_rot.reshape(group, width).astype(jnp.bfloat16)

    def stats_tile(carried, tile_set, seg_key):
        row_top, row_total = carried
        key_tile = tile_set[0].reshape(group, head_count, head_size)
        scores, allowed = tile_scores(query_low, key_tile, seg_query, seg_key, score_scale)
        new_top = jnp.maximum(row_top, jnp.max(scores, axis=2))
        shrink = jnp.exp(row_top - new_top)
        added = jnp.sum(jnp.where(allowed, jnp.exp(scores - new_top[:, :, None]), 0.0), axis=2)
        return ((new_top, row_total * shrink + added), jnp.zeros((1,), jnp.float32))

    init_stats = (
        jnp.full((head_count, group), NEG, jnp.float32),
        jnp.zeros((head_count, group), jnp.float32),
    )
    carried = init_stats
    carried, unused = run_groups(
        (lax.all_gather(key_low, "blk", axis=0, tiled=True),),
        group,
        lengths_row,
        seg_query,
        carried,
        stats_tile,
        (1,),
    )
    row_top, row_total = carried
    log_total = row_top + jnp.log(row_total)

    def output_tile(accum, tile_set, seg_key):
        key_tile = tile_set[0].reshape(group, head_count, head_size)
        value_tile = tile_set[1].reshape(group, head_count, head_size)
        scores, allowed = tile_scores(query_low, key_tile, seg_query, seg_key, score_scale)
        prob_low = jnp.where(allowed, jnp.exp(scores - log_total[:, :, None]), 0.0).astype(
            jnp.bfloat16
        )
        accum = accum + jnp.einsum(
            "hqk,khd->qhd", prob_low, value_tile, preferred_element_type=jnp.float32
        )
        return (accum, jnp.zeros((1,), jnp.float32))

    zero_accum = jnp.zeros((group, head_count, head_size), jnp.float32)
    accum = zero_accum
    accum, unused = run_groups(
        (
            lax.all_gather(key_low, "blk", axis=0, tiled=True),
            lax.all_gather(value_low, "blk", axis=0, tiled=True),
        ),
        group,
        lengths_row,
        seg_query,
        accum,
        output_tile,
        (1,),
    )
    attend_low = (accum * keep_float[:, None, None]).reshape(group, width).astype(jnp.bfloat16)
    branch = jnp.dot(attend_low, full_out, preferred_element_type=jnp.float32)
    residual_one = tokens_f + branch
    hidden, norm_one_pull = jax.vjp(layer_norm, residual_one, gain_one, bias_one)
    hidden_low = hidden.astype(jnp.bfloat16)
    gate_pre = jnp.dot(hidden_low, full_gate, preferred_element_type=jnp.float32)
    up_pre = jnp.dot(hidden_low, full_up, preferred_element_type=jnp.float32)
    activated, swiglu_pull = jax.vjp(
        lambda gate_in, up_in: jax.nn.silu(gate_in) * up_in, gate_pre, up_pre
    )
    active_low = activated.astype(jnp.bfloat16)
    mlp_out = jnp.dot(active_low, full_down, preferred_element_type=jnp.float32)
    outputs_f, norm_two_pull = jax.vjp(layer_norm, hidden + mlp_out, gain_two, bias_two)
    refetched = (
        lax.all_gather(project_in, ("dp", "blk"), axis=0, tiled=True),
        lax.all_gather(project_out, ("dp", "blk"), axis=0, tiled=True),
        lax.all_gather(gate_weight, ("dp", "blk"), axis=0, tiled=True),
        lax.all_gather(up_weight, ("dp", "blk"), axis=0, tiled=True),
        lax.all_gather(down_weight, ("dp", "blk"), axis=0, tiled=True),
    )
    full_in, full_out, full_gate, full_up, full_down = (
        refetched[0],
        refetched[1],
        refetched[2],
        refetched[3],
        refetched[4],
    )
    d_res_two, second_gain_part, second_bias_part = norm_two_pull(cotangent[0].astype(jnp.float32))
    d_mlp_low = d_res_two.astype(jnp.bfloat16)
    down_part = contract_rows(active_low, d_mlp_low)
    d_active = contract_cols(d_mlp_low, full_down)
    d_gate, d_up = swiglu_pull(d_active)
    d_gate_low = d_gate.astype(jnp.bfloat16)
    d_up_low = d_up.astype(jnp.bfloat16)
    gate_part = contract_rows(hidden_low, d_gate_low)
    up_part = contract_rows(hidden_low, d_up_low)
    d_hidden = d_res_two + contract_cols(d_gate_low, full_gate) + contract_cols(d_up_low, full_up)
    d_res_one, first_gain_part, first_bias_part = norm_one_pull(d_hidden)
    d_branch_low = d_res_one.astype(jnp.bfloat16)
    out_part = contract_rows(attend_low, d_branch_low)
    d_attend = contract_cols(d_branch_low, full_out).astype(jnp.bfloat16)
    d_attend_low = (d_attend * keep_mask[:, None].astype(jnp.bfloat16)).reshape(
        group, head_count, head_size
    )
    delta = jnp.einsum("qhd,qhd->hq", d_attend_low.astype(jnp.float32), accum)

    def back_tile(grad_query, tile_set, seg_key):
        key_tile = tile_set[0].reshape(group, head_count, head_size)
        value_tile = tile_set[1].reshape(group, head_count, head_size)
        scores, allowed = tile_scores(query_low, key_tile, seg_query, seg_key, score_scale)
        prob_rows = jnp.where(allowed, jnp.exp(scores - log_total[:, :, None]), 0.0)
        d_probs = jnp.einsum(
            "qhd,khd->hqk", d_attend_low, value_tile, preferred_element_type=jnp.float32
        )
        d_score_low = (prob_rows * (d_probs - delta[:, :, None])).astype(jnp.bfloat16)
        grad_query = (
            grad_query
            + jnp.einsum("hqk,khd->qhd", d_score_low, key_tile, preferred_element_type=jnp.float32)
            * score_scale
        )
        grad_key = (
            jnp.einsum("hqk,qhd->khd", d_score_low, query_low, preferred_element_type=jnp.float32)
            * score_scale
        )
        grad_value = jnp.einsum(
            "hqk,qhd->khd",
            prob_rows.astype(jnp.bfloat16),
            d_attend_low,
            preferred_element_type=jnp.float32,
        )
        return (
            grad_query,
            jnp.concatenate(
                [grad_key.reshape(group, width), grad_value.reshape(group, width)], axis=1
            ),
        )

    grad_query = zero_accum
    grad_query, blocks = run_groups(
        (
            lax.all_gather(key_low, "blk", axis=0, tiled=True),
            lax.all_gather(value_low, "blk", axis=0, tiled=True),
        ),
        group,
        lengths_row,
        seg_query,
        grad_query,
        back_tile,
        (group, 2 * width),
    )
    blocks = blocks.reshape(-1, 2 * width)
    back_result = (grad_query, blocks)
    grad_query = back_result[0]
    owned_pairs = lax.psum_scatter(
        back_result[1].astype(jnp.bfloat16), "blk", scatter_dimension=0, tiled=True
    ).astype(jnp.float32)
    key_sum = owned_pairs[:, :width]
    value_sum = owned_pairs[:, width:]
    d_query_pre = query_pull(grad_query.astype(jnp.bfloat16).astype(jnp.float32))[0]
    d_key_low = key_sum.astype(jnp.bfloat16).astype(jnp.float32)
    d_key_pre = key_pull(d_key_low.reshape(group, head_count, head_size))[0]
    d_value_low = value_sum.astype(jnp.bfloat16).astype(jnp.float32)
    d_joined_low = jnp.concatenate(
        [d_query_pre.reshape(group, width), d_key_pre.reshape(group, width), d_value_low], axis=1
    ).astype(jnp.bfloat16)
    in_part = contract_rows(tokens_low, d_joined_low)
    input_grad = (d_res_one + contract_cols(d_joined_low, full_in)).astype(jnp.bfloat16)
    by_rows = (
        lax.psum_scatter(
            in_part.astype(jnp.bfloat16), "dp", scatter_dimension=0, tiled=True
        ).astype(jnp.float32),
        lax.psum_scatter(
            out_part.astype(jnp.bfloat16), "dp", scatter_dimension=0, tiled=True
        ).astype(jnp.float32),
        lax.psum_scatter(
            gate_part.astype(jnp.bfloat16), "dp", scatter_dimension=0, tiled=True
        ).astype(jnp.float32),
        lax.psum_scatter(
            up_part.astype(jnp.bfloat16), "dp", scatter_dimension=0, tiled=True
        ).astype(jnp.float32),
        lax.psum_scatter(
            down_part.astype(jnp.bfloat16), "dp", scatter_dimension=0, tiled=True
        ).astype(jnp.float32),
        lax.psum_scatter(
            first_gain_part.astype(jnp.bfloat16), "dp", scatter_dimension=0, tiled=True
        ).astype(jnp.float32),
        lax.psum_scatter(
            first_bias_part.astype(jnp.bfloat16), "dp", scatter_dimension=0, tiled=True
        ).astype(jnp.float32),
        lax.psum_scatter(
            second_gain_part.astype(jnp.bfloat16), "dp", scatter_dimension=0, tiled=True
        ).astype(jnp.float32),
        lax.psum_scatter(
            second_bias_part.astype(jnp.bfloat16), "dp", scatter_dimension=0, tiled=True
        ).astype(jnp.float32),
    )
    summed = (
        lax.psum_scatter(
            by_rows[0].astype(jnp.bfloat16), "blk", scatter_dimension=0, tiled=True
        ).astype(jnp.float32),
        lax.psum_scatter(
            by_rows[1].astype(jnp.bfloat16), "blk", scatter_dimension=0, tiled=True
        ).astype(jnp.float32),
        lax.psum_scatter(
            by_rows[2].astype(jnp.bfloat16), "blk", scatter_dimension=0, tiled=True
        ).astype(jnp.float32),
        lax.psum_scatter(
            by_rows[3].astype(jnp.bfloat16), "blk", scatter_dimension=0, tiled=True
        ).astype(jnp.float32),
        lax.psum_scatter(
            by_rows[4].astype(jnp.bfloat16), "blk", scatter_dimension=0, tiled=True
        ).astype(jnp.float32),
        lax.psum_scatter(
            by_rows[5].astype(jnp.bfloat16), "blk", scatter_dimension=0, tiled=True
        ).astype(jnp.float32),
        lax.psum_scatter(
            by_rows[6].astype(jnp.bfloat16), "blk", scatter_dimension=0, tiled=True
        ).astype(jnp.float32),
        lax.psum_scatter(
            by_rows[7].astype(jnp.bfloat16), "blk", scatter_dimension=0, tiled=True
        ).astype(jnp.float32),
        lax.psum_scatter(
            by_rows[8].astype(jnp.bfloat16), "blk", scatter_dimension=0, tiled=True
        ).astype(jnp.float32),
    )
    return (
        outputs_f.astype(jnp.bfloat16)[None],
        input_grad[None],
        summed[0],
        summed[1],
        summed[2],
        summed[3],
        summed[4],
        summed[5],
        summed[6],
        summed[7],
        summed[8],
    )


MESH_IDS = pl.DeviceIdType.MESH
LANES = 128
HALF = 64
QUART = 32
DTF = 64
DTB = 64


def mm(left, right):
    return lax.dot_general(
        left, right, (((1,), (0,)), ((), ())), preferred_element_type=jnp.float32
    )


def mt(left, right):
    return lax.dot_general(
        left, right, (((1,), (1,)), ((), ())), preferred_element_type=jnp.float32
    )


def tm(left, right):
    return lax.dot_general(
        left, right, (((0,), (0,)), ((), ())), preferred_element_type=jnp.float32
    )


def window_at(value, start):
    aligned = min(max(start // LANES * LANES, 0), value.shape[1] - LANES)
    if aligned == start:
        return value[:, aligned : aligned + LANES]
    aligned = min(aligned, value.shape[1] - 2 * LANES)
    two = value[:, aligned : aligned + 2 * LANES]
    return pltpu.roll(two, (aligned - start) % (2 * LANES), 1)[:, :LANES]


def gather_lanes(value, block, first, source):
    lanes = lax.broadcasted_iota(jnp.int32, (1, LANES), 1)
    result = None
    for number in range(first // block, (first + LANES - 1) // block + 1):
        piece = window_at(value, source(number, first))
        begin = number * block - first
        result = piece if result is None else jnp.where(lanes < begin, result, piece)
    return result


class Wire:
    def __init__(self, send_sem, recv_sem, is_inner):
        self.send_sem, self.recv_sem, self.is_inner = send_sem, recv_sem, is_inner
        self.sends, self.slots = 0, 0
        self.sent = {None: [], True: [], False: []}

    def slot(self):
        self.slots += 1
        return self.slots - 1

    def copy(self, src, dst, peer, slot):
        self.sends += 1
        return pltpu.make_async_remote_copy(
            src_ref=src,
            dst_ref=dst,
            send_sem=self.send_sem.at[self.sends - 1],
            recv_sem=self.recv_sem.at[slot],
            device_id=peer,
            device_id_type=MESH_IDS,
        )

    def push(self, src, dst, peer, slot=None, inner=None):
        slot = self.slot() if slot is None else slot
        copy = self.copy(src, dst, peer, slot)
        self.sent[inner].append(copy)
        if inner is None:
            copy.start()
        else:
            pl.when(self.is_inner == inner)(copy.start)
        return slot

    def arrive(self, slot, dst, peer):
        pltpu.make_async_remote_copy(
            src_ref=dst,
            dst_ref=dst,
            send_sem=self.send_sem.at[0],
            recv_sem=self.recv_sem.at[slot],
            device_id=peer,
            device_id_type=MESH_IDS,
        ).wait_recv()

    def finish(self):
        for inner, copies in self.sent.items():

            def drain(copies=copies):
                for copy in copies:
                    copy.wait_send()

            if inner is None:
                drain()
            else:
                pl.when(self.is_inner == inner)(drain)


class Plane:
    def __init__(self, planes):
        dp, self.blk = lax.axis_index("dp"), lax.axis_index("blk")
        self.z, self.x = dp // 2, dp % 2
        self.dp = dp
        self.partner = self.z + 1 - 2 * (self.z % 2)
        self.other = planes // 2 - self.z // (planes // 2)
        self.outer = (planes - 1) * (self.other - 1)
        self.inner = ((self.z + 1) // 2) % 2
        self.order = (self.other, self.outer, self.partner, self.z)
        self.side = (self.z * 2 + (1 - self.x), self.blk)

    def at(self, plane):
        return (plane * 2 + self.x, self.blk)


class Spread:
    def __init__(self, wire, place, target, tail):
        self.wire, self.place, self.target = wire, place, target
        self.height, self.main = target.shape[1], target.shape[1] - tail

    def block(self, plane, column):
        return self.target.at[plane * 2 + column, 0 : self.main]

    def pair(self, plane):
        return self.target.at[pl.ds(plane * 2, 2), self.main : self.height]

    def along(self, own, slots):
        p = self.place
        self.wire.push(own, own, p.at(p.partner), slots[2], inner=False)
        self.wire.push(own, own, p.at(p.other), slots[0] + (1 - p.inner))

    def outward(self, own, slots):
        p = self.place
        self.wire.push(own, own, p.at(p.partner), slots[2], inner=True)

    def start(self):
        p, wire = self.place, self.wire
        self.z_slots = [wire.slot() for _ in range(3)]
        self.along(self.block(p.z, p.x), self.z_slots)

    def start_out(self):
        p = self.place
        self.outward(self.block(p.z, p.x), self.z_slots)

    def start_side(self):
        p, wire = self.place, self.wire
        self.x_slots = [wire.slot() for _ in range(4)]
        own = self.block(p.z, p.x)
        wire.push(own, own, p.side, self.x_slots[3])
        if self.main < self.height:
            self.out_slots = []
            self.rest_slot = wire.push(self.rest(p.x), self.rest(p.x), p.side)

    def tail(self):
        p, wire = self.place, self.wire
        rest = self.target.at[p.z * 2 + (1 - p.x), self.main : self.height]
        wire.arrive(self.rest_slot, rest, p.side)
        self.t_slots = [wire.slot() for _ in range(3)]
        self.along(self.pair(p.z), self.t_slots)

    def rest(self, column):
        p = self.place
        return self.target.at[p.z * 2 + column, self.main : self.height]

    def tail_out(self, own):
        p, wire = self.place, self.wire
        rest = self.rest(p.x if own else 1 - p.x)
        self.out_slots.append(wire.push(rest, rest, p.at(p.partner), inner=True))

    def relay(self, j, inner=None):
        p, wire = self.place, self.wire
        block = self.block(p.order[j], p.x)
        onward = wire.copy(block, block, p.side, self.x_slots[j])
        wire.sent[inner].append(onward)
        outward = None
        if j < 2 and inner is not False:
            outward = wire.copy(block, block, p.at(p.partner), self.z_slots[j])
            wire.sent[True].append(outward)

        def run():
            wire.arrive(self.z_slots[j], block, p.side)
            if outward is not None:
                if inner:
                    outward.start()
                else:
                    pl.when(wire.is_inner)(outward.start)
            onward.start()

        if inner is None:
            run()
        else:
            pl.when(wire.is_inner == inner)(run)

    def pass_tail(self, j):
        p, wire = self.place, self.wire
        pair = self.pair(p.order[j])
        copy = wire.copy(pair, pair, p.at(p.partner), self.t_slots[j])
        wire.sent[True].append(copy)

        @pl.when(wire.is_inner)
        def _():
            wire.arrive(self.t_slots[j], pair, p.side)
            copy.start()

    def settle_tail(self):
        p, wire = self.place, self.wire

        @pl.when(wire.is_inner)
        def _():
            wire.arrive(self.t_slots[2], self.pair(p.order[2]), p.side)

        @pl.when(jnp.logical_not(wire.is_inner))
        def _():
            for j in range(2):
                wire.arrive(self.t_slots[j], self.pair(p.order[j]), p.side)
            for slot, column in zip(self.out_slots, (p.x, 1 - p.x)):
                came = self.target.at[p.partner * 2 + column, self.main : self.height]
                wire.arrive(slot, came, p.side)

    def settle(self):
        p = self.place
        for j in range(4):
            self.wire.arrive(self.x_slots[j], self.block(p.order[j], 1 - p.x), p.side)


class Collect:
    def __init__(self, wire, place, buffers):
        self.wire, self.place = wire, place
        self.part, self.inbox, self.staged, self.landing = buffers[:4]
        self.height, self.main = self.part.shape[2], self.inbox.shape[1]
        self.split = self.main < self.height
        self.x_slots = [wire.slot() for _ in range(4)]
        self.z_slots = [wire.slot() for _ in range(4)]
        if self.split:
            self.t_landing, self.t_staged, self.t_cross, self.t_kept = buffers[4:]
            self.t_slots = [wire.slot() for _ in range(4)]

    def pair(self, plane):
        return self.part.at[:, plane, self.main : self.height]

    def send_side(self, j):
        p = self.place
        plane = p.order[j]
        self.wire.push(
            self.part.at[1 - p.x, plane, 0 : self.main],
            self.inbox.at[plane],
            p.side,
            self.x_slots[j],
        )

    def send(self, order=(1, 0, 2, 3)):
        for j in order:
            self.send_side(j)

    def send_tails(self):
        p = self.place
        for j in (1, 0, 2):
            self.wire.push(
                self.pair(p.order[j]),
                self.t_landing.at[j],
                p.at(p.partner),
                self.t_slots[j],
                inner=None if j == 2 else False,
            )

    def first(self, j):
        p, wire = self.place, self.wire
        plane = p.order[j]
        wire.arrive(self.x_slots[j], self.inbox.at[plane], p.side)
        both = self.part[p.x, plane, 0 : self.main].astype(jnp.float32)
        both = both + self.inbox[plane].astype(jnp.float32)
        self.staged[plane] = both.astype(jnp.bfloat16)
        wire.push(
            self.staged.at[plane],
            self.landing.at[j],
            p.at(p.partner),
            self.z_slots[j],
            inner=None if j == 2 else False,
        )

    def second(self, j):
        p, wire = self.place, self.wire
        plane = p.order[j]
        copy = wire.copy(self.staged.at[plane], self.landing.at[3], p.at(plane), self.z_slots[3])
        wire.sent[True].append(copy)

        @pl.when(wire.is_inner)
        def _():
            wire.arrive(self.z_slots[j], self.landing.at[j], p.side)
            both = self.staged[plane].astype(jnp.float32) + self.landing[j].astype(jnp.float32)
            self.staged[plane] = both.astype(jnp.bfloat16)
            copy.start()

    def second_tail(self, j):
        p, wire = self.place, self.wire
        plane = p.order[j]
        copy = wire.copy(self.t_staged.at[j], self.t_landing.at[3], p.at(plane), self.t_slots[3])
        wire.sent[True].append(copy)

        @pl.when(wire.is_inner)
        def _():
            wire.arrive(self.t_slots[j], self.t_landing.at[j], p.side)
            rest = self.part[:, plane, self.main : self.height].astype(jnp.float32)
            rest = rest + self.t_landing[j].astype(jnp.float32)
            self.t_staged[j] = rest.astype(jnp.bfloat16)
            copy.start()

    def tail(self):
        p, wire = self.place, self.wire
        for j in (2, 3):
            wire.arrive(self.t_slots[j], self.t_landing.at[j], p.side)

        def rest_of(column):
            rest = self.part[column, p.z, self.main : self.height].astype(jnp.float32)
            for j in (2, 3):
                rest = rest + self.t_landing[j, column].astype(jnp.float32)
            return rest

        self.t_kept[...] = rest_of(p.x)
        self.t_cross[0] = rest_of(1 - p.x).astype(jnp.bfloat16)
        self.cross_slot = wire.push(self.t_cross.at[0], self.t_cross.at[1], p.side)

    def total(self):
        p, wire = self.place, self.wire
        wire.arrive(self.x_slots[3], self.inbox.at[p.z], p.side)
        total = self.part[p.x, p.z, 0 : self.main].astype(jnp.float32)
        total = total + self.inbox[p.z].astype(jnp.float32)
        for j in (2, 3):
            wire.arrive(self.z_slots[j], self.landing.at[j], p.side)
            total = total + self.landing[j].astype(jnp.float32)
        if not self.split:
            return total
        wire.arrive(self.cross_slot, self.t_cross.at[1], p.side)
        rest = self.t_kept[...] + self.t_cross[1].astype(jnp.float32)
        return jnp.concatenate([total, rest], axis=0)


def fused(
    depth,
    lens,
    freq,
    xin_at,
    cot_at,
    in_at,
    gate_at,
    up_at,
    out_at,
    down_at,
    gain_a,
    bias_a,
    gain_b,
    bias_b,
    outputs_to,
    input_grad_to,
    g_in_to,
    g_mlp_to,
    g_out_to,
    g_down_to,
    cot,
    in_rows,
    gate_rows,
    up_rows,
    out_rows,
    outputs,
    input_grad,
    g_out,
    g_down,
    local_sem,
    xs,
    p_in,
    p_mlp,
    vectors_tab,
    r_in,
    r_mlp,
    s_out,
    w_in,
    w_value,
    w_gate,
    w_up,
    w_down,
    w_out,
    params,
    cos_tab,
    sin_tab,
    seg_tab,
    qm,
    kw,
    vw,
    prob,
    att,
    s_att,
    r_att,
    norm_one,
    hid,
    hs,
    gate_pre,
    up_pre,
    act,
    act_t,
    hs_t,
    s_mix,
    r_mix,
    t_mix,
    dres_two,
    dms,
    dgate,
    dup,
    s_dh,
    r_dh,
    t_dh,
    dres_one,
    s_da,
    r_da,
    acc_q,
    acc_k,
    acc_v,
    dj,
    s_ig,
    r_ig,
    t_ig,
    sum_in,
    sum_gate,
    sum_up,
    sum_down,
    b_out,
    rb_out,
    tb_out,
    sum_out,
    f_gate,
    s_gmlp,
    r_gmlp,
    s_gin,
    r_gin,
    send_sem,
    recv_sem,
):
    planes, cols = depth, 4
    tok = xin_at.shape[0]
    row_len = tok * cols
    place = Plane(planes)
    dp, blk = place.dp, place.blk
    bf16, f32 = jnp.bfloat16, jnp.float32

    row_of, core_of = blk // 2, blk % 2
    near_at = row_of * 2 + (1 - core_of)
    across_at = (1 - row_of) * 2 + core_of
    corner_at = (1 - row_of) * 2 + (1 - core_of)
    near, across = (dp, near_at), (dp, across_at)

    def lane(k):
        return (dp, (blk + k) % cols)

    def lane_from(k):
        return (blk + cols - k) % cols

    lanes = range(1, cols)
    local = []

    def move(source, target):
        copy = pltpu.make_async_copy(source, target, local_sem.at[len(local)])
        local.append(copy)
        copy.start()
        return copy

    xin = xs.at[blk]
    in_load = move(in_at, in_rows)
    out_load = move(out_at, out_rows)
    down_load = move(down_at, w_down.at[dp])
    x_load = move(xin_at, xin)
    gate_load = move(gate_at, gate_rows)
    up_load = move(up_at, up_rows)
    cot_load = move(cot_at, cot)
    wire = Wire(send_sem, recv_sem, place.inner == 1)
    barrier = pltpu.get_barrier_semaphore()
    peers = [place.side, place.at(place.partner), place.at(place.other)]
    peers = peers + [lane(k) for k in lanes]
    for peer in peers:
        pl.semaphore_signal(barrier, inc=1, device_id=peer, device_id_type=MESH_IDS)
    far = place.at(place.outer)

    @pl.when(place.inner == 1)
    def _():
        pl.semaphore_signal(barrier, inc=1, device_id=far, device_id_type=MESH_IDS)


    rows = 24
    width = xin_at.shape[1]
    lane_ids = lax.broadcasted_iota(jnp.int32, (1, LANES), 1)
    low_half = lane_ids < HALF
    head_width = width // cols
    vectors_tab[...] = jnp.zeros_like(vectors_tab)
    for number, vector in enumerate((gain_a, bias_a, gain_b, bias_b)):
        vectors_tab[number : number + 1, 0:rows] = vector[...].astype(f32)
    free_lane = lax.broadcasted_iota(jnp.int32, (8, LANES), 0) + HALF
    to_lane = jnp.where(
        free_lane == lax.broadcasted_iota(jnp.int32, (8, LANES), 1), 1.0, 0.0
    ).astype(bf16)
    vector_columns = tm(vectors_tab[...].astype(bf16), to_lane)[0:rows]
    in_load.wait()
    joined_rows = in_rows[...].astype(f32)
    for j in range(cols):
        starts = [kind * width + j * head_width for kind in range(3)]
        windows = [window_at(joined_rows, start) for start in starts]
        windows.append(
            jnp.where(
                low_half,
                window_at(joined_rows, starts[0] + LANES),
                window_at(joined_rows, starts[1] + LANES - HALF),
            )
        )
        windows.append(
            jnp.where(low_half, window_at(joined_rows, starts[2] + LANES), vector_columns)
        )
        packed = jnp.concatenate(windows, axis=1)
        p_in[j] = jnp.concatenate(
            [packed, jnp.zeros((8, packed.shape[1]), f32)], axis=0
        ).astype(bf16)
    out_load.wait()
    halved = [out_rows[:, n * width // 2 : (n + 1) * width // 2].astype(f32) for n in range(2)]
    s_out[blk, dp] = jnp.concatenate(halved, axis=0).astype(bf16)
    pl.semaphore_wait(barrier, len(peers) + place.inner)

    def to_lanes(source_of, target):
        return [wire.push(source_of((blk + k) % cols), target.at[blk], lane(k)) for k in lanes]

    def from_lanes(slots, target):
        for k, slot in zip(lanes, slots):
            wire.arrive(slot, target.at[lane_from(k)], lane(k))

    every = pl.ds(0, tok)

    def gather_start(own, target, cut=every):
        return [
            wire.push(own.at[cut], target.at[blk, cut], across),
            wire.push(own.at[cut], target.at[blk, cut], near),
        ]

    def gather_relay(slots, target, cut=every):
        came = target.at[across_at, cut]
        wire.arrive(slots[0], came, across)
        slots.append(wire.push(came, came, near))

    def gather_done(slots, target, cut=every):
        wire.arrive(slots[1], target.at[near_at, cut], near)
        wire.arrive(slots[2], target.at[corner_at, cut], near)

    def sum_start(part, inbox, cut=every):
        return [
            wire.push(part.at[corner_at, cut], inbox.at[0, cut], near),
            wire.push(part.at[near_at, cut], inbox.at[1, cut], near),
        ]

    def sum_relay(slots, part, inbox, staged, cut=every):
        wire.arrive(slots[0], inbox.at[0, cut], near)
        both = part[across_at, cut].astype(f32) + inbox[0, cut].astype(f32)
        staged[cut] = both.astype(bf16)
        slots.append(wire.push(staged.at[cut], inbox.at[2, cut], across))

    def sum_done(slots, part, inbox, cut=every):
        wire.arrive(slots[1], inbox.at[1, cut], near)
        total = part[blk, cut].astype(f32) + inbox[1, cut].astype(f32)
        wire.arrive(slots[2], inbox.at[2, cut], across)
        return total + inbox[2, cut].astype(f32)

    in_slots = to_lanes(lambda to: p_in.at[to], r_in)
    down_load.wait()
    tail = 0
    out_spread = Spread(wire, place, s_out.at[blk], 0)
    out_spread.start()
    out_spread.start_out()
    out_spread.start_side()
    down_spread = Spread(wire, place, w_down, DTF)
    down_spread.start()
    down_spread.start_out()
    down_spread.start_side()
    down_spread.tail_out(True)
    gate_load.wait()
    up_load.wait()
    units = gate_rows.shape[1] // cols
    unit_block = units // (planes * 2)
    for at, weight in ((0, gate_rows), (rows, up_rows)):
        whole = weight[...].astype(f32)
        for j in range(cols):
            packed = jnp.concatenate(
                [
                    gather_lanes(
                        whole,
                        unit_block,
                        n * LANES,
                        lambda ring_at, lane: lane + (cols - 1) * unit_block * ring_at + unit_block * j,
                    )
                    for n in range(units // LANES)
                ],
                axis=1,
            )
            p_mlp[j, at : at + rows] = packed.astype(bf16)
    mlp_slots = to_lanes(lambda to: p_mlp.at[to], r_mlp)
    x_load.wait()
    x_slots = gather_start(xin, xs)
    r_in[blk] = p_in[blk]
    r_mlp[blk] = p_mlp[blk]

    lengths = [lens[0, j] for j in range(lens.shape[1])]

    def layout(positions):
        segment = jnp.zeros_like(positions)
        begins = jnp.zeros_like(positions)
        bound = jnp.int32(0)
        for length in lengths:
            bound = bound + length
            passed = positions >= bound
            segment = segment + jnp.where(passed, 1, 0)
            begins = begins + jnp.where(passed, length, 0)
        return segment, positions - begins

    seg_rows, offsets = layout(lax.broadcasted_iota(jnp.int32, (row_len, LANES), 0))
    seg_tab[...] = seg_rows
    seg_key = layout(lax.broadcasted_iota(jnp.int32, (8, row_len), 1))[0][0:1]
    front = lane_ids % HALF < QUART
    angles = offsets.astype(f32) * freq[0:1]
    cos_tab[...] = jnp.cos(angles)
    sin_tab[...] = jnp.where(front, -1.0, 1.0) * jnp.sin(angles)

    def turn(window):
        return jnp.where(
            front, pltpu.roll(window, LANES - QUART, 1), pltpu.roll(window, QUART, 1)
        )

    from_lanes(in_slots, r_in)
    own_rows = cols * rows
    fold_rows = own_rows // 2
    heads_width = 4 * LANES

    def folded(last, tile):
        fold = jnp.where(low_half, last[0:fold_rows], pltpu.roll(last[fold_rows:], HALF, 1))
        chunks = [fold[n * 16 : (n + 1) * 16] for n in range(3)]
        chunks.append(jnp.concatenate([tile, jnp.zeros((8, LANES), f32)], axis=0))
        return jnp.concatenate(chunks, axis=1)

    def unfolded(below):
        fold = jnp.concatenate([below[:, n * LANES : (n + 1) * LANES] for n in range(3)], axis=0)
        return jnp.concatenate([fold, pltpu.roll(fold, HALF, 1)], axis=0), below[0:8, 3 * LANES :]

    gathered = jnp.concatenate(
        [r_in[j, 0:rows, :].astype(f32) for j in range(cols)], axis=0
    )
    last = gathered[:, heads_width:]
    padded = jnp.concatenate([last, jnp.zeros((LANES - own_rows, LANES), f32)], axis=0)
    w_in[dp] = jnp.concatenate(
        [gathered[:, :heads_width], folded(last, mt(to_lane, padded.astype(bf16)))], axis=0
    ).astype(bf16)
    in_spread = Spread(wire, place, w_in, tail)
    in_spread.start()
    in_spread.start_out()
    in_spread.start_side()
    from_lanes(mlp_slots, r_mlp)
    mlp_own = [r_mlp[j].astype(f32) for j in range(cols)]
    w_gate[dp] = jnp.concatenate([part[0:rows] for part in mlp_own], axis=0).astype(bf16)
    w_up[dp] = jnp.concatenate([part[rows:] for part in mlp_own], axis=0).astype(bf16)
    gate_spread = Spread(wire, place, w_gate, tail)
    up_spread = Spread(wire, place, w_up, tail)
    gate_spread.start()
    gate_spread.start_side()
    up_spread.start()
    out_spread.relay(2)
    for spread in (out_spread, down_spread):
        spread.relay(0, inner=True)
        spread.relay(1, inner=True)
    in_spread.relay(2)
    out_spread.relay(0, inner=False)
    out_spread.relay(1, inner=False)
    in_spread.relay(0)
    down_spread.relay(2)
    in_spread.relay(1)
    up_spread.start_side()
    gate_spread.start_out()
    up_spread.start_out()
    down_spread.tail()
    gate_spread.relay(0, inner=True)
    gate_spread.relay(1, inner=True)
    gather_relay(x_slots, xs)
    out_spread.settle()
    shards_here = pl.ds(0, planes * 2)
    out_lanes = gather_start(s_out.at[blk], s_out, shards_here)
    gate_spread.relay(2)
    up_spread.relay(2)
    gather_done(x_slots, xs)
    in_spread.settle()

    group = 2
    chunk = group * tok

    tiles = []
    for d in range(planes * 2):
        values, tile = unfolded(w_in[d, own_rows:, :].astype(f32))
        w_value[d] = jnp.where(low_half, values, 0.0).astype(bf16)
        tiles.append(tile)

    def project(step, carry):
        start = pl.multiple_of(step * chunk, chunk)
        here = pl.ds(start, chunk)
        tokens = xs[pl.ds(step * group, group)].reshape(chunk, width)
        joined = mm(tokens, w_in[:, 0:own_rows, :].reshape(width, heads_width))
        cosine, sine = cos_tab[here, :], sin_tab[here, :]

        def rotate(number):
            window = joined[:, number * LANES : (number + 1) * LANES]
            return window * cosine + turn(window) * sine

        scale = HALF ** -0.5
        queries = rotate(0).astype(bf16).astype(f32) * scale
        qm[0, here, :] = jnp.where(low_half, queries, 0.0).astype(bf16)
        qm[1, here, :] = jnp.where(low_half, 0.0, queries).astype(bf16)
        kw[0, here, :] = rotate(1).astype(bf16)
        vw[0, here, :] = joined[:, 2 * LANES : 3 * LANES].astype(bf16)
        both = rotate(3)
        qm[2, here, :] = jnp.where(low_half, both.astype(bf16).astype(f32) * scale, 0.0).astype(bf16)
        kw[1, here, :] = jnp.where(low_half, pltpu.roll(both, HALF, 1), 0.0).astype(bf16)
        vw[1, here, :] = mm(tokens, w_value[...].reshape(width, LANES)).astype(bf16)
        return carry

    lax.fori_loop(0, cols // group, project, 0)

    def attend(head):
        window = head // 2

        def step_fn(step, carry):
            here = pl.ds(pl.multiple_of(step * chunk, chunk), chunk)
            scores = mt(qm[head, here, :], kw[window])
            allowed = seg_tab[here, :][:, 0:1] == seg_key
            scores = jnp.where(allowed, scores, NEG)
            top = jnp.max(scores, axis=1, keepdims=True)
            raised = jnp.exp(scores - top)
            total = jnp.sum(raised, axis=1, keepdims=True)
            prob_low = (raised * (1.0 / total)).astype(bf16)
            prob[head, here, :] = prob_low
            mixed = mm(prob_low, vw[window])
            if head == 1:
                mixed = jnp.where(low_half, att[0, here, :], mixed)
            att[window, here, :] = mixed
            return carry

        lax.fori_loop(0, row_len // chunk, step_fn, 0)

    up_spread.relay(0, inner=True)
    attend(0)
    attend(1)
    up_spread.relay(1, inner=True)
    attend(2)
    last_segment = lens.shape[1] - 1
    for j in range(cols):
        here = slice(j * tok, (j + 1) * tok)
        kept = seg_tab[here, :] < last_segment
        s_att[j, :, 0:LANES] = jnp.where(kept, att[0, here, :], 0.0).astype(bf16)
        s_att[j, :, LANES : 2 * LANES] = jnp.where(kept, att[1, here, :], 0.0).astype(bf16)
    att_slots = to_lanes(lambda to: s_att.at[to], r_att)
    r_att[blk] = s_att[blk]

    down_spread.tail_out(False)
    gather_relay(out_lanes, s_out, shards_here)
    gate_spread.relay(0, inner=False)
    gate_spread.relay(1, inner=False)
    for j in range(2):
        down_spread.pass_tail(j)
    gather_done(out_lanes, s_out, shards_here)
    shards = planes * 2 * cols
    per_quarter = shards // cols
    head_rows = per_quarter * rows
    for quarter in range(cols):
        slots = [
            s_out[s % cols, s // cols].astype(f32)
            for s in range(quarter * per_quarter, (quarter + 1) * per_quarter)
        ]
        w_out[quarter, 0:head_rows, :] = jnp.concatenate(
            [
                jnp.concatenate([slot[n * rows : (n + 1) * rows] for slot in slots], axis=0)
                for n in range(2)
            ],
            axis=1,
        ).astype(bf16)
        w_out[quarter, head_rows:, :] = jnp.zeros(
            (w_out.shape[1] - head_rows, width), bf16
        )
    for n in range(width // LANES):
        first = n * LANES
        result = None
        for d in range(first // own_rows, (first + LANES - 1) // own_rows + 1):
            begin = d * own_rows - first
            piece = pltpu.roll(tiles[d], begin % LANES, 1)
            result = piece if result is None else jnp.where(lane_ids < begin, result, piece)
        params[:, first : first + LANES] = result
    gain_one, bias_one = params[0:1, :], params[1:2, :]
    gain_two, bias_two = params[2:3, :], params[3:4, :]

    def normalize(residual):
        centered = residual - jnp.mean(residual, axis=1, keepdims=True)
        variance = jnp.mean(centered * centered, axis=1, keepdims=True)
        spread = lax.rsqrt(variance + EPS)
        return centered * spread, spread

    def normalize_back(grad, normal, spread, gain):
        inner = grad * gain
        mean_inner = jnp.mean(inner, axis=1, keepdims=True)
        mean_both = jnp.mean(inner * normal, axis=1, keepdims=True)
        return (inner - mean_inner - normal * mean_both) * spread

    def column_sum(value):
        return jnp.sum(value, axis=0, keepdims=True)

    from_lanes(att_slots, r_att)
    branch = mm(r_att[0], w_out[0])
    for quarter in range(1, cols):
        branch = branch + mm(r_att[quarter], w_out[quarter])
    normal, spread_one = normalize(xin[...].astype(f32) + branch)
    hidden = normal * gain_one + bias_one
    hs[blk] = hidden.astype(bf16)
    hid_slots = gather_start(hs.at[blk], hs)
    norm_one[...] = normal
    hid[...] = hidden
    up_spread.relay(0, inner=False)
    up_spread.relay(1, inner=False)
    down_spread.relay(0, inner=False)
    down_spread.relay(1, inner=False)
    gather_relay(hid_slots, hs)
    gate_spread.settle()
    gather_done(hid_slots, hs)

    wide = 256
    strips = units // wide

    def each_strip(body):
        def step_fn(step, carry):
            body(pl.ds(pl.multiple_of(step * wide, wide), wide))
            return carry

        lax.fori_loop(0, strips, step_fn, 0)

    def expand_gate(here):
        tokens = hs[...].reshape(row_len, width)
        gate_pre[:, here] = mm(tokens, w_gate[:, :, here].reshape(width, wide))

    def expand_up(here):
        tokens = hs[...].reshape(row_len, width)
        up = mm(tokens, w_up[:, :, here].reshape(width, wide))
        gate = gate_pre[:, here]
        up_pre[:, here] = up
        act[:, here] = (gate / (1.0 + jnp.exp(-gate)) * up).astype(bf16)

    each_strip(expand_gate)
    hs_t[...] = hs[...].reshape(row_len, width).T
    up_spread.settle()
    each_strip(expand_up)
    down_spread.settle()
    down_spread.settle_tail()

    def contract(step, carry):
        here = pl.ds(pl.multiple_of(step * wide, wide), wide)
        mixed = mm(act[...], w_down[:, :, here].reshape(units, wide))
        s_mix[:, :, here] = mixed.reshape(cols, tok, wide).astype(bf16)
        return carry

    lax.fori_loop(0, width // wide, contract, 0)
    pieces = 4
    cot_load.wait()
    halves = [pl.ds(n * tok // pieces, tok // pieces) for n in range(pieces)]
    mix_slots = [sum_start(s_mix, r_mix, cut) for cut in halves]
    for slots, cut in zip(mix_slots, halves):
        sum_relay(slots, s_mix, r_mix, t_mix, cut)
    act_t[...] = act[...].T
    second_gain, second_bias, dm_slots = 0.0, 0.0, []
    for slots, cut in zip(mix_slots, halves):
        mlp_out = sum_done(slots, s_mix, r_mix, cut)
        normal, spread_two = normalize(hid[cut, :] + mlp_out)
        grad = cot[cut, :].astype(f32)
        d_two = normalize_back(grad, normal, spread_two, gain_two)
        dms[blk, cut] = d_two.astype(bf16)
        dm_slots.append(gather_start(dms.at[blk], dms, cut))
        dres_two[cut, :] = d_two
        outputs[cut, :] = (normal * gain_two + bias_two).astype(bf16)
        second_gain = second_gain + column_sum(grad * normal)
        second_bias = second_bias + column_sum(grad)
    writes = [move(outputs, outputs_to)]
    for slots, cut in zip(dm_slots, halves):
        gather_relay(slots, dms, cut)
    for slots, cut in zip(dm_slots, halves):
        gather_done(slots, dms, cut)

    down_sum = Collect(wire, place, sum_down)
    gate_sum = Collect(wire, place, sum_gate)
    up_sum = Collect(wire, place, sum_up)
    in_sum = Collect(wire, place, sum_in)
    out_sum = Collect(wire, place, sum_out)
    half = 4

    def fill_parts(part, left_of, right, more=lambda product, here: product):
        height = part.shape[2]

        def step_fn(step, carry):
            here = pl.ds(pl.multiple_of(step * half * height, LANES), half * height)
            product = more(mm(left_of(here), right()), here)
            for j in range(half):
                part[j % 2, step * (half // 2) + j // 2] = product[
                    j * height : (j + 1) * height
                ].astype(bf16)
            return carry

        lax.fori_loop(0, planes * 2 // half, step_fn, 0)

    fill_parts(down_sum.part, lambda here: act_t[here, :], lambda: dms[...].reshape(row_len, width))
    down_sum.send((1, 0,))
    down_sum.send_tails()

    block = w_down.shape[1]

    def active_grads(step, carry):
        here = pl.ds(pl.multiple_of(step * half * block, LANES), half * block)
        d_active = mt(
            dms[...].reshape(row_len, width),
            w_down[pl.ds(step * half, half)].reshape(half * block, width),
        )
        gate, up = gate_pre[:, here], up_pre[:, here]
        sg = 1.0 / (1.0 + jnp.exp(-gate))
        dgate[:, here] = (d_active * up * sg * (1.0 + gate * (1.0 - sg))).astype(bf16)
        dup[:, here] = (d_active * gate * sg).astype(bf16)
        return carry

    lax.fori_loop(0, planes * 2 // half, active_grads, 0)
    block = w_gate.shape[1]

    def hidden_rows(here):
        return hs_t[here, :]

    fill_parts(gate_sum.part, hidden_rows, lambda: dgate[...])
    gate_sum.send()
    def hidden_grads(step, carry):
        here = pl.ds(pl.multiple_of(step * half * block, LANES), half * block)
        those = pl.ds(step * half, half)
        mixed = mt(dgate[...], w_gate[those].reshape(half * block, units)) + mt(
            dup[...], w_up[those].reshape(half * block, units)
        )
        s_dh[:, :, here] = mixed.reshape(cols, tok, half * block).astype(bf16)
        return carry

    lax.fori_loop(0, planes * 2 // half, hidden_grads, 0)
    dh_slots = sum_start(s_dh, r_dh)

    sum_relay(dh_slots, s_dh, r_dh, t_dh)
    fill_parts(up_sum.part, hidden_rows, lambda: dup[...])
    up_sum.send((1, 0))
    down_sum.first(1)
    down_sum.first(0)
    d_hidden = dres_two[...] + sum_done(dh_slots, s_dh, r_dh)
    normal = norm_one[...]
    first_gain = column_sum(d_hidden * normal)
    first_bias = column_sum(d_hidden)
    d_one = normalize_back(d_hidden, normal, spread_one, gain_one)
    dres_one[...] = d_one
    d_branch = d_one.astype(bf16)
    mine = pl.ds(pl.multiple_of(blk * tok, tok), tok)
    kept = seg_tab[mine, :][:, 0:1] < last_segment
    for quarter in range(cols):
        pulled = mt(d_branch, w_out[quarter]).astype(bf16).astype(f32)
        s_da[quarter] = jnp.where(kept, pulled, 0.0).astype(bf16)
    da_slots = to_lanes(lambda to: s_da.at[to], r_da)
    r_da[blk] = s_da[blk]

    params[...] = jnp.concatenate(
        [first_gain, first_bias, second_gain, second_bias, jnp.zeros((4, width), f32)], axis=0
    )
    for quarter in range(cols):
        product = tm(r_att[quarter], d_branch)
        for t in range(per_quarter):
            s = quarter * per_quarter + t
            owner_dp = s // cols
            mine_rows = product[t * rows : (t + 1) * rows]
            halved = [mine_rows[:, n * width // 2 : (n + 1) * width // 2] for n in range(2)]
            b_out[s % cols, owner_dp % 2, owner_dp // 2] = jnp.concatenate(
                halved, axis=0
            ).astype(bf16)
    both_sides = pl.ds(0, 2)
    out_blk = sum_start(b_out, rb_out, both_sides)

    gate_sum.first(1)
    sum_relay(out_blk, b_out, rb_out, tb_out, both_sides)
    down_sum.second_tail(1)
    down_sum.second(1)
    gate_sum.first(0)
    from_lanes(da_slots, r_da)
    def attend_back(head):
        window = head // 2
        fresh = head != 1

        def step_fn(step, carry):
            here = pl.ds(pl.multiple_of(step * chunk, chunk), chunk)
            d_out = r_da[pl.ds(step * group, group), :, window * LANES : (window + 1) * LANES]
            d_out = d_out.reshape(chunk, LANES).astype(f32)
            if head == 0:
                d_out = jnp.where(low_half, d_out, 0.0)
            if head == 1:
                d_out = jnp.where(low_half, 0.0, d_out)
            d_low = d_out.astype(bf16)
            delta = jnp.sum(d_out * att[window, here, :], axis=1, keepdims=True)
            prob_low = prob[head, here, :]
            d_prob = mt(d_low, vw[window])
            d_score = (prob_low.astype(f32) * (d_prob - delta)).astype(bf16)
            d_query = mm(d_score, kw[window]) * (HALF ** -0.5)
            if head == 1:
                d_query = jnp.where(low_half, acc_q[0, here, :], d_query)
            acc_q[window, here, :] = d_query
            d_key = tm(d_score, qm[head, here, :])
            d_value = tm(prob_low, d_low)
            if fresh:

                @pl.when(step == 0)
                def _():
                    acc_k[window] = d_key
                    acc_v[window] = d_value

                @pl.when(step != 0)
                def _():
                    acc_k[window] = acc_k[window] + d_key
                    acc_v[window] = acc_v[window] + d_value
            else:
                acc_k[window] = acc_k[window] + d_key
                acc_v[window] = acc_v[window] + d_value
            return carry

        lax.fori_loop(0, row_len // chunk, step_fn, 0)

    attend_back(0)
    gate_sum.first(2)
    down_sum.second_tail(0)
    down_sum.second(0)
    attend_back(1)
    attend_back(2)

    cosine, sine = cos_tab[...], sin_tab[...]

    def rotate_back(vector):
        vector = vector.astype(bf16).astype(f32)
        return (vector * cosine - turn(vector) * sine).astype(bf16)

    dj[:, 0:LANES] = rotate_back(acc_q[0])
    dj[:, LANES : 2 * LANES] = rotate_back(acc_k[0])
    dj[:, 2 * LANES : 3 * LANES] = acc_v[0].astype(bf16)
    dj[:, 3 * LANES : 4 * LANES] = rotate_back(acc_q[1] + pltpu.roll(acc_k[1], HALF, 1))
    dj[:, 4 * LANES : 5 * LANES] = acc_v[1].astype(bf16)


    def input_parts(step, carry):
        here = pl.ds(pl.multiple_of(step * half * own_rows, LANES), half * own_rows)
        product = tm(xs[:, :, here].reshape(row_len, half * own_rows), dj[...])
        vectors = params[:, here]
        for j in range(half):
            mine_rows = product[j * own_rows : (j + 1) * own_rows]
            tile = jnp.where(lane_ids < own_rows, window_at(vectors, j * own_rows), 0.0)
            in_sum.part[j % 2, step * (half // 2) + j // 2] = jnp.concatenate(
                [mine_rows[:, :heads_width], folded(mine_rows[:, heads_width:], tile)], axis=0
            ).astype(bf16)
        return carry

    lax.fori_loop(0, planes * 2 // half, input_parts, 0)

    in_sum.send((1, 0))
    def input_grads(step, carry):
        here = pl.ds(pl.multiple_of(step * half * block, LANES), half * block)
        those = pl.ds(step * half, half)
        mixed = mt(dj[:, 0:heads_width], w_in[those, 0:own_rows].reshape(half * block, heads_width))
        mixed = mixed + mt(dj[:, heads_width:], w_value[those].reshape(half * block, LANES))
        s_ig[:, :, here] = mixed.reshape(cols, tok, half * block).astype(bf16)
        return carry

    lax.fori_loop(0, planes * 2 // half, input_grads, 0)
    ig_slots = sum_start(s_ig, r_ig)

    up_sum.first(1)
    gate_sum.second(1)
    sum_relay(ig_slots, s_ig, r_ig, t_ig)
    out_sum.part[...] = sum_done(out_blk, b_out, rb_out, both_sides).astype(bf16)
    out_sum.send((1, 0,))
    up_sum.send((2,))
    in_sum.send((2,))
    up_sum.send((3,))
    in_sum.send((3,))
    down_sum.send((2,))
    out_sum.send((2,))
    out_sum.send((3,))
    down_sum.send((3,))
    down_sum.tail()
    up_sum.first(0)
    gate_sum.second(0)
    in_sum.first(1)
    up_sum.second(1)
    in_sum.first(0)
    out_sum.first(1)
    out_sum.first(0)
    up_sum.second(0)
    in_sum.second(1)
    up_sum.first(2)
    grad_in = dres_one[...] + sum_done(ig_slots, s_ig, r_ig)
    input_grad[...] = grad_in.astype(bf16)
    writes.append(move(input_grad, input_grad_to))
    in_sum.second(0)
    out_sum.second(1)
    out_sum.second(0)
    in_sum.first(2)
    f_gate[...] = gate_sum.total()
    up_total = up_sum.total()
    gate_total = f_gate[...]
    for j in range(cols):
        here = slice(j * rows, (j + 1) * rows)
        s_gmlp[j] = jnp.concatenate([gate_total[here], up_total[here]], axis=0).astype(bf16)
    gmlp_slots = to_lanes(lambda to: s_gmlp.at[to], r_gmlp)
    r_gmlp[blk] = s_gmlp[blk]
    out_sum.first(2)
    down_sum.first(2)
    in_total = in_sum.total()
    values, tile = unfolded(in_total[own_rows:])
    columns = tm(tile.astype(bf16), to_lane)[0:own_rows]
    in_total = jnp.concatenate(
        [in_total[0:own_rows], jnp.where(low_half, values, columns)], axis=1
    )
    for j in range(cols):
        s_gin[j] = jnp.concatenate(
            [in_total[j * rows : (j + 1) * rows], jnp.zeros((8, in_total.shape[1]), f32)], axis=0
        ).astype(bf16)
    gin_slots = to_lanes(lambda to: s_gin.at[to], r_gin)
    r_gin[blk] = s_gin[blk]
    g_out[...] = out_sum.total()
    writes.append(move(g_out, g_out_to))
    g_down[...] = down_sum.total()
    writes.append(move(g_down, g_down_to))
    from_lanes(gmlp_slots, r_gmlp)
    writes.append(move(r_gmlp, g_mlp_to))
    from_lanes(gin_slots, r_gin)
    writes.append(move(r_gin, g_in_to))
    wire.finish()
    for write in writes:
        write.wait()


def unpack(
    rows,
    block,
    outputs,
    input_grad,
    g_in,
    g_mlp,
    g_out,
    g_down,
    outputs_to,
    input_grad_to,
    in_to,
    out_to,
    gate_to,
    up_to,
    down_to,
    *vectors_to,
):
    f32 = jnp.float32
    cols = g_in.shape[0]
    width = outputs.shape[1]
    outputs_to[0] = outputs[...]
    input_grad_to[0] = input_grad[...]
    down_to[...] = g_down[...]
    for n in range(2):
        out_to[:, n * width // 2 : (n + 1) * width // 2] = g_out[n * rows : (n + 1) * rows, :]
    low_half = lax.broadcasted_iota(jnp.int32, (1, LANES), 1) < HALF
    joined = [g_in[j].astype(f32)[0:rows] for j in range(cols)]
    vectors = joined[0][:, 4 * LANES :]
    for j in range(1, cols):
        vectors = vectors + joined[j][:, 4 * LANES :]
    vectors = jnp.concatenate([vectors, jnp.zeros((LANES - rows, LANES), f32)], axis=0).T
    for number, vector_to in enumerate(vectors_to):
        vector_to[...] = vectors[HALF + number, 0:rows]
    single_at = ((3, 0), (3, 1), (4, 0))

    def half(kind, number, want):
        owner, part = number // 3, number % 3
        window, at = (kind, part) if part < 2 else single_at[kind]
        value = joined[owner][:, window * LANES : (window + 1) * LANES]
        return value if at == want else pltpu.roll(value, HALF, 1)

    for kind in range(3):
        for n in range(width // LANES):
            at = kind * width + n * LANES
            in_to[:, at : at + LANES] = jnp.where(
                low_half, half(kind, 2 * n, 0), half(kind, 2 * n + 1, 1)
            )
    lanes = lax.broadcasted_iota(jnp.int32, (1, LANES), 1)
    mlp = [g_mlp[j].astype(f32) for j in range(cols)]
    for first_row, target in ((0, gate_to), (rows, up_to)):
        parts = [part[first_row : first_row + rows] for part in mlp]
        for n in range(target.shape[1] // LANES):
            first = n * LANES
            result = None
            for number in range(first // block, (first + LANES - 1) // block + 1):
                ring_at, owner = number // cols, number % cols
                piece = window_at(parts[owner], ring_at * block + first - number * block)
                begin = number * block - first
                result = piece if result is None else jnp.where(lanes < begin, result, piece)
            target[:, first : first + LANES] = result


def fast_shards(
    depth,
    inputs,
    doc_lengths,
    project_in,
    project_out,
    gate_weight,
    up_weight,
    down_weight,
    first_gain,
    first_bias,
    second_gain,
    second_bias,
    cotangent,
):
    cols = 4
    tok, width = inputs.shape[1:]
    rows = project_in.shape[0]
    ff = gate_weight.shape[1]
    ring = depth * 2
    row_len = tok * cols
    units = ff // cols
    block = units // ring
    head_width = width // cols
    in_width = 5 * LANES
    bf16, f32 = jnp.bfloat16, jnp.float32

    lane_ids = np.arange(LANES) % QUART
    freq = jnp.asarray(
        np.broadcast_to(BASE ** (-2.0 * lane_ids / HALF), (8, LANES)).astype(np.float32)
    )

    def scratch(*shape, kind=bf16):
        return pltpu.VMEM(shape, kind)

    def sums(height, across, tail=0):
        main = height - tail
        buffers = [
            scratch(2, depth, height, across),
            scratch(depth, main, across),
            scratch(depth, main, across),
            scratch(4, main, across),
        ]
        if tail:
            buffers = buffers + [
                scratch(4, 2, tail, across),
                scratch(2, 2, tail, across),
                scratch(2, tail, across),
                scratch(tail, across, kind=f32),
            ]
        return tuple(buffers)

    stacked = scratch(cols, tok, width)
    heads = 3
    buffers = [
        scratch(tok, width),
        scratch(rows, 3 * width),
        scratch(rows, ff),
        scratch(rows, ff),
        scratch(rows, width),
        scratch(tok, width),
        scratch(tok, width),
        scratch(2 * rows, width // 2, kind=f32),
        scratch(block, width, kind=f32),
        pltpu.SemaphoreType.DMA((16,)),
        stacked,
        scratch(cols, 32, in_width),
        scratch(cols, 2 * rows, units),
        scratch(8, LANES, kind=f32),
        scratch(cols, 32, in_width),
        scratch(cols, 2 * rows, units),
        scratch(cols, ring, 2 * rows, width // 2),
        scratch(ring, cols * rows + 16, 4 * LANES),
        scratch(ring, cols * rows, LANES),
        scratch(ring, cols * rows, units),
        scratch(ring, cols * rows, units),
        scratch(ring, block, width),
        scratch(cols, 2 * LANES, width),
        scratch(8, width, kind=f32),
        scratch(row_len, LANES, kind=f32),
        scratch(row_len, LANES, kind=f32),
        scratch(row_len, LANES, kind=jnp.int32),
        scratch(heads, row_len, LANES),
        scratch(2, row_len, LANES),
        scratch(2, row_len, LANES),
        scratch(heads, row_len, row_len),
        scratch(2, row_len, LANES, kind=f32),
        scratch(cols, tok, 2 * LANES),
        scratch(cols, tok, 2 * LANES),
        scratch(tok, width, kind=f32),
        scratch(tok, width, kind=f32),
        stacked,
        scratch(row_len, units, kind=f32),
        scratch(row_len, units, kind=f32),
        scratch(row_len, units),
        scratch(units, row_len),
        scratch(width, row_len),
        stacked,
        scratch(3, tok, width),
        scratch(tok, width),
        scratch(tok, width, kind=f32),
        stacked,
        scratch(row_len, units),
        scratch(row_len, units),
        stacked,
        scratch(3, tok, width),
        scratch(tok, width),
        scratch(tok, width, kind=f32),
        scratch(cols, tok, 2 * LANES),
        scratch(cols, tok, 2 * LANES),
        scratch(2, row_len, LANES, kind=f32),
        scratch(2, row_len, LANES, kind=f32),
        scratch(2, row_len, LANES, kind=f32),
        scratch(row_len, in_width),
        stacked,
        scratch(3, tok, width),
        scratch(tok, width),
        sums(cols * rows + 16, 4 * LANES),
        sums(cols * rows, units),
        sums(cols * rows, units),
        sums(block, width, DTB),
        scratch(cols, 2, depth, 2 * rows, width // 2),
        scratch(3, 2, depth, 2 * rows, width // 2),
        scratch(2, depth, 2 * rows, width // 2),
        sums(2 * rows, width // 2, 0),
        scratch(cols * rows, units, kind=f32),
        scratch(cols, 2 * rows, units),
        scratch(cols, 2 * rows, units),
        scratch(cols, 32, in_width),
        scratch(cols, 32, in_width),
        pltpu.SemaphoreType.DMA((240,)),
        pltpu.SemaphoreType.DMA((240,)),
    ]
    vmem = pl.BlockSpec(memory_space=pltpu.VMEM)
    anywhere = pl.BlockSpec(memory_space=pl.ANY)
    tokens = row_len * width
    outputs, input_grad, g_in, g_mlp, g_out, g_down = pl.pallas_call(
        functools.partial(fused, depth),
        out_shape=(
            jax.ShapeDtypeStruct((tok, width), bf16),
            jax.ShapeDtypeStruct((tok, width), bf16),
            jax.ShapeDtypeStruct((cols, 32, in_width), bf16),
            jax.ShapeDtypeStruct((cols, 2 * rows, units), bf16),
            jax.ShapeDtypeStruct((2 * rows, width // 2), f32),
            jax.ShapeDtypeStruct((block, width), f32),
        ),
        in_specs=[pl.BlockSpec(memory_space=pltpu.SMEM), vmem] + [anywhere] * 7 + [vmem] * 4,
        out_specs=(anywhere,) * 6,
        scratch_shapes=buffers,
        compiler_params=pltpu.CompilerParams(
            collective_id=0, has_side_effects=True, vmem_limit_bytes=60 * 2**20
        ),
        cost_estimate=pl.CostEstimate(
            flops=6 * tokens * (3 * units + 4 * head_width),
            bytes_accessed=8 * 2**20,
            transcendentals=3 * row_len * row_len,
        ),
        name="layer",
    )(
        doc_lengths,
        freq,
        inputs[0],
        cotangent[0],
        project_in,
        gate_weight,
        up_weight,
        project_out,
        down_weight,
        first_gain[None],
        first_bias[None],
        second_gain[None],
        second_bias[None],
    )

    vector = jax.ShapeDtypeStruct((rows,), f32)
    return pl.pallas_call(
        functools.partial(unpack, rows, block),
        out_shape=(
            jax.ShapeDtypeStruct((1, tok, width), bf16),
            jax.ShapeDtypeStruct((1, tok, width), bf16),
            jax.ShapeDtypeStruct((rows, 3 * width), f32),
            jax.ShapeDtypeStruct((rows, width), f32),
            jax.ShapeDtypeStruct((rows, ff), f32),
            jax.ShapeDtypeStruct((rows, ff), f32),
            jax.ShapeDtypeStruct((block, width), f32),
            vector,
            vector,
            vector,
            vector,
        ),
        in_specs=[vmem] * 6,
        out_specs=(vmem,) * 11,
        name="unpack",
    )(outputs, input_grad, g_in, g_mlp, g_out, g_down)


def pick(sizes):
    def chosen(*args):
        tok, width = args[0].shape[1:]
        ring, cols = sizes["dp"], sizes["blk"]
        fits = (
            ring == 8
            and cols == 4
            and tok == LANES
            and HEADS == 3 * cols
            and width == HEADS * HALF
            and args[2].shape[0] == 24
            and args[4].shape[1] == 4 * width
        )
        if fits:
            return fast_shards(ring // 2, *args)
        return shards(*args)

    return chosen


def solution(mesh):
    placed = (
        P("dp", "blk", None),
        P("dp", None),
        P(("dp", "blk"), None),
        P(("dp", "blk"), None),
        P(("dp", "blk"), None),
        P(("dp", "blk"), None),
        P(("dp", "blk"), None),
        P(("dp", "blk")),
        P(("dp", "blk")),
        P(("dp", "blk")),
        P(("dp", "blk")),
        P("dp", "blk", None),
    )
    return jax.shard_map(
        pick(dict(mesh.shape)),
        mesh=mesh,
        in_specs=placed,
        out_specs=(
            P("dp", "blk", None),
            P("dp", "blk", None),
            P(("dp", "blk"), None),
            P(("dp", "blk"), None),
            P(("dp", "blk"), None),
            P(("dp", "blk"), None),
            P(("dp", "blk"), None),
            P(("dp", "blk")),
            P(("dp", "blk")),
            P(("dp", "blk")),
            P(("dp", "blk")),
        ),
        check_vma=False,
    )
```

```python
import functools

import jax
import jax.numpy as jnp
import numpy as np
from jax import lax
from jax.experimental import pallas as pl
from jax.experimental.pallas import tpu as pltpu
from jax.sharding import PartitionSpec as P

HEADS = 12


NEG = -1e30
EPS = 1e-05
BASE = 1000.0


def doc_layout(lengths_row, positions):
    bounds = jnp.cumsum(lengths_row)
    passed = positions[:, None] >= bounds[None, :]
    segment = jnp.sum(passed.astype(jnp.int32), axis=1)
    begins = jnp.sum(jnp.where(passed, lengths_row[None, :], 0), axis=1)
    return (segment, positions - begins)


def rotary(vectors, offsets):
    half_size = vectors.shape[-1] // 2
    frequency = BASE ** (-2.0 * jnp.arange(half_size, dtype=jnp.float32) / vectors.shape[-1])
    angles = offsets.astype(jnp.float32)[:, None] * frequency[None, :]
    cosine = jnp.concatenate([jnp.cos(angles), jnp.cos(angles)], axis=1)[:, None, :]
    sine_rows = jnp.concatenate([jnp.sin(angles), jnp.sin(angles)], axis=1)[:, None, :]
    first_half = vectors[..., :half_size]
    second_half = vectors[..., half_size:]
    turned = jnp.concatenate([-second_half, first_half], axis=-1)
    return vectors * cosine + turned * sine_rows


def layer_norm(residual, gain_row, bias_row):
    row_mean = jnp.mean(residual, axis=-1, keepdims=True)
    centered = residual - row_mean
    variance = jnp.mean(centered * centered, axis=-1, keepdims=True)
    return centered * lax.rsqrt(variance + EPS) * gain_row + bias_row


def contract_rows(left, right):
    return lax.dot_general(
        left, right, (((0,), (0,)), ((), ())), preferred_element_type=jnp.float32
    )


def contract_cols(left, right):
    return lax.dot_general(
        left, right, (((1,), (1,)), ((), ())), preferred_element_type=jnp.float32
    )


def tile_scores(query_tile, key_tile, seg_query, seg_key, score_scale):
    scores = (
        jnp.einsum("qhd,khd->hqk", query_tile, key_tile, preferred_element_type=jnp.float32)
        * score_scale
    )
    allowed = (seg_query[:, None] == seg_key[None, :])[None, :, :]
    return (jnp.where(allowed, scores, NEG), allowed)


def run_groups(pieces, group, lengths_row, seg_query, carried, tile_fn, extra_shape):
    group_count = pieces[0].shape[0] // group

    def group_step(carried_in, number):
        offset = number * group
        tile_set = tuple(
            (lax.dynamic_slice_in_dim(piece_rows, offset, group, 0) for piece_rows in pieces)
        )
        positions = offset + jnp.arange(group, dtype=jnp.int32)
        seg_key, unused_offsets = doc_layout(lengths_row, positions)
        touches = (seg_key[0] <= seg_query[-1]) & (seg_query[0] <= seg_key[-1])

        def active(state_in):
            return tile_fn(state_in, tile_set, seg_key)

        def skipped(state_in):
            return (state_in, jnp.zeros(extra_shape, jnp.float32))

        return lax.cond(touches, active, skipped, carried_in)

    return lax.scan(group_step, carried, jnp.arange(group_count, dtype=jnp.int32))


def shards(
    inputs,
    doc_lengths,
    project_in,
    project_out,
    gate_weight,
    up_weight,
    down_weight,
    first_gain,
    first_bias,
    second_gain,
    second_bias,
    cotangent,
):
    group = inputs.shape[1]
    width = inputs.shape[2]
    head_count = HEADS
    head_size = width // head_count
    score_scale = head_size ** (-0.5)
    cycle_rank = lax.axis_index("blk")
    positions = cycle_rank * group + jnp.arange(group, dtype=jnp.int32)
    lengths_row = doc_lengths[0]
    seg_query, offsets = doc_layout(lengths_row, positions)
    keep_mask = seg_query < lengths_row.shape[0] - 1
    keep_float = keep_mask.astype(jnp.float32)
    fetched = (
        lax.all_gather(project_in, ("dp", "blk"), axis=0, tiled=True),
        lax.all_gather(project_out, ("dp", "blk"), axis=0, tiled=True),
        lax.all_gather(gate_weight, ("dp", "blk"), axis=0, tiled=True),
        lax.all_gather(up_weight, ("dp", "blk"), axis=0, tiled=True),
        lax.all_gather(down_weight, ("dp", "blk"), axis=0, tiled=True),
        lax.all_gather(first_gain, ("dp", "blk"), axis=0, tiled=True),
        lax.all_gather(first_bias, ("dp", "blk"), axis=0, tiled=True),
        lax.all_gather(second_gain, ("dp", "blk"), axis=0, tiled=True),
        lax.all_gather(second_bias, ("dp", "blk"), axis=0, tiled=True),
    )
    full_in, full_out, full_gate, full_up, full_down = (
        fetched[0],
        fetched[1],
        fetched[2],
        fetched[3],
        fetched[4],
    )
    gain_one = fetched[5].astype(jnp.float32)
    bias_one = fetched[6].astype(jnp.float32)
    gain_two = fetched[7].astype(jnp.float32)
    bias_two = fetched[8].astype(jnp.float32)
    tokens_low = inputs[0]
    tokens_f = tokens_low.astype(jnp.float32)
    joined = jnp.dot(tokens_low, full_in, preferred_element_type=jnp.float32)
    query_raw = joined[:, :width].reshape(group, head_count, head_size)
    key_raw = joined[:, width : 2 * width].reshape(group, head_count, head_size)
    value_low = joined[:, 2 * width :].astype(jnp.bfloat16)
    query_rot, query_pull = jax.vjp(lambda vectors: rotary(vectors, offsets), query_raw)
    key_rot, key_pull = jax.vjp(lambda vectors: rotary(vectors, offsets), key_raw)
    query_low = query_rot.astype(jnp.bfloat16)
    key_low = key_rot.reshape(group, width).astype(jnp.bfloat16)

    def stats_tile(carried, tile_set, seg_key):
        row_top, row_total = carried
        key_tile = tile_set[0].reshape(group, head_count, head_size)
        scores, allowed = tile_scores(query_low, key_tile, seg_query, seg_key, score_scale)
        new_top = jnp.maximum(row_top, jnp.max(scores, axis=2))
        shrink = jnp.exp(row_top - new_top)
        added = jnp.sum(jnp.where(allowed, jnp.exp(scores - new_top[:, :, None]), 0.0), axis=2)
        return ((new_top, row_total * shrink + added), jnp.zeros((1,), jnp.float32))

    init_stats = (
        jnp.full((head_count, group), NEG, jnp.float32),
        jnp.zeros((head_count, group), jnp.float32),
    )
    carried = init_stats
    carried, unused = run_groups(
        (lax.all_gather(key_low, "blk", axis=0, tiled=True),),
        group,
        lengths_row,
        seg_query,
        carried,
        stats_tile,
        (1,),
    )
    row_top, row_total = carried
    log_total = row_top + jnp.log(row_total)

    def output_tile(accum, tile_set, seg_key):
        key_tile = tile_set[0].reshape(group, head_count, head_size)
        value_tile = tile_set[1].reshape(group, head_count, head_size)
        scores, allowed = tile_scores(query_low, key_tile, seg_query, seg_key, score_scale)
        prob_low = jnp.where(allowed, jnp.exp(scores - log_total[:, :, None]), 0.0).astype(
            jnp.bfloat16
        )
        accum = accum + jnp.einsum(
            "hqk,khd->qhd", prob_low, value_tile, preferred_element_type=jnp.float32
        )
        return (accum, jnp.zeros((1,), jnp.float32))

    zero_accum = jnp.zeros((group, head_count, head_size), jnp.float32)
    accum = zero_accum
    accum, unused = run_groups(
        (
            lax.all_gather(key_low, "blk", axis=0, tiled=True),
            lax.all_gather(value_low, "blk", axis=0, tiled=True),
        ),
        group,
        lengths_row,
        seg_query,
        accum,
        output_tile,
        (1,),
    )
    attend_low = (accum * keep_float[:, None, None]).reshape(group, width).astype(jnp.bfloat16)
    branch = jnp.dot(attend_low, full_out, preferred_element_type=jnp.float32)
    residual_one = tokens_f + branch
    hidden, norm_one_pull = jax.vjp(layer_norm, residual_one, gain_one, bias_one)
    hidden_low = hidden.astype(jnp.bfloat16)
    gate_pre = jnp.dot(hidden_low, full_gate, preferred_element_type=jnp.float32)
    up_pre = jnp.dot(hidden_low, full_up, preferred_element_type=jnp.float32)
    activated, swiglu_pull = jax.vjp(
        lambda gate_in, up_in: jax.nn.silu(gate_in) * up_in, gate_pre, up_pre
    )
    active_low = activated.astype(jnp.bfloat16)
    mlp_out = jnp.dot(active_low, full_down, preferred_element_type=jnp.float32)
    outputs_f, norm_two_pull = jax.vjp(layer_norm, hidden + mlp_out, gain_two, bias_two)
    refetched = (
        lax.all_gather(project_in, ("dp", "blk"), axis=0, tiled=True),
        lax.all_gather(project_out, ("dp", "blk"), axis=0, tiled=True),
        lax.all_gather(gate_weight, ("dp", "blk"), axis=0, tiled=True),
        lax.all_gather(up_weight, ("dp", "blk"), axis=0, tiled=True),
        lax.all_gather(down_weight, ("dp", "blk"), axis=0, tiled=True),
    )
    full_in, full_out, full_gate, full_up, full_down = (
        refetched[0],
        refetched[1],
        refetched[2],
        refetched[3],
        refetched[4],
    )
    d_res_two, second_gain_part, second_bias_part = norm_two_pull(cotangent[0].astype(jnp.float32))
    d_mlp_low = d_res_two.astype(jnp.bfloat16)
    down_part = contract_rows(active_low, d_mlp_low)
    d_active = contract_cols(d_mlp_low, full_down)
    d_gate, d_up = swiglu_pull(d_active)
    d_gate_low = d_gate.astype(jnp.bfloat16)
    d_up_low = d_up.astype(jnp.bfloat16)
    gate_part = contract_rows(hidden_low, d_gate_low)
    up_part = contract_rows(hidden_low, d_up_low)
    d_hidden = d_res_two + contract_cols(d_gate_low, full_gate) + contract_cols(d_up_low, full_up)
    d_res_one, first_gain_part, first_bias_part = norm_one_pull(d_hidden)
    d_branch_low = d_res_one.astype(jnp.bfloat16)
    out_part = contract_rows(attend_low, d_branch_low)
    d_attend = contract_cols(d_branch_low, full_out).astype(jnp.bfloat16)
    d_attend_low = (d_attend * keep_mask[:, None].astype(jnp.bfloat16)).reshape(
        group, head_count, head_size
    )
    delta = jnp.einsum("qhd,qhd->hq", d_attend_low.astype(jnp.float32), accum)

    def back_tile(grad_query, tile_set, seg_key):
        key_tile = tile_set[0].reshape(group, head_count, head_size)
        value_tile = tile_set[1].reshape(group, head_count, head_size)
        scores, allowed = tile_scores(query_low, key_tile, seg_query, seg_key, score_scale)
        prob_rows = jnp.where(allowed, jnp.exp(scores - log_total[:, :, None]), 0.0)
        d_probs = jnp.einsum(
            "qhd,khd->hqk", d_attend_low, value_tile, preferred_element_type=jnp.float32
        )
        d_score_low = (prob_rows * (d_probs - delta[:, :, None])).astype(jnp.bfloat16)
        grad_query = (
            grad_query
            + jnp.einsum("hqk,khd->qhd", d_score_low, key_tile, preferred_element_type=jnp.float32)
            * score_scale
        )
        grad_key = (
            jnp.einsum("hqk,qhd->khd", d_score_low, query_low, preferred_element_type=jnp.float32)
            * score_scale
        )
        grad_value = jnp.einsum(
            "hqk,qhd->khd",
            prob_rows.astype(jnp.bfloat16),
            d_attend_low,
            preferred_element_type=jnp.float32,
        )
        return (
            grad_query,
            jnp.concatenate(
                [grad_key.reshape(group, width), grad_value.reshape(group, width)], axis=1
            ),
        )

    grad_query = zero_accum
    grad_query, blocks = run_groups(
        (
            lax.all_gather(key_low, "blk", axis=0, tiled=True),
            lax.all_gather(value_low, "blk", axis=0, tiled=True),
        ),
        group,
        lengths_row,
        seg_query,
        grad_query,
        back_tile,
        (group, 2 * width),
    )
    blocks = blocks.reshape(-1, 2 * width)
    back_result = (grad_query, blocks)
    grad_query = back_result[0]
    owned_pairs = lax.psum_scatter(
        back_result[1].astype(jnp.bfloat16), "blk", scatter_dimension=0, tiled=True
    ).astype(jnp.float32)
    key_sum = owned_pairs[:, :width]
    value_sum = owned_pairs[:, width:]
    d_query_pre = query_pull(grad_query.astype(jnp.bfloat16).astype(jnp.float32))[0]
    d_key_low = key_sum.astype(jnp.bfloat16).astype(jnp.float32)
    d_key_pre = key_pull(d_key_low.reshape(group, head_count, head_size))[0]
    d_value_low = value_sum.astype(jnp.bfloat16).astype(jnp.float32)
    d_joined_low = jnp.concatenate(
        [d_query_pre.reshape(group, width), d_key_pre.reshape(group, width), d_value_low], axis=1
    ).astype(jnp.bfloat16)
    in_part = contract_rows(tokens_low, d_joined_low)
    input_grad = (d_res_one + contract_cols(d_joined_low, full_in)).astype(jnp.bfloat16)
    by_rows = (
        lax.psum_scatter(
            in_part.astype(jnp.bfloat16), "dp", scatter_dimension=0, tiled=True
        ).astype(jnp.float32),
        lax.psum_scatter(
            out_part.astype(jnp.bfloat16), "dp", scatter_dimension=0, tiled=True
        ).astype(jnp.float32),
        lax.psum_scatter(
            gate_part.astype(jnp.bfloat16), "dp", scatter_dimension=0, tiled=True
        ).astype(jnp.float32),
        lax.psum_scatter(
            up_part.astype(jnp.bfloat16), "dp", scatter_dimension=0, tiled=True
        ).astype(jnp.float32),
        lax.psum_scatter(
            down_part.astype(jnp.bfloat16), "dp", scatter_dimension=0, tiled=True
        ).astype(jnp.float32),
        lax.psum_scatter(
            first_gain_part.astype(jnp.bfloat16), "dp", scatter_dimension=0, tiled=True
        ).astype(jnp.float32),
        lax.psum_scatter(
            first_bias_part.astype(jnp.bfloat16), "dp", scatter_dimension=0, tiled=True
        ).astype(jnp.float32),
        lax.psum_scatter(
            second_gain_part.astype(jnp.bfloat16), "dp", scatter_dimension=0, tiled=True
        ).astype(jnp.float32),
        lax.psum_scatter(
            second_bias_part.astype(jnp.bfloat16), "dp", scatter_dimension=0, tiled=True
        ).astype(jnp.float32),
    )
    summed = (
        lax.psum_scatter(
            by_rows[0].astype(jnp.bfloat16), "blk", scatter_dimension=0, tiled=True
        ).astype(jnp.float32),
        lax.psum_scatter(
            by_rows[1].astype(jnp.bfloat16), "blk", scatter_dimension=0, tiled=True
        ).astype(jnp.float32),
        lax.psum_scatter(
            by_rows[2].astype(jnp.bfloat16), "blk", scatter_dimension=0, tiled=True
        ).astype(jnp.float32),
        lax.psum_scatter(
            by_rows[3].astype(jnp.bfloat16), "blk", scatter_dimension=0, tiled=True
        ).astype(jnp.float32),
        lax.psum_scatter(
            by_rows[4].astype(jnp.bfloat16), "blk", scatter_dimension=0, tiled=True
        ).astype(jnp.float32),
        lax.psum_scatter(
            by_rows[5].astype(jnp.bfloat16), "blk", scatter_dimension=0, tiled=True
        ).astype(jnp.float32),
        lax.psum_scatter(
            by_rows[6].astype(jnp.bfloat16), "blk", scatter_dimension=0, tiled=True
        ).astype(jnp.float32),
        lax.psum_scatter(
            by_rows[7].astype(jnp.bfloat16), "blk", scatter_dimension=0, tiled=True
        ).astype(jnp.float32),
        lax.psum_scatter(
            by_rows[8].astype(jnp.bfloat16), "blk", scatter_dimension=0, tiled=True
        ).astype(jnp.float32),
    )
    return (
        outputs_f.astype(jnp.bfloat16)[None],
        input_grad[None],
        summed[0],
        summed[1],
        summed[2],
        summed[3],
        summed[4],
        summed[5],
        summed[6],
        summed[7],
        summed[8],
    )


MESH_IDS = pl.DeviceIdType.MESH
LANES = 128
HALF = 64
QUART = 32
DTF = 64
DTB = 64


def mm(left, right):
    return lax.dot_general(
        left, right, (((1,), (0,)), ((), ())), preferred_element_type=jnp.float32
    )


def mt(left, right):
    return lax.dot_general(
        left, right, (((1,), (1,)), ((), ())), preferred_element_type=jnp.float32
    )


def tm(left, right):
    return lax.dot_general(
        left, right, (((0,), (0,)), ((), ())), preferred_element_type=jnp.float32
    )


def window_at(value, start):
    aligned = min(max(start // LANES * LANES, 0), value.shape[1] - LANES)
    if aligned == start:
        return value[:, aligned : aligned + LANES]
    aligned = min(aligned, value.shape[1] - 2 * LANES)
    two = value[:, aligned : aligned + 2 * LANES]
    return pltpu.roll(two, (aligned - start) % (2 * LANES), 1)[:, :LANES]


def gather_lanes(value, block, first, source):
    lanes = lax.broadcasted_iota(jnp.int32, (1, LANES), 1)
    result = None
    for number in range(first // block, (first + LANES - 1) // block + 1):
        piece = window_at(value, source(number, first))
        begin = number * block - first
        result = piece if result is None else jnp.where(lanes < begin, result, piece)
    return result


class Wire:
    def __init__(self, send_sem, recv_sem, is_inner):
        self.send_sem, self.recv_sem, self.is_inner = send_sem, recv_sem, is_inner
        self.sends, self.slots = 0, 0
        self.sent = {None: [], True: [], False: []}

    def slot(self):
        self.slots += 1
        return self.slots - 1

    def copy(self, src, dst, peer, slot):
        self.sends += 1
        return pltpu.make_async_remote_copy(
            src_ref=src,
            dst_ref=dst,
            send_sem=self.send_sem.at[self.sends - 1],
            recv_sem=self.recv_sem.at[slot],
            device_id=peer,
            device_id_type=MESH_IDS,
        )

    def push(self, src, dst, peer, slot=None, inner=None):
        slot = self.slot() if slot is None else slot
        copy = self.copy(src, dst, peer, slot)
        self.sent[inner].append(copy)
        if inner is None:
            copy.start()
        else:
            pl.when(self.is_inner == inner)(copy.start)
        return slot

    def arrive(self, slot, dst, peer):
        pltpu.make_async_remote_copy(
            src_ref=dst,
            dst_ref=dst,
            send_sem=self.send_sem.at[0],
            recv_sem=self.recv_sem.at[slot],
            device_id=peer,
            device_id_type=MESH_IDS,
        ).wait_recv()

    def finish(self):
        for inner, copies in self.sent.items():

            def drain(copies=copies):
                for copy in copies:
                    copy.wait_send()

            if inner is None:
                drain()
            else:
                pl.when(self.is_inner == inner)(drain)


class Plane:
    def __init__(self, planes):
        dp, self.blk = lax.axis_index("dp"), lax.axis_index("blk")
        self.z, self.x = dp // 2, dp % 2
        self.dp = dp
        self.partner = self.z + 1 - 2 * (self.z % 2)
        self.other = planes // 2 - self.z // (planes // 2)
        self.outer = (planes - 1) * (self.other - 1)
        self.inner = ((self.z + 1) // 2) % 2
        self.order = (self.other, self.outer, self.partner, self.z)
        self.side = (self.z * 2 + (1 - self.x), self.blk)

    def at(self, plane):
        return (plane * 2 + self.x, self.blk)


class Spread:
    def __init__(self, wire, place, target, tail):
        self.wire, self.place, self.target = wire, place, target
        self.height, self.main = target.shape[1], target.shape[1] - tail

    def block(self, plane, column):
        return self.target.at[plane * 2 + column, 0 : self.main]

    def pair(self, plane):
        return self.target.at[pl.ds(plane * 2, 2), self.main : self.height]

    def along(self, own, slots):
        p = self.place
        self.wire.push(own, own, p.at(p.partner), slots[2], inner=False)
        self.wire.push(own, own, p.at(p.other), slots[0] + (1 - p.inner))

    def outward(self, own, slots):
        p = self.place
        self.wire.push(own, own, p.at(p.partner), slots[2], inner=True)

    def start(self):
        p, wire = self.place, self.wire
        self.z_slots = [wire.slot() for _ in range(3)]
        self.along(self.block(p.z, p.x), self.z_slots)

    def start_out(self):
        p = self.place
        self.outward(self.block(p.z, p.x), self.z_slots)

    def start_side(self):
        p, wire = self.place, self.wire
        self.x_slots = [wire.slot() for _ in range(4)]
        own = self.block(p.z, p.x)
        wire.push(own, own, p.side, self.x_slots[3])
        if self.main < self.height:
            self.out_slots = []
            self.rest_slot = wire.push(self.rest(p.x), self.rest(p.x), p.side)

    def tail(self):
        p, wire = self.place, self.wire
        rest = self.target.at[p.z * 2 + (1 - p.x), self.main : self.height]
        wire.arrive(self.rest_slot, rest, p.side)
        self.t_slots = [wire.slot() for _ in range(3)]
        self.along(self.pair(p.z), self.t_slots)

    def rest(self, column):
        p = self.place
        return self.target.at[p.z * 2 + column, self.main : self.height]

    def tail_out(self, own):
        p, wire = self.place, self.wire
        rest = self.rest(p.x if own else 1 - p.x)
        self.out_slots.append(wire.push(rest, rest, p.at(p.partner), inner=True))

    def relay(self, j, inner=None):
        p, wire = self.place, self.wire
        block = self.block(p.order[j], p.x)
        onward = wire.copy(block, block, p.side, self.x_slots[j])
        wire.sent[inner].append(onward)
        outward = None
        if j < 2 and inner is not False:
            outward = wire.copy(block, block, p.at(p.partner), self.z_slots[j])
            wire.sent[True].append(outward)

        def run():
            wire.arrive(self.z_slots[j], block, p.side)
            if outward is not None:
                if inner:
                    outward.start()
                else:
                    pl.when(wire.is_inner)(outward.start)
            onward.start()

        if inner is None:
            run()
        else:
            pl.when(wire.is_inner == inner)(run)

    def pass_tail(self, j):
        p, wire = self.place, self.wire
        pair = self.pair(p.order[j])
        copy = wire.copy(pair, pair, p.at(p.partner), self.t_slots[j])
        wire.sent[True].append(copy)

        @pl.when(wire.is_inner)
        def _():
            wire.arrive(self.t_slots[j], pair, p.side)
            copy.start()

    def settle_tail(self):
        p, wire = self.place, self.wire

        @pl.when(wire.is_inner)
        def _():
            wire.arrive(self.t_slots[2], self.pair(p.order[2]), p.side)

        @pl.when(jnp.logical_not(wire.is_inner))
        def _():
            for j in range(2):
                wire.arrive(self.t_slots[j], self.pair(p.order[j]), p.side)
            for slot, column in zip(self.out_slots, (p.x, 1 - p.x)):
                came = self.target.at[p.partner * 2 + column, self.main : self.height]
                wire.arrive(slot, came, p.side)

    def settle(self):
        p = self.place
        for j in range(4):
            self.wire.arrive(self.x_slots[j], self.block(p.order[j], 1 - p.x), p.side)


class Collect:
    def __init__(self, wire, place, buffers):
        self.wire, self.place = wire, place
        self.part, self.inbox, self.staged, self.landing = buffers[:4]
        self.height, self.main = self.part.shape[2], self.inbox.shape[1]
        self.split = self.main < self.height
        self.x_slots = [wire.slot() for _ in range(4)]
        self.z_slots = [wire.slot() for _ in range(4)]
        if self.split:
            self.t_landing, self.t_staged, self.t_cross, self.t_kept = buffers[4:]
            self.t_slots = [wire.slot() for _ in range(4)]

    def pair(self, plane):
        return self.part.at[:, plane, self.main : self.height]

    def send_side(self, j):
        p = self.place
        plane = p.order[j]
        self.wire.push(
            self.part.at[1 - p.x, plane, 0 : self.main],
            self.inbox.at[plane],
            p.side,
            self.x_slots[j],
        )

    def send(self, order=(1, 0, 2, 3)):
        for j in order:
            self.send_side(j)

    def send_tails(self):
        p = self.place
        for j in (1, 0, 2):
            self.wire.push(
                self.pair(p.order[j]),
                self.t_landing.at[j],
                p.at(p.partner),
                self.t_slots[j],
                inner=None if j == 2 else False,
            )

    def first(self, j):
        p, wire = self.place, self.wire
        plane = p.order[j]
        wire.arrive(self.x_slots[j], self.inbox.at[plane], p.side)
        both = self.part[p.x, plane, 0 : self.main].astype(jnp.float32)
        both = both + self.inbox[plane].astype(jnp.float32)
        self.staged[plane] = both.astype(jnp.bfloat16)
        wire.push(
            self.staged.at[plane],
            self.landing.at[j],
            p.at(p.partner),
            self.z_slots[j],
            inner=None if j == 2 else False,
        )

    def second(self, j):
        p, wire = self.place, self.wire
        plane = p.order[j]
        copy = wire.copy(self.staged.at[plane], self.landing.at[3], p.at(plane), self.z_slots[3])
        wire.sent[True].append(copy)

        @pl.when(wire.is_inner)
        def _():
            wire.arrive(self.z_slots[j], self.landing.at[j], p.side)
            both = self.staged[plane].astype(jnp.float32) + self.landing[j].astype(jnp.float32)
            self.staged[plane] = both.astype(jnp.bfloat16)
            copy.start()

    def second_tail(self, j):
        p, wire = self.place, self.wire
        plane = p.order[j]
        copy = wire.copy(self.t_staged.at[j], self.t_landing.at[3], p.at(plane), self.t_slots[3])
        wire.sent[True].append(copy)

        @pl.when(wire.is_inner)
        def _():
            wire.arrive(self.t_slots[j], self.t_landing.at[j], p.side)
            rest = self.part[:, plane, self.main : self.height].astype(jnp.float32)
            rest = rest + self.t_landing[j].astype(jnp.float32)
            self.t_staged[j] = rest.astype(jnp.bfloat16)
            copy.start()

    def tail(self):
        p, wire = self.place, self.wire
        for j in (2, 3):
            wire.arrive(self.t_slots[j], self.t_landing.at[j], p.side)

        def rest_of(column):
            rest = self.part[column, p.z, self.main : self.height].astype(jnp.float32)
            for j in (2, 3):
                rest = rest + self.t_landing[j, column].astype(jnp.float32)
            return rest

        self.t_kept[...] = rest_of(p.x)
        self.t_cross[0] = rest_of(1 - p.x).astype(jnp.bfloat16)
        self.cross_slot = wire.push(self.t_cross.at[0], self.t_cross.at[1], p.side)

    def total(self):
        p, wire = self.place, self.wire
        wire.arrive(self.x_slots[3], self.inbox.at[p.z], p.side)
        total = self.part[p.x, p.z, 0 : self.main].astype(jnp.float32)
        total = total + self.inbox[p.z].astype(jnp.float32)
        for j in (2, 3):
            wire.arrive(self.z_slots[j], self.landing.at[j], p.side)
            total = total + self.landing[j].astype(jnp.float32)
        if not self.split:
            return total
        wire.arrive(self.cross_slot, self.t_cross.at[1], p.side)
        rest = self.t_kept[...] + self.t_cross[1].astype(jnp.float32)
        return jnp.concatenate([total, rest], axis=0)


def fused(
    depth,
    lens,
    freq,
    xin_at,
    cot_at,
    in_at,
    gate_at,
    up_at,
    out_at,
    down_at,
    gain_a,
    bias_a,
    gain_b,
    bias_b,
    outputs_to,
    input_grad_to,
    g_in_to,
    g_mlp_to,
    g_out_to,
    g_down_to,
    cot,
    in_rows,
    gate_rows,
    up_rows,
    out_rows,
    outputs,
    input_grad,
    g_out,
    g_down,
    local_sem,
    xs,
    p_in,
    p_mlp,
    vectors_tab,
    r_in,
    r_mlp,
    s_out,
    w_in,
    w_value,
    w_gate,
    w_up,
    w_down,
    w_out,
    params,
    cos_tab,
    sin_tab,
    seg_tab,
    qm,
    kw,
    vw,
    prob,
    att,
    s_att,
    r_att,
    norm_one,
    hid,
    hs,
    gate_pre,
    up_pre,
    act,
    act_t,
    hs_t,
    s_mix,
    r_mix,
    t_mix,
    dres_two,
    dms,
    dgate,
    dup,
    s_dh,
    r_dh,
    t_dh,
    dres_one,
    s_da,
    r_da,
    acc_q,
    acc_k,
    acc_v,
    dj,
    s_ig,
    r_ig,
    t_ig,
    sum_in,
    sum_gate,
    sum_up,
    sum_down,
    b_out,
    rb_out,
    tb_out,
    sum_out,
    f_gate,
    s_gmlp,
    r_gmlp,
    s_gin,
    r_gin,
    send_sem,
    recv_sem,
):
    planes, cols = depth, 4
    tok = xin_at.shape[0]
    row_len = tok * cols
    place = Plane(planes)
    dp, blk = place.dp, place.blk
    bf16, f32 = jnp.bfloat16, jnp.float32

    row_of, core_of = blk // 2, blk % 2
    near_at = row_of * 2 + (1 - core_of)
    across_at = (1 - row_of) * 2 + core_of
    corner_at = (1 - row_of) * 2 + (1 - core_of)
    near, across = (dp, near_at), (dp, across_at)

    def lane(k):
        return (dp, (blk + k) % cols)

    def lane_from(k):
        return (blk + cols - k) % cols

    lanes = range(1, cols)
    local = []

    def move(source, target):
        copy = pltpu.make_async_copy(source, target, local_sem.at[len(local)])
        local.append(copy)
        copy.start()
        return copy

    xin = xs.at[blk]
    in_load = move(in_at, in_rows)
    out_load = move(out_at, out_rows)
    down_load = move(down_at, w_down.at[dp])
    x_load = move(xin_at, xin)
    gate_load = move(gate_at, gate_rows)
    up_load = move(up_at, up_rows)
    cot_load = move(cot_at, cot)
    wire = Wire(send_sem, recv_sem, place.inner == 1)
    barrier = pltpu.get_barrier_semaphore()
    peers = [place.side, place.at(place.partner), place.at(place.other)]
    peers = peers + [lane(k) for k in lanes]
    for peer in peers:
        pl.semaphore_signal(barrier, inc=1, device_id=peer, device_id_type=MESH_IDS)
    far = place.at(place.outer)

    @pl.when(place.inner == 1)
    def _():
        pl.semaphore_signal(barrier, inc=1, device_id=far, device_id_type=MESH_IDS)


    rows = 24
    width = xin_at.shape[1]
    lane_ids = lax.broadcasted_iota(jnp.int32, (1, LANES), 1)
    low_half = lane_ids < HALF
    head_width = width // cols
    vectors_tab[...] = jnp.zeros_like(vectors_tab)
    for number, vector in enumerate((gain_a, bias_a, gain_b, bias_b)):
        vectors_tab[number : number + 1, 0:rows] = vector[...].astype(f32)
    free_lane = lax.broadcasted_iota(jnp.int32, (8, LANES), 0) + HALF
    to_lane = jnp.where(
        free_lane == lax.broadcasted_iota(jnp.int32, (8, LANES), 1), 1.0, 0.0
    ).astype(bf16)
    vector_columns = tm(vectors_tab[...].astype(bf16), to_lane)[0:rows]
    in_load.wait()
    joined_rows = in_rows[...].astype(f32)
    for j in range(cols):
        starts = [kind * width + j * head_width for kind in range(3)]
        windows = [window_at(joined_rows, start) for start in starts]
        windows.append(
            jnp.where(
                low_half,
                window_at(joined_rows, starts[0] + LANES),
                window_at(joined_rows, starts[1] + LANES - HALF),
            )
        )
        windows.append(
            jnp.where(low_half, window_at(joined_rows, starts[2] + LANES), vector_columns)
        )
        packed = jnp.concatenate(windows, axis=1)
        p_in[j] = jnp.concatenate(
            [packed, jnp.zeros((8, packed.shape[1]), f32)], axis=0
        ).astype(bf16)
    out_load.wait()
    halved = [out_rows[:, n * width // 2 : (n + 1) * width // 2].astype(f32) for n in range(2)]
    s_out[blk, dp] = jnp.concatenate(halved, axis=0).astype(bf16)
    pl.semaphore_wait(barrier, len(peers) + place.inner)

    def to_lanes(source_of, target):
        return [wire.push(source_of((blk + k) % cols), target.at[blk], lane(k)) for k in lanes]

    def from_lanes(slots, target):
        for k, slot in zip(lanes, slots):
            wire.arrive(slot, target.at[lane_from(k)], lane(k))

    every = pl.ds(0, tok)

    def gather_start(own, target, cut=every):
        return [
            wire.push(own.at[cut], target.at[blk, cut], across),
            wire.push(own.at[cut], target.at[blk, cut], near),
        ]

    def gather_relay(slots, target, cut=every):
        came = target.at[across_at, cut]
        wire.arrive(slots[0], came, across)
        slots.append(wire.push(came, came, near))

    def gather_done(slots, target, cut=every):
        wire.arrive(slots[1], target.at[near_at, cut], near)
        wire.arrive(slots[2], target.at[corner_at, cut], near)

    def sum_start(part, inbox, cut=every):
        return [
            wire.push(part.at[corner_at, cut], inbox.at[0, cut], near),
            wire.push(part.at[near_at, cut], inbox.at[1, cut], near),
        ]

    def sum_relay(slots, part, inbox, staged, cut=every):
        wire.arrive(slots[0], inbox.at[0, cut], near)
        both = part[across_at, cut].astype(f32) + inbox[0, cut].astype(f32)
        staged[cut] = both.astype(bf16)
        slots.append(wire.push(staged.at[cut], inbox.at[2, cut], across))

    def sum_done(slots, part, inbox, cut=every):
        wire.arrive(slots[1], inbox.at[1, cut], near)
        total = part[blk, cut].astype(f32) + inbox[1, cut].astype(f32)
        wire.arrive(slots[2], inbox.at[2, cut], across)
        return total + inbox[2, cut].astype(f32)

    in_slots = to_lanes(lambda to: p_in.at[to], r_in)
    down_load.wait()
    tail = 0
    out_spread = Spread(wire, place, s_out.at[blk], 0)
    out_spread.start()
    out_spread.start_out()
    out_spread.start_side()
    down_spread = Spread(wire, place, w_down, DTF)
    down_spread.start()
    down_spread.start_out()
    down_spread.start_side()
    down_spread.tail_out(True)
    gate_load.wait()
    up_load.wait()
    units = gate_rows.shape[1] // cols
    unit_block = units // (planes * 2)
    for at, weight in ((0, gate_rows), (rows, up_rows)):
        whole = weight[...].astype(f32)
        for j in range(cols):
            packed = jnp.concatenate(
                [
                    gather_lanes(
                        whole,
                        unit_block,
                        n * LANES,
                        lambda ring_at, lane: lane + (cols - 1) * unit_block * ring_at + unit_block * j,
                    )
                    for n in range(units // LANES)
                ],
                axis=1,
            )
            p_mlp[j, at : at + rows] = packed.astype(bf16)
    mlp_slots = to_lanes(lambda to: p_mlp.at[to], r_mlp)
    x_load.wait()
    x_slots = gather_start(xin, xs)
    r_in[blk] = p_in[blk]
    r_mlp[blk] = p_mlp[blk]

    lengths = [lens[0, j] for j in range(lens.shape[1])]

    def layout(positions):
        segment = jnp.zeros_like(positions)
        begins = jnp.zeros_like(positions)
        bound = jnp.int32(0)
        for length in lengths:
            bound = bound + length
            passed = positions >= bound
            segment = segment + jnp.where(passed, 1, 0)
            begins = begins + jnp.where(passed, length, 0)
        return segment, positions - begins

    seg_rows, offsets = layout(lax.broadcasted_iota(jnp.int32, (row_len, LANES), 0))
    seg_tab[...] = seg_rows
    seg_key = layout(lax.broadcasted_iota(jnp.int32, (8, row_len), 1))[0][0:1]
    front = lane_ids % HALF < QUART
    angles = offsets.astype(f32) * freq[0:1]
    cos_tab[...] = jnp.cos(angles)
    sin_tab[...] = jnp.where(front, -1.0, 1.0) * jnp.sin(angles)

    def turn(window):
        return jnp.where(
            front, pltpu.roll(window, LANES - QUART, 1), pltpu.roll(window, QUART, 1)
        )

    from_lanes(in_slots, r_in)
    own_rows = cols * rows
    fold_rows = own_rows // 2
    heads_width = 4 * LANES

    def folded(last, tile):
        fold = jnp.where(low_half, last[0:fold_rows], pltpu.roll(last[fold_rows:], HALF, 1))
        chunks = [fold[n * 16 : (n + 1) * 16] for n in range(3)]
        chunks.append(jnp.concatenate([tile, jnp.zeros((8, LANES), f32)], axis=0))
        return jnp.concatenate(chunks, axis=1)

    def unfolded(below):
        fold = jnp.concatenate([below[:, n * LANES : (n + 1) * LANES] for n in range(3)], axis=0)
        return jnp.concatenate([fold, pltpu.roll(fold, HALF, 1)], axis=0), below[0:8, 3 * LANES :]

    gathered = jnp.concatenate(
        [r_in[j, 0:rows, :].astype(f32) for j in range(cols)], axis=0
    )
    last = gathered[:, heads_width:]
    padded = jnp.concatenate([last, jnp.zeros((LANES - own_rows, LANES), f32)], axis=0)
    w_in[dp] = jnp.concatenate(
        [gathered[:, :heads_width], folded(last, mt(to_lane, padded.astype(bf16)))], axis=0
    ).astype(bf16)
    in_spread = Spread(wire, place, w_in, tail)
    in_spread.start()
    in_spread.start_out()
    in_spread.start_side()
    from_lanes(mlp_slots, r_mlp)
    mlp_own = [r_mlp[j].astype(f32) for j in range(cols)]
    w_gate[dp] = jnp.concatenate([part[0:rows] for part in mlp_own], axis=0).astype(bf16)
    w_up[dp] = jnp.concatenate([part[rows:] for part in mlp_own], axis=0).astype(bf16)
    gate_spread = Spread(wire, place, w_gate, tail)
    up_spread = Spread(wire, place, w_up, tail)
    gate_spread.start()
    gate_spread.start_side()
    up_spread.start()
    out_spread.relay(2)
    for spread in (out_spread, down_spread):
        spread.relay(0, inner=True)
        spread.relay(1, inner=True)
    in_spread.relay(2)
    out_spread.relay(0, inner=False)
    out_spread.relay(1, inner=False)
    in_spread.relay(0)
    down_spread.relay(2)
    in_spread.relay(1)
    up_spread.start_side()
    gate_spread.start_out()
    up_spread.start_out()
    down_spread.tail()
    gate_spread.relay(0, inner=True)
    gate_spread.relay(1, inner=True)
    gather_relay(x_slots, xs)
    out_spread.settle()
    shards_here = pl.ds(0, planes * 2)
    out_lanes = gather_start(s_out.at[blk], s_out, shards_here)
    gate_spread.relay(2)
    up_spread.relay(2)
    gather_done(x_slots, xs)
    in_spread.settle()

    group = 2
    chunk = group * tok

    tiles = []
    for d in range(planes * 2):
        values, tile = unfolded(w_in[d, own_rows:, :].astype(f32))
        w_value[d] = jnp.where(low_half, values, 0.0).astype(bf16)
        tiles.append(tile)

    def project(step, carry):
        start = pl.multiple_of(step * chunk, chunk)
        here = pl.ds(start, chunk)
        tokens = xs[pl.ds(step * group, group)].reshape(chunk, width)
        joined = mm(tokens, w_in[:, 0:own_rows, :].reshape(width, heads_width))
        cosine, sine = cos_tab[here, :], sin_tab[here, :]

        def rotate(number):
            window = joined[:, number * LANES : (number + 1) * LANES]
            return window * cosine + turn(window) * sine

        scale = HALF ** -0.5
        queries = rotate(0).astype(bf16).astype(f32) * scale
        qm[0, here, :] = jnp.where(low_half, queries, 0.0).astype(bf16)
        qm[1, here, :] = jnp.where(low_half, 0.0, queries).astype(bf16)
        kw[0, here, :] = rotate(1).astype(bf16)
        vw[0, here, :] = joined[:, 2 * LANES : 3 * LANES].astype(bf16)
        both = rotate(3)
        qm[2, here, :] = jnp.where(low_half, both.astype(bf16).astype(f32) * scale, 0.0).astype(bf16)
        kw[1, here, :] = jnp.where(low_half, pltpu.roll(both, HALF, 1), 0.0).astype(bf16)
        vw[1, here, :] = mm(tokens, w_value[...].reshape(width, LANES)).astype(bf16)
        return carry

    lax.fori_loop(0, cols // group, project, 0)

    def attend(head):
        window = head // 2

        def step_fn(step, carry):
            here = pl.ds(pl.multiple_of(step * chunk, chunk), chunk)
            scores = mt(qm[head, here, :], kw[window])
            allowed = seg_tab[here, :][:, 0:1] == seg_key
            scores = jnp.where(allowed, scores, NEG)
            top = jnp.max(scores, axis=1, keepdims=True)
            raised = jnp.exp(scores - top)
            total = jnp.sum(raised, axis=1, keepdims=True)
            prob_low = (raised * (1.0 / total)).astype(bf16)
            prob[head, here, :] = prob_low
            mixed = mm(prob_low, vw[window])
            if head == 1:
                mixed = jnp.where(low_half, att[0, here, :], mixed)
            att[window, here, :] = mixed
            return carry

        lax.fori_loop(0, row_len // chunk, step_fn, 0)

    up_spread.relay(0, inner=True)
    attend(0)
    attend(1)
    up_spread.relay(1, inner=True)
    attend(2)
    last_segment = lens.shape[1] - 1
    for j in range(cols):
        here = slice(j * tok, (j + 1) * tok)
        kept = seg_tab[here, :] < last_segment
        s_att[j, :, 0:LANES] = jnp.where(kept, att[0, here, :], 0.0).astype(bf16)
        s_att[j, :, LANES : 2 * LANES] = jnp.where(kept, att[1, here, :], 0.0).astype(bf16)
    att_slots = to_lanes(lambda to: s_att.at[to], r_att)
    r_att[blk] = s_att[blk]

    down_spread.tail_out(False)
    gather_relay(out_lanes, s_out, shards_here)
    gate_spread.relay(0, inner=False)
    gate_spread.relay(1, inner=False)
    for j in range(2):
        down_spread.pass_tail(j)
    gather_done(out_lanes, s_out, shards_here)
    shards = planes * 2 * cols
    per_quarter = shards // cols
    head_rows = per_quarter * rows
    for quarter in range(cols):
        slots = [
            s_out[s % cols, s // cols].astype(f32)
            for s in range(quarter * per_quarter, (quarter + 1) * per_quarter)
        ]
        w_out[quarter, 0:head_rows, :] = jnp.concatenate(
            [
                jnp.concatenate([slot[n * rows : (n + 1) * rows] for slot in slots], axis=0)
                for n in range(2)
            ],
            axis=1,
        ).astype(bf16)
        w_out[quarter, head_rows:, :] = jnp.zeros(
            (w_out.shape[1] - head_rows, width), bf16
        )
    for n in range(width // LANES):
        first = n * LANES
        result = None
        for d in range(first // own_rows, (first + LANES - 1) // own_rows + 1):
            begin = d * own_rows - first
            piece = pltpu.roll(tiles[d], begin % LANES, 1)
            result = piece if result is None else jnp.where(lane_ids < begin, result, piece)
        params[:, first : first + LANES] = result
    gain_one, bias_one = params[0:1, :], params[1:2, :]
    gain_two, bias_two = params[2:3, :], params[3:4, :]

    def normalize(residual):
        centered = residual - jnp.mean(residual, axis=1, keepdims=True)
        variance = jnp.mean(centered * centered, axis=1, keepdims=True)
        spread = lax.rsqrt(variance + EPS)
        return centered * spread, spread

    def normalize_back(grad, normal, spread, gain):
        inner = grad * gain
        mean_inner = jnp.mean(inner, axis=1, keepdims=True)
        mean_both = jnp.mean(inner * normal, axis=1, keepdims=True)
        return (inner - mean_inner - normal * mean_both) * spread

    def column_sum(value):
        return jnp.sum(value, axis=0, keepdims=True)

    from_lanes(att_slots, r_att)
    branch = mm(r_att[0], w_out[0])
    for quarter in range(1, cols):
        branch = branch + mm(r_att[quarter], w_out[quarter])
    normal, spread_one = normalize(xin[...].astype(f32) + branch)
    hidden = normal * gain_one + bias_one
    hs[blk] = hidden.astype(bf16)
    hid_slots = gather_start(hs.at[blk], hs)
    norm_one[...] = normal
    hid[...] = hidden
    up_spread.relay(0, inner=False)
    up_spread.relay(1, inner=False)
    down_spread.relay(0, inner=False)
    down_spread.relay(1, inner=False)
    gather_relay(hid_slots, hs)
    gate_spread.settle()
    gather_done(hid_slots, hs)

    wide = 256
    strips = units // wide

    def each_strip(body):
        def step_fn(step, carry):
            body(pl.ds(pl.multiple_of(step * wide, wide), wide))
            return carry

        lax.fori_loop(0, strips, step_fn, 0)

    def expand_gate(here):
        tokens = hs[...].reshape(row_len, width)
        gate_pre[:, here] = mm(tokens, w_gate[:, :, here].reshape(width, wide))

    def expand_up(here):
        tokens = hs[...].reshape(row_len, width)
        up = mm(tokens, w_up[:, :, here].reshape(width, wide))
        gate = gate_pre[:, here]
        up_pre[:, here] = up
        act[:, here] = (gate / (1.0 + jnp.exp(-gate)) * up).astype(bf16)

    each_strip(expand_gate)
    hs_t[...] = hs[...].reshape(row_len, width).T
    up_spread.settle()
    each_strip(expand_up)
    down_spread.settle()
    down_spread.settle_tail()

    def contract(step, carry):
        here = pl.ds(pl.multiple_of(step * wide, wide), wide)
        mixed = mm(act[...], w_down[:, :, here].reshape(units, wide))
        s_mix[:, :, here] = mixed.reshape(cols, tok, wide).astype(bf16)
        return carry

    lax.fori_loop(0, width // wide, contract, 0)
    pieces = 4
    cot_load.wait()
    halves = [pl.ds(n * tok // pieces, tok // pieces) for n in range(pieces)]
    mix_slots = [sum_start(s_mix, r_mix, cut) for cut in halves]
    for slots, cut in zip(mix_slots, halves):
        sum_relay(slots, s_mix, r_mix, t_mix, cut)
    act_t[...] = act[...].T
    second_gain, second_bias, dm_slots = 0.0, 0.0, []
    for slots, cut in zip(mix_slots, halves):
        mlp_out = sum_done(slots, s_mix, r_mix, cut)
        normal, spread_two = normalize(hid[cut, :] + mlp_out)
        grad = cot[cut, :].astype(f32)
        d_two = normalize_back(grad, normal, spread_two, gain_two)
        dms[blk, cut] = d_two.astype(bf16)
        dm_slots.append(gather_start(dms.at[blk], dms, cut))
        dres_two[cut, :] = d_two
        outputs[cut, :] = (normal * gain_two + bias_two).astype(bf16)
        second_gain = second_gain + column_sum(grad * normal)
        second_bias = second_bias + column_sum(grad)
    writes = [move(outputs, outputs_to)]
    for slots, cut in zip(dm_slots, halves):
        gather_relay(slots, dms, cut)
    for slots, cut in zip(dm_slots, halves):
        gather_done(slots, dms, cut)

    down_sum = Collect(wire, place, sum_down)
    gate_sum = Collect(wire, place, sum_gate)
    up_sum = Collect(wire, place, sum_up)
    in_sum = Collect(wire, place, sum_in)
    out_sum = Collect(wire, place, sum_out)
    half = 4

    def fill_parts(part, left_of, right, more=lambda product, here: product):
        height = part.shape[2]

        def step_fn(step, carry):
            here = pl.ds(pl.multiple_of(step * half * height, LANES), half * height)
            product = more(mm(left_of(here), right()), here)
            for j in range(half):
                part[j % 2, step * (half // 2) + j // 2] = product[
                    j * height : (j + 1) * height
                ].astype(bf16)
            return carry

        lax.fori_loop(0, planes * 2 // half, step_fn, 0)

    fill_parts(down_sum.part, lambda here: act_t[here, :], lambda: dms[...].reshape(row_len, width))
    down_sum.send_tails()
    down_sum.send((1, 0))

    block = w_down.shape[1]

    def active_grads(step, carry):
        here = pl.ds(pl.multiple_of(step * half * block, LANES), half * block)
        d_active = mt(
            dms[...].reshape(row_len, width),
            w_down[pl.ds(step * half, half)].reshape(half * block, width),
        )
        gate, up = gate_pre[:, here], up_pre[:, here]
        sg = 1.0 / (1.0 + jnp.exp(-gate))
        dgate[:, here] = (d_active * up * sg * (1.0 + gate * (1.0 - sg))).astype(bf16)
        dup[:, here] = (d_active * gate * sg).astype(bf16)
        return carry

    lax.fori_loop(0, planes * 2 // half, active_grads, 0)
    block = w_gate.shape[1]

    def hidden_rows(here):
        return hs_t[here, :]

    fill_parts(gate_sum.part, hidden_rows, lambda: dgate[...])
    gate_sum.send()
    def hidden_grads(step, carry):
        here = pl.ds(pl.multiple_of(step * half * block, LANES), half * block)
        those = pl.ds(step * half, half)
        mixed = mt(dgate[...], w_gate[those].reshape(half * block, units)) + mt(
            dup[...], w_up[those].reshape(half * block, units)
        )
        s_dh[:, :, here] = mixed.reshape(cols, tok, half * block).astype(bf16)
        return carry

    lax.fori_loop(0, planes * 2 // half, hidden_grads, 0)
    dh_slots = sum_start(s_dh, r_dh)

    sum_relay(dh_slots, s_dh, r_dh, t_dh)
    fill_parts(up_sum.part, hidden_rows, lambda: dup[...])
    up_sum.send((1, 0))
    down_sum.first(1)
    down_sum.first(0)
    d_hidden = dres_two[...] + sum_done(dh_slots, s_dh, r_dh)
    normal = norm_one[...]
    first_gain = column_sum(d_hidden * normal)
    first_bias = column_sum(d_hidden)
    d_one = normalize_back(d_hidden, normal, spread_one, gain_one)
    dres_one[...] = d_one
    d_branch = d_one.astype(bf16)
    mine = pl.ds(pl.multiple_of(blk * tok, tok), tok)
    kept = seg_tab[mine, :][:, 0:1] < last_segment
    for quarter in range(cols):
        pulled = mt(d_branch, w_out[quarter]).astype(bf16).astype(f32)
        s_da[quarter] = jnp.where(kept, pulled, 0.0).astype(bf16)
    da_slots = to_lanes(lambda to: s_da.at[to], r_da)
    r_da[blk] = s_da[blk]

    params[...] = jnp.concatenate(
        [first_gain, first_bias, second_gain, second_bias, jnp.zeros((4, width), f32)], axis=0
    )
    for quarter in range(cols):
        product = tm(r_att[quarter], d_branch)
        for t in range(per_quarter):
            s = quarter * per_quarter + t
            owner_dp = s // cols
            mine_rows = product[t * rows : (t + 1) * rows]
            halved = [mine_rows[:, n * width // 2 : (n + 1) * width // 2] for n in range(2)]
            b_out[s % cols, owner_dp % 2, owner_dp // 2] = jnp.concatenate(
                halved, axis=0
            ).astype(bf16)
    both_sides = pl.ds(0, 2)
    out_blk = sum_start(b_out, rb_out, both_sides)

    gate_sum.first(1)
    sum_relay(out_blk, b_out, rb_out, tb_out, both_sides)
    down_sum.second_tail(1)
    down_sum.second(1)
    gate_sum.first(0)
    from_lanes(da_slots, r_da)
    def attend_back(head):
        window = head // 2
        fresh = head != 1

        def step_fn(step, carry):
            here = pl.ds(pl.multiple_of(step * chunk, chunk), chunk)
            d_out = r_da[pl.ds(step * group, group), :, window * LANES : (window + 1) * LANES]
            d_out = d_out.reshape(chunk, LANES).astype(f32)
            if head == 0:
                d_out = jnp.where(low_half, d_out, 0.0)
            if head == 1:
                d_out = jnp.where(low_half, 0.0, d_out)
            d_low = d_out.astype(bf16)
            delta = jnp.sum(d_out * att[window, here, :], axis=1, keepdims=True)
            prob_low = prob[head, here, :]
            d_prob = mt(d_low, vw[window])
            d_score = (prob_low.astype(f32) * (d_prob - delta)).astype(bf16)
            d_query = mm(d_score, kw[window]) * (HALF ** -0.5)
            if head == 1:
                d_query = jnp.where(low_half, acc_q[0, here, :], d_query)
            acc_q[window, here, :] = d_query
            d_key = tm(d_score, qm[head, here, :])
            d_value = tm(prob_low, d_low)
            if fresh:

                @pl.when(step == 0)
                def _():
                    acc_k[window] = d_key
                    acc_v[window] = d_value

                @pl.when(step != 0)
                def _():
                    acc_k[window] = acc_k[window] + d_key
                    acc_v[window] = acc_v[window] + d_value
            else:
                acc_k[window] = acc_k[window] + d_key
                acc_v[window] = acc_v[window] + d_value
            return carry

        lax.fori_loop(0, row_len // chunk, step_fn, 0)

    attend_back(0)
    gate_sum.first(2)
    down_sum.second_tail(0)
    down_sum.second(0)
    attend_back(1)
    attend_back(2)

    cosine, sine = cos_tab[...], sin_tab[...]

    def rotate_back(vector):
        vector = vector.astype(bf16).astype(f32)
        return (vector * cosine - turn(vector) * sine).astype(bf16)

    dj[:, 0:LANES] = rotate_back(acc_q[0])
    dj[:, LANES : 2 * LANES] = rotate_back(acc_k[0])
    dj[:, 2 * LANES : 3 * LANES] = acc_v[0].astype(bf16)
    dj[:, 3 * LANES : 4 * LANES] = rotate_back(acc_q[1] + pltpu.roll(acc_k[1], HALF, 1))
    dj[:, 4 * LANES : 5 * LANES] = acc_v[1].astype(bf16)


    def input_parts(step, carry):
        here = pl.ds(pl.multiple_of(step * half * own_rows, LANES), half * own_rows)
        product = tm(xs[:, :, here].reshape(row_len, half * own_rows), dj[...])
        vectors = params[:, here]
        for j in range(half):
            mine_rows = product[j * own_rows : (j + 1) * own_rows]
            tile = jnp.where(lane_ids < own_rows, window_at(vectors, j * own_rows), 0.0)
            in_sum.part[j % 2, step * (half // 2) + j // 2] = jnp.concatenate(
                [mine_rows[:, :heads_width], folded(mine_rows[:, heads_width:], tile)], axis=0
            ).astype(bf16)
        return carry

    lax.fori_loop(0, planes * 2 // half, input_parts, 0)

    in_sum.send((1, 0))
    def input_grads(step, carry):
        here = pl.ds(pl.multiple_of(step * half * block, LANES), half * block)
        those = pl.ds(step * half, half)
        mixed = mt(dj[:, 0:heads_width], w_in[those, 0:own_rows].reshape(half * block, heads_width))
        mixed = mixed + mt(dj[:, heads_width:], w_value[those].reshape(half * block, LANES))
        s_ig[:, :, here] = mixed.reshape(cols, tok, half * block).astype(bf16)
        return carry

    lax.fori_loop(0, planes * 2 // half, input_grads, 0)
    ig_slots = sum_start(s_ig, r_ig)

    up_sum.first(1)
    gate_sum.second(1)
    sum_relay(ig_slots, s_ig, r_ig, t_ig)
    out_sum.part[...] = sum_done(out_blk, b_out, rb_out, both_sides).astype(bf16)
    out_sum.send((1, 0,))
    up_sum.send((2,))
    in_sum.send((2,))
    up_sum.send((3,))
    in_sum.send((3,))
    down_sum.send((2,))
    out_sum.send((2,))
    out_sum.send((3,))
    down_sum.send((3,))
    down_sum.tail()
    up_sum.first(0)
    gate_sum.second(0)
    in_sum.first(1)
    up_sum.second(1)
    in_sum.first(0)
    out_sum.first(1)
    out_sum.first(0)
    up_sum.second(0)
    in_sum.second(1)
    up_sum.first(2)
    grad_in = dres_one[...] + sum_done(ig_slots, s_ig, r_ig)
    input_grad[...] = grad_in.astype(bf16)
    writes.append(move(input_grad, input_grad_to))
    in_sum.second(0)
    out_sum.second(1)
    out_sum.second(0)
    in_sum.first(2)
    f_gate[...] = gate_sum.total()
    up_total = up_sum.total()
    gate_total = f_gate[...]
    for j in range(cols):
        here = slice(j * rows, (j + 1) * rows)
        s_gmlp[j] = jnp.concatenate([gate_total[here], up_total[here]], axis=0).astype(bf16)
    gmlp_slots = to_lanes(lambda to: s_gmlp.at[to], r_gmlp)
    r_gmlp[blk] = s_gmlp[blk]
    out_sum.first(2)
    down_sum.first(2)
    in_total = in_sum.total()
    values, tile = unfolded(in_total[own_rows:])
    columns = tm(tile.astype(bf16), to_lane)[0:own_rows]
    in_total = jnp.concatenate(
        [in_total[0:own_rows], jnp.where(low_half, values, columns)], axis=1
    )
    for j in range(cols):
        s_gin[j] = jnp.concatenate(
            [in_total[j * rows : (j + 1) * rows], jnp.zeros((8, in_total.shape[1]), f32)], axis=0
        ).astype(bf16)
    gin_slots = to_lanes(lambda to: s_gin.at[to], r_gin)
    r_gin[blk] = s_gin[blk]
    g_out[...] = out_sum.total()
    writes.append(move(g_out, g_out_to))
    g_down[...] = down_sum.total()
    writes.append(move(g_down, g_down_to))
    from_lanes(gmlp_slots, r_gmlp)
    writes.append(move(r_gmlp, g_mlp_to))
    from_lanes(gin_slots, r_gin)
    writes.append(move(r_gin, g_in_to))
    wire.finish()
    for write in writes:
        write.wait()


def unpack(
    rows,
    block,
    outputs,
    input_grad,
    g_in,
    g_mlp,
    g_out,
    g_down,
    outputs_to,
    input_grad_to,
    in_to,
    out_to,
    gate_to,
    up_to,
    down_to,
    *vectors_to,
):
    f32 = jnp.float32
    cols = g_in.shape[0]
    width = outputs.shape[1]
    outputs_to[0] = outputs[...]
    input_grad_to[0] = input_grad[...]
    down_to[...] = g_down[...]
    for n in range(2):
        out_to[:, n * width // 2 : (n + 1) * width // 2] = g_out[n * rows : (n + 1) * rows, :]
    low_half = lax.broadcasted_iota(jnp.int32, (1, LANES), 1) < HALF
    joined = [g_in[j].astype(f32)[0:rows] for j in range(cols)]
    vectors = joined[0][:, 4 * LANES :]
    for j in range(1, cols):
        vectors = vectors + joined[j][:, 4 * LANES :]
    vectors = jnp.concatenate([vectors, jnp.zeros((LANES - rows, LANES), f32)], axis=0).T
    for number, vector_to in enumerate(vectors_to):
        vector_to[...] = vectors[HALF + number, 0:rows]
    single_at = ((3, 0), (3, 1), (4, 0))

    def half(kind, number, want):
        owner, part = number // 3, number % 3
        window, at = (kind, part) if part < 2 else single_at[kind]
        value = joined[owner][:, window * LANES : (window + 1) * LANES]
        return value if at == want else pltpu.roll(value, HALF, 1)

    for kind in range(3):
        for n in range(width // LANES):
            at = kind * width + n * LANES
            in_to[:, at : at + LANES] = jnp.where(
                low_half, half(kind, 2 * n, 0), half(kind, 2 * n + 1, 1)
            )
    lanes = lax.broadcasted_iota(jnp.int32, (1, LANES), 1)
    mlp = [g_mlp[j].astype(f32) for j in range(cols)]
    for first_row, target in ((0, gate_to), (rows, up_to)):
        parts = [part[first_row : first_row + rows] for part in mlp]
        for n in range(target.shape[1] // LANES):
            first = n * LANES
            result = None
            for number in range(first // block, (first + LANES - 1) // block + 1):
                ring_at, owner = number // cols, number % cols
                piece = window_at(parts[owner], ring_at * block + first - number * block)
                begin = number * block - first
                result = piece if result is None else jnp.where(lanes < begin, result, piece)
            target[:, first : first + LANES] = result


def fast_shards(
    depth,
    inputs,
    doc_lengths,
    project_in,
    project_out,
    gate_weight,
    up_weight,
    down_weight,
    first_gain,
    first_bias,
    second_gain,
    second_bias,
    cotangent,
):
    cols = 4
    tok, width = inputs.shape[1:]
    rows = project_in.shape[0]
    ff = gate_weight.shape[1]
    ring = depth * 2
    row_len = tok * cols
    units = ff // cols
    block = units // ring
    head_width = width // cols
    in_width = 5 * LANES
    bf16, f32 = jnp.bfloat16, jnp.float32

    lane_ids = np.arange(LANES) % QUART
    freq = jnp.asarray(
        np.broadcast_to(BASE ** (-2.0 * lane_ids / HALF), (8, LANES)).astype(np.float32)
    )

    def scratch(*shape, kind=bf16):
        return pltpu.VMEM(shape, kind)

    def sums(height, across, tail=0):
        main = height - tail
        buffers = [
            scratch(2, depth, height, across),
            scratch(depth, main, across),
            scratch(depth, main, across),
            scratch(4, main, across),
        ]
        if tail:
            buffers = buffers + [
                scratch(4, 2, tail, across),
                scratch(2, 2, tail, across),
                scratch(2, tail, across),
                scratch(tail, across, kind=f32),
            ]
        return tuple(buffers)

    stacked = scratch(cols, tok, width)
    heads = 3
    buffers = [
        scratch(tok, width),
        scratch(rows, 3 * width),
        scratch(rows, ff),
        scratch(rows, ff),
        scratch(rows, width),
        scratch(tok, width),
        scratch(tok, width),
        scratch(2 * rows, width // 2, kind=f32),
        scratch(block, width, kind=f32),
        pltpu.SemaphoreType.DMA((16,)),
        stacked,
        scratch(cols, 32, in_width),
        scratch(cols, 2 * rows, units),
        scratch(8, LANES, kind=f32),
        scratch(cols, 32, in_width),
        scratch(cols, 2 * rows, units),
        scratch(cols, ring, 2 * rows, width // 2),
        scratch(ring, cols * rows + 16, 4 * LANES),
        scratch(ring, cols * rows, LANES),
        scratch(ring, cols * rows, units),
        scratch(ring, cols * rows, units),
        scratch(ring, block, width),
        scratch(cols, 2 * LANES, width),
        scratch(8, width, kind=f32),
        scratch(row_len, LANES, kind=f32),
        scratch(row_len, LANES, kind=f32),
        scratch(row_len, LANES, kind=jnp.int32),
        scratch(heads, row_len, LANES),
        scratch(2, row_len, LANES),
        scratch(2, row_len, LANES),
        scratch(heads, row_len, row_len),
        scratch(2, row_len, LANES, kind=f32),
        scratch(cols, tok, 2 * LANES),
        scratch(cols, tok, 2 * LANES),
        scratch(tok, width, kind=f32),
        scratch(tok, width, kind=f32),
        stacked,
        scratch(row_len, units, kind=f32),
        scratch(row_len, units, kind=f32),
        scratch(row_len, units),
        scratch(units, row_len),
        scratch(width, row_len),
        stacked,
        scratch(3, tok, width),
        scratch(tok, width),
        scratch(tok, width, kind=f32),
        stacked,
        scratch(row_len, units),
        scratch(row_len, units),
        stacked,
        scratch(3, tok, width),
        scratch(tok, width),
        scratch(tok, width, kind=f32),
        scratch(cols, tok, 2 * LANES),
        scratch(cols, tok, 2 * LANES),
        scratch(2, row_len, LANES, kind=f32),
        scratch(2, row_len, LANES, kind=f32),
        scratch(2, row_len, LANES, kind=f32),
        scratch(row_len, in_width),
        stacked,
        scratch(3, tok, width),
        scratch(tok, width),
        sums(cols * rows + 16, 4 * LANES),
        sums(cols * rows, units),
        sums(cols * rows, units),
        sums(block, width, DTB),
        scratch(cols, 2, depth, 2 * rows, width // 2),
        scratch(3, 2, depth, 2 * rows, width // 2),
        scratch(2, depth, 2 * rows, width // 2),
        sums(2 * rows, width // 2, 0),
        scratch(cols * rows, units, kind=f32),
        scratch(cols, 2 * rows, units),
        scratch(cols, 2 * rows, units),
        scratch(cols, 32, in_width),
        scratch(cols, 32, in_width),
        pltpu.SemaphoreType.DMA((240,)),
        pltpu.SemaphoreType.DMA((240,)),
    ]
    vmem = pl.BlockSpec(memory_space=pltpu.VMEM)
    anywhere = pl.BlockSpec(memory_space=pl.ANY)
    tokens = row_len * width
    outputs, input_grad, g_in, g_mlp, g_out, g_down = pl.pallas_call(
        functools.partial(fused, depth),
        out_shape=(
            jax.ShapeDtypeStruct((tok, width), bf16),
            jax.ShapeDtypeStruct((tok, width), bf16),
            jax.ShapeDtypeStruct((cols, 32, in_width), bf16),
            jax.ShapeDtypeStruct((cols, 2 * rows, units), bf16),
            jax.ShapeDtypeStruct((2 * rows, width // 2), f32),
            jax.ShapeDtypeStruct((block, width), f32),
        ),
        in_specs=[pl.BlockSpec(memory_space=pltpu.SMEM), vmem] + [anywhere] * 7 + [vmem] * 4,
        out_specs=(anywhere,) * 6,
        scratch_shapes=buffers,
        compiler_params=pltpu.CompilerParams(
            collective_id=0, has_side_effects=True, vmem_limit_bytes=60 * 2**20
        ),
        cost_estimate=pl.CostEstimate(
            flops=6 * tokens * (3 * units + 4 * head_width),
            bytes_accessed=8 * 2**20,
            transcendentals=3 * row_len * row_len,
        ),
        name="layer",
    )(
        doc_lengths,
        freq,
        inputs[0],
        cotangent[0],
        project_in,
        gate_weight,
        up_weight,
        project_out,
        down_weight,
        first_gain[None],
        first_bias[None],
        second_gain[None],
        second_bias[None],
    )

    vector = jax.ShapeDtypeStruct((rows,), f32)
    return pl.pallas_call(
        functools.partial(unpack, rows, block),
        out_shape=(
            jax.ShapeDtypeStruct((1, tok, width), bf16),
            jax.ShapeDtypeStruct((1, tok, width), bf16),
            jax.ShapeDtypeStruct((rows, 3 * width), f32),
            jax.ShapeDtypeStruct((rows, width), f32),
            jax.ShapeDtypeStruct((rows, ff), f32),
            jax.ShapeDtypeStruct((rows, ff), f32),
            jax.ShapeDtypeStruct((block, width), f32),
            vector,
            vector,
            vector,
            vector,
        ),
        in_specs=[vmem] * 6,
        out_specs=(vmem,) * 11,
        name="unpack",
    )(outputs, input_grad, g_in, g_mlp, g_out, g_down)


def pick(sizes):
    def chosen(*args):
        tok, width = args[0].shape[1:]
        ring, cols = sizes["dp"], sizes["blk"]
        fits = (
            ring == 8
            and cols == 4
            and tok == LANES
            and HEADS == 3 * cols
            and width == HEADS * HALF
            and args[2].shape[0] == 24
            and args[4].shape[1] == 4 * width
        )
        if fits:
            return fast_shards(ring // 2, *args)
        return shards(*args)

    return chosen


def solution(mesh):
    placed = (
        P("dp", "blk", None),
        P("dp", None),
        P(("dp", "blk"), None),
        P(("dp", "blk"), None),
        P(("dp", "blk"), None),
        P(("dp", "blk"), None),
        P(("dp", "blk"), None),
        P(("dp", "blk")),
        P(("dp", "blk")),
        P(("dp", "blk")),
        P(("dp", "blk")),
        P("dp", "blk", None),
    )
    return jax.shard_map(
        pick(dict(mesh.shape)),
        mesh=mesh,
        in_specs=placed,
        out_specs=(
            P("dp", "blk", None),
            P("dp", "blk", None),
            P(("dp", "blk"), None),
            P(("dp", "blk"), None),
            P(("dp", "blk"), None),
            P(("dp", "blk"), None),
            P(("dp", "blk"), None),
            P(("dp", "blk")),
            P(("dp", "blk")),
            P(("dp", "blk")),
            P(("dp", "blk")),
        ),
        check_vma=False,
    )
```
